32 devices in a mesh: dp: 8 (over z, y), fsdp: 4 (over x, core).
Axes of the slice: x: 2, y: 2, z: 4, core: 2. Of those that a mesh axis runs over, the one named last changes fastest.
Arguments:
- inputs: bfloat16 [32, 784, 384], P(('dp', 'fsdp')), may hold values from -6 to 6
- items: int32 [32, 784], P(('dp', 'fsdp')), may hold values from 0 to 5, never falling along the last dimension, each value on 1 to 320 neighbouring positions
- routes: int32 [2, 32, 784], P(None, ('dp', 'fsdp')), may hold values from 0 to 1, as said below
- slots: int32 [2, 32, 784], P(None, ('dp', 'fsdp')), may hold values from 0 to 255, as said below
- cotangent: bfloat16 [32, 784, 384], P(('dp', 'fsdp')), may hold values from -6 to 6
- params: float32 [2, 2961408], P(None, ('dp', 'fsdp'))
- momentum: float32 [2, 2961408], P(None, ('dp', 'fsdp'))
- average: float32 [2, 2961408], P(None, ('dp', 'fsdp'))
Outputs:
- outputs: bfloat16 [32, 784, 384], P(('dp', 'fsdp'))
- input_grad: float32 [32, 784, 384], P(('dp', 'fsdp'))
- new_params: float32 [2, 2961408], P(None, ('dp', 'fsdp'))
- new_momentum: float32 [2, 2961408], P(None, ('dp', 'fsdp'))
- new_average: float32 [2, 2961408], P(None, ('dp', 'fsdp'))
- vector_grads: float32 [2, 9, 384], replicated
The draws below stay inside these ranges and needn't reach their ends.
Inputs may be any that keep to these rules, and one draw needn't show every extreme that they name: `routes`: in every half canvas (392 consecutive patches of one canvas) of each block no expert is named by more than 256 patches, and one expert by exactly 256. `slots`: within a half canvas of one block no two patches share both route and slot.
All inputs are finite; a program needn't handle non-finite values.
Results may differ from the reference program's by a relative error of at most 0.02.
The reference program's roundings to bfloat16 on the way count: a program that leaves them out, or rounds other values in their place, can miss the bound.
Values may be sent and summed in bfloat16 or wider, within the bound.
No kernel may reach another device: no remote copies, remote signals or barrier semaphores. Data moves between devices by JAX's collectives and lax.ppermute only.
A program may use at most 256 MiB of HBM per device.

```python
import math
import jax
import jax.numpy as jnp
import numpy as np
from jax import lax

D = 384
HEADS = 12
F = 1536
HEAD_DIM = 32
EXPERTS = 2
CAP = 256
SIDE = 28
WIN = 7
SHIFT = 3
ITEMS = 6
CROP = 320
BLOCKS = 2
CANVAS_DEV = 1
CELLS = 784
GROUP = 392
RELS = 169
CANVASES = 32
TOKENS = 25088
PSIZE = 2961408


def layout_drawn():
    return [('gain_first', (D,)), ('bias_first', (D,)), ('gain_second', (D,)), ('bias_second', (D,)), ('position_table', (RELS, HEADS)), ('query_bias', (D,)), ('value_bias', (D,)), ('output_bias', (D,)), ('router_weight', (D, EXPERTS)), ('router_bias', (EXPERTS,)), ('expert_in_bias', (EXPERTS, F)), ('expert_out_bias', (EXPERTS, D)), ('project_in', (D, 3 * D)), ('project_out', (D, D)), ('expert_in', (EXPERTS, D, F)), ('expert_out', (EXPERTS, F, D))]


def segment_values(settings):
    position = jnp.arange(PSIZE, dtype=jnp.int32)
    values = jnp.full((PSIZE,), settings['padding'], jnp.float32)
    offset = 0
    for entry_name, extent in layout_drawn():
        count_rows = math.prod(extent)
        inside = (position >= offset) & (position < offset + count_rows)
        values = jnp.where(inside, jnp.float32(settings[entry_name]), values)
        offset = offset + count_rows
    return values


def weight_centres():
    settings = {}
    for entry_name, extent in layout_drawn():
        settings[entry_name] = 0.0
    settings['gain_first'] = 1.0
    settings['gain_second'] = 1.0
    settings['padding'] = 0.0
    return settings


def weight_spreads(factor):
    settings = {'gain_first': 0.1, 'bias_first': 0.1, 'gain_second': 0.1, 'bias_second': 0.1, 'position_table': 0.5, 'query_bias': 0.1, 'value_bias': 0.1, 'output_bias': 0.1, 'router_weight': 0.7 / math.sqrt(D), 'router_bias': 0.1, 'expert_in_bias': 0.1, 'expert_out_bias': 0.05, 'project_in': 1.3 / math.sqrt(D), 'project_out': 3.0 / math.sqrt(D), 'expert_in': 1.0 / math.sqrt(D), 'expert_out': 3.5 / math.sqrt(F), 'padding': 0.05}
    scaled = {}
    for entry_name in settings:
        scaled[entry_name] = settings[entry_name] * factor
    return scaled


def moment_spreads():
    factor = math.sqrt(TOKENS)
    settings = {'gain_first': 0.5, 'bias_first': 0.5, 'gain_second': 0.5, 'bias_second': 0.5, 'position_table': 0.02, 'query_bias': 0.1, 'value_bias': 0.3, 'output_bias': 1.0, 'router_weight': 1.0, 'router_bias': 1.0, 'expert_in_bias': 0.2, 'expert_out_bias': 0.35, 'project_in': 0.1, 'project_out': 0.3, 'expert_in': 0.3, 'expert_out': 0.2, 'padding': 0.1}
    scaled = {}
    for entry_name in settings:
        scaled[entry_name] = settings[entry_name] * factor
    return scaled


def draw_params(key, part):
    noise_key = jax.random.fold_in(key, 3)
    unit_noise = jnp.clip(jax.random.normal(noise_key, (BLOCKS, PSIZE), jnp.float32), -4.0, 4.0)
    return segment_values(weight_centres())[None, :] + segment_values(weight_spreads(1.0))[None, :] * unit_noise


def draw_momentum(key, part):
    noise_key = jax.random.fold_in(key, 11)
    unit_noise = jnp.clip(jax.random.normal(noise_key, (BLOCKS, PSIZE), jnp.float32), -4.0, 4.0)
    return segment_values(moment_spreads())[None, :] * unit_noise


def draw_average(key, part):
    noise_key = jax.random.fold_in(key, 13)
    unit_noise = jnp.clip(jax.random.normal(noise_key, (BLOCKS, PSIZE), jnp.float32), -4.0, 4.0)
    return segment_values(weight_centres())[None, :] + segment_values(weight_spreads(0.6))[None, :] * unit_noise


def route_table(key):
    group_total = BLOCKS * CANVASES * (CELLS // GROUP)

    def one_group(group_key):
        full_key, order_key, place_key = jax.random.split(group_key, 3)
        full_expert = jax.random.randint(full_key, (), 0, EXPERTS)
        pair_ids = jnp.arange(EXPERTS * CAP, dtype=jnp.int32)
        shuffled = jax.random.permutation(order_key, EXPERTS * CAP).astype(jnp.int32)
        pair_rank = jnp.zeros((EXPERTS * CAP,), jnp.int32).at[shuffled].set(pair_ids)
        priority = jnp.where(pair_ids // CAP == full_expert, 0, 1) * (EXPERTS * CAP) + pair_rank
        chosen = jnp.argsort(priority)[:GROUP].astype(jnp.int32)
        placed = chosen[jax.random.permutation(place_key, GROUP)]
        return placed
    group_keys = jax.random.split(jax.random.fold_in(key, 7), group_total)
    pair_table = jax.vmap(one_group)(group_keys)
    return pair_table.reshape(BLOCKS, CANVASES, CELLS)


def draw_routes(key, part):
    return route_table(key) // CAP


def draw_slots(key, part):
    return route_table(key) % CAP


def block_scale(rng, shape, cuts, low, largest):
    loudness, own = 1.0, jax.random.fold_in(rng, 6)
    for axis_at, parts in cuts:
        draws = jnp.exp(jax.random.uniform(jax.random.fold_in(own, axis_at), (parts,), jnp.float32, low / len(cuts), largest / len(cuts)))
        loudness = loudness * jnp.repeat(draws, shape[axis_at] // parts).reshape([-1 if axis == axis_at else 1 for axis in range(len(shape))])
    return loudness


def profile(count, total, most, skew):
    loads = [(1 << 20) // math.isqrt(rank ** skew) + 1 for rank in range(2, count + 1)]
    spare, given = total - most - (count - 1), [1] * (count - 1)
    while spare > 0:
        free = [i for i in range(count - 1) if given[i] < most]
        mass, remaining = sum([loads[i] for i in free]), spare
        for i in free:
            extra = min(most - given[i], max(1, remaining * loads[i] // mass), spare)
            given[i] = given[i] + extra
            spare = spare - extra
    return np.array([most] + given)


def ragged_sizes(key, amount, total, bound, skew):
    if amount == 2:
        one = jax.random.randint(key, (), max(1, total - bound), min(bound, total - 1) + 1)
        return jnp.stack([one, total - one])
    lengths = jnp.asarray(profile(amount, total, bound, skew), jnp.int32)
    pairs = (amount - 1) // 2
    giver, taker = lengths[1:1 + 2 * pairs:2], lengths[2:2 + 2 * pairs:2]
    margin = jnp.minimum(giver - 1, bound - taker)
    moved = jax.random.randint(jax.random.fold_in(key, 1), (pairs,), 0, 1 << 20) % (margin + 1)
    lengths = lengths.at[1:1 + 2 * pairs:2].set(giver - moved).at[2:2 + 2 * pairs:2].set(taker + moved)
    return lengths[jax.random.permutation(jax.random.fold_in(key, 2), amount)]


def normal_values(key, shape, scale, most, cuts=(), held_as=jnp.bfloat16):
    entries = scale * jax.random.normal(key, shape, jnp.float32)
    if cuts:
        entries = entries * block_scale(key, shape, cuts, -0.22, 0.18)
    return jnp.clip(entries, -most, most).astype(held_as)


def setup_inputs(seed: int = 0) -> dict:
    key_of = jax.random.split(jax.random.key(seed), 9)
    inputs = normal_values(key_of[0], (CANVASES, CELLS, D), 1.0, 6.0, ((0, 32),))
    items = jax.vmap(lambda own: jnp.searchsorted(jnp.cumsum(ragged_sizes(own, ITEMS, CELLS, CROP, 0)), jnp.arange(CELLS), side="right"))(jax.random.split(key_of[1], CANVASES)).reshape((CANVASES, CELLS)).astype(jnp.int32)
    routes = draw_routes(jax.random.fold_in(key_of[8], 71), 0)
    slots = draw_slots(jax.random.fold_in(key_of[8], 71), 0)
    cotangent = normal_values(key_of[4], (CANVASES, CELLS, D), 1.0, 6.0, ((0, 32),))
    params = draw_params(jax.random.fold_in(key_of[8], 71), 0)
    momentum = draw_momentum(jax.random.fold_in(key_of[8], 71), 0)
    average = draw_average(jax.random.fold_in(key_of[8], 71), 0)
    return {"inputs": inputs, "items": items, "routes": routes, "slots": slots, "cotangent": cotangent, "params": params, "momentum": momentum, "average": average}


@jax.custom_vjp
def low(v):
    return lax.optimization_barrier(v.astype(jnp.bfloat16)).astype(jnp.float32)

@jax.custom_vjp
def low_back(v):
    return v

def low_keep(v):
    return (low(v), None)

def low_pass(kept, grad):
    return (grad,)

def back_keep(v):
    return (v, None)

def back_low(kept, grad):
    return (low(grad),)
low.defvjp(low_keep, low_pass)
low_back.defvjp(back_keep, back_low)
NORM_EPSILON = 1e-05
MOMENTUM_DECAY = 0.9
AVERAGE_DECAY = 0.9
RATE_BASE = 0.1
PRECISE = lax.Precision.HIGHEST

def layout():
    return [('gain_first', (D,)), ('bias_first', (D,)), ('gain_second', (D,)), ('bias_second', (D,)), ('position_table', (RELS, HEADS)), ('query_bias', (D,)), ('value_bias', (D,)), ('output_bias', (D,)), ('router_weight', (D, EXPERTS)), ('router_bias', (EXPERTS,)), ('expert_in_bias', (EXPERTS, F)), ('expert_out_bias', (EXPERTS, D)), ('project_in', (D, 3 * D)), ('project_out', (D, D)), ('expert_in', (EXPERTS, D, F)), ('expert_out', (EXPERTS, F, D))]

def unpack(flat_vec):
    pieces = {}
    offset = 0
    for entry_name, extent in layout():
        count_rows = math.prod(extent)
        pieces[entry_name] = flat_vec[offset:offset + count_rows].reshape(extent)
        offset = offset + count_rows
    return pieces

def vector_rows(pieces):
    names = ['gain_first', 'bias_first', 'gain_second', 'bias_second', 'query_bias', 'value_bias', 'output_bias']
    return jnp.concatenate([jnp.stack([pieces[entry_name] for entry_name in names]), pieces['expert_out_bias']], axis=0)

def layer_norm(hidden, gain_vec, bias_vec):
    centre = hidden - lax.optimization_barrier(jnp.mean(hidden, axis=-1, keepdims=True))
    spread = lax.optimization_barrier(jnp.mean(centre * centre, axis=-1, keepdims=True))
    return centre * lax.rsqrt(spread + NORM_EPSILON) * gain_vec + bias_vec

def to_windows(grid, canvases):
    per_side = SIDE // WIN
    feature_count = grid.shape[-1]
    split_grid = grid.reshape(canvases, per_side, WIN, per_side, WIN, feature_count)
    return jnp.transpose(split_grid, (0, 1, 3, 2, 4, 5)).reshape(canvases * per_side * per_side, WIN * WIN, feature_count)

def from_windows(blocks, canvases):
    per_side = SIDE // WIN
    feature_count = blocks.shape[-1]
    split_grid = blocks.reshape(canvases, per_side, per_side, WIN, WIN, feature_count)
    return jnp.transpose(split_grid, (0, 1, 3, 2, 4, 5)).reshape(canvases, SIDE, SIDE, feature_count)

def window_allowed(items_grid, shifted):
    canvases = items_grid.shape[0]
    labels = items_grid
    if shifted:
        labels = jnp.roll(items_grid, (-SHIFT, -SHIFT), axis=(1, 2))
        wrapped = (jnp.arange(SIDE, dtype=jnp.int32) >= SIDE - SHIFT).astype(jnp.int32)
        labels = labels * 4 + 2 * wrapped[None, :, None] + wrapped[None, None, :]
    groups = to_windows(labels[..., None], canvases)[..., 0]
    allowed = groups[:, :, None] == groups[:, None, :]
    return jnp.transpose(allowed, (1, 2, 0))[:, :, :, None]

def relative_index():
    coords = np.arange(WIN * WIN)
    rows_of = coords // WIN
    cols_of = coords % WIN
    return (rows_of[:, None] - rows_of[None, :] + WIN - 1) * (2 * WIN - 1) + cols_of[:, None] - cols_of[None, :] + WIN - 1

def block_forward(hidden, pieces, items_grid, route_rows, slot_rows, shifted):
    canvases = items_grid.shape[0]
    normed = low(layer_norm(hidden, pieces['gain_first'], pieces['bias_first']))
    in_bias = jnp.concatenate([pieces['query_bias'], jnp.zeros((D,), jnp.float32), pieces['value_bias']])
    qkv_rows = jnp.dot(normed, pieces['project_in'], precision=PRECISE, preferred_element_type=jnp.float32)
    qkv_rows = low(low_back(qkv_rows + in_bias))
    grid = qkv_rows.reshape(canvases, SIDE, SIDE, 3 * D)
    if shifted:
        grid = jnp.roll(grid, (-SHIFT, -SHIFT), axis=(1, 2))
    windows = to_windows(grid, canvases).reshape(-1, WIN * WIN, 3, HEADS, HEAD_DIM)
    allowed = window_allowed(items_grid, shifted)
    bias_table = pieces['position_table'][relative_index()]
    scores = jnp.einsum('wihd,wjhd->ijwh', windows[:, :, 0], windows[:, :, 1], precision=PRECISE) * HEAD_DIM ** (-0.5) + bias_table[:, :, None, :]
    scores = jnp.where(allowed, low_back(scores), -1e+30)
    attn_weights = jax.nn.softmax(scores, axis=1)
    mixed_rows = jnp.einsum('ijwh,wjhd->wihd', low(attn_weights), windows[:, :, 2], precision=PRECISE)
    mixed_grid = from_windows(mixed_rows.reshape(-1, WIN * WIN, D), canvases)
    if shifted:
        mixed_grid = jnp.roll(mixed_grid, (SHIFT, SHIFT), axis=(1, 2))
    mixed_flat = low(low_back(mixed_grid.reshape(-1, D)))
    attended = low_back(jnp.dot(mixed_flat, pieces['project_out'], precision=PRECISE, preferred_element_type=jnp.float32) + pieces['output_bias'])
    hidden_one = hidden + attended
    normed_two = low(layer_norm(hidden_one, pieces['gain_second'], pieces['bias_second']))
    logits = low_back(jnp.dot(normed_two, pieces['router_weight'], precision=PRECISE, preferred_element_type=jnp.float32) + pieces['router_bias'])
    router_probs = jax.nn.softmax(logits, axis=-1)
    chosen = route_rows[:, None] == jnp.arange(EXPERTS, dtype=jnp.int32)[None, :]
    gate_prob = lax.optimization_barrier(jnp.sum(jnp.where(chosen, router_probs, 0.0), axis=-1))
    token_count = route_rows.shape[0]
    group_count = token_count // GROUP
    position = jnp.arange(token_count, dtype=jnp.int32) // GROUP * (EXPERTS * CAP) + route_rows * CAP + slot_rows
    dispatched = jnp.zeros((group_count * EXPERTS * CAP, D), jnp.float32).at[position].add(normed_two)
    dispatched = low_back(dispatched).reshape(group_count, EXPERTS, CAP, D)
    pre_act = jnp.einsum('gecd,edf->gecf', dispatched, pieces['expert_in'], precision=PRECISE) + pieces['expert_in_bias'][None, :, None, :]
    pre_act = low_back(pre_act)
    inner_act = low(jax.nn.gelu(pre_act, approximate=False))
    expert_rows = jnp.einsum('gecf,efd->gecd', inner_act, pieces['expert_out'], precision=PRECISE) + pieces['expert_out_bias'][None, :, None, :]
    expert_rows = low(expert_rows)
    picked = low_back(expert_rows.reshape(-1, D)[position])
    return hidden_one + gate_prob[:, None] * picked

def reference(inputs, items, routes, slots, cotangent, params, momentum, average):
    steps_count = CANVASES // CANVAS_DEV
    inputs_parts = inputs.reshape(steps_count, CANVAS_DEV * CELLS, D)
    items_parts = items.reshape(steps_count, CANVAS_DEV, SIDE, SIDE)
    routes_parts = jnp.transpose(routes.reshape(BLOCKS, steps_count, CANVAS_DEV * CELLS), (1, 0, 2))
    slots_parts = jnp.transpose(slots.reshape(BLOCKS, steps_count, CANVAS_DEV * CELLS), (1, 0, 2))
    cotangent_parts = cotangent.reshape(steps_count, CANVAS_DEV * CELLS, D)

    def advance(running, portion):
        part_in, part_items, part_routes, part_slots, part_cot = portion

        def forward(flat_params, hidden):
            for block_index in range(BLOCKS):
                pieces = unpack(low(flat_params[block_index]))
                hidden = block_forward(hidden, pieces, part_items, part_routes[block_index], part_slots[block_index], block_index % 2 == 1)
            return hidden
        result, pullback = jax.vjp(forward, params, part_in.astype(jnp.float32))
        grad_params, grad_hidden = pullback(part_cot.astype(jnp.float32))
        return (running + grad_params, (result.astype(jnp.bfloat16), grad_hidden))
    grads, (outputs, input_grad) = lax.scan(advance, jnp.zeros_like(params), (inputs_parts, items_parts, routes_parts, slots_parts, cotangent_parts))
    vector_grads = jnp.stack([vector_rows(unpack(grads[block_index])) for block_index in range(BLOCKS)])
    step_rate = RATE_BASE / math.sqrt(TOKENS)
    new_momentum = MOMENTUM_DECAY * momentum + grads
    new_params = params - step_rate * (grads + MOMENTUM_DECAY * new_momentum)
    new_average = AVERAGE_DECAY * average + (1.0 - AVERAGE_DECAY) * new_params
    return (outputs.reshape(CANVASES, CELLS, D), input_grad.reshape(CANVASES, CELLS, D), new_params, new_momentum, new_average, vector_grads)
```

```python
import functools
import math
from typing import Any, NamedTuple

import jax
import jax.numpy as jnp
import numpy as np
from jax import lax
from jax.experimental import pallas as pl
from jax.experimental.pallas import tpu as pltpu
from jax.sharding import PartitionSpec as P

D = 384
HEADS = 12
F = 1536
HEAD_DIM = 32
EXPERTS = 2
CAP = 256
SIDE = 28
WIN = 7
SHIFT = 3
BLOCKS = 2
CELLS = 784
GROUP = 392
RELS = 169
NORM_EPSILON = 1e-05
MOMENTUM_DECAY = 0.9
AVERAGE_DECAY = 0.9
RATE_BASE = 0.1

DP = "dp"
FSDP = "fsdp"
LANES = 128
WROWS = 64
WINDOWS = 16
WTOK = WINDOWS * WROWS
SLOTS = EXPERTS * 2 * CAP
PAIR = 4 * WROWS
QUADS = HEADS // 4
SCALE = HEAD_DIM ** (-0.5)
BF = jnp.bfloat16
F32 = jnp.float32
VMEM_BYTES = 60 * 1024 * 1024


def call(body, out_shape, n_in, scratch=(), aliases=None, smem=0):
    return pl.pallas_call(
        body,
        out_shape=out_shape,
        in_specs=[pl.BlockSpec(memory_space=pltpu.SMEM)] * smem
        + [pl.BlockSpec(memory_space=pltpu.VMEM)] * (n_in - smem),
        out_specs=jax.tree.map(lambda _: pl.BlockSpec(memory_space=pltpu.VMEM), out_shape),
        scratch_shapes=list(scratch),
        compiler_params=pltpu.CompilerParams(vmem_limit_bytes=VMEM_BYTES),
    )


def sds(shape, dtype):
    return jax.ShapeDtypeStruct(shape, dtype)


def nn(a, b):
    return lax.dot_general(a, b, (((1,), (0,)), ((), ())), preferred_element_type=F32)


def nt(a, b):
    return lax.dot_general(a, b, (((1,), (1,)), ((), ())), preferred_element_type=F32)


def tn(a, b):
    return lax.dot_general(a, b, (((0,), (0,)), ((), ())), preferred_element_type=F32)


def normalize(hidden):
    centre = hidden - jnp.mean(hidden, axis=-1, keepdims=True)
    inverse = lax.rsqrt(jnp.mean(centre * centre, axis=-1, keepdims=True) + NORM_EPSILON)
    return centre * inverse, inverse


def norm_backward(grad_normed, normal_rows, inverse, gain_row):
    scaled = grad_normed * gain_row
    return inverse * (
        scaled
        - jnp.mean(scaled, axis=-1, keepdims=True)
        - normal_rows * jnp.mean(scaled * normal_rows, axis=-1, keepdims=True)
    )


def head_masks():
    lane = lax.broadcasted_iota(jnp.int32, (1, LANES), 1) // HEAD_DIM
    return [lane == h for h in range(4)]


def stack_heads(rows, masks):
    zero = jnp.zeros_like(rows)
    return jnp.concatenate([jnp.where(mask, rows, zero) for mask in masks], axis=0)


def fold_heads(tall, masks):
    out = jnp.where(masks[0], tall[0:WROWS], 0.0)
    for h in range(1, 4):
        out = jnp.where(masks[h], tall[h * WROWS : (h + 1) * WROWS], out)
    return out


def attn_fwd_body(hid, vec, w_in, w_out, perm, perm_t, bias, mask, h_one, wn, qkv, mixed, attn):
    normal, _ = normalize(hid[...].astype(F32))
    normed = (normal * vec[0:1] + vec[1:2]).astype(BF)
    wn[...] = nn(perm[...], normed).astype(BF)
    in_bias = jnp.concatenate([vec[4:5], jnp.zeros((1, D), F32), vec[5:6]], axis=1)

    @pl.loop(0, 4)
    def _(t):
        rows = pl.ds(pl.multiple_of(t * 256, 256), 256)
        qkv[rows, :] = (nn(wn[rows, :], w_in[...]) + in_bias).astype(BF)

    masks = head_masks()

    @pl.loop(0, WINDOWS)
    def _(w):
        rows = pl.ds(pl.multiple_of(w * WROWS, WROWS), WROWS)
        allow = mask[w] > 0.0
        allow = jnp.concatenate([allow, allow], axis=1)
        for g in range(QUADS):
            cols = slice(g * LANES, (g + 1) * LANES)
            q4 = stack_heads(qkv[rows, g * LANES : (g + 1) * LANES], masks)
            kg = qkv[rows, D + g * LANES : D + (g + 1) * LANES]
            vg = qkv[rows, 2 * D + g * LANES : 2 * D + (g + 1) * LANES]
            s = jnp.where(allow, nt(kg, q4) * SCALE + bias[g], -1e30)
            e = jnp.exp(s - jnp.max(s, axis=0, keepdims=True))
            a = e * (1.0 / jnp.sum(e, axis=0, keepdims=True))
            attn[w * QUADS + g] = a
            mixed[rows, cols] = fold_heads(tn(a.astype(BF), vg), masks).astype(BF)

    back = nn(perm_t[...], mixed[...]).astype(BF)
    h_one[...] = hid[...].astype(F32) + nn(back, w_out[...]) + vec[6:7]


def attn_fwd(hid, vec, w_in, w_out, perm, perm_t, bias, mask):
    return call(
        attn_fwd_body,
        (
            sds((CELLS, D), F32),
            sds((WTOK, D), BF),
            sds((WTOK, 3 * D), BF),
            sds((WTOK, D), BF),
            sds((WINDOWS * QUADS, WROWS, PAIR), F32),
        ),
        8,
    )(hid, vec, w_in, w_out, perm, perm_t, bias, mask)


def moe_fwd_body(
    h_one, vec, w1, w2, b1, router, router_bias, chosen, onehot, onehot_t,
    out, normed_two, disp, act, slope, picked, gate, other, rows_out,
):
    normal, _ = normalize(h_one[...])
    two = (normal * vec[2:3] + vec[3:4]).astype(BF)
    normed_two[...] = two
    logits = nn(two, router[...])
    gap = (logits[:, LANES:] + router_bias[1:2]) - (logits[:, :LANES] + router_bias[0:1])
    gap = jnp.where(chosen[...] > 0.0, gap, -gap)
    gate[...] = 1.0 / (1.0 + jnp.exp(-gap))
    other[...] = 1.0 / (1.0 + jnp.exp(gap))
    disp[...] = nn(onehot_t[...], two).astype(BF)

    @pl.loop(0, 4)
    def _(t):
        rows = pl.ds(pl.multiple_of(t * 256, 256), 256)
        e = t // 2
        own = disp[rows, :]
        for c in range(3):
            cols = slice(c * 512, (c + 1) * 512)
            pre = nn(own, w1[e, :, cols]) + b1[pl.ds(e, 1), cols]
            phi = 0.5 * (1.0 + lax.erf(pre * 0.7071067811865476))
            act[rows, cols] = (pre * phi).astype(BF)
            slope[rows, cols] = (
                phi + pre * jnp.exp(-0.5 * pre * pre) * 0.3989422804014327
            ).astype(BF)
        rows_out[rows, :] = (nn(act[rows, :], w2[e]) + vec[pl.ds(7 + e, 1)]).astype(BF)

    taken = nn(onehot[...], rows_out[...])
    picked[...] = taken.astype(BF)
    for c in range(3):
        cols = slice(c * LANES, (c + 1) * LANES)
        out[:, cols] = (h_one[:, cols] + gate[...] * taken[:, cols]).astype(out.dtype)


def moe_fwd(h_one, vec, w1, w2, b1, router, router_bias, chosen, onehot, onehot_t, out_dtype):
    return call(
        moe_fwd_body,
        (
            sds((CELLS, D), out_dtype),
            sds((CELLS, D), BF),
            sds((SLOTS, D), BF),
            sds((SLOTS, F), BF),
            sds((SLOTS, F), BF),
            sds((CELLS, D), BF),
            sds((CELLS, LANES), F32),
            sds((CELLS, LANES), F32),
        ),
        10,
        scratch=[pltpu.VMEM((SLOTS, D), BF)],
    )(h_one, vec, w1, w2, b1, router, router_bias, chosen, onehot, onehot_t)


def moe_bwd_body(
    grad, h_one, vec, w1, w2, router_gap, chosen, onehot, onehot_t,
    normed_two, disp, act, slope, picked, gate, other,
    grad_one, dw1, dw2, db1, drouter, small, g_rows, g_pre, g_disp,
):
    go = grad[...].astype(F32)
    gate_wide = jnp.concatenate([gate[...]] * 3, axis=1)
    g_picked = (go * gate_wide).astype(BF)
    g_gate = jnp.sum(go * picked[...].astype(F32), axis=-1, keepdims=True)
    sign = jnp.where(chosen[...] > 0.0, 1.0, -1.0)
    gl = (g_gate * gate[...] * other[...] * sign).astype(BF).astype(F32)
    g_rows[...] = nn(onehot_t[...], g_picked).astype(BF)

    @pl.loop(0, EXPERTS)
    def _(e):
        total = jnp.zeros((1, F), F32)
        for t in range(2):
            rows = pl.ds(pl.multiple_of(e * 512 + t * 256, 256), 256)
            own = g_rows[rows, :]
            parts = []
            for c in range(3):
                cols = slice(c * 512, (c + 1) * 512)
                gp = (nt(own, w2[e, cols, :]) * slope[rows, cols].astype(F32)).astype(BF)
                g_pre[t * 256 : (t + 1) * 256, cols] = gp
                parts.append(jnp.sum(gp.astype(F32), axis=0, keepdims=True))
            total = total + jnp.concatenate(parts, axis=1)
            g_disp[rows, :] = nt(g_pre[t * 256 : (t + 1) * 256, :], w1[e]).astype(BF)
        db1[pl.ds(e, 1), :] = total
        both = pl.ds(pl.multiple_of(e * 512, 512), 512)
        small[pl.ds(7 + e, 1), :] = jnp.sum(g_rows[both, :].astype(F32), axis=0, keepdims=True)
        for c in range(3):
            cols = slice(c * 512, (c + 1) * 512)
            dw1[e, :, cols] = tn(disp[both, :], g_pre[:, cols])
            dw2[e, cols, :] = tn(act[both, cols], g_rows[both, :])

    g_two = nn(onehot[...], g_disp[...])
    gl_wide = jnp.concatenate([gl] * 3, axis=1)
    g_two = g_two + gl_wide * router_gap[0:1]
    lane = lax.broadcasted_iota(jnp.int32, (1, LANES), 1)
    drouter[...] = tn(normed_two[...], jnp.where(lane == 0, -gl, gl).astype(BF))
    normal, inverse = normalize(h_one[...])
    small[0:1] = jnp.zeros((1, D), F32)
    small[1:2] = jnp.zeros((1, D), F32)
    small[2:3] = jnp.sum(g_two * normal, axis=0, keepdims=True)
    small[3:4] = jnp.sum(g_two, axis=0, keepdims=True)
    small[4:7] = jnp.zeros((3, D), F32)
    small[9:16] = jnp.zeros((7, D), F32)
    small[9:10] = jnp.sum(gl_wide, axis=0, keepdims=True)
    grad_one[...] = go + norm_backward(g_two, normal, inverse, vec[2:3])


def moe_bwd(grad, h_one, vec, w1, w2, router_gap, chosen, onehot, onehot_t, saved):
    return call(
        moe_bwd_body,
        (
            sds((CELLS, D), F32),
            sds((EXPERTS, D, F), F32),
            sds((EXPERTS, F, D), F32),
            sds((8, F), F32),
            sds((D, LANES), F32),
            sds((16, D), F32),
        ),
        16,
        scratch=[pltpu.VMEM((SLOTS, D), BF), pltpu.VMEM((512, F), BF), pltpu.VMEM((SLOTS, D), BF)],
    )(grad, h_one, vec, w1, w2, router_gap, chosen, onehot, onehot_t, *saved)


def attn_bwd_body(
    grad_one, hid, vec, w_in, w_out, perm, perm_t, wn, qkv, mixed, attn,
    grad_in, dw_in, dw_out, dbias, small, g_mix, g_qkv,
):
    gao = grad_one[...].astype(BF)
    small[...] = jnp.zeros((16, D), F32)
    small[6:7] = jnp.sum(gao.astype(F32), axis=0, keepdims=True)
    gao_w = nn(perm[...], gao).astype(BF)
    dw_out[...] = tn(mixed[...], gao_w)
    g_mix[...] = nt(gao_w, w_out[...]).astype(BF)
    dbias[...] = jnp.zeros_like(dbias)
    masks = head_masks()

    @pl.loop(0, WINDOWS)
    def _(w):
        rows = pl.ds(pl.multiple_of(w * WROWS, WROWS), WROWS)
        for g in range(QUADS):
            cols = slice(g * LANES, (g + 1) * LANES)
            kcols = slice(D + g * LANES, D + (g + 1) * LANES)
            vcols = slice(2 * D + g * LANES, 2 * D + (g + 1) * LANES)
            q4 = stack_heads(qkv[rows, cols], masks)
            kg = qkv[rows, kcols]
            vg = qkv[rows, vcols]
            d4 = stack_heads(g_mix[rows, cols], masks)
            a = attn[w * QUADS + g]
            t = a * nt(vg, d4)
            ds = (t - a * jnp.sum(t, axis=0, keepdims=True)).astype(BF)
            dbias[g] += ds.astype(F32)
            g_qkv[rows, cols] = (fold_heads(tn(ds, kg), masks) * SCALE).astype(BF)
            g_qkv[rows, kcols] = (nn(ds, q4) * SCALE).astype(BF)
            g_qkv[rows, vcols] = nn(a.astype(BF), d4).astype(BF)

    small[4:5] = jnp.sum(g_qkv[:, :D].astype(F32), axis=0, keepdims=True)
    small[5:6] = jnp.sum(g_qkv[:, 2 * D :].astype(F32), axis=0, keepdims=True)
    for c in range(3):
        cols = slice(c * D, (c + 1) * D)
        dw_in[:, cols] = tn(wn[...], g_qkv[:, cols])
    g_flat = nn(perm_t[...], g_qkv[...]).astype(BF)
    g_normed = nt(g_flat, w_in[...])
    normal, inverse = normalize(hid[...].astype(F32))
    small[0:1] = jnp.sum(g_normed * normal, axis=0, keepdims=True)
    small[1:2] = jnp.sum(g_normed, axis=0, keepdims=True)
    grad_in[...] = grad_one[...] + norm_backward(g_normed, normal, inverse, vec[0:1])


def attn_bwd(grad_one, hid, vec, w_in, w_out, perm, perm_t, saved):
    return call(
        attn_bwd_body,
        (
            sds((CELLS, D), F32),
            sds((D, 3 * D), F32),
            sds((D, D), F32),
            sds((QUADS, WROWS, PAIR), F32),
            sds((16, D), F32),
        ),
        11,
        scratch=[pltpu.VMEM((WTOK, D), BF), pltpu.VMEM((WTOK, 3 * D), BF)],
    )(grad_one, hid, vec, w_in, w_out, perm, perm_t, *saved)


def window_source(shifted):
    source = np.full((WTOK,), -1, np.int32)
    for w in range(WINDOWS):
        for p in range(WIN * WIN):
            r, s = (w // 4) * WIN + p // WIN, (w % 4) * WIN + p % WIN
            if shifted:
                r, s = (r + SHIFT) % SIDE, (s + SHIFT) % SIDE
            source[w * WROWS + p] = r * SIDE + s
    return source


def window_perm(shifted):
    source = window_source(shifted)
    return (source[:, None] == np.arange(CELLS)[None, :]).astype(np.float32)


def wrap_codes(shifted):
    code = np.zeros((CELLS,), np.float32)
    if shifted:
        for r in range(SIDE):
            for s in range(SIDE):
                rr, ss = (r - SHIFT) % SIDE, (s - SHIFT) % SIDE
                code[r * SIDE + s] = 2 * (rr >= SIDE - SHIFT) + (ss >= SIDE - SHIFT)
    return code


def relative_onehot():
    table = np.zeros((WROWS, WROWS, RELS), np.float32)
    for j in range(WIN * WIN):
        for i in range(WIN * WIN):
            a = i // WIN - j // WIN + WIN - 1
            b = i % WIN - j % WIN + WIN - 1
            table[j, i, a * (2 * WIN - 1) + b] = 1.0
    return table


def window_masks(items, shifted, perm_t):
    labels = items.astype(F32)
    if shifted:
        labels = labels * 4.0 + jnp.asarray(wrap_codes(True))
    placed = nn(jnp.broadcast_to((labels + 1.0).astype(BF), (8, CELLS)), perm_t)[0]
    placed = placed.reshape(WINDOWS, WROWS)
    same = (placed[:, :, None] == placed[:, None, :]) & (placed[:, :, None] > 0.0)
    same = same.astype(F32)
    return jnp.concatenate([same, same], axis=2)


def bias_tables(position_table):
    rel = jnp.asarray(relative_onehot().reshape(WROWS * WROWS, RELS), BF)
    rows = lax.dot_general(
        position_table.astype(BF), rel, (((0,), (1,)), ((), ())), preferred_element_type=F32
    )
    rows = rows.reshape(QUADS, 4, WROWS, WROWS)
    return jnp.transpose(rows, (0, 2, 1, 3)).reshape(QUADS, WROWS, PAIR)


def bias_table_grad(dbias):
    rel = jnp.asarray(relative_onehot().reshape(WROWS * WROWS, RELS), BF)
    rows = jnp.transpose(dbias.reshape(QUADS, WROWS, 4, WROWS), (0, 2, 1, 3))
    rows = rows.reshape(HEADS, WROWS * WROWS)
    high = rows.astype(BF)
    low = (rows - high.astype(F32)).astype(BF)
    both = nn(jnp.concatenate([high, low], axis=0), rel)
    return (both[:HEADS] + both[HEADS:]).T


def slot_tables(routes, slots):
    group = (jnp.arange(CELLS, dtype=jnp.int32) // GROUP) * CAP
    place = routes * (2 * CAP) + group + slots
    wide = jnp.arange(SLOTS, dtype=jnp.int32)
    onehot = (place[:, None] == wide[None, :]).astype(BF)
    onehot_t = (wide[:, None] == place[None, :]).astype(BF)
    chosen = jnp.broadcast_to(routes[:, None].astype(F32), (CELLS, LANES))
    return onehot, onehot_t, chosen

LEAD = 73
SMALL = 9326
LAG = LEAD * LANES - SMALL
SPANS = ((LEAD, D, 9), (LEAD + 3456, D, 3), (LEAD + 4608, 2 * D, 12), (LEAD + 4608 + 9216, 2 * F, 3))
ALIGNED = LEAD + 4608 + 2 * 9216


def unpack_body(rows, devices, padded, got, w_in, w_out, w1, w2, flat):
    @pl.loop(0, devices)
    def _(d):
        flat[pl.ds(d * rows, rows), :] = got[pl.ds(pl.multiple_of(d * padded, 16), rows), :].astype(F32)

    lane = lax.broadcasted_iota(jnp.int32, (1, LANES), 1)
    for (base, height, tiles), out in zip(SPANS, (w_in, w_out, w1, w2)):
        step = 64

        @pl.loop(0, height // step)
        def _(t, base=base, tiles=tiles, out=out):
            first = base - 1 + t * (step * tiles)
            before = flat[pl.ds(first, step, stride=tiles), :]
            for j in range(tiles):
                here = flat[pl.ds(first + 1 + j, step, stride=tiles), :]
                tile = pltpu.roll(jnp.where(lane >= LANES - LAG, before, here), LAG, 1)
                out[pl.ds(pl.multiple_of(t * step, step), step), j * LANES : (j + 1) * LANES] = tile.astype(BF)
                before = here


def unpack_weights(gathered, rows, devices):
    padded = gathered.shape[0] // devices
    return call(
        functools.partial(unpack_body, rows, devices, padded),
        (sds((D, 3 * D), BF), sds((D, D), BF), sds((2 * D, F), BF), sds((2 * F, D), BF)),
        1,
        scratch=[pltpu.VMEM((devices * rows + 8, LANES), F32)],
    )(gathered)


def pack_body(rows, devices, padded, orders, small, dw_in, dw_out, dw1, dw2, part_a, part_b, al):
    al[0:LEAD, :] = small[0:LEAD, :]
    tail = al.shape[0] - ALIGNED
    al[pl.ds(ALIGNED, tail), :] = jnp.zeros((tail, LANES), F32)
    for (base, height, tiles), grad in zip(SPANS, (dw_in, dw_out, dw1, dw2)):
        step = 64

        @pl.loop(0, height // step)
        def _(t, base=base, tiles=tiles, grad=grad):
            first = base + t * (step * tiles)
            own = pl.ds(pl.multiple_of(t * step, step), step)
            for j in range(tiles):
                al[pl.ds(first + j, step, stride=tiles), :] = grad[own, j * LANES : (j + 1) * LANES]

    half = padded // 2
    for at, (order, part) in enumerate(zip(orders, (part_a, part_b))):
        count = len(order)

        @pl.loop(0, devices)
        def _(k, at=at, order=order, part=part):
            device = 0
            for place, bit in enumerate(order):
                device = device + (((k >> (count - 1 - place)) & 1) << bit)
            part[k] = al[pl.ds(device * rows + at * half, half), :].astype(BF)


def pack_grads(small, dw_in, dw_out, dw1, dw2, rows, devices, padded, orders):
    half = padded // 2
    return call(
        functools.partial(pack_body, rows, devices, padded, orders),
        (sds((devices, half, LANES), BF), sds((devices, half, LANES), BF)),
        5,
        scratch=[pltpu.VMEM((devices * rows + padded, LANES), F32)],
    )(small, dw_in, dw_out, dw1, dw2)


def flip_pairs(axis, bit):
    return [(i, i ^ (1 << bit)) for i in range(lax.axis_size(axis))]


def stage_orders():
    dp, fsdp = (lax.axis_size(axis).bit_length() - 1 for axis in (DP, FSDP))
    rest = [(DP, bit) for bit in range(1, dp)] + [(FSDP, bit) for bit in range(2, fsdp)]
    core, x, y = (FSDP, 0), (FSDP, 1), (DP, 0)
    return [core, y, x] + rest, [core, x, y] + rest


def device_bit(axis, bit):
    return bit if axis == FSDP else bit + lax.axis_size(FSDP).bit_length() - 1


def halve(keep, axis, bit):
    half = keep.shape[0] // 2
    mine = (lax.axis_index(axis) >> bit) & 1
    send = lax.dynamic_slice_in_dim(keep, (1 - mine) * half, half).astype(BF)
    got = lax.ppermute(send, axis, flip_pairs(axis, bit))
    return lax.dynamic_slice_in_dim(keep, mine * half, half).astype(F32) + got.astype(F32)


def shards(inputs, items, routes, slots, cotangent, params, momentum, average):
    fsdp, dp = lax.axis_size(FSDP), lax.axis_size(DP)
    devices = fsdp * dp
    share = params.shape[1]
    rows = share // LANES
    padded = -(-(rows + 1) // 32) * 32
    step_rate = RATE_BASE / math.sqrt(CELLS * devices)
    orders = stage_orders()
    places = [[device_bit(*stage) for stage in order] for order in orders]

    pieces, perms, tables = [], [], []
    hidden = inputs.reshape(CELLS, D)
    gathered = []
    for b in range(BLOCKS):
        own = params[b].astype(BF).reshape(rows, LANES)
        own = jnp.pad(own, ((0, padded - rows), (0, 0)))
        gathered.append(lax.all_gather(own, (DP, FSDP), axis=0, tiled=True))
    saves = []
    for b in range(BLOCKS):
        shifted = b % 2 == 1
        one = window_perm(shifted)
        perm, perm_t = jnp.asarray(one, BF), jnp.asarray(one.T, BF)
        mask = window_masks(items.reshape(CELLS), shifted, perm_t)
        table = slot_tables(routes[b].reshape(CELLS), slots[b].reshape(CELLS))
        w_in, w_out, w1, w2 = unpack_weights(gathered[b], rows, devices)
        w1, w2 = w1.reshape(EXPERTS, D, F), w2.reshape(EXPERTS, F, D)
        flat = gathered[b][:LEAD].astype(F32).reshape(-1)
        small = unpack_small(flat)
        bias = bias_tables(small.position_table)
        vec = jnp.concatenate([small.norms, small.biases, small.expert_out_bias, jnp.zeros((7, D), F32)])
        b1 = jnp.pad(small.expert_in_bias, ((0, 6), (0, 0)))
        rw = small.router_weight
        router = jnp.concatenate([jnp.broadcast_to(rw[:, e : e + 1], (D, LANES)) for e in range(2)], axis=1).astype(BF)
        gap = jnp.broadcast_to((rw[:, 1] - rw[:, 0])[None], (8, D))
        rb = jnp.broadcast_to(small.router_bias[:, None], (2, LANES))
        h_one, *kept_attn = attn_fwd(hidden, vec, w_in, w_out, perm, perm_t, bias, mask)
        last = b == BLOCKS - 1
        following, *kept_moe = moe_fwd(h_one, vec, w1, w2, b1, router, rb, table[2], table[0], table[1], BF if last else F32)
        saves.append((hidden, h_one, vec, w_in, w_out, w1, w2, gap, perm, perm_t, table, kept_attn, kept_moe))
        hidden = following
    outputs = hidden.reshape(1, CELLS, D)

    gradient = cotangent.reshape(CELLS, D)
    sums = [None] * BLOCKS
    vectors = [None] * BLOCKS
    for b in range(BLOCKS - 1, -1, -1):
        hidden, h_one, vec, w_in, w_out, w1, w2, gap, perm, perm_t, table, kept_attn, kept_moe = saves[b]
        g_one, dw1, dw2, db1, drouter, small_moe = moe_bwd(
            gradient, h_one, vec, w1, w2, gap, table[2], table[0], table[1], kept_moe
        )
        gradient, dw_in, dw_out, dbias, small_attn = attn_bwd(g_one, hidden, vec, w_in, w_out, perm, perm_t, kept_attn)
        both = small_moe + small_attn
        flat = jnp.concatenate(
            [
                jnp.zeros((LAG,), F32),
                both[0:4].reshape(-1),
                bias_table_grad(dbias).reshape(-1),
                both[4:7].reshape(-1),
                drouter[:, :2].reshape(-1),
                jnp.stack([-both[9, 0], both[9, 0]]),
                db1[:2].reshape(-1),
                both[7:9].reshape(-1),
            ]
        )
        small = flat.reshape(LEAD, LANES)
        vectors[b] = both[0:9]
        parts = pack_grads(
            small, dw_in, dw_out, dw1.reshape(2 * D, F), dw2.reshape(2 * F, D), rows, devices, padded, places
        )
        done = []
        for part, order in zip(parts, orders):
            for stage in order:
                part = halve(part, *stage)
            done.append(part[0])
        total = jnp.concatenate(done, axis=0).reshape(-1)
        sums[b] = total[LAG : LAG + share]
    vector_grads = jnp.stack(vectors)
    for axis, bit in orders[0]:
        vector_grads = vector_grads + lax.ppermute(vector_grads, axis, flip_pairs(axis, bit))
    grad_all = jnp.stack(sums)
    new_momentum = MOMENTUM_DECAY * momentum + grad_all
    new_params = params - step_rate * (grad_all + MOMENTUM_DECAY * new_momentum)
    new_average = AVERAGE_DECAY * average + (1.0 - AVERAGE_DECAY) * new_params
    return outputs, gradient.reshape(1, CELLS, D), new_params, new_momentum, new_average, vector_grads


class Small(NamedTuple):
    norms: Any
    position_table: Any
    biases: Any
    router_weight: Any
    router_bias: Any
    expert_in_bias: Any
    expert_out_bias: Any


def unpack_small(flat):
    shapes = ((4, D), (RELS, HEADS), (3, D), (D, EXPERTS), (EXPERTS,), (EXPERTS, F), (EXPERTS, D))
    cuts = [0]
    for shape in shapes:
        cuts.append(cuts[-1] + math.prod(shape))
    return Small(*[flat[a:b].reshape(shape) for a, b, shape in zip(cuts, cuts[1:], shapes)])


def solution(mesh):
    both = (DP, FSDP)
    canvas, vector = P(both), P(None, both)
    return jax.shard_map(
        shards,
        mesh=mesh,
        in_specs=(canvas, canvas, vector, vector, canvas, vector, vector, vector),
        out_specs=(canvas, canvas, vector, vector, vector, P()),
        check_vma=False,
    )
```

```python
import functools
import math
from typing import Any, NamedTuple

import jax
import jax.numpy as jnp
import numpy as np
from jax import lax
from jax.experimental import pallas as pl
from jax.experimental.pallas import tpu as pltpu
from jax.sharding import PartitionSpec as P

D = 384
HEADS = 12
F = 1536
HEAD_DIM = 32
EXPERTS = 2
CAP = 256
SIDE = 28
WIN = 7
SHIFT = 3
BLOCKS = 2
CELLS = 784
GROUP = 392
RELS = 169
NORM_EPSILON = 1e-05
MOMENTUM_DECAY = 0.9
AVERAGE_DECAY = 0.9
RATE_BASE = 0.1

DP = "dp"
FSDP = "fsdp"
LANES = 128
WROWS = 64
WINDOWS = 16
WTOK = WINDOWS * WROWS
SLOTS = EXPERTS * 2 * CAP
PAIR = 4 * WROWS
QUADS = HEADS // 4
SCALE = HEAD_DIM ** (-0.5)
US_FLOPS = 1.1e9
BF = jnp.bfloat16
F32 = jnp.float32
VMEM_BYTES = 20 * 1024 * 1024


def call(body, out_shape, n_in, scratch=(), smem=0, deps=(), us=1, vmem=VMEM_BYTES):
    def skipping(*refs):
        body(*refs[:n_in], *refs[n_in + len(deps) :])

    run = pl.pallas_call(
        skipping,
        out_shape=out_shape,
        in_specs=[pl.BlockSpec(memory_space=pltpu.SMEM)] * smem
        + [pl.BlockSpec(memory_space=pltpu.VMEM)] * (n_in - smem)
        + [pl.BlockSpec(memory_space=pl.ANY)] * len(deps),
        out_specs=jax.tree.map(lambda _: pl.BlockSpec(memory_space=pltpu.VMEM), out_shape),
        scratch_shapes=list(scratch),
        compiler_params=pltpu.CompilerParams(vmem_limit_bytes=vmem),
        cost_estimate=pl.CostEstimate(flops=int(us * US_FLOPS), bytes_accessed=0, transcendentals=0),
    )
    return lambda *args: run(*args, *deps)


def sds(shape, dtype):
    return jax.ShapeDtypeStruct(shape, dtype)


def nn(a, b):
    return lax.dot_general(a, b, (((1,), (0,)), ((), ())), preferred_element_type=F32)


def nt(a, b):
    return lax.dot_general(a, b, (((1,), (1,)), ((), ())), preferred_element_type=F32)


def tn(a, b):
    return lax.dot_general(a, b, (((0,), (0,)), ((), ())), preferred_element_type=F32)


def normalize(hidden):
    centre = hidden - jnp.mean(hidden, axis=-1, keepdims=True)
    inverse = lax.rsqrt(jnp.mean(centre * centre, axis=-1, keepdims=True) + NORM_EPSILON)
    return centre * inverse, inverse


def norm_backward(grad_normed, normal_rows, inverse, gain_row):
    scaled = grad_normed * gain_row
    return inverse * (
        scaled
        - jnp.mean(scaled, axis=-1, keepdims=True)
        - normal_rows * jnp.mean(scaled * normal_rows, axis=-1, keepdims=True)
    )


def head_masks():
    lane = lax.broadcasted_iota(jnp.int32, (1, LANES), 1) // HEAD_DIM
    return [lane == h for h in range(4)]


def stack_heads(rows, masks):
    zero = jnp.zeros_like(rows)
    return jnp.concatenate([jnp.where(mask, rows, zero) for mask in masks], axis=0)


def fold_heads(tall, masks):
    out = jnp.where(masks[0], tall[0:WROWS], 0.0)
    for h in range(1, 4):
        out = jnp.where(masks[h], tall[h * WROWS : (h + 1) * WROWS], out)
    return out


def patch_of(row, shifted):
    w, p = row >> 6, row & 63
    pr = (p * 37) >> 8
    r = (w >> 2) * WIN + pr
    s = (w & 3) * WIN + p - pr * WIN
    if shifted:
        r, s = r + SHIFT, s + SHIFT
        r = jnp.where(r >= SIDE, r - SIDE, r)
        s = jnp.where(s >= SIDE, s - SIDE, s)
    return jnp.where(p < WIN * WIN, r * SIDE + s, -1)


def fill_perm(perm, shifted):
    @pl.loop(0, 8)
    def _(t):
        row = lax.broadcasted_iota(jnp.int32, (128, 1), 0) + t * 128
        same = patch_of(row, shifted) == lax.broadcasted_iota(jnp.int32, (128, CELLS), 1)
        perm[pl.ds(pl.multiple_of(t * 128, 128), 128), :] = jnp.where(same, 1.0, 0.0).astype(BF)


def fill_perm_t(perm_t, shifted):
    source = patch_of(lax.broadcasted_iota(jnp.int32, (1, WTOK), 1), shifted)

    @pl.loop(0, 7)
    def _(t):
        row = lax.broadcasted_iota(jnp.int32, (112, WTOK), 0) + t * 112
        perm_t[pl.ds(pl.multiple_of(t * 112, 112), 112), :] = jnp.where(row == source, 1.0, 0.0).astype(BF)


def fill_slots(onehot, onehot_t, place_col, place_row):
    @pl.loop(0, 7)
    def _(t):
        rows = pl.ds(pl.multiple_of(t * 112, 112), 112)
        place = jnp.concatenate([place_col[rows, :]] * 8, axis=1)
        same = place == lax.broadcasted_iota(jnp.int32, (112, SLOTS), 1)
        onehot[rows, :] = jnp.where(same, 1.0, 0.0).astype(BF)

    @pl.loop(0, 8)
    def _(t):
        row = lax.broadcasted_iota(jnp.int32, (128, CELLS), 0) + t * 128
        same = row == place_row[0:1, :]
        onehot_t[pl.ds(pl.multiple_of(t * 128, 128), 128), :] = jnp.where(same, 1.0, 0.0).astype(BF)


PERM = pltpu.VMEM((WTOK, CELLS), BF)
PERM_T = pltpu.VMEM((CELLS, WTOK), BF)


def attn_fwd_body(shifted, hid, vec, w_in, w_out, bias, mask, h_one, wn, qkv, mixed, attn, perm, perm_t):
    fill_perm(perm, shifted)
    fill_perm_t(perm_t, shifted)
    normal, _ = normalize(hid[...].astype(F32))
    normed = (normal * vec[0:1] + vec[1:2]).astype(BF)
    wn[...] = nn(perm[...], normed).astype(BF)
    in_bias = jnp.concatenate([vec[4:5], jnp.zeros((1, D), F32), vec[5:6]], axis=1)

    @pl.loop(0, 4)
    def _(t):
        rows = pl.ds(pl.multiple_of(t * 256, 256), 256)
        qkv[rows, :] = (nn(wn[rows, :], w_in[...]) + in_bias).astype(BF)

    masks = head_masks()

    @pl.loop(0, WINDOWS)
    def _(w):
        rows = pl.ds(pl.multiple_of(w * WROWS, WROWS), WROWS)
        allow = mask[w] > 0.0
        allow = jnp.concatenate([allow, allow], axis=1)
        for g in range(QUADS):
            cols = slice(g * LANES, (g + 1) * LANES)
            q4 = stack_heads(qkv[rows, g * LANES : (g + 1) * LANES], masks)
            kg = qkv[rows, D + g * LANES : D + (g + 1) * LANES]
            vg = qkv[rows, 2 * D + g * LANES : 2 * D + (g + 1) * LANES]
            s = jnp.where(allow, nt(kg, q4) * SCALE + bias[g], -1e30)
            e = jnp.exp(s - jnp.max(s, axis=0, keepdims=True))
            a = e * (1.0 / jnp.sum(e, axis=0, keepdims=True))
            a = a.astype(BF)
            attn[w * QUADS + g] = a
            mixed[rows, cols] = fold_heads(tn(a, vg), masks).astype(BF)

    back = nn(perm_t[...], mixed[...]).astype(BF)
    h_one[...] = hid[...].astype(F32) + nn(back, w_out[...]) + vec[6:7]


def attn_fwd(shifted, hid, vec, w_in, w_out, bias, mask, deps=()):
    return call(
        functools.partial(attn_fwd_body, shifted),
        (
            sds((CELLS, D), F32),
            sds((WTOK, D), BF),
            sds((WTOK, 3 * D), BF),
            sds((WTOK, D), BF),
            sds((WINDOWS * QUADS, WROWS, PAIR), BF),
        ),
        6,
        scratch=[PERM, PERM_T],
        us=17,
        deps=deps,
    )(hid, vec, w_in, w_out, bias, mask)


def moe_fwd_body(
    h_one, vec, w1, w2, b1, router, router_bias, place_col, place_row,
    out, normed_two, disp, act, slope, picked, gap_out, rows_out, onehot, onehot_t,
):
    fill_slots(onehot, onehot_t, place_col, place_row)
    normal, _ = normalize(h_one[...])
    two = (normal * vec[2:3] + vec[3:4]).astype(BF)
    normed_two[...] = two
    logits = nn(two, router[...])
    gap = (logits[:, LANES:] + router_bias[1:2]) - (logits[:, :LANES] + router_bias[0:1])
    gap = jnp.where(place_col[...] >= SLOTS // 2, gap, -gap)
    gap_out[...] = gap
    gate = 1.0 / (1.0 + jnp.exp(-gap))
    disp[...] = nn(onehot_t[...], two).astype(BF)

    @pl.loop(0, 4)
    def _(t):
        rows = pl.ds(pl.multiple_of(t * 256, 256), 256)
        e = t // 2
        own = disp[rows, :]
        for c in range(3):
            cols = slice(c * 512, (c + 1) * 512)
            pre = nn(own, w1[e, :, cols]) + b1[pl.ds(e, 1), cols]
            phi = 0.5 * (1.0 + lax.erf(pre * 0.7071067811865476))
            act[rows, cols] = (pre * phi).astype(BF)
            slope[rows, cols] = (
                phi + pre * jnp.exp(-0.5 * pre * pre) * 0.3989422804014327
            ).astype(BF)
        rows_out[rows, :] = (nn(act[rows, :], w2[e]) + vec[pl.ds(7 + e, 1)]).astype(BF)

    taken = nn(onehot[...], rows_out[...])
    picked[...] = taken.astype(BF)
    for c in range(3):
        cols = slice(c * LANES, (c + 1) * LANES)
        out[:, cols] = (h_one[:, cols] + gate * taken[:, cols]).astype(out.dtype)


def moe_fwd(h_one, vec, w1, w2, b1, router, router_bias, place, out_dtype, deps=()):
    return call(
        moe_fwd_body,
        (
            sds((CELLS, D), out_dtype),
            sds((CELLS, D), BF),
            sds((SLOTS, D), BF),
            sds((SLOTS, F), BF),
            sds((SLOTS, F), BF),
            sds((CELLS, D), BF),
            sds((CELLS, LANES), F32),
        ),
        9,
        scratch=[pltpu.VMEM((SLOTS, D), BF), PERM_T, PERM],
        us=9.5,
        deps=deps,
    )(h_one, vec, w1, w2, b1, router, router_bias, *place)


def moe_bwd_body(
    grad, h_one, vec, w1, w2, place_col, place_row,
    normed_two, disp, act, slope, picked, gap,
    grad_one, dw1, dw2, db1, drouter, small, g_rows, g_pre, g_disp, onehot, onehot_t,
):
    fill_slots(onehot, onehot_t, place_col, place_row)
    go = grad[...].astype(F32)
    gate = 1.0 / (1.0 + jnp.exp(-gap[...]))
    other = 1.0 / (1.0 + jnp.exp(gap[...]))
    gate_wide = jnp.concatenate([gate] * 3, axis=1)
    g_picked = (go * gate_wide).astype(BF)
    g_gate = jnp.sum(go * picked[...].astype(F32), axis=-1, keepdims=True)
    sign = jnp.where(place_col[...] >= SLOTS // 2, 1.0, -1.0)
    gl = (g_gate * gate * other * sign).astype(BF).astype(F32)
    g_rows[...] = nn(onehot_t[...], g_picked).astype(BF)

    @pl.loop(0, EXPERTS)
    def _(e):
        total = jnp.zeros((1, F), F32)
        for t in range(2):
            rows = pl.ds(pl.multiple_of(e * 512 + t * 256, 256), 256)
            own = g_rows[rows, :]
            parts = []
            for c in range(3):
                cols = slice(c * 512, (c + 1) * 512)
                gp = (nt(own, w2[e, cols, :]) * slope[rows, cols].astype(F32)).astype(BF)
                g_pre[t * 256 : (t + 1) * 256, cols] = gp
                parts.append(jnp.sum(gp.astype(F32), axis=0, keepdims=True))
            total = total + jnp.concatenate(parts, axis=1)
            g_disp[rows, :] = nt(g_pre[t * 256 : (t + 1) * 256, :], w1[e]).astype(BF)
        db1[pl.ds(e, 1), :] = total
        both = pl.ds(pl.multiple_of(e * 512, 512), 512)
        small[pl.ds(7 + e, 1), :] = jnp.sum(g_rows[both, :].astype(F32), axis=0, keepdims=True)
        for c in range(3):
            cols = slice(c * 512, (c + 1) * 512)
            dw1[e, :, cols] = tn(disp[both, :], g_pre[:, cols])
            dw2[e, cols, :] = tn(act[both, cols], g_rows[both, :])

    g_two = nn(onehot[...], g_disp[...])
    gl_wide = jnp.concatenate([gl] * 3, axis=1)
    g_two = g_two + gl_wide * vec[9:10]
    drouter[...] = tn(gl.astype(BF), normed_two[...])[0:8]
    normal, inverse = normalize(h_one[...])
    small[0:1] = jnp.zeros((1, D), F32)
    small[1:2] = jnp.zeros((1, D), F32)
    small[2:3] = jnp.sum(g_two * normal, axis=0, keepdims=True)
    small[3:4] = jnp.sum(g_two, axis=0, keepdims=True)
    small[4:7] = jnp.zeros((3, D), F32)
    small[9:16] = jnp.zeros((7, D), F32)
    small[9:10] = jnp.sum(gl_wide, axis=0, keepdims=True)
    grad_one[...] = go + norm_backward(g_two, normal, inverse, vec[2:3])


def moe_bwd(grad, h_one, vec, w1, w2, place, saved, deps=()):
    return call(
        moe_bwd_body,
        (
            sds((CELLS, D), F32),
            sds((EXPERTS, D, F), F32),
            sds((EXPERTS, F, D), F32),
            sds((8, F), F32),
            sds((8, D), F32),
            sds((16, D), F32),
        ),
        13,
        scratch=[
            pltpu.VMEM((SLOTS, D), BF),
            pltpu.VMEM((512, F), BF),
            pltpu.VMEM((SLOTS, D), BF),
            PERM_T,
            PERM,
        ],
        us=10.5,
        deps=deps,
    )(grad, h_one, vec, w1, w2, *place, *saved)


def attn_bwd_body(
    shifted, grad_one, w_out, qkv, mixed, attn,
    g_qkv, dw_out, dbias, small, g_mix, perm,
):
    fill_perm(perm, shifted)
    gao = grad_one[...].astype(BF)
    small[...] = jnp.zeros((16, D), F32)
    small[6:7] = jnp.sum(gao.astype(F32), axis=0, keepdims=True)
    gao_w = nn(perm[...], gao).astype(BF)
    dw_out[...] = tn(mixed[...], gao_w)
    g_mix[...] = nt(gao_w, w_out[...]).astype(BF)
    dbias[...] = jnp.zeros_like(dbias)
    masks = head_masks()

    @pl.loop(0, WINDOWS)
    def _(w):
        rows = pl.ds(pl.multiple_of(w * WROWS, WROWS), WROWS)
        for g in range(QUADS):
            cols = slice(g * LANES, (g + 1) * LANES)
            kcols = slice(D + g * LANES, D + (g + 1) * LANES)
            vcols = slice(2 * D + g * LANES, 2 * D + (g + 1) * LANES)
            q4 = stack_heads(qkv[rows, cols], masks)
            kg = qkv[rows, kcols]
            vg = qkv[rows, vcols]
            d4 = stack_heads(g_mix[rows, cols], masks)
            a = attn[w * QUADS + g]
            a32 = a.astype(F32)
            t = a32 * nt(vg, d4)
            ds = (t - a32 * jnp.sum(t, axis=0, keepdims=True)).astype(BF)
            dbias[g] += ds.astype(F32)
            g_qkv[rows, cols] = (fold_heads(tn(ds, kg), masks) * SCALE).astype(BF)
            g_qkv[rows, kcols] = (nn(ds, q4) * SCALE).astype(BF)
            g_qkv[rows, vcols] = nn(a, d4).astype(BF)

    small[4:5] = jnp.sum(g_qkv[:, :D].astype(F32), axis=0, keepdims=True)
    small[5:6] = jnp.sum(g_qkv[:, 2 * D :].astype(F32), axis=0, keepdims=True)


def attn_bwd(shifted, grad_one, w_out, saved, deps=()):
    return call(
        functools.partial(attn_bwd_body, shifted),
        (
            sds((WTOK, 3 * D), BF),
            sds((D, D), F32),
            sds((QUADS, WROWS, PAIR), F32),
            sds((16, D), F32),
        ),
        5,
        scratch=[pltpu.VMEM((WTOK, D), BF), PERM],
        us=16.5,
        deps=deps,
    )(grad_one, w_out, *saved)


def proj_bwd_body(shifted, grad_one, hid, vec, w_in, wn, g_qkv, grad_in, dw_in, small, perm_t):
    fill_perm_t(perm_t, shifted)
    for c in range(3):
        cols = slice(c * D, (c + 1) * D)
        dw_in[:, cols] = tn(wn[...], g_qkv[:, cols])
    g_flat = nn(perm_t[...], g_qkv[...]).astype(BF)
    g_normed = nt(g_flat, w_in[...])
    normal, inverse = normalize(hid[...].astype(F32))
    small[...] = jnp.zeros((16, D), F32)
    small[0:1] = jnp.sum(g_normed * normal, axis=0, keepdims=True)
    small[1:2] = jnp.sum(g_normed, axis=0, keepdims=True)
    grad_in[...] = grad_one[...] + norm_backward(g_normed, normal, inverse, vec[0:1])


def proj_bwd(shifted, grad_one, hid, vec, w_in, wn, g_qkv, deps=()):
    return call(
        functools.partial(proj_bwd_body, shifted),
        (sds((CELLS, D), F32), sds((D, 3 * D), F32), sds((16, D), F32)),
        6,
        scratch=[PERM_T],
        us=5.5,
        deps=deps,
    )(grad_one, hid, vec, w_in, wn, g_qkv)


def window_perm_t(shifted):
    source = patch_of(jnp.arange(WTOK, dtype=jnp.int32), shifted)
    return (jnp.arange(CELLS, dtype=jnp.int32)[:, None] == source[None, :]).astype(BF)


def wrap_codes(shifted):
    code = np.zeros((CELLS,), np.float32)
    if shifted:
        for r in range(SIDE):
            for s in range(SIDE):
                rr, ss = (r - SHIFT) % SIDE, (s - SHIFT) % SIDE
                code[r * SIDE + s] = 2 * (rr >= SIDE - SHIFT) + (ss >= SIDE - SHIFT)
    return code


def window_masks(items, shifted):
    labels = items.astype(F32)
    if shifted:
        labels = labels * 4.0 + jnp.asarray(wrap_codes(True))
    placed = nn(jnp.broadcast_to((labels + 1.0).astype(BF), (8, CELLS)), window_perm_t(shifted))[0]
    placed = placed.reshape(WINDOWS, WROWS)
    same = (placed[:, :, None] == placed[:, None, :]) & (placed[:, :, None] > 0.0)
    same = same.astype(F32)
    return jnp.concatenate([same, same], axis=2)


def slot_places(routes, slots):
    group = (jnp.arange(CELLS, dtype=jnp.int32) // GROUP) * CAP
    place = routes * (2 * CAP) + group + slots
    return jnp.broadcast_to(place[:, None], (CELLS, LANES)), jnp.broadcast_to(place[None, :], (8, CELLS))

LEAD = 73
SMALL = 9326
LAG = LEAD * LANES - SMALL
SPANS = ((LEAD, D, 9), (LEAD + 3456, D, 3), (LEAD + 4608, 2 * D, 12), (LEAD + 4608 + 9216, 2 * F, 3))
ALIGNED = LEAD + 4608 + 2 * 9216


def relative(k, bits):
    total = 0
    for place, bit in enumerate(bits):
        total = total + (((k >> (len(bits) - 1 - place)) & 1) << bit)
    return total


def lanes_of(count=LANES):
    return lax.broadcasted_iota(jnp.int32, (1, count), 1)


def equal(rows, columns):
    return jnp.where(rows == columns, 1.0, 0.0).astype(BF)


def spread(shape):
    return lax.broadcasted_iota(jnp.int32, shape, 0), lax.broadcasted_iota(jnp.int32, shape, 1)


def exact(left, one, product):
    high = left.astype(BF)
    low = (left - high.astype(F32)).astype(BF)
    return product(high, one) + product(low, one)


def head_major():
    f, g = spread((D, D))
    return equal(f, 12 * (g & 31) + (g >> 5))


def head_rows(m):
    f, g = spread((D, 2 * LANES))
    return equal((f & 31) + 32 * m, g)


def offset_lanes():
    f, g = spread((LANES, LANES))
    i = g & 63
    r = (i * 37) >> 8
    return equal(f, jnp.where(i < WIN * WIN, 13 * r + i - WIN * r, -1))


def turns():
    return [13 * (6 - j // WIN) + 6 - j % WIN for j in range(WIN * WIN)]


def unpack_bias(flat, wide, tall, bias):
    wide[...] = jnp.zeros_like(wide)
    for m in range(6):
        for c in range(3):
            wide[m : m + 1, c * LANES : (c + 1) * LANES] = flat[12 + 3 * m + c : 13 + 3 * m + c, :]
    by_head = nn(wide[...].astype(BF), head_major())
    sub = lax.broadcasted_iota(jnp.int32, (16, D), 0)
    own = (lanes_of(D) >> 5) == sub
    table = jnp.zeros((16, 2 * LANES), F32)
    for m in range(6):
        table = table + nn(jnp.where(own, by_head[m : m + 1], 0.0).astype(BF), head_rows(m))
    tall[...] = jnp.zeros_like(tall)
    for j, turn in enumerate(turns()):
        row = pltpu.roll(table, (2 * LANES - turn) % (2 * LANES), 1)[:, :LANES]
        tall[pl.ds(j, 16, stride=WROWS), :] = row
    tall[...] = nn(tall[...].astype(BF), offset_lanes())
    for g in range(QUADS):
        for t in range(2):
            h = 4 * g + 2 * t
            left, right = tall[h * WROWS : (h + 1) * WROWS], tall[(h + 1) * WROWS : (h + 2) * WROWS]
            bias[g, :, t * LANES : (t + 1) * LANES] = jnp.where(lanes_of() < WROWS, left, right)


def unpack_small(flat, rows, wide, tall, vec, b1, router, router_bias, bias):
    def shifted(first, count, by):
        near, far = flat[first : first + count, :], flat[first + 1 : first + 1 + count, :]
        return pltpu.roll(jnp.where(lanes_of() >= by, near, far), LANES - by, 1)

    rows[0:16, :] = shifted(27, 16, 108)
    rows[16:46, :] = shifted(42, 30, 110)
    vec[...] = jnp.zeros_like(vec)
    b1[...] = jnp.zeros_like(b1)
    for c in range(3):
        cols = slice(c * LANES, (c + 1) * LANES)
        for n in range(4):
            vec[n : n + 1, cols] = flat[3 * n + c : 3 * n + c + 1, :]
        for n in range(3):
            vec[4 + n : 5 + n, cols] = rows[3 * n + c : 3 * n + c + 1, :]
        for e in range(EXPERTS):
            vec[7 + e : 8 + e, cols] = rows[40 + 3 * e + c : 41 + 3 * e + c, :]
    for e in range(EXPERTS):
        for c in range(12):
            b1[e : e + 1, c * LANES : (c + 1) * LANES] = rows[16 + 12 * e + c : 17 + 12 * e + c, :]
        one = jnp.sum(jnp.where(lanes_of() == e, rows[15:16, :], 0.0), axis=1, keepdims=True)
        router_bias[e : e + 1, :] = jnp.broadcast_to(one, (1, LANES))
    pairs = jnp.concatenate([rows[9 + c : 10 + c, :] for c in range(6)], axis=1)
    pairs = jnp.broadcast_to(pairs, (LANES, 2 * D)).astype(BF)
    d, f = spread((D, 2 * D))
    for e in range(EXPERTS):
        router[:, e * LANES : (e + 1) * LANES] = nt(equal(f, 2 * d + e), pairs).astype(BF)
    gap = nt(pairs[0:16], equal(f, 2 * d + 1)) - nt(pairs[0:16], equal(f, 2 * d))
    vec[9:10, :] = gap[0:1]
    unpack_bias(flat, wide, tall, bias)


def unpack_body(rows, padded, runs, me, *refs):
    got = refs[: len(runs)]
    w_in, w_out, w1, w2, vec, b1, router, router_bias, bias, flat, few, wide, tall = refs[len(runs) :]
    for (bits, fixed), part in zip(runs, got):

        @pl.loop(0, 1 << len(bits))
        def _(k, bits=bits, fixed=fixed, part=part):
            d = me[0] ^ (relative(k, bits) + fixed)
            flat[pl.ds(d * rows, rows), :] = part[k, :rows, :].astype(F32)

    unpack_small(flat, few, wide, tall, vec, b1, router, router_bias, bias)
    for (base, height, tiles), out in zip(SPANS, (w_in, w_out, w1, w2)):
        step = 64

        @pl.loop(0, height // step)
        def _(t, base=base, tiles=tiles, out=out):
            first = base - 1 + t * (step * tiles)
            before = flat[pl.ds(first, step, stride=tiles), :]
            for j in range(tiles):
                here = flat[pl.ds(first + 1 + j, step, stride=tiles), :]
                tile = pltpu.roll(jnp.where(lanes_of() >= LANES - LAG, before, here), LAG, 1)
                out[pl.ds(pl.multiple_of(t * step, step), step), j * LANES : (j + 1) * LANES] = tile.astype(BF)
                before = here


class Weights(NamedTuple):
    w_in: Any
    w_out: Any
    w1: Any
    w2: Any
    vec: Any
    b1: Any
    router: Any
    router_bias: Any
    bias: Any


def unpack_weights(me, parts, runs, rows, devices, deps=()):
    padded = parts[0].shape[1]
    got = Weights(
        *call(
            functools.partial(unpack_body, rows, padded, runs),
            (
                sds((D, 3 * D), BF),
                sds((D, D), BF),
                sds((2 * D, F), BF),
                sds((2 * F, D), BF),
                sds((16, D), F32),
                sds((8, F), F32),
                sds((D, 2 * LANES), BF),
                sds((8, LANES), F32),
                sds((QUADS, WROWS, PAIR), F32),
            ),
            1 + len(parts),
            scratch=[
                pltpu.VMEM((devices * rows + 8, LANES), F32),
                pltpu.VMEM((48, LANES), F32),
                pltpu.VMEM((8, D), F32),
                pltpu.VMEM((16 * WROWS, LANES), F32),
            ],
            smem=1,
            us=10,
            deps=deps,
        )(me, *parts)
    )
    return got._replace(w1=got.w1.reshape(EXPERTS, D, F), w2=got.w2.reshape(EXPERTS, F, D))


def pack_bias(dbias, wide, tall):
    tall[HEADS * WROWS :, :] = jnp.zeros((4 * WROWS, LANES), F32)
    for h in range(HEADS):
        g, t, side = h // 4, (h % 4) // 2, h % 2
        tile = dbias[g, :, t * LANES : (t + 1) * LANES]
        tall[h * WROWS : (h + 1) * WROWS, :] = jnp.where((lanes_of() >> 6) == side, tile, 0.0)
    used = HEADS * WROWS
    tall[0:used, :] = exact(tall[0:used, :], offset_lanes(), nt)
    table = jnp.zeros((16, 2 * LANES), F32)
    for j, turn in enumerate(turns()):
        row = tall[pl.ds(j, 16, stride=WROWS), :]
        table = table + pltpu.roll(jnp.concatenate([row, jnp.zeros_like(row)], axis=1), turn, 1)
    sub = lax.broadcasted_iota(jnp.int32, (16, D), 0)
    own = (lanes_of(D) >> 5) == sub
    wide[...] = jnp.zeros_like(wide)
    for m in range(6):
        placed = jnp.where(own, exact(table, head_rows(m), nt), 0.0)
        wide[m : m + 1, :] = jnp.sum(placed, axis=0, keepdims=True)
    wide[...] = exact(wide[...], head_major(), nt)


def pack_small(al, vectors, drouter, db1, dbias, one, two, wide, tall):
    one[...] = jnp.zeros_like(one)
    two[...] = jnp.zeros_like(two)
    pack_bias(dbias, wide, tall)
    d, f = spread((D, 2 * D))
    signs = equal(f, 2 * d + 1) - equal(f, 2 * d)
    pairs = exact(drouter[...], signs, nn)
    for c in range(3):
        cols = slice(c * LANES, (c + 1) * LANES)
        for n in range(4):
            one[1 + 3 * n + c : 2 + 3 * n + c, :] = vectors[n : n + 1, cols]
        for m in range(6):
            one[13 + 3 * m + c : 14 + 3 * m + c, :] = wide[m : m + 1, cols]
        for n in range(3):
            two[1 + 3 * n + c : 2 + 3 * n + c, :] = vectors[4 + n : 5 + n, cols]
        for e in range(EXPERTS):
            al[67 + 3 * e + c : 68 + 3 * e + c, :] = vectors[7 + e : 8 + e, cols]
    for c in range(6):
        two[10 + c : 11 + c, :] = pairs[0:1, c * LANES : (c + 1) * LANES]
    total = vectors[9:10, 0:LANES]
    two[16:17, :] = jnp.where(lanes_of() == 0, -total, jnp.where(lanes_of() == 1, total, 0.0))
    for e in range(EXPERTS):
        for c in range(12):
            al[43 + 12 * e + c : 44 + 12 * e + c, :] = db1[e : e + 1, c * LANES : (c + 1) * LANES]
    first = pltpu.roll(jnp.where(lanes_of() >= LANES - 18, one[0:28, :], one[1:29, :]), 18, 1)
    second = pltpu.roll(jnp.where(lanes_of() >= LANES - 126, two[0:16, :], two[1:17, :]), 126, 1)
    al[27:43, :] = second
    al[0:27, :] = first[0:27]
    al[27:28, :] += first[27:28]


def pack_body(
    rows, padded, runs, me, moe, attn, proj, drouter, db1, dbias, dw_in, dw_out, dw1, dw2,
    keep, send, vectors, al, one, two, wide, tall,
):
    vectors[...] = moe[...] + attn[...] + proj[...]
    pack_small(al, vectors, drouter, db1, dbias, one, two, wide, tall)
    tail = al.shape[0] - ALIGNED
    al[pl.ds(ALIGNED, tail), :] = jnp.zeros((tail, LANES), F32)
    for (base, height, tiles), grad in zip(SPANS, (dw_in, dw_out, dw1, dw2)):
        step = 64

        @pl.loop(0, height // step)
        def _(t, base=base, tiles=tiles, grad=grad):
            first = base + t * (step * tiles)
            own = pl.ds(pl.multiple_of(t * step, step), step)
            for j in range(tiles):
                al[pl.ds(first + j, step, stride=tiles), :] = grad[own, j * LANES : (j + 1) * LANES]

    at = 0
    for bits, fixed in runs:
        for other, out in enumerate((keep, send)):

            @pl.loop(0, 1 << len(bits))
            def _(k, bits=bits, fixed=fixed, at=at, other=other, out=out):
                d = me[0] ^ (relative(k, bits) + fixed + other)
                out[at + k] = al[pl.ds(d * rows, padded), :].astype(BF)

        at += 1 << len(bits)


def pack_grads(me, small, dw_in, dw_out, dw1, dw2, runs, rows, devices, padded, deps=()):
    shape = sds((devices // 2, padded, LANES), BF)
    return call(
        functools.partial(pack_body, rows, padded, runs),
        (shape, shape, sds((16, D), F32)),
        11,
        scratch=[
            pltpu.VMEM((devices * rows + padded, LANES), F32),
            pltpu.VMEM((40, LANES), F32),
            pltpu.VMEM((24, LANES), F32),
            pltpu.VMEM((8, D), F32),
            pltpu.VMEM((16 * WROWS, LANES), F32),
        ],
        smem=1,
        us=4,
        deps=deps,
    )(me, *small, dw_in, dw_out, dw1.reshape(2 * D, F), dw2.reshape(2 * F, D))


def join_body(a, b, out):
    n = a.shape[0]

    @pl.loop(0, n)
    def _(i):
        out[i] = a[i]
        out[n + i] = b[i]


def join(a, b):
    return call(join_body, sds((2 * a.shape[0], *a.shape[1:]), a.dtype), 2)(a, b)


class Ways(NamedTuple):
    core: Any
    x: Any
    y: Any
    low: Any
    high: Any
    rest: Any


def ways():
    dp, fsdp = (lax.axis_size(axis).bit_length() - 1 for axis in (DP, FSDP))
    rest = [(DP, bit) for bit in range(1, dp - 2)] + [(FSDP, bit) for bit in range(2, fsdp)]
    return Ways((FSDP, 0), (FSDP, 1), (DP, 0), (DP, dp - 2), (DP, dp - 1), rest)


def weight_bit(way):
    axis, bit = way
    return bit if axis == FSDP else bit + lax.axis_size(FSDP).bit_length() - 1


def flip(array, way):
    axis, bit = way
    return lax.ppermute(array, axis, [(i, i ^ (1 << bit)) for i in range(lax.axis_size(axis))])


def tie(arrays, others):
    return lax.optimization_barrier((arrays, others))[0]


def bits_of(*order):
    return [weight_bit(way) for way in order]


class Gather:
    def __init__(self, own, way):
        for extra in way.rest:
            own = join(own, flip(own, extra))
        self.way, self.own = way, own
        self.rest = bits_of(*reversed(way.rest))

    def far(self):
        own, way = self.own, self.way
        self.pair = join(own, flip(own, way.high))
        self.over = flip(self.pair, way.low)

    def near(self):
        way = self.way
        self.a = join(self.pair, flip(self.pair, way.x))
        self.b = join(self.over, flip(self.over, way.y))

    def last(self):
        way = self.way
        self.parts = [self.a, flip(self.a, way.y), self.b, flip(self.b, way.x)]
        self.parts += [flip(part, way.core) for part in self.parts]
        high, rest = bits_of(way.high), self.rest
        one, two = bits_of(way.x) + high + rest, bits_of(way.y) + high + rest
        x, y, low, core = (1 << weight_bit(w) for w in (way.x, way.y, way.low, way.core))
        self.runs = [(one, 0), (one, y), (two, low), (two, low + x)]
        self.runs += [(bits, fixed + core) for bits, fixed in self.runs]


def scatter_runs(way):
    tail = bits_of(way.high, *way.rest)
    x, y, low = (1 << weight_bit(w) for w in (way.x, way.y, way.low))
    bx, by = bits_of(way.x), bits_of(way.y)
    return [(bx + tail, y), (tail, x), (tail, 0), (by + tail, low + x), (tail, low + y), (tail, low)]


class Scatter:
    def __init__(self, keep, send, way):
        self.way, self.keep, self.n = way, keep, keep.shape[0] // 16
        self.got = flip(send, way.core)

    def sum(self, first, count):
        cut = slice(first * self.n, (first + count) * self.n)
        return self.keep[cut].astype(F32) + self.got[cut].astype(F32)

    def near(self):
        way = self.way
        self.a = flip(self.sum(0, 4).astype(BF), way.y)
        self.b = flip(self.sum(8, 4).astype(BF), way.x)

    def next(self):
        way, n = self.way, self.n
        a, b = self.a.astype(F32), self.b.astype(F32)
        a_sent = flip((self.sum(4, 2) + a[2 * n :]).astype(BF), way.x)
        b_sent = flip((self.sum(12, 2) + b[2 * n :]).astype(BF), way.y)
        self.a = self.sum(6, 2) + a[: 2 * n] + a_sent.astype(F32)
        self.b = self.sum(14, 2) + b[: 2 * n] + b_sent.astype(F32)

    def low(self):
        self.total = self.a + flip(self.b.astype(BF), self.way.low).astype(F32)

    def high(self):
        total = self.total
        for way in [self.way.high] + self.way.rest:
            half = total.shape[0] // 2
            total = total[:half] + flip(total[half:].astype(BF), way).astype(F32)
        self.total = total[0]


def shards(inputs, items, routes, slots, cotangent, params, momentum, average):
    fsdp, dp = lax.axis_size(FSDP), lax.axis_size(DP)
    devices = fsdp * dp
    share = params.shape[1]
    rows = share // LANES
    padded = -(-(rows + 1) // 16) * 16
    step_rate = RATE_BASE / math.sqrt(CELLS * devices)
    way = ways()
    me = (lax.axis_index(DP) * fsdp + lax.axis_index(FSDP)).astype(jnp.int32).reshape(1)

    gathers = []
    for b in range(BLOCKS):
        own = params[b].astype(BF).reshape(1, rows, LANES)
        gathers.append(Gather(jnp.pad(own, ((0, 0), (0, padded - rows), (0, 0))), way))
    masks, places = [], []
    for b in range(BLOCKS):
        masks.append(window_masks(items.reshape(CELLS), b % 2 == 1))
        places.append(slot_places(routes[b].reshape(CELLS), slots[b].reshape(CELLS)))

    first, second = gathers
    first.far()
    second.own = tie(second.own, first.over)
    first.near()
    second.far()
    first.last()
    hidden = inputs.reshape(CELLS, D)
    saves = []

    w = unpack_weights(me, first.parts, first.runs, rows, devices)
    second.pair, second.over = tie((second.pair, second.over), first.parts)
    second.near()
    h_one, *kept_attn = attn_fwd(False, hidden, w.vec, w.w_in, w.w_out, w.bias, masks[0], (second.over,))
    second.a, second.b = tie((second.a, second.b), h_one)
    second.last()
    following, *kept_moe = moe_fwd(
        h_one, w.vec, w.w1, w.w2, w.b1, w.router, w.router_bias, places[0], F32
    )
    saves.append((hidden, h_one, w, kept_attn, kept_moe))
    hidden = following
    w = unpack_weights(me, second.parts, second.runs, rows, devices, (hidden,))
    h_one, *kept_attn = attn_fwd(True, hidden, w.vec, w.w_in, w.w_out, w.bias, masks[1])
    outputs, *kept_moe = moe_fwd(
        h_one, w.vec, w.w1, w.w2, w.b1, w.router, w.router_bias, places[1], BF
    )
    saves.append((hidden, h_one, w, kept_attn, kept_moe))

    gradient = cotangent.reshape(CELLS, D)
    runs = scatter_runs(way)
    scatters, vectors = [None] * BLOCKS, [None] * BLOCKS
    for b in range(BLOCKS - 1, -1, -1):
        hidden, h_one, w, kept_attn, kept_moe = saves[b]
        shifted = b % 2 == 1
        before = scatters[-1]
        g_one, dw1, dw2, db1, drouter, small_moe = moe_bwd(gradient, h_one, w.vec, w.w1, w.w2, places[b], kept_moe)
        if before is not None:
            before.got = tie(before.got, g_one)
            before.near()
        g_qkv, dw_out, dbias, small_attn = attn_bwd(shifted, g_one, w.w_out, kept_attn[1:])
        if before is not None:
            before.a, before.b = tie((before.a, before.b), g_qkv)
            before.next()
        gradient, dw_in, small_proj = proj_bwd(shifted, g_one, hidden, w.vec, w.w_in, kept_attn[0], g_qkv)
        small = (small_moe, small_attn, small_proj, drouter, db1, dbias)
        keep, send, vectors[b] = pack_grads(me, small, dw_in, dw_out, dw1, dw2, runs, rows, devices, padded)
        if before is not None:
            before.a, before.b = tie((before.a, before.b), send)
        else:
            gradient = tie(gradient, send)
        scatters[b] = Scatter(keep, send, way)
    early, late = scatters[1], scatters[0]
    vector_grads = jnp.stack(vectors)[:, :9]
    vector_grads = vector_grads + flip(vector_grads, way.core)
    early.low()
    late.near()
    early.total, vector_grads = tie((early.total, vector_grads), late.got)
    vector_grads = vector_grads + flip(vector_grads, way.x)
    early.high()
    late.next()
    vector_grads = tie(vector_grads, (late.a, late.b))
    vector_grads = vector_grads + flip(vector_grads, way.y)
    late.low()
    vector_grads = tie(vector_grads, late.total)
    vector_grads = vector_grads + flip(vector_grads, way.low)
    late.high()
    for step in [way.high] + way.rest:
        vector_grads = vector_grads + flip(vector_grads, step)
    grad_all = jnp.stack([scatter.total.reshape(-1)[LAG : LAG + share] for scatter in scatters])
    new_momentum = MOMENTUM_DECAY * momentum + grad_all
    new_params = params - step_rate * (grad_all + MOMENTUM_DECAY * new_momentum)
    new_average = AVERAGE_DECAY * average + (1.0 - AVERAGE_DECAY) * new_params
    return (
        outputs.reshape(1, CELLS, D),
        gradient.reshape(1, CELLS, D),
        new_params,
        new_momentum,
        new_average,
        vector_grads,
    )


def solution(mesh):
    both = (DP, FSDP)
    canvas, vector = P(both), P(None, both)
    return jax.shard_map(
        shards,
        mesh=mesh,
        in_specs=(canvas, canvas, vector, vector, canvas, vector, vector, vector),
        out_specs=(canvas, canvas, vector, vector, vector, P()),
        check_vma=False,
    )
```

```python
import functools
import math
from typing import Any, NamedTuple

import jax
import jax.numpy as jnp
import numpy as np
from jax import lax
from jax.experimental import pallas as pl
from jax.experimental.pallas import tpu as pltpu
from jax.sharding import PartitionSpec as P

D = 384
HEADS = 12
F = 1536
HEAD_DIM = 32
EXPERTS = 2
CAP = 256
SIDE = 28
WIN = 7
SHIFT = 3
BLOCKS = 2
CELLS = 784
GROUP = 392
RELS = 169
NORM_EPSILON = 1e-05
MOMENTUM_DECAY = 0.9
AVERAGE_DECAY = 0.9
RATE_BASE = 0.1

DP = "dp"
FSDP = "fsdp"
LANES = 128
WROWS = 64
WINDOWS = 16
WTOK = WINDOWS * WROWS
SLOTS = EXPERTS * 2 * CAP
FIRST = 8
PAIR = 4 * WROWS
QUADS = HEADS // 4
SCALE = HEAD_DIM ** (-0.5)
US_FLOPS = 1.0e9
BF = jnp.bfloat16
F32 = jnp.float32
VMEM_BYTES = 20 * 1024 * 1024


def call(body, out_shape, n_in, scratch=(), smem=0, deps=(), us=1, vmem=VMEM_BYTES):
    def skipping(*refs):
        body(*refs[:n_in], *refs[n_in + len(deps) :])

    run = pl.pallas_call(
        skipping,
        out_shape=out_shape,
        in_specs=[pl.BlockSpec(memory_space=pltpu.SMEM)] * smem
        + [pl.BlockSpec(memory_space=pltpu.VMEM)] * (n_in - smem)
        + [pl.BlockSpec(memory_space=pl.ANY)] * len(deps),
        out_specs=jax.tree.map(lambda _: pl.BlockSpec(memory_space=pltpu.VMEM), out_shape),
        scratch_shapes=list(scratch),
        compiler_params=pltpu.CompilerParams(vmem_limit_bytes=vmem),
        cost_estimate=pl.CostEstimate(flops=int(us * US_FLOPS), bytes_accessed=0, transcendentals=0),
    )
    return lambda *args: run(*args, *deps)


def sds(shape, dtype):
    return jax.ShapeDtypeStruct(shape, dtype)


def nn(a, b):
    return lax.dot_general(a, b, (((1,), (0,)), ((), ())), preferred_element_type=F32)


def nt(a, b):
    return lax.dot_general(a, b, (((1,), (1,)), ((), ())), preferred_element_type=F32)


def tn(a, b):
    return lax.dot_general(a, b, (((0,), (0,)), ((), ())), preferred_element_type=F32)


def normalize(hidden):
    centre = hidden - jnp.mean(hidden, axis=-1, keepdims=True)
    inverse = lax.rsqrt(jnp.mean(centre * centre, axis=-1, keepdims=True) + NORM_EPSILON)
    return centre * inverse, inverse


def norm_backward(grad_normed, normal_rows, inverse, gain_row):
    scaled = grad_normed * gain_row
    return inverse * (
        scaled
        - jnp.mean(scaled, axis=-1, keepdims=True)
        - normal_rows * jnp.mean(scaled * normal_rows, axis=-1, keepdims=True)
    )


def head_masks():
    lane = lax.broadcasted_iota(jnp.int32, (1, LANES), 1) // HEAD_DIM
    return [lane == h for h in range(4)]


def stack_heads(rows, masks):
    zero = jnp.zeros_like(rows)
    return jnp.concatenate([jnp.where(mask, rows, zero) for mask in masks], axis=0)


def fold_heads(tall, masks):
    out = jnp.where(masks[0], tall[0:WROWS], 0.0)
    for h in range(1, 4):
        out = jnp.where(masks[h], tall[h * WROWS : (h + 1) * WROWS], out)
    return out


def patch_of(row, shifted):
    w, p = row >> 6, row & 63
    pr = (p * 37) >> 8
    r = (w >> 2) * WIN + pr
    s = (w & 3) * WIN + p - pr * WIN
    if shifted:
        r, s = r + SHIFT, s + SHIFT
        r = jnp.where(r >= SIDE, r - SIDE, r)
        s = jnp.where(s >= SIDE, s - SIDE, s)
    return jnp.where(p < WIN * WIN, r * SIDE + s, -1)


def runs_of(shifted):
    runs = []
    for w in range(WINDOWS):
        for p in range(WIN):
            r, s = (w // 4) * WIN + p, (w % 4) * WIN
            if shifted:
                r, s = (r + SHIFT) % SIDE, s + SHIFT
            here = min(WIN, SIDE - s)
            runs.append((w * WROWS + p * WIN, r * SIDE + s, here))
            if here < WIN:
                runs.append((w * WROWS + p * WIN + here, r * SIDE, WIN - here))
    return runs


def to_windows(patches, windows, shifted):
    windows[...] = jnp.zeros_like(windows)
    for row, patch, length in runs_of(shifted):
        windows[row : row + length, :] = patches[patch : patch + length, :]


def to_patches(windows, patches, shifted):
    for row, patch, length in runs_of(shifted):
        patches[patch : patch + length, :] = windows[row : row + length, :]


def fill_slots(onehot, onehot_t, place_col, place_row):
    @pl.loop(0, 7)
    def _(t):
        rows = pl.ds(pl.multiple_of(t * 112, 112), 112)
        place = jnp.concatenate([place_col[rows, :]] * 8, axis=1)
        same = place == lax.broadcasted_iota(jnp.int32, (112, SLOTS), 1)
        onehot[rows, :] = jnp.where(same, 1.0, 0.0).astype(BF)

    @pl.loop(0, 8)
    def _(t):
        row = lax.broadcasted_iota(jnp.int32, (128, CELLS), 0) + t * 128
        same = row == place_row[0:1, :]
        onehot_t[pl.ds(pl.multiple_of(t * 128, 128), 128), :] = jnp.where(same, 1.0, 0.0).astype(BF)


PATCHES = pltpu.VMEM((CELLS, D), F32)
PADDED = pltpu.VMEM((WTOK, D), F32)
ONEHOT = pltpu.VMEM((CELLS, SLOTS), BF)
ONEHOT_T = pltpu.VMEM((SLOTS, CELLS), BF)


def attn_fwd_body(shifted, hid, vec, w_in, w_out, bias, mask, h_one, wn, qkv, mixed, attn, patches, windows):
    normal, _ = normalize(hid[...].astype(F32))
    patches[...] = normal * vec[0:1] + vec[1:2]
    to_windows(patches, windows, shifted)
    wn[...] = windows[...].astype(BF)
    in_bias = jnp.concatenate([vec[4:5], jnp.zeros((1, D), F32), vec[5:6]], axis=1)

    @pl.loop(0, 4)
    def _(t):
        rows = pl.ds(pl.multiple_of(t * 256, 256), 256)
        qkv[rows, :] = (nn(wn[rows, :], w_in[...]) + in_bias).astype(BF)

    masks = head_masks()

    @pl.loop(0, WINDOWS // 8)
    def _(wo):
        units = [(i, g) for i in range(8) for g in range(QUADS)]
        rows = [pl.ds(pl.multiple_of((wo * 8 + i) * WROWS, WROWS), WROWS) for i in range(8)]
        allow = []
        for i in range(8):
            one = mask[wo * 8 + i] > 0.0
            allow.append(jnp.concatenate([one, one], axis=1))
        scores = []
        for i, g in units:
            q4 = stack_heads(qkv[rows[i], g * LANES : (g + 1) * LANES], masks)
            scores.append(nt(qkv[rows[i], D + g * LANES : D + (g + 1) * LANES], q4))
        probs = []
        for (i, g), s in zip(units, scores):
            s = jnp.where(allow[i], s * SCALE + bias[g], -1e30)
            e = jnp.exp(s - jnp.max(s, axis=0, keepdims=True))
            a = (e * (1.0 / jnp.sum(e, axis=0, keepdims=True))).astype(BF)
            attn[(wo * 8 + i) * QUADS + g] = a
            probs.append(a)
        tall = [tn(a, qkv[rows[i], 2 * D + g * LANES : 2 * D + (g + 1) * LANES]) for (i, g), a in zip(units, probs)]
        for (i, g), t in zip(units, tall):
            t = fold_heads(t, masks)
            windows[rows[i], g * LANES : (g + 1) * LANES] = t
            mixed[rows[i], g * LANES : (g + 1) * LANES] = t.astype(BF)

    to_patches(windows, patches, shifted)
    h_one[...] = hid[...].astype(F32) + nn(patches[...].astype(BF), w_out[...]) + vec[6:7]


def attn_fwd(shifted, hid, vec, w_in, w_out, bias, mask, deps=()):
    return call(
        functools.partial(attn_fwd_body, shifted),
        (
            sds((CELLS, D), F32),
            sds((WTOK, D), BF),
            sds((WTOK, 3 * D), BF),
            sds((WTOK, D), BF),
            sds((WINDOWS * QUADS, WROWS, PAIR), BF),
        ),
        6,
        scratch=[PATCHES, PADDED],
        us=8,
        deps=deps,
    )(hid, vec, w_in, w_out, bias, mask)


def moe_fwd_body(
    h_one, vec, w1, w2, b1, router, router_bias, place_col, place_row,
    out, normed_two, disp, act, slope, picked, gap_out, rows_out, onehot, onehot_t,
):
    fill_slots(onehot, onehot_t, place_col, place_row)
    normal, _ = normalize(h_one[...])
    two = (normal * vec[2:3] + vec[3:4]).astype(BF)
    normed_two[...] = two
    logits = nn(two, router[...])
    gap = (logits[:, LANES:] + router_bias[1:2]) - (logits[:, :LANES] + router_bias[0:1])
    gap = jnp.where(place_col[...] >= SLOTS // 2, gap, -gap)
    gap_out[...] = gap
    gate = 1.0 / (1.0 + jnp.exp(-gap))
    disp[...] = nn(onehot_t[...], two).astype(BF)

    @pl.loop(0, 4, unroll=4)
    def _(t):
        rows = pl.ds(pl.multiple_of(t * 256, 256), 256)
        e = t // 2
        own = disp[rows, :]
        for c in range(3):
            cols = slice(c * 512, (c + 1) * 512)
            pre = nn(own, w1[e, :, cols]) + b1[pl.ds(e, 1), cols]
            phi = 0.5 * (1.0 + lax.erf(pre * 0.7071067811865476))
            act[rows, cols] = (pre * phi).astype(BF)
            slope[rows, cols] = (
                phi + pre * jnp.exp(-0.5 * pre * pre) * 0.3989422804014327
            ).astype(BF)
        rows_out[rows, :] = (nn(act[rows, :], w2[e]) + vec[pl.ds(7 + e, 1)]).astype(BF)

    taken = nn(onehot[...], rows_out[...])
    picked[...] = taken.astype(BF)
    for c in range(3):
        cols = slice(c * LANES, (c + 1) * LANES)
        out[:, cols] = (h_one[:, cols] + gate * taken[:, cols]).astype(out.dtype)


def moe_fwd(h_one, vec, w1, w2, b1, router, router_bias, place, out_dtype, deps=()):
    return call(
        moe_fwd_body,
        (
            sds((CELLS, D), out_dtype),
            sds((CELLS, D), BF),
            sds((SLOTS, D), BF),
            sds((SLOTS, F), BF),
            sds((SLOTS, F), BF),
            sds((CELLS, D), BF),
            sds((CELLS, LANES), F32),
        ),
        9,
        scratch=[pltpu.VMEM((SLOTS, D), BF), ONEHOT, ONEHOT_T],
        us=9.5,
        deps=deps,
    )(h_one, vec, w1, w2, b1, router, router_bias, *place)


def moe_bwd_body(
    grad, h_one, vec, w1, w2, place_col, place_row,
    normed_two, disp, act, slope, picked, gap,
    grad_one, dw1, dw2, db1, drouter, small, g_rows, g_pre, g_disp, onehot, onehot_t,
):
    fill_slots(onehot, onehot_t, place_col, place_row)
    go = grad[...].astype(F32)
    gate = 1.0 / (1.0 + jnp.exp(-gap[...]))
    other = 1.0 / (1.0 + jnp.exp(gap[...]))
    gate_wide = jnp.concatenate([gate] * 3, axis=1)
    g_picked = (go * gate_wide).astype(BF)
    g_gate = jnp.sum(go * picked[...].astype(F32), axis=-1, keepdims=True)
    sign = jnp.where(place_col[...] >= SLOTS // 2, 1.0, -1.0)
    gl = (g_gate * gate * other * sign).astype(BF).astype(F32)
    g_rows[...] = nn(onehot_t[...], g_picked).astype(BF)

    @pl.loop(0, EXPERTS)
    def _(e):
        total = jnp.zeros((1, F), F32)
        for t in range(2):
            rows = pl.ds(pl.multiple_of(e * 512 + t * 256, 256), 256)
            own = g_rows[rows, :]
            parts = []
            for c in range(3):
                cols = slice(c * 512, (c + 1) * 512)
                gp = (nt(own, w2[e, cols, :]) * slope[rows, cols].astype(F32)).astype(BF)
                g_pre[t * 256 : (t + 1) * 256, cols] = gp
                parts.append(jnp.sum(gp.astype(F32), axis=0, keepdims=True))
            total = total + jnp.concatenate(parts, axis=1)
            g_disp[rows, :] = nt(g_pre[t * 256 : (t + 1) * 256, :], w1[e]).astype(BF)
        db1[pl.ds(e, 1), :] = total
        both = pl.ds(pl.multiple_of(e * 512, 512), 512)
        small[pl.ds(7 + e, 1), :] = jnp.sum(g_rows[both, :].astype(F32), axis=0, keepdims=True)
        for c in range(3):
            cols = slice(c * 512, (c + 1) * 512)
            dw1[e, :, cols] = tn(disp[both, :], g_pre[:, cols])
            dw2[e, cols, :] = tn(act[both, cols], g_rows[both, :])

    g_two = nn(onehot[...], g_disp[...])
    gl_wide = jnp.concatenate([gl] * 3, axis=1)
    g_two = g_two + gl_wide * vec[9:10]
    drouter[...] = tn(gl.astype(BF), normed_two[...])[0:8]
    normal, inverse = normalize(h_one[...])
    small[0:1] = jnp.zeros((1, D), F32)
    small[1:2] = jnp.zeros((1, D), F32)
    small[2:3] = jnp.sum(g_two * normal, axis=0, keepdims=True)
    small[3:4] = jnp.sum(g_two, axis=0, keepdims=True)
    small[4:7] = jnp.zeros((3, D), F32)
    small[9:16] = jnp.zeros((7, D), F32)
    small[9:10] = jnp.sum(gl_wide, axis=0, keepdims=True)
    grad_one[...] = go + norm_backward(g_two, normal, inverse, vec[2:3])


def moe_bwd(grad, h_one, vec, w1, w2, place, saved, deps=()):
    return call(
        moe_bwd_body,
        (
            sds((CELLS, D), F32),
            sds((EXPERTS, D, F), F32),
            sds((EXPERTS, F, D), F32),
            sds((8, F), F32),
            sds((8, D), F32),
            sds((16, D), F32),
        ),
        13,
        scratch=[
            pltpu.VMEM((SLOTS, D), BF),
            pltpu.VMEM((512, F), BF),
            pltpu.VMEM((SLOTS, D), BF),
            ONEHOT,
            ONEHOT_T,
        ],
        us=10.5,
        deps=deps,
    )(grad, h_one, vec, w1, w2, *place, *saved)


def attn_bwd_windows(windows, qkv, g_mix, attn, g_qkv, dbias, base=None):
    masks = head_masks()
    base = windows[0] if base is None else base

    start, stop = windows
    per = min(4, stop - start)

    @pl.loop(0, (stop - start) // per)
    def _(wo):
        units = [(i, g) for i in range(per) for g in range(QUADS)]
        first = [start + wo * per + i for i in range(per)]
        rows = [pl.ds(pl.multiple_of(w * WROWS, WROWS), WROWS) for w in first]
        outs = [pl.ds(pl.multiple_of((w - base) * WROWS, WROWS), WROWS) for w in first]
        cols = [[slice(n * D + g * LANES, n * D + (g + 1) * LANES) for g in range(QUADS)] for n in range(3)]
        d4s = [stack_heads(g_mix[rows[i], cols[0][g]], masks) for i, g in units]
        grads = [nt(qkv[rows[i], cols[2][g]], d4) for (i, g), d4 in zip(units, d4s)]
        probs = [attn[first[i] * QUADS + g] for i, g in units]
        for (i, g), a, d4 in zip(units, probs, d4s):
            g_qkv[outs[i], cols[2][g]] = nn(a, d4).astype(BF)
        dss = []
        for a, grad in zip(probs, grads):
            a = a.astype(F32)
            t = a * grad
            dss.append((t - a * jnp.sum(t, axis=0, keepdims=True)).astype(BF))
        for g in range(QUADS):
            total = dbias[g]
            for (_, other), ds in zip(units, dss):
                if other == g:
                    total = total + ds.astype(F32)
            dbias[g] = total
        talls = [tn(ds, qkv[rows[i], cols[1][g]]) for (i, g), ds in zip(units, dss)]
        for (i, g), ds in zip(units, dss):
            q4 = stack_heads(qkv[rows[i], cols[0][g]], masks)
            g_qkv[outs[i], cols[1][g]] = (nn(ds, q4) * SCALE).astype(BF)
        for (i, g), tall in zip(units, talls):
            g_qkv[outs[i], cols[0][g]] = (fold_heads(tall, masks) * SCALE).astype(BF)


def attn_bwd_one_body(
    shifted, windows, grad_one, w_out, qkv, mixed, attn,
    g_qkv, g_mix, dw_out, dbias, small, windows_of,
):
    gao = grad_one[...].astype(BF)
    small[...] = jnp.zeros((16, D), F32)
    small[6:7] = jnp.sum(gao.astype(F32), axis=0, keepdims=True)
    to_windows(grad_one, windows_of, shifted)
    gao_w = windows_of[...].astype(BF)
    dw_out[...] = tn(mixed[...], gao_w)
    g_mix[...] = nt(gao_w, w_out[...]).astype(BF)
    dbias[...] = jnp.zeros_like(dbias)
    attn_bwd_windows(windows, qkv, g_mix, attn, g_qkv, dbias)


def attn_bwd_one(shifted, grad_one, w_out, saved):
    return call(
        functools.partial(attn_bwd_one_body, shifted, (0, FIRST)),
        (
            sds((FIRST * WROWS, 3 * D), BF),
            sds((WTOK, D), BF),
            sds((D, D), F32),
            sds((QUADS, WROWS, PAIR), F32),
            sds((16, D), F32),
        ),
        5,
        scratch=[PADDED],
        us=5,
    )(grad_one, w_out, *saved)


def attn_bwd_two_body(
    shifted, windows, grad_one, hid, vec, w_in, wn, qkv, attn, g_first, g_mix, dbias_before,
    grad_in, dw_in, dbias, small, g_qkv, patches, windows_of,
):
    dbias[...] = dbias_before[...]
    g_qkv[: FIRST * WROWS, :] = g_first[...]
    attn_bwd_windows(windows, qkv, g_mix, attn, g_qkv, dbias, 0)
    for c in range(3):
        cols = slice(c * D, (c + 1) * D)
        dw_in[:, cols] = tn(wn[...], g_qkv[:, cols])
    windows_of[...] = nt(g_qkv[...], w_in[...])
    to_patches(windows_of, patches, shifted)
    g_normed = patches[...]
    normal, inverse = normalize(hid[...].astype(F32))
    small[...] = jnp.zeros((16, D), F32)
    small[0:1] = jnp.sum(g_normed * normal, axis=0, keepdims=True)
    small[1:2] = jnp.sum(g_normed, axis=0, keepdims=True)
    small[4:5] = jnp.sum(g_qkv[:, :D].astype(F32), axis=0, keepdims=True)
    small[5:6] = jnp.sum(g_qkv[:, 2 * D :].astype(F32), axis=0, keepdims=True)
    grad_in[...] = grad_one[...] + norm_backward(g_normed, normal, inverse, vec[0:1])


def attn_bwd_two(shifted, grad_one, hid, vec, w_in, wn, qkv, attn, g_first, g_mix, dbias):
    return call(
        functools.partial(attn_bwd_two_body, shifted, (FIRST, WINDOWS)),
        (
            sds((CELLS, D), F32),
            sds((D, 3 * D), F32),
            sds((QUADS, WROWS, PAIR), F32),
            sds((16, D), F32),
        ),
        10,
        scratch=[pltpu.VMEM((WTOK, 3 * D), BF), PATCHES, PADDED],
        us=9,
    )(grad_one, hid, vec, w_in, wn, qkv, attn, g_first, g_mix, dbias)


def window_perm_t(shifted):
    source = patch_of(jnp.arange(WTOK, dtype=jnp.int32), shifted)
    return (jnp.arange(CELLS, dtype=jnp.int32)[:, None] == source[None, :]).astype(BF)


def wrap_codes(shifted):
    code = np.zeros((CELLS,), np.float32)
    if shifted:
        for r in range(SIDE):
            for s in range(SIDE):
                rr, ss = (r - SHIFT) % SIDE, (s - SHIFT) % SIDE
                code[r * SIDE + s] = 2 * (rr >= SIDE - SHIFT) + (ss >= SIDE - SHIFT)
    return code


def window_masks(items, shifted):
    labels = items.astype(F32)
    if shifted:
        labels = labels * 4.0 + jnp.asarray(wrap_codes(True))
    placed = nn(jnp.broadcast_to((labels + 1.0).astype(BF), (8, CELLS)), window_perm_t(shifted))[0]
    placed = placed.reshape(WINDOWS, WROWS)
    same = (placed[:, :, None] == placed[:, None, :]) & (placed[:, :, None] > 0.0)
    same = same.astype(F32)
    return jnp.concatenate([same, same], axis=2)


def slot_places(routes, slots):
    group = (jnp.arange(CELLS, dtype=jnp.int32) // GROUP) * CAP
    place = routes * (2 * CAP) + group + slots
    return jnp.broadcast_to(place[:, None], (CELLS, LANES)), jnp.broadcast_to(place[None, :], (8, CELLS))

LEAD = 73
SMALL = 9326
LAG = LEAD * LANES - SMALL
VECTORS = 9
LINES = 32
SPANS = ((LEAD, D, 9), (LEAD + 3456, D, 3), (LEAD + 4608, 2 * D, 12), (LEAD + 4608 + 9216, 2 * F, 3))
EDGE = LEAD + 4608
ALIGNED = LEAD + 4608 + 2 * 9216


def relative(k, bits):
    total = 0
    for place, bit in enumerate(bits):
        total = total + (((k >> (len(bits) - 1 - place)) & 1) << bit)
    return total


def lanes_of(count=LANES):
    return lax.broadcasted_iota(jnp.int32, (1, count), 1)


def equal(rows, columns):
    return jnp.where(rows == columns, 1.0, 0.0).astype(BF)


def spread(shape):
    return lax.broadcasted_iota(jnp.int32, shape, 0), lax.broadcasted_iota(jnp.int32, shape, 1)


def exact(left, one, product):
    high = left.astype(BF)
    low = (left - high.astype(F32)).astype(BF)
    return product(high, one) + product(low, one)


def head_major():
    f, g = spread((D, D))
    return equal(f, 12 * (g & 31) + (g >> 5))


def head_rows(m):
    f, g = spread((D, 2 * LANES))
    return equal((f & 31) + 32 * m, g)


def offset_lanes():
    f, g = spread((LANES, LANES))
    i = g & 63
    r = (i * 37) >> 8
    return equal(f, jnp.where(i < WIN * WIN, 13 * r + i - WIN * r, -1))


def turns():
    return [13 * (6 - j // WIN) + 6 - j % WIN for j in range(WIN * WIN)]


def unpack_bias(flat, wide, tall, bias):
    wide[...] = jnp.zeros_like(wide)
    for m in range(6):
        for c in range(3):
            wide[m : m + 1, c * LANES : (c + 1) * LANES] = flat[12 + 3 * m + c : 13 + 3 * m + c, :]
    by_head = nn(wide[...].astype(BF), head_major())
    sub = lax.broadcasted_iota(jnp.int32, (16, D), 0)
    own = (lanes_of(D) >> 5) == sub
    table = jnp.zeros((16, 2 * LANES), F32)
    for m in range(6):
        table = table + nn(jnp.where(own, by_head[m : m + 1], 0.0).astype(BF), head_rows(m))
    tall[...] = jnp.zeros_like(tall)
    for j, turn in enumerate(turns()):
        row = pltpu.roll(table, (2 * LANES - turn) % (2 * LANES), 1)[:, :LANES]
        tall[pl.ds(j, 16, stride=WROWS), :] = row
    tall[...] = nn(tall[...].astype(BF), offset_lanes())
    for g in range(QUADS):
        for t in range(2):
            h = 4 * g + 2 * t
            left, right = tall[h * WROWS : (h + 1) * WROWS], tall[(h + 1) * WROWS : (h + 2) * WROWS]
            bias[g, :, t * LANES : (t + 1) * LANES] = jnp.where(lanes_of() < WROWS, left, right)


def unpack_small(flat, rows, wide, tall, vec, b1, router, router_bias, bias):
    def shifted(first, count, by):
        near, far = flat[first : first + count, :], flat[first + 1 : first + 1 + count, :]
        return pltpu.roll(jnp.where(lanes_of() >= by, near, far), LANES - by, 1)

    rows[0:16, :] = shifted(27, 16, 108)
    rows[16:46, :] = shifted(42, 30, 110)
    vec[...] = jnp.zeros_like(vec)
    b1[...] = jnp.zeros_like(b1)
    for c in range(3):
        cols = slice(c * LANES, (c + 1) * LANES)
        for n in range(4):
            vec[n : n + 1, cols] = flat[3 * n + c : 3 * n + c + 1, :]
        for n in range(3):
            vec[4 + n : 5 + n, cols] = rows[3 * n + c : 3 * n + c + 1, :]
        for e in range(EXPERTS):
            vec[7 + e : 8 + e, cols] = rows[40 + 3 * e + c : 41 + 3 * e + c, :]
    for e in range(EXPERTS):
        for c in range(12):
            b1[e : e + 1, c * LANES : (c + 1) * LANES] = rows[16 + 12 * e + c : 17 + 12 * e + c, :]
        one = jnp.sum(jnp.where(lanes_of() == e, rows[15:16, :], 0.0), axis=1, keepdims=True)
        router_bias[e : e + 1, :] = jnp.broadcast_to(one, (1, LANES))
    pairs = jnp.concatenate([rows[9 + c : 10 + c, :] for c in range(6)], axis=1)
    pairs = jnp.broadcast_to(pairs, (LANES, 2 * D)).astype(BF)
    d, f = spread((D, 2 * D))
    for e in range(EXPERTS):
        router[:, e * LANES : (e + 1) * LANES] = nt(equal(f, 2 * d + e), pairs).astype(BF)
    gap = nt(pairs[0:16], equal(f, 2 * d + 1)) - nt(pairs[0:16], equal(f, 2 * d))
    vec[9:10, :] = gap[0:1]
    unpack_bias(flat, wide, tall, bias)


def unpack_matrices(flat, spans, outs, skipped):
    for (base, height, tiles), out in zip(spans, outs):
        step = 64

        @pl.loop(0, height // step)
        def _(t, base=base, tiles=tiles, out=out):
            first = base - 1 - skipped + t * (step * tiles)
            before = flat[pl.ds(first, step, stride=tiles), :]
            for j in range(tiles):
                here = flat[pl.ds(first + 1 + j, step, stride=tiles), :]
                tile = pltpu.roll(jnp.where(lanes_of() >= LANES - LAG, before, here), LAG, 1)
                out[pl.ds(pl.multiple_of(t * step, step), step), j * LANES : (j + 1) * LANES] = tile.astype(BF)
                before = here


def unpack_head_body(rows, runs, me, *refs):
    got = refs[: len(runs)]
    w_in, w_out, rest, vec, b1, router, router_bias, bias, flat, few, wide, tall = refs[len(runs) :]
    for (bits, fixed), part in zip(runs, got):

        @pl.loop(0, 1 << len(bits))
        def _(k, bits=bits, fixed=fixed, part=part):
            d = me[1] ^ (relative(k, bits) + fixed)
            flat[pl.ds(d * rows, rows), :] = part[k, :rows, :].astype(F32)

    unpack_small(flat, few, wide, tall, vec, b1, router, router_bias, bias)
    unpack_matrices(flat, SPANS[:2], (w_in, w_out), 0)
    rest[...] = flat[EDGE - 1 : EDGE - 1 + rest.shape[0], :]


def unpack_tail_body(rows, heads, runs, me, rest, *refs):
    got = refs[: len(runs)]
    w1, w2, flat = refs[len(runs) :]
    flat[0 : rest.shape[0], :] = rest[...]
    for (outer, inner, fixed, upper), part in zip(runs, got):
        count = 1 << len(inner)
        half = part.shape[1]
        first = half if upper else 0
        used = min(half, rows - first)

        @pl.loop(0, part.shape[0])
        def _(k, outer=outer, inner=inner, fixed=fixed, part=part, count=count, first=first, used=used):
            own = (relative(k // (3 * count), outer) + relative(k % count, inner) + fixed) ^ me[1]
            d = ((k // count) % 3 + 1) * heads + own
            flat[pl.ds(d * rows + first - (EDGE - 1), used), :] = part[k, :used, :].astype(F32)

    unpack_matrices(flat, SPANS[2:], (w1, w2), EDGE - 1)


class Weights(NamedTuple):
    w_in: Any
    w_out: Any
    w1: Any
    w2: Any
    vec: Any
    b1: Any
    router: Any
    router_bias: Any
    bias: Any


SMALL_SHAPES = (
    sds((16, D), F32),
    sds((8, F), F32),
    sds((D, 2 * LANES), BF),
    sds((8, LANES), F32),
    sds((QUADS, WROWS, PAIR), F32),
)
SMALL_SCRATCH = [pltpu.VMEM((48, LANES), F32), pltpu.VMEM((8, D), F32), pltpu.VMEM((16 * WROWS, LANES), F32)]
HEAD_SHAPES = (sds((D, 3 * D), BF), sds((D, D), BF))
TAIL_SHAPES = (sds((2 * D, F), BF), sds((2 * F, D), BF))


def experts(w1, w2):
    return w1.reshape(EXPERTS, D, F), w2.reshape(EXPERTS, F, D)


def unpack_head(me, parts, runs, rows, devices):
    heads = devices // 4
    w_in, w_out, rest, *small = call(
        functools.partial(unpack_head_body, rows, runs),
        HEAD_SHAPES + (sds((heads * rows - EDGE + 1, LANES), F32),) + SMALL_SHAPES,
        1 + len(parts),
        scratch=[pltpu.VMEM((heads * rows + 8, LANES), F32)] + SMALL_SCRATCH,
        smem=1,
        us=4,
    )(me, *parts)
    return Weights(w_in, w_out, None, None, *small), rest


def unpack_tail(me, rest, parts, runs, rows, devices):
    return experts(
        *call(
            functools.partial(unpack_tail_body, rows, devices // 4, runs),
            TAIL_SHAPES,
            2 + len(parts),
            scratch=[pltpu.VMEM((devices * rows - EDGE + 9, LANES), F32)],
            smem=1,
            us=7,
        )(me, rest, *parts)
    )


def pack_bias(dbias, wide, tall):
    tall[HEADS * WROWS :, :] = jnp.zeros((4 * WROWS, LANES), F32)
    for h in range(HEADS):
        g, t, side = h // 4, (h % 4) // 2, h % 2
        tile = dbias[g, :, t * LANES : (t + 1) * LANES]
        tall[h * WROWS : (h + 1) * WROWS, :] = jnp.where((lanes_of() >> 6) == side, tile, 0.0)
    used = HEADS * WROWS
    tall[0:used, :] = exact(tall[0:used, :], offset_lanes(), nt)
    table = jnp.zeros((16, 2 * LANES), F32)
    for j, turn in enumerate(turns()):
        row = tall[pl.ds(j, 16, stride=WROWS), :]
        table = table + pltpu.roll(jnp.concatenate([row, jnp.zeros_like(row)], axis=1), turn, 1)
    sub = lax.broadcasted_iota(jnp.int32, (16, D), 0)
    own = (lanes_of(D) >> 5) == sub
    wide[...] = jnp.zeros_like(wide)
    for m in range(6):
        placed = jnp.where(own, exact(table, head_rows(m), nt), 0.0)
        wide[m : m + 1, :] = jnp.sum(placed, axis=0, keepdims=True)
    wide[...] = exact(wide[...], head_major(), nt)


def pack_small(al, vectors, drouter, db1, dbias, one, two, wide, tall):
    one[...] = jnp.zeros_like(one)
    two[...] = jnp.zeros_like(two)
    pack_bias(dbias, wide, tall)
    d, f = spread((D, 2 * D))
    signs = equal(f, 2 * d + 1) - equal(f, 2 * d)
    pairs = exact(drouter[...], signs, nn)
    for c in range(3):
        cols = slice(c * LANES, (c + 1) * LANES)
        for n in range(4):
            one[1 + 3 * n + c : 2 + 3 * n + c, :] = vectors[n : n + 1, cols]
        for m in range(6):
            one[13 + 3 * m + c : 14 + 3 * m + c, :] = wide[m : m + 1, cols]
        for n in range(3):
            two[1 + 3 * n + c : 2 + 3 * n + c, :] = vectors[4 + n : 5 + n, cols]
        for e in range(EXPERTS):
            al[67 + 3 * e + c : 68 + 3 * e + c, :] = vectors[7 + e : 8 + e, cols]
    for c in range(6):
        two[10 + c : 11 + c, :] = pairs[0:1, c * LANES : (c + 1) * LANES]
    total = vectors[9:10, 0:LANES]
    two[16:17, :] = jnp.where(lanes_of() == 0, -total, jnp.where(lanes_of() == 1, total, 0.0))
    for e in range(EXPERTS):
        for c in range(12):
            al[43 + 12 * e + c : 44 + 12 * e + c, :] = db1[e : e + 1, c * LANES : (c + 1) * LANES]
    first = pltpu.roll(jnp.where(lanes_of() >= LANES - 18, one[0:28, :], one[1:29, :]), 18, 1)
    second = pltpu.roll(jnp.where(lanes_of() >= LANES - 126, two[0:16, :], two[1:17, :]), 126, 1)
    al[27:43, :] = second
    al[0:27, :] = first[0:27]
    al[27:28, :] += first[27:28]


def pack_matrices(al, spans, grads, skipped):
    for (base, height, tiles), grad in zip(spans, grads):
        step = 64

        @pl.loop(0, height // step)
        def _(t, base=base, tiles=tiles, grad=grad):
            first = base - skipped + t * (step * tiles)
            own = pl.ds(pl.multiple_of(t * step, step), step)
            for j in range(tiles):
                al[pl.ds(first + j, step, stride=tiles), :] = grad[own, j * LANES : (j + 1) * LANES]


def clear(al, first):
    al[pl.ds(first, al.shape[0] - first), :] = jnp.zeros((al.shape[0] - first, LANES), F32)


def pack_head_body(
    rows, padded, runs, me, moe, attn, proj, drouter, db1, dbias, dw_in, dw_out, rest,
    keep, send, al, vectors, lines, one, two, wide, tall,
):
    vectors[...] = moe[...] + attn[...] + proj[...]
    lines[...] = jnp.zeros_like(lines)
    for n in range(VECTORS):
        for c in range(3):
            lines[3 * n + c : 3 * n + c + 1, :] = vectors[n : n + 1, c * LANES : (c + 1) * LANES]
    pack_small(al, vectors, drouter, db1, dbias, one, two, wide, tall)
    pack_matrices(al, SPANS[:2], (dw_in, dw_out), 0)
    al[EDGE : EDGE + rest.shape[0], :] = rest[...]
    at = 0
    for bits, fixed in runs:
        for other, out in enumerate((keep, send)):

            @pl.loop(0, 1 << len(bits))
            def _(k, bits=bits, fixed=fixed, at=at, other=other, out=out):
                d = me[1] ^ (relative(k, bits) + fixed + other)
                out[at + k, :padded, :] = al[pl.ds(d * rows, padded), :].astype(BF)
                out[at + k, padded:, :] = lines[...].astype(BF)

        at += 1 << len(bits)


def pack_tail_body(rows, padded, heads, runs, me, dw1, dw2, keep, send, rest, al):
    clear(al, ALIGNED - EDGE)
    pack_matrices(al, SPANS[2:], (dw1, dw2), EDGE)
    rest[...] = al[0 : rest.shape[0], :]
    half = padded // 2
    at = 0
    for outer, inner, fixed, upper in runs:
        count = 1 << len(inner)
        total = 3 * count << len(outer)
        for other, out in enumerate((keep, send)):

            @pl.loop(0, total)
            def _(k, outer=outer, inner=inner, fixed=fixed, upper=upper, count=count, at=at, other=other, out=out):
                own = (relative(k // (3 * count), outer) + relative(k % count, inner) + fixed + other) ^ me[1]
                d = ((k // count) % 3 + 1) * heads + own
                out[at + k] = al[pl.ds(d * rows + (half if upper else 0) - EDGE, half), :].astype(BF)

        at += total


SMALL_PACK = [
    pltpu.VMEM((40, LANES), F32),
    pltpu.VMEM((24, LANES), F32),
    pltpu.VMEM((8, D), F32),
    pltpu.VMEM((16 * WROWS, LANES), F32),
]


def pack_head(me, small, dw_in, dw_out, rest, runs, rows, devices, padded):
    heads = devices // 4
    shape = sds((heads // 2, padded + LINES, LANES), BF)
    return call(
        functools.partial(pack_head_body, rows, padded, runs),
        (shape, shape),
        10,
        scratch=[
            pltpu.VMEM((EDGE + rest.shape[0], LANES), F32),
            pltpu.VMEM((16, D), F32),
            pltpu.VMEM((LINES, LANES), F32),
        ]
        + SMALL_PACK,
        smem=1,
        us=3,
    )(me, *small, dw_in, dw_out, rest)


def pack_tail(me, dw1, dw2, runs, rows, devices, padded):
    heads = devices // 4
    shape = sds((3 * heads, padded // 2, LANES), BF)
    over = -(-(heads * rows + padded - EDGE) // 8) * 8
    return call(
        functools.partial(pack_tail_body, rows, padded, heads, runs),
        (shape, shape, sds((over, LANES), F32)),
        3,
        scratch=[pltpu.VMEM((devices * rows + padded - EDGE, LANES), F32)],
        smem=1,
        us=3,
    )(me, dw1.reshape(2 * D, F), dw2.reshape(2 * F, D))


def levels_body(me, own, low, high, both, head, a, b):
    n, half = own.shape[0], a.shape[1]
    for level in range(4):
        for step, source in enumerate((own, low, high, both)):

            @pl.when((me[2] ^ step) == level)
            def _(level=level, source=source):
                for i in range(n):
                    if level == 0:
                        head[i] = source[i]
                    else:
                        a[(level - 1) * n + i] = source[i, :half, :]
                        b[(level - 1) * n + i] = source[i, half:, :]


def levels(me, *pieces):
    n, padded, _ = pieces[0].shape
    dtype = pieces[0].dtype
    shape = sds((3 * n, padded // 2, LANES), dtype)
    return call(levels_body, (sds((n, padded, LANES), dtype), shape, shape), 5, smem=1)(me, *pieces)


def targets_body(with_head, me, a, a_got, b, b_got, *refs):
    *head, keep, send = refs
    n, half = keep.shape[0] // 2, a.shape[1]
    places = {0: (keep, 0), 2: (keep, n), 1: (send, 0), 3: (send, n)}
    for step, (out, first) in places.items():
        level = me[2] ^ step

        @pl.when(level == 0)
        def _(out=out, first=first):
            for i in range(n):
                if with_head:
                    out[first + i] = head[0][i, : 2 * half, :].astype(out.dtype)
                else:
                    out[first + i] = jnp.zeros((2 * half, LANES), out.dtype)

        @pl.when(level > 0)
        def _(out=out, first=first, level=level):
            for i in range(n):
                at = (level - 1) * n + i
                out[first + i, :half, :] = (a[at] + a_got[at].astype(F32)).astype(out.dtype)
                out[first + i, half:, :] = (b[at] + b_got[at].astype(F32)).astype(out.dtype)


def targets(me, a, a_got, b, b_got, *head):
    n, half, _ = a.shape
    n = n // 3
    shape = (2 * n, 2 * half, LANES)
    return call(
        functools.partial(targets_body, bool(head)), (sds(shape, F32), sds(shape, BF)), 5 + len(head), smem=1
    )(me, a, a_got, b, b_got, *head)


def combine_body(plan, count, *refs):
    for (size, _, terms), out in zip(plan, refs[count:]):

        @pl.loop(0, size)
        def _(i, terms=terms, out=out):
            parts = [refs[at][first + i].astype(F32) for at, first in terms]
            while len(parts) > 1:
                parts = [sum(parts[at + 1 : at + 2], parts[at]) for at in range(0, len(parts), 2)]
            out[i] = parts[0].astype(out.dtype)


def combine(plan, *arrays):
    tail = arrays[0].shape[1:]
    shapes = [sds((size, *tail), dtype) for size, dtype, _ in plan]
    return call(functools.partial(combine_body, plan, len(arrays)), shapes, len(arrays))(*arrays)


def finish_body(rows, me, keep, got, upper_keep, upper_got, out):
    def shift(keep, got):
        total = keep[0] + got[0].astype(F32)
        here, below = total[0:rows, :], total[1 : rows + 1, :]
        out[...] = pltpu.roll(jnp.where(lanes_of() >= LAG, here, below), LANES - LAG, 1)

    pl.when(me[2] == 0)(lambda: shift(keep, got))
    pl.when(me[2] != 0)(lambda: shift(upper_keep, upper_got))


def finish(me, rows, lowest, upper):
    parts = (lowest.keep, lowest.got, upper.keep, upper.got)
    return call(functools.partial(finish_body, rows), sds((rows, LANES), F32), 5, smem=1)(me, *parts)


def join_body(a, b, out):
    n = a.shape[0]

    @pl.loop(0, n)
    def _(i):
        out[i] = a[i]
        out[n + i] = b[i]


def join(a, b):
    return call(join_body, sds((2 * a.shape[0], *a.shape[1:]), a.dtype), 2)(a, b)


class Ways(NamedTuple):
    core: Any
    x: Any
    y: Any
    low: Any
    high: Any
    rest: Any


def ways():
    dp, fsdp = (lax.axis_size(axis).bit_length() - 1 for axis in (DP, FSDP))
    rest = [1 << (fsdp + bit) for bit in range(1, dp - 2)] + [1 << bit for bit in range(2, fsdp)]
    return Ways(1, 2, 1 << fsdp, 1 << (fsdp + dp - 2), 1 << (fsdp + dp - 1), rest)


def device_count():
    return lax.axis_size(DP) * lax.axis_size(FSDP)


def flip(array, step):
    return lax.ppermute(array, (DP, FSDP), [(i, i ^ step) for i in range(device_count())])


def move(array, levels):
    width = device_count() // 4
    pairs = [(a * width + i, b * width + i) for a, b in levels.items() for i in range(width)]
    return lax.ppermute(array, (DP, FSDP), pairs)


def tie(arrays, *others):
    if isinstance(arrays, tuple):
        return tuple(tie(array, *others) for array in arrays)
    return lax.optimization_barrier((arrays, *others))[0]


def sync(*arrays):
    return lax.optimization_barrier(arrays)


def bits_of(*steps):
    return [step.bit_length() - 1 for step in steps]


class Gather:
    def __init__(self, own, way, me):
        for extra in way.rest:
            own = join(own, flip(own, extra))
        self.way, self.own, self.me = way, own, me
        self.rest = bits_of(*reversed(way.rest))

    def far(self):
        own, way = self.own, self.way
        self.others = flip(own, way.low), flip(own, way.high), flip(own, way.low + way.high)

    def levels(self):
        self.head, self.a, self.b = levels(self.me, self.own, *self.others)

    def head_near(self):
        way = self.way
        self.steps = way.x, way.y, way.x + way.y
        self.head_got = tuple(flip(self.head, step) for step in self.steps)

    def head_core(self):
        core = self.way.core
        parts = [self.head, *self.head_got]
        self.head_parts = parts + [flip(part, core) for part in parts]
        self.head_runs = [(self.rest, step) for step in (0, *self.steps)]
        self.head_runs += [(self.rest, step + core) for step in (0, *self.steps)]

    def near_a(self):
        self.a_got = flip(self.a, self.way.x)

    def near_b(self):
        self.b_got = flip(self.b, self.way.y)

    def last(self):
        way = self.way
        self.parts = [join(self.a, self.a_got), join(self.b, self.b_got)]
        self.got = flip(self.parts[0], way.y), flip(self.parts[1], way.x)

    def cores(self):
        way = self.way
        parts = self.parts + list(self.got)
        self.parts = parts + [flip(part, way.core) for part in parts]
        bx, by = bits_of(way.x), bits_of(way.y)
        self.runs = []
        for fixed in (0, way.core):
            for fx, fy in ((0, 0), (way.y, way.x)):
                self.runs += [(bx, self.rest, fx + fixed, False), (by, self.rest, fy + fixed, True)]


def head_runs(way):
    rest = bits_of(*way.rest)
    return [(rest, step) for step in (way.y, way.x + way.y, way.x, 0)]


def tail_runs(way):
    rest, bx, by = (bits_of(*steps) for steps in (way.rest, [way.x], [way.y]))
    return [
        (bx, rest, way.y, False), ([], rest, way.x, False), ([], rest, 0, False),
        (by, rest, way.x, True), ([], rest, way.y, True), ([], rest, 0, True),
    ]


class HeadScatter:
    def __init__(self, keep, send, way):
        self.way, self.keep, self.n = way, keep, keep.shape[0] // 4
        self.got = flip(send, way.core)

    def plane(self):
        n, way = self.n, self.way
        y, xy, x, self.keep = combine([(n, BF, ((0, i * n), (1, i * n))) for i in range(4)], self.keep, self.got)
        self.got = flip(x, way.x), flip(y, way.y), flip(xy, way.x + way.y)

    def near(self):
        n = 2 * self.n
        sent, self.keep = combine([(n, BF, ((0, i * n), (1, i * n))) for i in range(2)], self.keep, self.got)
        self.got = flip(sent, self.way.y)

    def next(self):
        n = self.n
        sent, self.keep = combine(((n, BF, ((0, 0), (1, n))), (n, BF, ((0, n), (1, 0)))), self.keep, self.got)
        self.got = flip(sent, self.way.x)

    def add(self):
        n, got = self.n, self.got if isinstance(self.got, (tuple, list)) else (self.got,)
        terms = tuple((i, 0) for i in range(1 + len(got)))
        sent, self.keep = combine(((n, BF, terms), (n, F32, terms)), self.keep, *got)
        return sent

    def lines(self):
        return self.keep[0, -LINES : 3 * VECTORS - LINES].reshape(VECTORS, D)

    def low(self, sent):
        self.got = move(sent, {1: 0, 3: 2})

    def high(self):
        self.got = move(self.add(), {2: 0})
        self.keep, self.got = fold(self.keep, self.got, self.way.rest)


class TailScatter:
    def __init__(self, keep, send, way, me):
        self.way, self.keep, self.n, self.me = way, keep, keep.shape[0] // 24, me
        self.got = flip(send, way.core)

    def near(self):
        n = 6 * self.n
        plan = [(n, dtype, ((0, first), (1, first))) for dtype, first in ((BF, 0), (F32, n), (BF, 2 * n), (F32, 3 * n))]
        a, self.a, b, self.b = combine(plan, self.keep, self.got)
        self.a_got, self.b_got = flip(a, self.way.y), flip(b, self.way.x)

    def next(self):
        n = 3 * self.n
        plan = [(n, BF, ((0, 0), (1, n))), (n, F32, ((0, n), (1, 0)))]
        plan += [(n, BF, ((2, 0), (3, n))), (n, F32, ((2, n), (3, 0)))]
        a, self.a, b, self.b = combine(plan, self.a, self.a_got, self.b, self.b_got)
        self.a_got, self.b_got = flip(a, self.way.x), flip(b, self.way.y)

    def low(self, *head):
        self.keep, sent = targets(self.me, self.a, self.a_got, self.b, self.b_got, *head)
        self.got = flip(sent, self.way.low)

    def high(self):
        self.keep, self.got = fold(self.keep, self.got, [self.way.high] + self.way.rest)


def fold(keep, got, steps):
    for way in steps:
        half = keep.shape[0] // 2
        plan = ((half, BF, ((0, half), (1, half))), (half, F32, ((0, 0), (1, 0))))
        sent, keep = combine(plan, keep, got)
        got = flip(sent, way)
    return keep, got


def shards(inputs, items, routes, slots, cotangent, params, momentum, average):
    fsdp, dp = lax.axis_size(FSDP), lax.axis_size(DP)
    devices = fsdp * dp
    share = params.shape[1]
    rows = share // LANES
    padded = -(-(rows + 1) // 32) * 32
    step_rate = RATE_BASE / math.sqrt(CELLS * devices)
    way = ways()
    own = lax.axis_index(DP) * fsdp + lax.axis_index(FSDP)
    me = jnp.stack([own, own % (devices // 4), own // (devices // 4)]).astype(jnp.int32)

    shares = []
    for b in range(BLOCKS):
        share_rows = params[b].astype(BF).reshape(1, rows, LANES)
        shares.append(jnp.pad(share_rows, ((0, 0), (0, padded - rows), (0, 0))))
    one, two = (Gather(rows_own, way, me) for rows_own in shares)
    masks, places = [], []
    for b in range(BLOCKS):
        masks.append(window_masks(items.reshape(CELLS), b % 2 == 1))
        places.append(slot_places(routes[b].reshape(CELLS), slots[b].reshape(CELLS)))

    hidden_zero = inputs.reshape(CELLS, D)
    one.far()
    one.levels()
    one.head_near()
    one.a, one.b, two.own = tie((one.a, one.b, two.own), *one.head_got)
    one.near_a()
    one.near_b()
    one.head_core()
    w, rest = unpack_head(me, one.head_parts, one.head_runs, rows, devices)
    one.a_got, one.b_got, vec = sync(one.a_got, one.b_got, w.vec)
    one.last()
    two.own = tie(two.own, vec)
    two.far()
    w = w._replace(vec=tie(vec, *one.parts))
    h_zero, *attn_zero = attn_fwd(False, hidden_zero, w.vec, w.w_in, w.w_out, w.bias, masks[0])
    h_zero, *one.got = sync(h_zero, *one.got)
    one.cores()
    w1, w2 = unpack_tail(me, rest, one.parts, one.runs, rows, devices)
    w1, *two.others = sync(w1, *two.others)
    w_zero = w._replace(w1=w1, w2=w2)
    w = w_zero
    two.levels()
    two.head_near()
    two.near_a()
    two.near_b()
    hidden_one, *moe_zero = moe_fwd(
        tie(h_zero, two.head), w.vec, w.w1, w.w2, w.b1, w.router, w.router_bias, places[0], F32
    )

    hidden_one, two.a_got, two.b_got, *two.head_got = sync(hidden_one, two.a_got, two.b_got, *two.head_got)
    two.head_core()
    two.last()
    two.head_parts[0] = tie(two.head_parts[0], *two.parts)
    w, rest = unpack_head(me, two.head_parts, two.head_runs, rows, devices)
    h_one, *attn_one = attn_fwd(True, hidden_one, w.vec, w.w_in, w.w_out, w.bias, masks[1])
    h_one, *two.got = sync(h_one, *two.got)
    two.cores()
    w1, w2 = unpack_tail(me, rest, two.parts, two.runs, rows, devices)
    w_one = w._replace(w1=w1, w2=w2)
    w = w_one
    outputs, *moe_one = moe_fwd(h_one, w.vec, w.w1, w.w2, w.b1, w.router, w.router_bias, places[1], BF)

    gradient = cotangent.reshape(CELLS, D)
    wn, qkv, mixed, attn = attn_one
    g_one, dw1, dw2, db1, drouter, small_moe = moe_bwd(gradient, h_one, w.vec, w.w1, w.w2, places[1], moe_one)
    keep, send, rest = pack_tail(me, dw1, dw2, tail_runs(way), rows, devices, padded)
    tail_one = TailScatter(keep, send, way, me)
    g_one = tie(g_one, send)
    g_first, g_mix, dw_out, dbias, small_attn = attn_bwd_one(True, g_one, w.w_out, (qkv, mixed, attn))
    g_mix, tail_one.got = sync(g_mix, tail_one.got)
    tail_one.near()
    gradient, dw_in, dbias, small_proj = attn_bwd_two(
        True, tie(g_one, tail_one.a), hidden_one, w.vec, w.w_in, wn, qkv, attn, g_first, g_mix, dbias
    )
    small = (small_moe, small_attn, small_proj, drouter, db1, dbias)
    keep, send = pack_head(me, small, dw_in, dw_out, rest, head_runs(way), rows, devices, padded)
    send, tail_one.a_got, tail_one.b_got, gradient = sync(send, tail_one.a_got, tail_one.b_got, gradient)
    head_one = HeadScatter(keep, send, way)
    tail_one.next()

    w = w_zero
    wn, qkv, mixed, attn = attn_zero
    gradient = tie(gradient, tail_one.a)
    g_one, dw1, dw2, db1, drouter, small_moe = moe_bwd(gradient, h_zero, w.vec, w.w1, w.w2, places[0], moe_zero)
    g_one, dw2, head_one.got, tail_one.a_got, tail_one.b_got = sync(
        g_one, dw2, head_one.got, tail_one.a_got, tail_one.b_got
    )
    head_one.near()
    tail_one.low()
    keep, send, rest = pack_tail(me, dw1, tie(dw2, head_one.keep, tail_one.keep), tail_runs(way), rows, devices, padded)
    tail_zero = TailScatter(keep, send, way, me)
    g_one = tie(g_one, send)
    g_first, g_mix, dw_out, dbias, small_attn = attn_bwd_one(False, g_one, w.w_out, (qkv, mixed, attn))
    g_mix, tail_zero.got, tail_one.got, head_one.got = sync(g_mix, tail_zero.got, tail_one.got, head_one.got)
    tail_zero.near()
    head_one.next()
    tail_one.high()
    gradient, dw_in, dbias, small_proj = attn_bwd_two(
        False, tie(g_one, tail_zero.a, tail_one.keep, head_one.keep), hidden_zero, w.vec, w.w_in, wn, qkv, attn,
        g_first, g_mix, dbias,
    )
    small = (small_moe, small_attn, small_proj, drouter, db1, dbias)
    keep, send = pack_head(me, small, dw_in, dw_out, rest, head_runs(way), rows, devices, padded)
    send, tail_zero.a_got, tail_zero.b_got, tail_one.got, head_one.got = sync(
        send, tail_zero.a_got, tail_zero.b_got, tail_one.got, head_one.got
    )

    head_zero = HeadScatter(keep, send, way)
    tail_zero.next()
    head_zero.plane()
    head_one.add()
    tail_zero.low(head_one.keep)
    sent = head_zero.add()
    head_zero.low(sent)
    vector_grads = jnp.stack([head_zero.lines(), head_one.lines()])
    got = flip(vector_grads, way.low)
    tail_zero.high()
    vector_grads = vector_grads + got
    head_zero.keep = tie(head_zero.keep, vector_grads)
    head_zero.high()
    for step in [way.high] + way.rest:
        vector_grads = vector_grads + flip(vector_grads, step)
    grads_zero = finish(me, rows, head_zero, tail_zero)
    grads_one = finish(me, rows, tail_zero, tail_one)
    grad_all = jnp.stack([grads_zero.reshape(-1), grads_one.reshape(-1)])
    new_momentum = MOMENTUM_DECAY * momentum + grad_all
    new_params = params - step_rate * (grad_all + MOMENTUM_DECAY * new_momentum)
    new_average = AVERAGE_DECAY * average + (1.0 - AVERAGE_DECAY) * new_params
    return (
        outputs.reshape(1, CELLS, D),
        gradient.reshape(1, CELLS, D),
        new_params,
        new_momentum,
        new_average,
        vector_grads,
    )


def solution(mesh):
    both = (DP, FSDP)
    canvas, vector = P(both), P(None, both)
    return jax.shard_map(
        shards,
        mesh=mesh,
        in_specs=(canvas, canvas, vector, vector, canvas, vector, vector, vector),
        out_specs=(canvas, canvas, vector, vector, vector, P()),
        check_vma=False,
    )
```

```python
import functools
import math
from typing import Any, NamedTuple

import jax
import jax.numpy as jnp
import numpy as np
from jax import lax
from jax.experimental import pallas as pl
from jax.experimental.pallas import tpu as pltpu
from jax.sharding import PartitionSpec as P

D = 384
HEADS = 12
F = 1536
HEAD_DIM = 32
EXPERTS = 2
CAP = 256
SIDE = 28
WIN = 7
SHIFT = 3
BLOCKS = 2
CELLS = 784
GROUP = 392
RELS = 169
NORM_EPSILON = 1e-05
MOMENTUM_DECAY = 0.9
AVERAGE_DECAY = 0.9
RATE_BASE = 0.1

DP = "dp"
FSDP = "fsdp"
LANES = 128
WROWS = 64
WINDOWS = 16
WTOK = WINDOWS * WROWS
SLOTS = EXPERTS * 2 * CAP
PAIR = 4 * WROWS
QUADS = HEADS // 4
SCALE = HEAD_DIM ** (-0.5)
US_FLOPS = 1.0e9
BF = jnp.bfloat16
F32 = jnp.float32
VMEM_BYTES = 20 * 1024 * 1024


def call(body, out_shape, n_in, scratch=(), smem=0, deps=(), us=1, vmem=VMEM_BYTES):
    def skipping(*refs):
        body(*refs[:n_in], *refs[n_in + len(deps) :])

    run = pl.pallas_call(
        skipping,
        out_shape=out_shape,
        in_specs=[pl.BlockSpec(memory_space=pltpu.SMEM)] * smem
        + [pl.BlockSpec(memory_space=pltpu.VMEM)] * (n_in - smem)
        + [pl.BlockSpec(memory_space=pl.ANY)] * len(deps),
        out_specs=jax.tree.map(lambda _: pl.BlockSpec(memory_space=pltpu.VMEM), out_shape),
        scratch_shapes=list(scratch),
        compiler_params=pltpu.CompilerParams(vmem_limit_bytes=vmem),
        cost_estimate=pl.CostEstimate(flops=int(us * US_FLOPS), bytes_accessed=0, transcendentals=0),
    )
    return lambda *args: run(*args, *deps)


def sds(shape, dtype):
    return jax.ShapeDtypeStruct(shape, dtype)


def nn(a, b):
    return lax.dot_general(a, b, (((1,), (0,)), ((), ())), preferred_element_type=F32)


def nt(a, b):
    return lax.dot_general(a, b, (((1,), (1,)), ((), ())), preferred_element_type=F32)


def tn(a, b):
    return lax.dot_general(a, b, (((0,), (0,)), ((), ())), preferred_element_type=F32)


def normalize(hidden):
    centre = hidden - jnp.mean(hidden, axis=-1, keepdims=True)
    inverse = lax.rsqrt(jnp.mean(centre * centre, axis=-1, keepdims=True) + NORM_EPSILON)
    return centre * inverse, inverse


def norm_backward(grad_normed, normal_rows, inverse, gain_row):
    scaled = grad_normed * gain_row
    return inverse * (
        scaled
        - jnp.mean(scaled, axis=-1, keepdims=True)
        - normal_rows * jnp.mean(scaled * normal_rows, axis=-1, keepdims=True)
    )


def head_masks():
    lane = lax.broadcasted_iota(jnp.int32, (1, LANES), 1) // HEAD_DIM
    return [lane == h for h in range(4)]


def stack_heads(rows, masks):
    zero = jnp.zeros_like(rows)
    return jnp.concatenate([jnp.where(mask, rows, zero) for mask in masks], axis=0)


def fold_heads(tall, masks):
    out = jnp.where(masks[0], tall[0:WROWS], 0.0)
    for h in range(1, 4):
        out = jnp.where(masks[h], tall[h * WROWS : (h + 1) * WROWS], out)
    return out


def patch_of(row, shifted):
    w, p = row >> 6, row & 63
    pr = (p * 37) >> 8
    r = (w >> 2) * WIN + pr
    s = (w & 3) * WIN + p - pr * WIN
    if shifted:
        r, s = r + SHIFT, s + SHIFT
        r = jnp.where(r >= SIDE, r - SIDE, r)
        s = jnp.where(s >= SIDE, s - SIDE, s)
    return jnp.where(p < WIN * WIN, r * SIDE + s, -1)


def runs_of(shifted):
    runs = []
    for w in range(WINDOWS):
        for p in range(WIN):
            r, s = (w // 4) * WIN + p, (w % 4) * WIN
            if shifted:
                r, s = (r + SHIFT) % SIDE, s + SHIFT
            here = min(WIN, SIDE - s)
            runs.append((w * WROWS + p * WIN, r * SIDE + s, here))
            if here < WIN:
                runs.append((w * WROWS + p * WIN + here, r * SIDE, WIN - here))
    return runs


def to_windows(patches, windows, shifted):
    windows[...] = jnp.zeros_like(windows)
    for row, patch, length in runs_of(shifted):
        windows[row : row + length, :] = patches[patch : patch + length, :]


def to_patches(windows, patches, shifted):
    for row, patch, length in runs_of(shifted):
        patches[patch : patch + length, :] = windows[row : row + length, :]


PATCHES = pltpu.VMEM((CELLS, D), F32)
PADDED = pltpu.VMEM((WTOK, D), F32)
ONEHOT = pltpu.VMEM((CELLS, SLOTS), BF)
ONEHOT_T = pltpu.VMEM((SLOTS, CELLS), BF)


def attn_fwd_body(shifted, hid, vec, w_in, w_out, bias, mask, h_one, wn, qkv, mixed, attn, patches, windows):
    normal, _ = normalize(hid[...].astype(F32))
    patches[...] = normal * vec[0:1] + vec[1:2]
    to_windows(patches, windows, shifted)
    wn[...] = windows[...].astype(BF)
    in_bias = jnp.concatenate([vec[4:5], jnp.zeros((1, D), F32), vec[5:6]], axis=1)

    @pl.loop(0, 4)
    def _(t):
        rows = pl.ds(pl.multiple_of(t * 256, 256), 256)
        qkv[rows, :] = (nn(wn[rows, :], w_in[...]) + in_bias).astype(BF)

    masks = head_masks()

    @pl.loop(0, WINDOWS // 8)
    def _(wo):
        units = [(i, g) for i in range(8) for g in range(QUADS)]
        rows = [pl.ds(pl.multiple_of((wo * 8 + i) * WROWS, WROWS), WROWS) for i in range(8)]
        allow = []
        for i in range(8):
            one = mask[wo * 8 + i] > 0.0
            allow.append(jnp.concatenate([one, one], axis=1))
        scores = []
        for i, g in units:
            q4 = stack_heads(qkv[rows[i], g * LANES : (g + 1) * LANES], masks)
            scores.append(nt(qkv[rows[i], D + g * LANES : D + (g + 1) * LANES], q4))
        probs = []
        for (i, g), s in zip(units, scores):
            s = jnp.where(allow[i], s * SCALE + bias[g], -1e30)
            e = jnp.exp(s - jnp.max(s, axis=0, keepdims=True))
            a = (e * (1.0 / jnp.sum(e, axis=0, keepdims=True))).astype(BF)
            attn[(wo * 8 + i) * QUADS + g] = a
            probs.append(a)
        tall = [tn(a, qkv[rows[i], 2 * D + g * LANES : 2 * D + (g + 1) * LANES]) for (i, g), a in zip(units, probs)]
        for (i, g), t in zip(units, tall):
            t = fold_heads(t, masks)
            windows[rows[i], g * LANES : (g + 1) * LANES] = t
            mixed[rows[i], g * LANES : (g + 1) * LANES] = t.astype(BF)

    to_patches(windows, patches, shifted)
    h_one[...] = hid[...].astype(F32) + nn(patches[...].astype(BF), w_out[...]) + vec[6:7]


def attn_fwd(shifted, hid, vec, w_in, w_out, bias, mask, deps=()):
    return call(
        functools.partial(attn_fwd_body, shifted),
        (
            sds((CELLS, D), F32),
            sds((WTOK, D), BF),
            sds((WTOK, 3 * D), BF),
            sds((WTOK, D), BF),
            sds((WINDOWS * QUADS, WROWS, PAIR), BF),
        ),
        6,
        scratch=[PATCHES, PADDED],
        us=8,
        deps=deps,
    )(hid, vec, w_in, w_out, bias, mask)


def moe_fwd_body(
    h_one, vec, w1, w2, b1, router, router_bias, place_col, place_row,
    out, normed_two, disp, act, slope, picked, gap_out, rows_out, onehot, onehot_t,
):
    fill_onehot(onehot, place_col)
    fill_onehot_t(onehot_t, place_row)
    normal, _ = normalize(h_one[...])
    two = (normal * vec[2:3] + vec[3:4]).astype(BF)
    normed_two[...] = two
    logits = nn(two, router[...])
    gap = (logits[:, LANES:] + router_bias[1:2]) - (logits[:, :LANES] + router_bias[0:1])
    gap = jnp.where(place_col[...] >= SLOTS // 2, gap, -gap)
    gap_out[...] = gap
    gate = 1.0 / (1.0 + jnp.exp(-gap))
    disp[...] = nn(onehot_t[...], two).astype(BF)

    @pl.loop(0, 4, unroll=4)
    def _(t):
        rows = pl.ds(pl.multiple_of(t * 256, 256), 256)
        e = t // 2
        own = disp[rows, :]
        for c in range(3):
            cols = slice(c * 512, (c + 1) * 512)
            pre = nn(own, w1[e, :, cols]) + b1[pl.ds(e, 1), cols]
            phi = 0.5 * (1.0 + lax.erf(pre * 0.7071067811865476))
            act[rows, cols] = (pre * phi).astype(BF)
            slope[rows, cols] = (
                phi + pre * jnp.exp(-0.5 * pre * pre) * 0.3989422804014327
            ).astype(BF)
        rows_out[rows, :] = (nn(act[rows, :], w2[e]) + vec[pl.ds(7 + e, 1)]).astype(BF)

    taken = nn(onehot[...], rows_out[...])
    picked[...] = taken.astype(BF)
    for c in range(3):
        cols = slice(c * LANES, (c + 1) * LANES)
        out[:, cols] = (h_one[:, cols] + gate * taken[:, cols]).astype(out.dtype)


def moe_fwd(h_one, vec, w1, w2, b1, router, router_bias, place, out_dtype, deps=()):
    return call(
        moe_fwd_body,
        (
            sds((CELLS, D), out_dtype),
            sds((CELLS, D), BF),
            sds((SLOTS, D), BF),
            sds((SLOTS, F), BF),
            sds((SLOTS, F), BF),
            sds((CELLS, D), BF),
            sds((CELLS, LANES), F32),
        ),
        9,
        scratch=[pltpu.VMEM((SLOTS, D), BF), ONEHOT, ONEHOT_T],
        us=9.5,
        deps=deps,
    )(h_one, vec, w1, w2, b1, router, router_bias, *place)


def fill_onehot(onehot, place_col):
    @pl.loop(0, 7)
    def _(t):
        rows = pl.ds(pl.multiple_of(t * 112, 112), 112)
        place = jnp.concatenate([place_col[rows, :]] * 8, axis=1)
        same = place == lax.broadcasted_iota(jnp.int32, (112, SLOTS), 1)
        onehot[rows, :] = jnp.where(same, 1.0, 0.0).astype(BF)


def fill_onehot_t(onehot_t, place_row):
    @pl.loop(0, 8)
    def _(t):
        row = lax.broadcasted_iota(jnp.int32, (128, CELLS), 0) + t * 128
        same = row == place_row[0:1, :]
        onehot_t[pl.ds(pl.multiple_of(t * 128, 128), 128), :] = jnp.where(same, 1.0, 0.0).astype(BF)


def moe_bwd_body(
    grad, w2, place_col, place_row, disp, act, slope, picked, gap,
    dw1, dw2, db1, small, g_pre, gate_grad, g_rows, onehot_t,
):
    fill_onehot_t(onehot_t, place_row)
    go = grad[...].astype(F32)
    gate = 1.0 / (1.0 + jnp.exp(-gap[...]))
    other = 1.0 / (1.0 + jnp.exp(gap[...]))
    g_picked = (go * jnp.concatenate([gate] * 3, axis=1)).astype(BF)
    g_gate = jnp.sum(go * picked[...].astype(F32), axis=-1, keepdims=True)
    sign = jnp.where(place_col[...] >= SLOTS // 2, 1.0, -1.0)
    gl = (g_gate * gate * other * sign).astype(BF)
    gate_grad[...] = gl
    small[...] = jnp.zeros((16, D), F32)
    small[9:10, 0:LANES] = jnp.sum(gl.astype(F32), axis=0, keepdims=True)
    g_rows[...] = nn(onehot_t[...], g_picked).astype(BF)

    @pl.loop(0, EXPERTS, unroll=2)
    def _(e):
        both = pl.ds(pl.multiple_of(e * 512, 512), 512)
        own = g_rows[both, :]
        total = []
        grads = [nt(own, w2[e, c * 256 : (c + 1) * 256, :]) for c in range(6)]
        for c, part in enumerate(grads):
            cols = slice(c * 256, (c + 1) * 256)
            gp = (part * slope[both, cols].astype(F32)).astype(BF)
            g_pre[both, cols] = gp
            total.append(jnp.sum(gp.astype(F32), axis=0, keepdims=True))
        db1[pl.ds(e, 1), :] = jnp.concatenate(total, axis=1)
        small[pl.ds(7 + e, 1), :] = jnp.sum(own.astype(F32), axis=0, keepdims=True)
        for c in range(6):
            cols = slice(c * 256, (c + 1) * 256)
            dw1[e, :, cols] = tn(disp[both, :], g_pre[both, cols])
            dw2[e, cols, :] = tn(act[both, cols], own)


def moe_bwd(grad, w2, place, saved):
    return call(
        moe_bwd_body,
        (
            sds((EXPERTS, D, F), F32),
            sds((EXPERTS, F, D), F32),
            sds((8, F), F32),
            sds((16, D), F32),
            sds((SLOTS, F), BF),
            sds((CELLS, LANES), BF),
        ),
        9,
        scratch=[pltpu.VMEM((SLOTS, D), BF), ONEHOT_T],
        us=8,
    )(grad, w2, *place, *saved)


def middle_bwd_body(
    shifted, grad, h_one, vec, w1, w_out, place_col, normed_two, g_pre, gate_grad, mixed,
    grad_one, g_mix, dw_out, drouter, small, onehot, g_disp, windows_of,
):
    fill_onehot(onehot, place_col)
    for e in range(EXPERTS):
        both = slice(e * 512, (e + 1) * 512)
        g_disp[both, :] = nt(g_pre[both, :], w1[e]).astype(BF)
    gl = gate_grad[...].astype(F32)
    g_two = nn(onehot[...], g_disp[...]) + jnp.concatenate([gl] * 3, axis=1) * vec[9:10]
    drouter[...] = tn(gate_grad[...], normed_two[...])[0:8]
    normal, inverse = normalize(h_one[...])
    small[...] = jnp.zeros((16, D), F32)
    small[2:3] = jnp.sum(g_two * normal, axis=0, keepdims=True)
    small[3:4] = jnp.sum(g_two, axis=0, keepdims=True)
    grad_one[...] = grad[...].astype(F32) + norm_backward(g_two, normal, inverse, vec[2:3])
    small[6:7] = jnp.sum(grad_one[...].astype(BF).astype(F32), axis=0, keepdims=True)
    to_windows(grad_one, windows_of, shifted)
    gao_w = windows_of[...].astype(BF)
    dw_out[...] = tn(mixed[...], gao_w)
    g_mix[...] = nt(gao_w, w_out[...]).astype(BF)


def middle_bwd(shifted, grad, h_one, vec, w1, w_out, place_col, normed_two, g_pre, gate_grad, mixed):
    return call(
        functools.partial(middle_bwd_body, shifted),
        (
            sds((CELLS, D), F32),
            sds((WTOK, D), BF),
            sds((D, D), F32),
            sds((8, D), F32),
            sds((16, D), F32),
        ),
        10,
        scratch=[ONEHOT, pltpu.VMEM((SLOTS, D), BF), PADDED],
        us=5,
    )(grad, h_one, vec, w1, w_out, place_col, normed_two, g_pre, gate_grad, mixed)


def attn_bwd_windows(windows, qkv, g_mix, attn, g_qkv, dbias, base=None):
    masks = head_masks()
    base = windows[0] if base is None else base

    start, stop = windows
    per = min(4, stop - start)

    @pl.loop(0, (stop - start) // per)
    def _(wo):
        units = [(i, g) for i in range(per) for g in range(QUADS)]
        first = [start + wo * per + i for i in range(per)]
        rows = [pl.ds(pl.multiple_of(w * WROWS, WROWS), WROWS) for w in first]
        outs = [pl.ds(pl.multiple_of((w - base) * WROWS, WROWS), WROWS) for w in first]
        cols = [[slice(n * D + g * LANES, n * D + (g + 1) * LANES) for g in range(QUADS)] for n in range(3)]
        d4s = [stack_heads(g_mix[rows[i], cols[0][g]], masks) for i, g in units]
        grads = [nt(qkv[rows[i], cols[2][g]], d4) for (i, g), d4 in zip(units, d4s)]
        probs = [attn[first[i] * QUADS + g] for i, g in units]
        for (i, g), a, d4 in zip(units, probs, d4s):
            g_qkv[outs[i], cols[2][g]] = nn(a, d4).astype(BF)
        dss = []
        for a, grad in zip(probs, grads):
            a = a.astype(F32)
            t = a * grad
            dss.append((t - a * jnp.sum(t, axis=0, keepdims=True)).astype(BF))
        for g in range(QUADS):
            total = dbias[g]
            for (_, other), ds in zip(units, dss):
                if other == g:
                    total = total + ds.astype(F32)
            dbias[g] = total
        talls = [tn(ds, qkv[rows[i], cols[1][g]]) for (i, g), ds in zip(units, dss)]
        for (i, g), ds in zip(units, dss):
            q4 = stack_heads(qkv[rows[i], cols[0][g]], masks)
            g_qkv[outs[i], cols[1][g]] = (nn(ds, q4) * SCALE).astype(BF)
        for (i, g), tall in zip(units, talls):
            g_qkv[outs[i], cols[0][g]] = (fold_heads(tall, masks) * SCALE).astype(BF)


def attn_bwd_body(
    shifted, grad_one, hid, vec, w_in, wn, qkv, attn, g_mix,
    grad_in, dw_in, dbias, small, g_qkv, patches, windows_of,
):
    dbias[...] = jnp.zeros_like(dbias)
    attn_bwd_windows((0, WINDOWS), qkv, g_mix, attn, g_qkv, dbias)
    for c in range(3):
        cols = slice(c * D, (c + 1) * D)
        dw_in[:, cols] = tn(wn[...], g_qkv[:, cols])
    windows_of[...] = nt(g_qkv[...], w_in[...])
    to_patches(windows_of, patches, shifted)
    g_normed = patches[...]
    normal, inverse = normalize(hid[...].astype(F32))
    small[...] = jnp.zeros((16, D), F32)
    small[0:1] = jnp.sum(g_normed * normal, axis=0, keepdims=True)
    small[1:2] = jnp.sum(g_normed, axis=0, keepdims=True)
    small[4:5] = jnp.sum(g_qkv[:, :D].astype(F32), axis=0, keepdims=True)
    small[5:6] = jnp.sum(g_qkv[:, 2 * D :].astype(F32), axis=0, keepdims=True)
    grad_in[...] = grad_one[...] + norm_backward(g_normed, normal, inverse, vec[0:1])


def attn_bwd(shifted, grad_one, hid, vec, w_in, wn, qkv, attn, g_mix):
    return call(
        functools.partial(attn_bwd_body, shifted),
        (
            sds((CELLS, D), F32),
            sds((D, 3 * D), F32),
            sds((QUADS, WROWS, PAIR), F32),
            sds((16, D), F32),
        ),
        8,
        scratch=[pltpu.VMEM((WTOK, 3 * D), BF), PATCHES, PADDED],
        us=10,
    )(grad_one, hid, vec, w_in, wn, qkv, attn, g_mix)


def window_perm_t(shifted):
    source = patch_of(jnp.arange(WTOK, dtype=jnp.int32), shifted)
    return (jnp.arange(CELLS, dtype=jnp.int32)[:, None] == source[None, :]).astype(BF)


def wrap_codes(shifted):
    code = np.zeros((CELLS,), np.float32)
    if shifted:
        for r in range(SIDE):
            for s in range(SIDE):
                rr, ss = (r - SHIFT) % SIDE, (s - SHIFT) % SIDE
                code[r * SIDE + s] = 2 * (rr >= SIDE - SHIFT) + (ss >= SIDE - SHIFT)
    return code


def window_masks(items, shifted):
    labels = items.astype(F32)
    if shifted:
        labels = labels * 4.0 + jnp.asarray(wrap_codes(True))
    placed = nn(jnp.broadcast_to((labels + 1.0).astype(BF), (8, CELLS)), window_perm_t(shifted))[0]
    placed = placed.reshape(WINDOWS, WROWS)
    same = (placed[:, :, None] == placed[:, None, :]) & (placed[:, :, None] > 0.0)
    same = same.astype(F32)
    return jnp.concatenate([same, same], axis=2)


def slot_places(routes, slots):
    group = (jnp.arange(CELLS, dtype=jnp.int32) // GROUP) * CAP
    place = routes * (2 * CAP) + group + slots
    return jnp.broadcast_to(place[:, None], (CELLS, LANES)), jnp.broadcast_to(place[None, :], (8, CELLS))

LEAD = 73
SMALL = 9326
LAG = LEAD * LANES - SMALL
VECTORS = 9
LINES = 32
SPANS = ((LEAD, D, 9), (LEAD + 3456, D, 3), (LEAD + 4608, 2 * D, 12), (LEAD + 4608 + 9216, 2 * F, 3))
EDGE = LEAD + 4608
ALIGNED = LEAD + 4608 + 2 * 9216


def relative(k, bits):
    total = 0
    for place, bit in enumerate(bits):
        total = total + (((k >> (len(bits) - 1 - place)) & 1) << bit)
    return total


def lanes_of(count=LANES):
    return lax.broadcasted_iota(jnp.int32, (1, count), 1)


def equal(rows, columns):
    return jnp.where(rows == columns, 1.0, 0.0).astype(BF)


def spread(shape):
    return lax.broadcasted_iota(jnp.int32, shape, 0), lax.broadcasted_iota(jnp.int32, shape, 1)


def exact(left, one, product):
    high = left.astype(BF)
    low = (left - high.astype(F32)).astype(BF)
    return product(high, one) + product(low, one)


def head_major():
    f, g = spread((D, D))
    return equal(f, 12 * (g & 31) + (g >> 5))


def head_rows(m):
    f, g = spread((D, 2 * LANES))
    return equal((f & 31) + 32 * m, g)


def offset_lanes():
    f, g = spread((LANES, LANES))
    i = g & 63
    r = (i * 37) >> 8
    return equal(f, jnp.where(i < WIN * WIN, 13 * r + i - WIN * r, -1))


def turns():
    return [13 * (6 - j // WIN) + 6 - j % WIN for j in range(WIN * WIN)]


def unpack_bias(flat, wide, tall, bias):
    wide[...] = jnp.zeros_like(wide)
    for m in range(6):
        for c in range(3):
            wide[m : m + 1, c * LANES : (c + 1) * LANES] = flat[12 + 3 * m + c : 13 + 3 * m + c, :]
    by_head = nn(wide[...].astype(BF), head_major())
    sub = lax.broadcasted_iota(jnp.int32, (16, D), 0)
    own = (lanes_of(D) >> 5) == sub
    table = jnp.zeros((16, 2 * LANES), F32)
    for m in range(6):
        table = table + nn(jnp.where(own, by_head[m : m + 1], 0.0).astype(BF), head_rows(m))
    tall[...] = jnp.zeros_like(tall)
    for j, turn in enumerate(turns()):
        row = pltpu.roll(table, (2 * LANES - turn) % (2 * LANES), 1)[:, :LANES]
        tall[pl.ds(j, 16, stride=WROWS), :] = row
    tall[...] = nn(tall[...].astype(BF), offset_lanes())
    for g in range(QUADS):
        for t in range(2):
            h = 4 * g + 2 * t
            left, right = tall[h * WROWS : (h + 1) * WROWS], tall[(h + 1) * WROWS : (h + 2) * WROWS]
            bias[g, :, t * LANES : (t + 1) * LANES] = jnp.where(lanes_of() < WROWS, left, right)


def unpack_small(flat, rows, wide, tall, vec, b1, router, router_bias, bias):
    def shifted(first, count, by):
        near, far = flat[first : first + count, :], flat[first + 1 : first + 1 + count, :]
        return pltpu.roll(jnp.where(lanes_of() >= by, near, far), LANES - by, 1)

    rows[0:16, :] = shifted(27, 16, 108)
    rows[16:46, :] = shifted(42, 30, 110)
    vec[...] = jnp.zeros_like(vec)
    b1[...] = jnp.zeros_like(b1)
    for c in range(3):
        cols = slice(c * LANES, (c + 1) * LANES)
        for n in range(4):
            vec[n : n + 1, cols] = flat[3 * n + c : 3 * n + c + 1, :]
        for n in range(3):
            vec[4 + n : 5 + n, cols] = rows[3 * n + c : 3 * n + c + 1, :]
        for e in range(EXPERTS):
            vec[7 + e : 8 + e, cols] = rows[40 + 3 * e + c : 41 + 3 * e + c, :]
    for e in range(EXPERTS):
        for c in range(12):
            b1[e : e + 1, c * LANES : (c + 1) * LANES] = rows[16 + 12 * e + c : 17 + 12 * e + c, :]
        one = jnp.sum(jnp.where(lanes_of() == e, rows[15:16, :], 0.0), axis=1, keepdims=True)
        router_bias[e : e + 1, :] = jnp.broadcast_to(one, (1, LANES))
    pairs = jnp.concatenate([rows[9 + c : 10 + c, :] for c in range(6)], axis=1)
    pairs = jnp.broadcast_to(pairs, (LANES, 2 * D)).astype(BF)
    d, f = spread((D, 2 * D))
    for e in range(EXPERTS):
        router[:, e * LANES : (e + 1) * LANES] = nt(equal(f, 2 * d + e), pairs).astype(BF)
    gap = nt(pairs[0:16], equal(f, 2 * d + 1)) - nt(pairs[0:16], equal(f, 2 * d))
    vec[9:10, :] = gap[0:1]
    unpack_bias(flat, wide, tall, bias)


def unpack_matrices(flat, spans, outs, skipped):
    for (base, height, tiles), out in zip(spans, outs):
        step = 128

        @pl.loop(0, height // step, unroll=min(6, height // step))
        def _(t, base=base, tiles=tiles, out=out):
            first = base - 1 - skipped + t * (step * tiles)
            before = flat[pl.ds(first, step, stride=tiles), :]
            for j in range(tiles):
                here = flat[pl.ds(first + 1 + j, step, stride=tiles), :]
                tile = pltpu.roll(jnp.where(lanes_of() >= LANES - LAG, before, here), LAG, 1)
                out[pl.ds(pl.multiple_of(t * step, step), step), j * LANES : (j + 1) * LANES] = tile.astype(BF)
                before = here


def unpack_head_body(rows, runs, me, *refs):
    got = refs[: len(runs)]
    w_in, w_out, rest, vec, b1, router, router_bias, bias, flat, few, wide, tall = refs[len(runs) :]
    for (bits, fixed), part in zip(runs, got):

        @pl.loop(0, 1 << len(bits))
        def _(k, bits=bits, fixed=fixed, part=part):
            d = me[1] ^ (relative(k, bits) + fixed)
            flat[pl.ds(d * rows, rows), :] = part[k, :rows, :].astype(F32)

    unpack_small(flat, few, wide, tall, vec, b1, router, router_bias, bias)
    unpack_matrices(flat, SPANS[:2], (w_in, w_out), 0)
    rest[...] = flat[EDGE - 1 : EDGE - 1 + rest.shape[0], :]


def unpack_tail_body(rows, heads, runs, me, rest, *refs):
    got = refs[: len(runs)]
    w1, w2, flat = refs[len(runs) :]
    flat[0 : rest.shape[0], :] = rest[...]
    for (outer, inner, fixed, upper), part in zip(runs, got):
        count = 1 << len(inner)
        half = part.shape[1]
        first = half if upper else 0
        used = min(half, rows - first)

        @pl.loop(0, part.shape[0], unroll=6)
        def _(k, outer=outer, inner=inner, fixed=fixed, part=part, count=count, first=first, used=used):
            own = (relative(k // (3 * count), outer) + relative(k % count, inner) + fixed) ^ me[1]
            d = ((k // count) % 3 + 1) * heads + own
            flat[pl.ds(d * rows + first - (EDGE - 1), used), :] = part[k, :used, :].astype(F32)

    unpack_matrices(flat, SPANS[2:], (w1, w2), EDGE - 1)


class Weights(NamedTuple):
    w_in: Any
    w_out: Any
    w1: Any
    w2: Any
    vec: Any
    b1: Any
    router: Any
    router_bias: Any
    bias: Any


SMALL_SHAPES = (
    sds((16, D), F32),
    sds((8, F), F32),
    sds((D, 2 * LANES), BF),
    sds((8, LANES), F32),
    sds((QUADS, WROWS, PAIR), F32),
)
SMALL_SCRATCH = [pltpu.VMEM((48, LANES), F32), pltpu.VMEM((8, D), F32), pltpu.VMEM((16 * WROWS, LANES), F32)]
HEAD_SHAPES = (sds((D, 3 * D), BF), sds((D, D), BF))
TAIL_SHAPES = (sds((2 * D, F), BF), sds((2 * F, D), BF))


def experts(w1, w2):
    return w1.reshape(EXPERTS, D, F), w2.reshape(EXPERTS, F, D)


def unpack_head(me, parts, runs, rows, devices):
    heads = devices // 4
    w_in, w_out, rest, *small = call(
        functools.partial(unpack_head_body, rows, runs),
        HEAD_SHAPES + (sds((heads * rows - EDGE + 1, LANES), F32),) + SMALL_SHAPES,
        1 + len(parts),
        scratch=[pltpu.VMEM((heads * rows + 8, LANES), F32)] + SMALL_SCRATCH,
        smem=1,
        us=4,
    )(me, *parts)
    return Weights(w_in, w_out, None, None, *small), rest


def unpack_tail(me, rest, parts, runs, rows, devices):
    return experts(
        *call(
            functools.partial(unpack_tail_body, rows, devices // 4, runs),
            TAIL_SHAPES,
            2 + len(parts),
            scratch=[pltpu.VMEM((devices * rows - EDGE + 9, LANES), F32)],
            smem=1,
            us=4,
        )(me, rest, *parts)
    )


def pack_bias(dbias, wide, tall):
    tall[HEADS * WROWS :, :] = jnp.zeros((4 * WROWS, LANES), F32)
    for h in range(HEADS):
        g, t, side = h // 4, (h % 4) // 2, h % 2
        tile = dbias[g, :, t * LANES : (t + 1) * LANES]
        tall[h * WROWS : (h + 1) * WROWS, :] = jnp.where((lanes_of() >> 6) == side, tile, 0.0)
    used = HEADS * WROWS
    tall[0:used, :] = exact(tall[0:used, :], offset_lanes(), nt)
    table = jnp.zeros((16, 2 * LANES), F32)
    for j, turn in enumerate(turns()):
        row = tall[pl.ds(j, 16, stride=WROWS), :]
        table = table + pltpu.roll(jnp.concatenate([row, jnp.zeros_like(row)], axis=1), turn, 1)
    sub = lax.broadcasted_iota(jnp.int32, (16, D), 0)
    own = (lanes_of(D) >> 5) == sub
    wide[...] = jnp.zeros_like(wide)
    for m in range(6):
        placed = jnp.where(own, exact(table, head_rows(m), nt), 0.0)
        wide[m : m + 1, :] = jnp.sum(placed, axis=0, keepdims=True)
    wide[...] = exact(wide[...], head_major(), nt)


def pack_small(al, vectors, drouter, db1, dbias, one, two, wide, tall):
    one[...] = jnp.zeros_like(one)
    two[...] = jnp.zeros_like(two)
    pack_bias(dbias, wide, tall)
    d, f = spread((D, 2 * D))
    signs = equal(f, 2 * d + 1) - equal(f, 2 * d)
    pairs = exact(drouter[...], signs, nn)
    for c in range(3):
        cols = slice(c * LANES, (c + 1) * LANES)
        for n in range(4):
            one[1 + 3 * n + c : 2 + 3 * n + c, :] = vectors[n : n + 1, cols]
        for m in range(6):
            one[13 + 3 * m + c : 14 + 3 * m + c, :] = wide[m : m + 1, cols]
        for n in range(3):
            two[1 + 3 * n + c : 2 + 3 * n + c, :] = vectors[4 + n : 5 + n, cols]
        for e in range(EXPERTS):
            al[67 + 3 * e + c : 68 + 3 * e + c, :] = vectors[7 + e : 8 + e, cols]
    for c in range(6):
        two[10 + c : 11 + c, :] = pairs[0:1, c * LANES : (c + 1) * LANES]
    total = vectors[9:10, 0:LANES]
    two[16:17, :] = jnp.where(lanes_of() == 0, -total, jnp.where(lanes_of() == 1, total, 0.0))
    for e in range(EXPERTS):
        for c in range(12):
            al[43 + 12 * e + c : 44 + 12 * e + c, :] = db1[e : e + 1, c * LANES : (c + 1) * LANES]
    first = pltpu.roll(jnp.where(lanes_of() >= LANES - 18, one[0:28, :], one[1:29, :]), 18, 1)
    second = pltpu.roll(jnp.where(lanes_of() >= LANES - 126, two[0:16, :], two[1:17, :]), 126, 1)
    al[27:43, :] = second
    al[0:27, :] = first[0:27]
    al[27:28, :] += first[27:28]


def pack_matrices(al, spans, grads, skipped):
    for (base, height, tiles), grad in zip(spans, grads):
        step = 128

        @pl.loop(0, height // step, unroll=min(6, height // step))
        def _(t, base=base, tiles=tiles, grad=grad):
            first = base - skipped + t * (step * tiles)
            own = pl.ds(pl.multiple_of(t * step, step), step)
            for j in range(tiles):
                al[pl.ds(first + j, step, stride=tiles), :] = grad[own, j * LANES : (j + 1) * LANES]


def clear(al, first):
    al[pl.ds(first, al.shape[0] - first), :] = jnp.zeros((al.shape[0] - first, LANES), F32)


def pack_head_body(
    rows, padded, runs, me, moe, attn, proj, drouter, db1, dbias, dw_in, dw_out, rest,
    keep, send, al, vectors, lines, one, two, wide, tall,
):
    vectors[...] = moe[...] + attn[...] + proj[...]
    lines[...] = jnp.zeros_like(lines)
    for n in range(VECTORS):
        for c in range(3):
            lines[3 * n + c : 3 * n + c + 1, :] = vectors[n : n + 1, c * LANES : (c + 1) * LANES]
    pack_small(al, vectors, drouter, db1, dbias, one, two, wide, tall)
    pack_matrices(al, SPANS[:2], (dw_in, dw_out), 0)
    al[EDGE : EDGE + rest.shape[0], :] = rest[...]
    at = 0
    for bits, fixed in runs:
        for other, out in enumerate((keep, send)):

            @pl.loop(0, 1 << len(bits))
            def _(k, bits=bits, fixed=fixed, at=at, other=other, out=out):
                d = me[1] ^ (relative(k, bits) + fixed + other)
                out[at + k, :padded, :] = al[pl.ds(d * rows, padded), :].astype(BF)
                out[at + k, padded:, :] = lines[...].astype(BF)

        at += 1 << len(bits)


def pack_tail_body(rows, padded, heads, runs, me, dw1, dw2, keep, send, rest, al):
    clear(al, ALIGNED - EDGE)
    pack_matrices(al, SPANS[2:], (dw1, dw2), EDGE)
    rest[...] = al[0 : rest.shape[0], :]
    half = padded // 2
    at = 0
    for outer, inner, fixed, upper in runs:
        count = 1 << len(inner)
        total = 3 * count << len(outer)
        for other, out in enumerate((keep, send)):

            @pl.loop(0, total, unroll=3)
            def _(k, outer=outer, inner=inner, fixed=fixed, upper=upper, count=count, at=at, other=other, out=out):
                own = (relative(k // (3 * count), outer) + relative(k % count, inner) + fixed + other) ^ me[1]
                d = ((k // count) % 3 + 1) * heads + own
                out[at + k] = al[pl.ds(d * rows + (half if upper else 0) - EDGE, half), :].astype(BF)

        at += total


SMALL_PACK = [
    pltpu.VMEM((40, LANES), F32),
    pltpu.VMEM((24, LANES), F32),
    pltpu.VMEM((8, D), F32),
    pltpu.VMEM((16 * WROWS, LANES), F32),
]


def pack_head(me, small, dw_in, dw_out, rest, runs, rows, devices, padded):
    heads = devices // 4
    shape = sds((heads // 2, padded + LINES, LANES), BF)
    return call(
        functools.partial(pack_head_body, rows, padded, runs),
        (shape, shape),
        10,
        scratch=[
            pltpu.VMEM((EDGE + rest.shape[0], LANES), F32),
            pltpu.VMEM((16, D), F32),
            pltpu.VMEM((LINES, LANES), F32),
        ]
        + SMALL_PACK,
        smem=1,
        us=3,
    )(me, *small, dw_in, dw_out, rest)


def pack_tail(me, dw1, dw2, runs, rows, devices, padded):
    heads = devices // 4
    shape = sds((3 * heads, padded // 2, LANES), BF)
    over = -(-(heads * rows + padded - EDGE) // 8) * 8
    return call(
        functools.partial(pack_tail_body, rows, padded, heads, runs),
        (shape, shape, sds((over, LANES), F32)),
        3,
        scratch=[pltpu.VMEM((devices * rows + padded - EDGE, LANES), F32)],
        smem=1,
        us=3,
    )(me, dw1.reshape(2 * D, F), dw2.reshape(2 * F, D))


def levels_body(sources, me, *refs):
    pieces, (head, a, b) = refs[: len(refs) - 3], refs[len(refs) - 3 :]
    n, half = head.shape[0], a.shape[1]
    for level in range(4):
        for step, (at, first) in enumerate(sources):

            @pl.when((me[2] ^ step) == level)
            def _(level=level, at=at, first=first):
                for i in range(n):
                    if level == 0:
                        head[i] = pieces[at][first * n + i]
                    else:
                        a[(level - 1) * n + i] = pieces[at][first * n + i, :half, :]
                        b[(level - 1) * n + i] = pieces[at][first * n + i, half:, :]


def levels(me, *pieces):
    sources = ((0, 0), (1, 0), (2, 0), (3, 0)) if len(pieces) == 4 else ((0, 0), (1, 0), (0, 1), (1, 1))
    n, padded, _ = pieces[0].shape
    n = n * len(pieces) // 4
    dtype = pieces[0].dtype
    shape = sds((3 * n, padded // 2, LANES), dtype)
    shapes = (sds((n, padded, LANES), dtype), shape, shape)
    return call(functools.partial(levels_body, sources), shapes, 1 + len(pieces), smem=1)(me, *pieces)


def targets_body(with_head, me, a, a_got, b, b_got, *refs):
    *head, keep, send = refs
    n, half = keep.shape[0] // 2, a.shape[1]
    places = {0: (keep, 0), 2: (keep, n), 1: (send, 0), 3: (send, n)}
    for step, (out, first) in places.items():
        level = me[2] ^ step

        @pl.when(level == 0)
        def _(out=out, first=first):
            for i in range(n):
                if with_head:
                    out[first + i] = head[0][i, : 2 * half, :].astype(out.dtype)
                else:
                    out[first + i] = jnp.zeros((2 * half, LANES), out.dtype)

        @pl.when(level > 0)
        def _(out=out, first=first, level=level):
            for i in range(n):
                at = (level - 1) * n + i
                out[first + i, :half, :] = (a[at] + a_got[at].astype(F32)).astype(out.dtype)
                out[first + i, half:, :] = (b[at] + b_got[at].astype(F32)).astype(out.dtype)


def targets(me, a, a_got, b, b_got, *head):
    n, half, _ = a.shape
    n = n // 3
    shape = (2 * n, 2 * half, LANES)
    return call(
        functools.partial(targets_body, bool(head)), (sds(shape, F32), sds(shape, BF)), 5 + len(head), smem=1
    )(me, a, a_got, b, b_got, *head)


def combine_body(plan, count, *refs):
    for (size, _, terms), out in zip(plan, refs[count:]):

        @pl.loop(0, size)
        def _(i, terms=terms, out=out):
            parts = [refs[at][first + i].astype(F32) for at, first in terms]
            while len(parts) > 1:
                parts = [sum(parts[at + 1 : at + 2], parts[at]) for at in range(0, len(parts), 2)]
            out[i] = parts[0].astype(out.dtype)


def combine(plan, *arrays):
    tail = arrays[0].shape[1:]
    shapes = [sds((size, *tail), dtype) for size, dtype, _ in plan]
    return call(functools.partial(combine_body, plan, len(arrays)), shapes, len(arrays))(*arrays)


def finish_body(rows, me, keep, got, upper_keep, upper_got, out):
    def shift(keep, got):
        total = keep[0] + got[0].astype(F32)
        here, below = total[0:rows, :], total[1 : rows + 1, :]
        out[...] = pltpu.roll(jnp.where(lanes_of() >= LAG, here, below), LANES - LAG, 1)

    pl.when(me[2] == 0)(lambda: shift(keep, got))
    pl.when(me[2] != 0)(lambda: shift(upper_keep, upper_got))


def finish(me, rows, lowest, upper):
    parts = (lowest.keep, lowest.got, upper.keep, upper.got)
    return call(functools.partial(finish_body, rows), sds((rows, LANES), F32), 5, smem=1)(me, *parts)


def join_body(a, b, out):
    n = a.shape[0]

    @pl.loop(0, n)
    def _(i):
        out[i] = a[i]
        out[n + i] = b[i]


def join(a, b):
    return call(join_body, sds((2 * a.shape[0], *a.shape[1:]), a.dtype), 2)(a, b)


class Ways(NamedTuple):
    core: Any
    x: Any
    y: Any
    low: Any
    high: Any
    rest: Any


def ways():
    dp, fsdp = (lax.axis_size(axis).bit_length() - 1 for axis in (DP, FSDP))
    rest = [1 << (fsdp + bit) for bit in range(1, dp - 2)] + [1 << bit for bit in range(2, fsdp)]
    return Ways(1, 2, 1 << fsdp, 1 << (fsdp + dp - 2), 1 << (fsdp + dp - 1), rest)


def device_count():
    return lax.axis_size(DP) * lax.axis_size(FSDP)


def flip(array, step):
    return lax.ppermute(array, (DP, FSDP), [(i, i ^ step) for i in range(device_count())])


def move(array, levels):
    width = device_count() // 4
    pairs = [(a * width + i, b * width + i) for a, b in levels.items() for i in range(width)]
    return lax.ppermute(array, (DP, FSDP), pairs)


def tie(arrays, *others):
    if isinstance(arrays, tuple):
        return tuple(tie(array, *others) for array in arrays)
    return lax.optimization_barrier((arrays, *others))[0]


def sync(*arrays):
    return lax.optimization_barrier(arrays)


def bits_of(*steps):
    return [step.bit_length() - 1 for step in steps]


class Gather:
    def __init__(self, own, way, me):
        for extra in way.rest:
            own = join(own, flip(own, extra))
        self.way, self.own, self.me = way, own, me
        self.rest = bits_of(*reversed(way.rest))

    def high(self):
        self.other = flip(self.own, self.way.high)

    def low(self):
        self.pair = join(self.own, self.other)
        self.over = flip(self.pair, self.way.low)

    def far(self):
        own, way = self.own, self.way
        self.others = own, flip(own, way.low), flip(own, way.high), flip(own, way.low + way.high)

    def levels(self):
        self.head, self.a, self.b = levels(self.me, *self.others)

    def head_near(self):
        way = self.way
        self.steps = way.x, way.y, way.x + way.y
        self.head_got = tuple(flip(self.head, step) for step in self.steps)

    def head_core(self):
        core = self.way.core
        parts = [self.head, *self.head_got]
        self.head_parts = parts + [flip(part, core) for part in parts]
        self.head_runs = [(self.rest, step) for step in (0, *self.steps)]
        self.head_runs += [(self.rest, step + core) for step in (0, *self.steps)]

    def near_a(self):
        self.a_got = flip(self.a, self.way.x)

    def near_b(self):
        self.b_got = flip(self.b, self.way.y)

    def last(self):
        way = self.way
        self.parts = [join(self.a, self.a_got), join(self.b, self.b_got)]
        self.got = flip(self.parts[0], way.y), flip(self.parts[1], way.x)

    def cores(self):
        way = self.way
        parts = self.parts + list(self.got)
        self.parts = parts + [flip(part, way.core) for part in parts]
        bx, by = bits_of(way.x), bits_of(way.y)
        self.runs = []
        for fixed in (0, way.core):
            for fx, fy in ((0, 0), (way.y, way.x)):
                self.runs += [(bx, self.rest, fx + fixed, False), (by, self.rest, fy + fixed, True)]


def head_runs(way):
    rest = bits_of(*way.rest)
    return [(rest, step) for step in (way.y, way.x + way.y, way.x, 0)]


def tail_runs(way):
    rest, bx, by = (bits_of(*steps) for steps in (way.rest, [way.x], [way.y]))
    return [
        (bx, rest, way.y, False), ([], rest, way.x, False), ([], rest, 0, False),
        (by, rest, way.x, True), ([], rest, way.y, True), ([], rest, 0, True),
    ]


class HeadScatter:
    def __init__(self, keep, send, way):
        self.way, self.keep, self.n = way, keep, keep.shape[0] // 4
        self.got = flip(send, way.core)

    def plane(self):
        n, way = self.n, self.way
        y, xy, x, self.keep = combine([(n, BF, ((0, i * n), (1, i * n))) for i in range(4)], self.keep, self.got)
        self.got = flip(x, way.x), flip(y, way.y), flip(xy, way.x + way.y)

    def near(self):
        n = 2 * self.n
        sent, self.keep = combine([(n, BF, ((0, i * n), (1, i * n))) for i in range(2)], self.keep, self.got)
        self.got = flip(sent, self.way.y)

    def next(self):
        n = self.n
        sent, self.keep = combine(((n, BF, ((0, 0), (1, n))), (n, BF, ((0, n), (1, 0)))), self.keep, self.got)
        self.got = flip(sent, self.way.x)

    def add(self):
        n, got = self.n, self.got if isinstance(self.got, (tuple, list)) else (self.got,)
        terms = tuple((i, 0) for i in range(1 + len(got)))
        sent, self.keep = combine(((n, BF, terms), (n, F32, terms)), self.keep, *got)
        return sent

    def lines(self):
        return self.keep[0, -LINES : 3 * VECTORS - LINES].reshape(VECTORS, D)

    def low(self, sent):
        self.got = move(sent, {1: 0, 3: 2})

    def high(self):
        self.got = move(self.add(), {2: 0})
        self.keep, self.got = fold(self.keep, self.got, self.way.rest)


class TailScatter:
    def __init__(self, keep, send, way, me):
        self.way, self.keep, self.n, self.me = way, keep, keep.shape[0] // 24, me
        self.got = flip(send, way.core)

    def near(self):
        n = 6 * self.n
        plan = [(n, dtype, ((0, first), (1, first))) for dtype, first in ((BF, 0), (F32, n), (BF, 2 * n), (F32, 3 * n))]
        a, self.a, b, self.b = combine(plan, self.keep, self.got)
        self.a_got, self.b_got = flip(a, self.way.y), flip(b, self.way.x)

    def next(self):
        n = 3 * self.n
        plan = [(n, BF, ((0, 0), (1, n))), (n, F32, ((0, n), (1, 0)))]
        plan += [(n, BF, ((2, 0), (3, n))), (n, F32, ((2, n), (3, 0)))]
        a, self.a, b, self.b = combine(plan, self.a, self.a_got, self.b, self.b_got)
        self.a_got, self.b_got = flip(a, self.way.x), flip(b, self.way.y)

    def low(self, *head):
        self.keep, sent = targets(self.me, self.a, self.a_got, self.b, self.b_got, *head)
        self.got = flip(sent, self.way.low)

    def high(self):
        self.keep, self.got = fold(self.keep, self.got, [self.way.high] + self.way.rest)


def fold(keep, got, steps):
    for way in steps:
        half = keep.shape[0] // 2
        plan = ((half, BF, ((0, half), (1, half))), (half, F32, ((0, 0), (1, 0))))
        sent, keep = combine(plan, keep, got)
        got = flip(sent, way)
    return keep, got


def shards(inputs, items, routes, slots, cotangent, params, momentum, average):
    fsdp, dp = lax.axis_size(FSDP), lax.axis_size(DP)
    devices = fsdp * dp
    share = params.shape[1]
    rows = share // LANES
    padded = -(-(rows + 1) // 32) * 32
    step_rate = RATE_BASE / math.sqrt(CELLS * devices)
    way = ways()
    own = lax.axis_index(DP) * fsdp + lax.axis_index(FSDP)
    me = jnp.stack([own, own % (devices // 4), own // (devices // 4)]).astype(jnp.int32)

    shares = []
    for b in range(BLOCKS):
        share_rows = params[b].astype(BF).reshape(1, rows, LANES)
        shares.append(jnp.pad(share_rows, ((0, 0), (0, padded - rows), (0, 0))))
    one, two = (Gather(rows_own, way, me) for rows_own in shares)
    masks, places = [], []
    for b in range(BLOCKS):
        masks.append(window_masks(items.reshape(CELLS), b % 2 == 1))
        places.append(slot_places(routes[b].reshape(CELLS), slots[b].reshape(CELLS)))

    hidden_zero = inputs.reshape(CELLS, D)
    one.far()
    one.levels()
    one.head_near()
    one.near_a()
    one.near_b()
    one.a_got, one.b_got, *one.head_got = sync(one.a_got, one.b_got, *one.head_got)
    one.head_core()
    one.last()
    two.own = tie(two.own, one.a_got)
    two.far()
    one.head_parts[0] = tie(one.head_parts[0], *one.parts)
    w, rest = unpack_head(me, one.head_parts, one.head_runs, rows, devices)
    h_zero, *attn_zero = attn_fwd(False, hidden_zero, w.vec, w.w_in, w.w_out, w.bias, masks[0])
    h_zero, *got = sync(h_zero, *one.got, *two.others)
    one.got, two.others = got[:2], got[2:]
    one.cores()
    two.levels()
    two.head_near()
    two.near_a()
    two.near_b()
    w1, w2 = unpack_tail(me, tie(rest, two.head), one.parts, one.runs, rows, devices)
    w_zero = w._replace(w1=w1, w2=w2)
    w = w_zero
    hidden_one, *moe_zero = moe_fwd(h_zero, w.vec, w.w1, w.w2, w.b1, w.router, w.router_bias, places[0], F32)

    hidden_one, two.a_got, two.b_got, *two.head_got = sync(hidden_one, two.a_got, two.b_got, *two.head_got)
    two.head_core()
    two.last()
    two.head_parts[0] = tie(two.head_parts[0], *two.parts)
    w, rest = unpack_head(me, two.head_parts, two.head_runs, rows, devices)
    h_one, *attn_one = attn_fwd(True, hidden_one, w.vec, w.w_in, w.w_out, w.bias, masks[1])
    h_one, *two.got = sync(h_one, *two.got)
    two.cores()
    w1, w2 = unpack_tail(me, rest, two.parts, two.runs, rows, devices)
    w_one = w._replace(w1=w1, w2=w2)
    w = w_one
    outputs, *moe_one = moe_fwd(h_one, w.vec, w.w1, w.w2, w.b1, w.router, w.router_bias, places[1], BF)

    gradient = cotangent.reshape(CELLS, D)
    wn, qkv, mixed, attn = attn_one
    normed_two, *saved = moe_one
    dw1, dw2, db1, small_moe, g_pre, gate_grad = moe_bwd(gradient, w.w2, places[1], saved)
    keep, send, rest = pack_tail(me, dw1, dw2, tail_runs(way), rows, devices, padded)
    tail_one = TailScatter(keep, send, way, me)
    g_one, g_mix, dw_out, drouter, small_mid = middle_bwd(
        True, gradient, h_one, w.vec, w.w1, w.w_out, places[1][0], normed_two, tie(g_pre, send), gate_grad, mixed
    )
    g_mix, tail_one.got = sync(g_mix, tail_one.got)
    tail_one.near()
    gradient, dw_in, dbias, small_attn = attn_bwd(
        True, tie(g_one, tail_one.a), hidden_one, w.vec, w.w_in, wn, qkv, attn, g_mix
    )
    small = (small_moe, small_mid, small_attn, drouter, db1, dbias)
    keep, send = pack_head(me, small, dw_in, dw_out, rest, head_runs(way), rows, devices, padded)
    send, tail_one.a_got, tail_one.b_got, gradient = sync(send, tail_one.a_got, tail_one.b_got, gradient)
    head_one = HeadScatter(keep, send, way)
    tail_one.next()

    w = w_zero
    wn, qkv, mixed, attn = attn_zero
    normed_two, *saved = moe_zero
    gradient = tie(gradient, tail_one.a)
    dw1, dw2, db1, small_moe, g_pre, gate_grad = moe_bwd(gradient, w.w2, places[0], saved)
    g_pre, dw2, head_one.got, tail_one.a_got, tail_one.b_got = sync(
        g_pre, dw2, head_one.got, tail_one.a_got, tail_one.b_got
    )
    head_one.near()
    tail_one.low()
    keep, send, rest = pack_tail(me, dw1, tie(dw2, head_one.keep, tail_one.keep), tail_runs(way), rows, devices, padded)
    tail_zero = TailScatter(keep, send, way, me)
    g_one, g_mix, dw_out, drouter, small_mid = middle_bwd(
        False, gradient, h_zero, w.vec, w.w1, w.w_out, places[0][0], normed_two, tie(g_pre, send), gate_grad, mixed
    )
    g_mix, tail_zero.got = sync(g_mix, tail_zero.got)
    tail_zero.near()
    gradient, dw_in, dbias, small_attn = attn_bwd(
        False, tie(g_one, tail_zero.a), hidden_zero, w.vec, w.w_in, wn, qkv, attn, g_mix
    )
    dw_in, tail_one.got, head_one.got = sync(dw_in, tail_one.got, head_one.got)
    head_one.next()
    tail_one.high()
    small = (small_moe, small_mid, small_attn, drouter, db1, tie(dbias, head_one.keep, tail_one.keep))
    keep, send = pack_head(me, small, dw_in, dw_out, rest, head_runs(way), rows, devices, padded)
    send, tail_zero.a_got, tail_zero.b_got, head_one.got, tail_one.got = sync(
        send, tail_zero.a_got, tail_zero.b_got, head_one.got, tail_one.got
    )

    head_zero = HeadScatter(keep, send, way)
    tail_zero.next()
    head_zero.plane()
    head_one.add()
    tail_zero.low(head_one.keep)
    sent = head_zero.add()
    head_zero.low(sent)
    vector_grads = jnp.stack([head_zero.lines(), head_one.lines()])
    got = flip(vector_grads, way.low)
    tail_zero.high()
    vector_grads = vector_grads + got
    head_zero.keep = tie(head_zero.keep, vector_grads)
    head_zero.high()
    for step in [way.high] + way.rest:
        vector_grads = vector_grads + flip(vector_grads, step)
    grads_zero = finish(me, rows, head_zero, tail_zero)
    grads_one = finish(me, rows, tail_zero, tail_one)
    grad_all = jnp.stack([grads_zero.reshape(-1), grads_one.reshape(-1)])
    new_momentum = MOMENTUM_DECAY * momentum + grad_all
    new_params = params - step_rate * (grad_all + MOMENTUM_DECAY * new_momentum)
    new_average = AVERAGE_DECAY * average + (1.0 - AVERAGE_DECAY) * new_params
    return (
        outputs.reshape(1, CELLS, D),
        gradient.reshape(1, CELLS, D),
        new_params,
        new_momentum,
        new_average,
        vector_grads,
    )


def solution(mesh):
    both = (DP, FSDP)
    canvas, vector = P(both), P(None, both)
    return jax.shard_map(
        shards,
        mesh=mesh,
        in_specs=(canvas, canvas, vector, vector, canvas, vector, vector, vector),
        out_specs=(canvas, canvas, vector, vector, vector, P()),
        check_vma=False,
    )
```

```python
import functools
import math
from typing import Any, NamedTuple

import jax
import jax.numpy as jnp
import numpy as np
from jax import lax
from jax.experimental import pallas as pl
from jax.experimental.pallas import tpu as pltpu
from jax.sharding import PartitionSpec as P

D = 384
HEADS = 12
F = 1536
HEAD_DIM = 32
EXPERTS = 2
CAP = 256
SIDE = 28
WIN = 7
SHIFT = 3
BLOCKS = 2
CELLS = 784
GROUP = 392
RELS = 169
NORM_EPSILON = 1e-05
MOMENTUM_DECAY = 0.9
AVERAGE_DECAY = 0.9
RATE_BASE = 0.1

DP = "dp"
FSDP = "fsdp"
LANES = 128
WROWS = 64
WINDOWS = 16
WTOK = WINDOWS * WROWS
SLOTS = EXPERTS * 2 * CAP
PAIR = 4 * WROWS
QUADS = HEADS // 4
SCALE = HEAD_DIM ** (-0.5)
US_FLOPS = 1.0e9
BF = jnp.bfloat16
F32 = jnp.float32
VMEM_BYTES = 8 * 1024 * 1024
BIG_VMEM = 13 * 1024 * 1024


def call(body, out_shape, n_in, scratch=(), smem=0, deps=(), us=1, vmem=VMEM_BYTES):
    def skipping(*refs):
        body(*refs[:n_in], *refs[n_in + len(deps) :])

    run = pl.pallas_call(
        skipping,
        out_shape=out_shape,
        in_specs=[pl.BlockSpec(memory_space=pltpu.SMEM)] * smem
        + [pl.BlockSpec(memory_space=pltpu.VMEM)] * (n_in - smem)
        + [pl.BlockSpec(memory_space=pl.ANY)] * len(deps),
        out_specs=jax.tree.map(lambda _: pl.BlockSpec(memory_space=pltpu.VMEM), out_shape),
        scratch_shapes=list(scratch),
        compiler_params=pltpu.CompilerParams(vmem_limit_bytes=vmem),
        cost_estimate=pl.CostEstimate(flops=int(us * US_FLOPS), bytes_accessed=0, transcendentals=0),
    )
    return lambda *args: run(*args, *deps)


def sds(shape, dtype):
    return jax.ShapeDtypeStruct(shape, dtype)


def nn(a, b):
    return lax.dot_general(a, b, (((1,), (0,)), ((), ())), preferred_element_type=F32)


def nt(a, b):
    return lax.dot_general(a, b, (((1,), (1,)), ((), ())), preferred_element_type=F32)


def tn(a, b):
    return lax.dot_general(a, b, (((0,), (0,)), ((), ())), preferred_element_type=F32)


def normalize(hidden):
    centre = hidden - jnp.mean(hidden, axis=-1, keepdims=True)
    inverse = lax.rsqrt(jnp.mean(centre * centre, axis=-1, keepdims=True) + NORM_EPSILON)
    return centre * inverse, inverse


def norm_backward(grad_normed, normal_rows, inverse, gain_row):
    scaled = grad_normed * gain_row
    return inverse * (
        scaled
        - jnp.mean(scaled, axis=-1, keepdims=True)
        - normal_rows * jnp.mean(scaled * normal_rows, axis=-1, keepdims=True)
    )


def head_masks():
    lane = lax.broadcasted_iota(jnp.int32, (1, LANES), 1) // HEAD_DIM
    return [lane == h for h in range(4)]


def stack_heads(rows, masks):
    zero = jnp.zeros_like(rows)
    return jnp.concatenate([jnp.where(mask, rows, zero) for mask in masks], axis=0)


def fold_heads(tall, masks):
    out = jnp.where(masks[0], tall[0:WROWS], 0.0)
    for h in range(1, 4):
        out = jnp.where(masks[h], tall[h * WROWS : (h + 1) * WROWS], out)
    return out


def patch_of(row, shifted):
    w, p = row >> 6, row & 63
    pr = (p * 37) >> 8
    r = (w >> 2) * WIN + pr
    s = (w & 3) * WIN + p - pr * WIN
    if shifted:
        r, s = r + SHIFT, s + SHIFT
        r = jnp.where(r >= SIDE, r - SIDE, r)
        s = jnp.where(s >= SIDE, s - SIDE, s)
    return jnp.where(p < WIN * WIN, r * SIDE + s, -1)


def runs_of(shifted):
    runs = []
    for w in range(WINDOWS):
        for p in range(WIN):
            r, s = (w // 4) * WIN + p, (w % 4) * WIN
            if shifted:
                r, s = (r + SHIFT) % SIDE, s + SHIFT
            here = min(WIN, SIDE - s)
            runs.append((w * WROWS + p * WIN, r * SIDE + s, here))
            if here < WIN:
                runs.append((w * WROWS + p * WIN + here, r * SIDE, WIN - here))
    return runs


def to_windows(patches, windows, shifted):
    windows[...] = jnp.zeros_like(windows)
    for row, patch, length in runs_of(shifted):
        windows[row : row + length, :] = patches[patch : patch + length, :]


def to_patches(windows, patches, shifted):
    for row, patch, length in runs_of(shifted):
        patches[patch : patch + length, :] = windows[row : row + length, :]


PATCHES = pltpu.VMEM((CELLS, D), F32)
PADDED = pltpu.VMEM((WTOK, D), F32)
ONEHOT = pltpu.VMEM((CELLS, SLOTS), BF)
ONEHOT_T = pltpu.VMEM((SLOTS, CELLS), BF)


def attn_fwd_body(shifted, hid, vec, w_in, w_out, bias, mask, h_one, wn, qkv, mixed, attn, patches, windows):
    normal, _ = normalize(hid[...].astype(F32))
    patches[...] = normal * vec[0:1] + vec[1:2]
    to_windows(patches, windows, shifted)
    wn[...] = windows[...].astype(BF)
    in_bias = jnp.concatenate([vec[4:5], jnp.zeros((1, D), F32), vec[5:6]], axis=1)

    @pl.loop(0, 4)
    def _(t):
        rows = pl.ds(pl.multiple_of(t * 256, 256), 256)
        qkv[rows, :] = (nn(wn[rows, :], w_in[...]) + in_bias).astype(BF)

    masks = head_masks()

    @pl.loop(0, WINDOWS // 8)
    def _(wo):
        units = [(i, g) for i in range(8) for g in range(QUADS)]
        rows = [pl.ds(pl.multiple_of((wo * 8 + i) * WROWS, WROWS), WROWS) for i in range(8)]
        allow = []
        for i in range(8):
            one = mask[wo * 8 + i] > 0.0
            allow.append(jnp.concatenate([one, one], axis=1))
        scores = []
        for i, g in units:
            q4 = stack_heads(qkv[rows[i], g * LANES : (g + 1) * LANES], masks)
            scores.append(nt(qkv[rows[i], D + g * LANES : D + (g + 1) * LANES], q4))
        probs = []
        for (i, g), s in zip(units, scores):
            s = jnp.where(allow[i], s * SCALE + bias[g], -1e30)
            e = jnp.exp(s - jnp.max(s, axis=0, keepdims=True))
            a = (e * (1.0 / jnp.sum(e, axis=0, keepdims=True))).astype(BF)
            attn[(wo * 8 + i) * QUADS + g] = a
            probs.append(a)
        tall = [tn(a, qkv[rows[i], 2 * D + g * LANES : 2 * D + (g + 1) * LANES]) for (i, g), a in zip(units, probs)]
        for (i, g), t in zip(units, tall):
            t = fold_heads(t, masks)
            windows[rows[i], g * LANES : (g + 1) * LANES] = t
            mixed[rows[i], g * LANES : (g + 1) * LANES] = t.astype(BF)

    to_patches(windows, patches, shifted)
    h_one[...] = hid[...].astype(F32) + nn(patches[...].astype(BF), w_out[...]) + vec[6:7]


def attn_fwd(shifted, hid, vec, w_in, w_out, bias, mask, deps=()):
    return call(
        functools.partial(attn_fwd_body, shifted),
        (
            sds((CELLS, D), F32),
            sds((WTOK, D), BF),
            sds((WTOK, 3 * D), BF),
            sds((WTOK, D), BF),
            sds((WINDOWS * QUADS, WROWS, PAIR), BF),
        ),
        6,
        scratch=[PATCHES, PADDED],
        us=8,
        deps=deps,
    )(hid, vec, w_in, w_out, bias, mask)


def moe_fwd_body(
    h_one, vec, w1, w2, b1, router, router_bias, place_col, place_row,
    out, normed_two, disp, act, slope, picked, gap_out, rows_out, onehot, onehot_t,
):
    fill_onehot(onehot, place_col)
    fill_onehot_t(onehot_t, place_row)
    normal, _ = normalize(h_one[...])
    two = (normal * vec[2:3] + vec[3:4]).astype(BF)
    normed_two[...] = two
    logits = nn(two, router[...])
    gap = (logits[:, LANES:] + router_bias[1:2]) - (logits[:, :LANES] + router_bias[0:1])
    gap = jnp.where(place_col[...] >= SLOTS // 2, gap, -gap)
    gap_out[...] = gap
    gate = 1.0 / (1.0 + jnp.exp(-gap))
    disp[...] = nn(onehot_t[...], two).astype(BF)

    @pl.loop(0, 4, unroll=4)
    def _(t):
        rows = pl.ds(pl.multiple_of(t * 256, 256), 256)
        e = t // 2
        own = disp[rows, :]
        for c in range(3):
            cols = slice(c * 512, (c + 1) * 512)
            pre = nn(own, w1[e, :, cols]) + b1[pl.ds(e, 1), cols]
            phi = 0.5 * (1.0 + lax.erf(pre * 0.7071067811865476))
            act[rows, cols] = (pre * phi).astype(BF)
            slope[rows, cols] = (
                phi + pre * jnp.exp(-0.5 * pre * pre) * 0.3989422804014327
            ).astype(BF)
        rows_out[rows, :] = (nn(act[rows, :], w2[e]) + vec[pl.ds(7 + e, 1)]).astype(BF)

    taken = nn(onehot[...], rows_out[...])
    picked[...] = taken.astype(BF)
    for c in range(3):
        cols = slice(c * LANES, (c + 1) * LANES)
        out[:, cols] = (h_one[:, cols] + gate * taken[:, cols]).astype(out.dtype)


def moe_fwd(h_one, vec, w1, w2, b1, router, router_bias, place, out_dtype, deps=()):
    return call(
        moe_fwd_body,
        (
            sds((CELLS, D), out_dtype),
            sds((CELLS, D), BF),
            sds((SLOTS, D), BF),
            sds((SLOTS, F), BF),
            sds((SLOTS, F), BF),
            sds((CELLS, D), BF),
            sds((CELLS, LANES), F32),
        ),
        9,
        scratch=[pltpu.VMEM((SLOTS, D), BF), ONEHOT, ONEHOT_T],
        us=9.5,
        deps=deps,
    )(h_one, vec, w1, w2, b1, router, router_bias, *place)


def fill_onehot(onehot, place_col):
    @pl.loop(0, 7)
    def _(t):
        rows = pl.ds(pl.multiple_of(t * 112, 112), 112)
        place = jnp.concatenate([place_col[rows, :]] * 8, axis=1)
        same = place == lax.broadcasted_iota(jnp.int32, (112, SLOTS), 1)
        onehot[rows, :] = jnp.where(same, 1.0, 0.0).astype(BF)


def fill_onehot_t(onehot_t, place_row):
    @pl.loop(0, 8)
    def _(t):
        row = lax.broadcasted_iota(jnp.int32, (128, CELLS), 0) + t * 128
        same = row == place_row[0:1, :]
        onehot_t[pl.ds(pl.multiple_of(t * 128, 128), 128), :] = jnp.where(same, 1.0, 0.0).astype(BF)


def moe_bwd_body(
    grad, w2, place_col, place_row, disp, act, slope, picked, gap,
    dw1, dw2, db1, small, g_pre, gate_grad, g_rows, onehot_t,
):
    fill_onehot_t(onehot_t, place_row)
    go = grad[...].astype(F32)
    gate = 1.0 / (1.0 + jnp.exp(-gap[...]))
    other = 1.0 / (1.0 + jnp.exp(gap[...]))
    g_picked = (go * jnp.concatenate([gate] * 3, axis=1)).astype(BF)
    g_gate = jnp.sum(go * picked[...].astype(F32), axis=-1, keepdims=True)
    sign = jnp.where(place_col[...] >= SLOTS // 2, 1.0, -1.0)
    gl = (g_gate * gate * other * sign).astype(BF)
    gate_grad[...] = gl
    small[...] = jnp.zeros((16, D), F32)
    small[9:10, 0:LANES] = jnp.sum(gl.astype(F32), axis=0, keepdims=True)
    g_rows[...] = nn(onehot_t[...], g_picked).astype(BF)

    @pl.loop(0, EXPERTS, unroll=2)
    def _(e):
        both = pl.ds(pl.multiple_of(e * 512, 512), 512)
        own = g_rows[both, :]
        total = []
        grads = [nt(own, w2[e, c * 256 : (c + 1) * 256, :]) for c in range(6)]
        for c, part in enumerate(grads):
            cols = slice(c * 256, (c + 1) * 256)
            gp = (part * slope[both, cols].astype(F32)).astype(BF)
            g_pre[both, cols] = gp
            total.append(jnp.sum(gp.astype(F32), axis=0, keepdims=True))
        db1[pl.ds(e, 1), :] = jnp.concatenate(total, axis=1)
        small[pl.ds(7 + e, 1), :] = jnp.sum(own.astype(F32), axis=0, keepdims=True)
        for c in range(6):
            cols = slice(c * 256, (c + 1) * 256)
            dw1[e, :, cols] = tn(disp[both, :], g_pre[both, cols])
            dw2[e, cols, :] = tn(act[both, cols], own)


def moe_bwd(grad, w2, place, saved):
    return call(
        moe_bwd_body,
        (
            sds((EXPERTS, D, F), F32),
            sds((EXPERTS, F, D), F32),
            sds((8, F), F32),
            sds((16, D), F32),
            sds((SLOTS, F), BF),
            sds((CELLS, LANES), BF),
        ),
        9,
        scratch=[pltpu.VMEM((SLOTS, D), BF), ONEHOT_T],
        us=8,
    )(grad, w2, *place, *saved)


def middle_bwd_body(
    shifted, grad, h_one, vec, w1, w_out, place_col, normed_two, g_pre, gate_grad, mixed,
    grad_one, g_mix, dw_out, drouter, small, onehot, g_disp, windows_of,
):
    fill_onehot(onehot, place_col)
    for e in range(EXPERTS):
        both = slice(e * 512, (e + 1) * 512)
        g_disp[both, :] = nt(g_pre[both, :], w1[e]).astype(BF)
    gl = gate_grad[...].astype(F32)
    g_two = nn(onehot[...], g_disp[...]) + jnp.concatenate([gl] * 3, axis=1) * vec[9:10]
    drouter[...] = tn(gate_grad[...], normed_two[...])[0:8]
    normal, inverse = normalize(h_one[...])
    small[...] = jnp.zeros((16, D), F32)
    small[2:3] = jnp.sum(g_two * normal, axis=0, keepdims=True)
    small[3:4] = jnp.sum(g_two, axis=0, keepdims=True)
    grad_one[...] = grad[...].astype(F32) + norm_backward(g_two, normal, inverse, vec[2:3])
    small[6:7] = jnp.sum(grad_one[...].astype(BF).astype(F32), axis=0, keepdims=True)
    to_windows(grad_one, windows_of, shifted)
    gao_w = windows_of[...].astype(BF)
    dw_out[...] = tn(mixed[...], gao_w)
    g_mix[...] = nt(gao_w, w_out[...]).astype(BF)


def middle_bwd(shifted, grad, h_one, vec, w1, w_out, place_col, normed_two, g_pre, gate_grad, mixed):
    return call(
        functools.partial(middle_bwd_body, shifted),
        (
            sds((CELLS, D), F32),
            sds((WTOK, D), BF),
            sds((D, D), F32),
            sds((8, D), F32),
            sds((16, D), F32),
        ),
        10,
        scratch=[ONEHOT, pltpu.VMEM((SLOTS, D), BF), PADDED],
        us=5,
    )(grad, h_one, vec, w1, w_out, place_col, normed_two, g_pre, gate_grad, mixed)


def attn_bwd_windows(windows, qkv, g_mix, attn, g_qkv, dbias, base=None):
    masks = head_masks()
    base = windows[0] if base is None else base

    start, stop = windows
    per = min(4, stop - start)

    @pl.loop(0, (stop - start) // per)
    def _(wo):
        units = [(i, g) for i in range(per) for g in range(QUADS)]
        first = [start + wo * per + i for i in range(per)]
        rows = [pl.ds(pl.multiple_of(w * WROWS, WROWS), WROWS) for w in first]
        outs = [pl.ds(pl.multiple_of((w - base) * WROWS, WROWS), WROWS) for w in first]
        cols = [[slice(n * D + g * LANES, n * D + (g + 1) * LANES) for g in range(QUADS)] for n in range(3)]
        d4s = [stack_heads(g_mix[rows[i], cols[0][g]], masks) for i, g in units]
        grads = [nt(qkv[rows[i], cols[2][g]], d4) for (i, g), d4 in zip(units, d4s)]
        probs = [attn[first[i] * QUADS + g] for i, g in units]
        for (i, g), a, d4 in zip(units, probs, d4s):
            g_qkv[outs[i], cols[2][g]] = nn(a, d4).astype(BF)
        dss = []
        for a, grad in zip(probs, grads):
            a = a.astype(F32)
            t = a * grad
            dss.append((t - a * jnp.sum(t, axis=0, keepdims=True)).astype(BF))
        for g in range(QUADS):
            total = dbias[g]
            for (_, other), ds in zip(units, dss):
                if other == g:
                    total = total + ds.astype(F32)
            dbias[g] = total
        talls = [tn(ds, qkv[rows[i], cols[1][g]]) for (i, g), ds in zip(units, dss)]
        for (i, g), ds in zip(units, dss):
            q4 = stack_heads(qkv[rows[i], cols[0][g]], masks)
            g_qkv[outs[i], cols[1][g]] = (nn(ds, q4) * SCALE).astype(BF)
        for (i, g), tall in zip(units, talls):
            g_qkv[outs[i], cols[0][g]] = (fold_heads(tall, masks) * SCALE).astype(BF)


def attn_bwd_body(qkv, attn, g_mix, g_qkv, dbias):
    dbias[...] = jnp.zeros_like(dbias)
    attn_bwd_windows((0, WINDOWS), qkv, g_mix, attn, g_qkv, dbias)


def attn_bwd(qkv, attn, g_mix):
    return call(attn_bwd_body, (sds((WTOK, 3 * D), BF), sds((QUADS, WROWS, PAIR), F32)), 3, us=5)(qkv, attn, g_mix)


def proj_bwd_body(
    shifted, grad_one, hid, vec, w_in, wn, g_qkv, grad_in, dw_in, small, patches, windows_of,
):
    for c in range(3):
        cols = slice(c * D, (c + 1) * D)
        dw_in[:, cols] = tn(wn[...], g_qkv[:, cols])
    windows_of[...] = nt(g_qkv[...], w_in[...])
    to_patches(windows_of, patches, shifted)
    g_normed = patches[...]
    normal, inverse = normalize(hid[...].astype(F32))
    small[...] = jnp.zeros((16, D), F32)
    small[0:1] = jnp.sum(g_normed * normal, axis=0, keepdims=True)
    small[1:2] = jnp.sum(g_normed, axis=0, keepdims=True)
    small[4:5] = jnp.sum(g_qkv[:, :D].astype(F32), axis=0, keepdims=True)
    small[5:6] = jnp.sum(g_qkv[:, 2 * D :].astype(F32), axis=0, keepdims=True)
    grad_in[...] = grad_one[...] + norm_backward(g_normed, normal, inverse, vec[0:1])


def proj_bwd(shifted, grad_one, hid, vec, w_in, wn, g_qkv):
    return call(
        functools.partial(proj_bwd_body, shifted),
        (sds((CELLS, D), F32), sds((D, 3 * D), F32), sds((16, D), F32)),
        6,
        scratch=[PATCHES, PADDED],
        us=0.5,
    )(grad_one, hid, vec, w_in, wn, g_qkv)


def window_perm_t(shifted):
    source = patch_of(jnp.arange(WTOK, dtype=jnp.int32), shifted)
    return (jnp.arange(CELLS, dtype=jnp.int32)[:, None] == source[None, :]).astype(BF)


def wrap_codes(shifted):
    code = np.zeros((CELLS,), np.float32)
    if shifted:
        for r in range(SIDE):
            for s in range(SIDE):
                rr, ss = (r - SHIFT) % SIDE, (s - SHIFT) % SIDE
                code[r * SIDE + s] = 2 * (rr >= SIDE - SHIFT) + (ss >= SIDE - SHIFT)
    return code


def window_masks(items, shifted):
    labels = items.astype(F32)
    if shifted:
        labels = labels * 4.0 + jnp.asarray(wrap_codes(True))
    placed = nn(jnp.broadcast_to((labels + 1.0).astype(BF), (8, CELLS)), window_perm_t(shifted))[0]
    placed = placed.reshape(WINDOWS, WROWS)
    same = (placed[:, :, None] == placed[:, None, :]) & (placed[:, :, None] > 0.0)
    same = same.astype(F32)
    return jnp.concatenate([same, same], axis=2)


def slot_places(routes, slots):
    group = (jnp.arange(CELLS, dtype=jnp.int32) // GROUP) * CAP
    place = routes * (2 * CAP) + group + slots
    return jnp.broadcast_to(place[:, None], (CELLS, LANES)), jnp.broadcast_to(place[None, :], (8, CELLS))

LEAD = 73
SMALL = 9326
LAG = LEAD * LANES - SMALL
VECTORS = 9
LINES = 32
SPANS = ((LEAD, D, 9), (LEAD + 3456, D, 3), (LEAD + 4608, 2 * D, 12), (LEAD + 4608 + 9216, 2 * F, 3))
EDGE = LEAD + 4608
ALIGNED = LEAD + 4608 + 2 * 9216


def relative(k, bits):
    total = 0
    for place, bit in enumerate(bits):
        total = total + (((k >> (len(bits) - 1 - place)) & 1) << bit)
    return total


def lanes_of(count=LANES):
    return lax.broadcasted_iota(jnp.int32, (1, count), 1)


def equal(rows, columns):
    return jnp.where(rows == columns, 1.0, 0.0).astype(BF)


def spread(shape):
    return lax.broadcasted_iota(jnp.int32, shape, 0), lax.broadcasted_iota(jnp.int32, shape, 1)


def exact(left, one, product):
    high = left.astype(BF)
    low = (left - high.astype(F32)).astype(BF)
    return product(high, one) + product(low, one)


def head_major():
    f, g = spread((D, D))
    return equal(f, 12 * (g & 31) + (g >> 5))


def head_rows(m):
    f, g = spread((D, 2 * LANES))
    return equal((f & 31) + 32 * m, g)


def offset_lanes():
    f, g = spread((LANES, LANES))
    i = g & 63
    r = (i * 37) >> 8
    return equal(f, jnp.where(i < WIN * WIN, 13 * r + i - WIN * r, -1))


def turns():
    return [13 * (6 - j // WIN) + 6 - j % WIN for j in range(WIN * WIN)]


def unpack_bias(flat, wide, tall, bias):
    wide[...] = jnp.zeros_like(wide)
    for m in range(6):
        for c in range(3):
            wide[m : m + 1, c * LANES : (c + 1) * LANES] = flat[12 + 3 * m + c : 13 + 3 * m + c, :]
    by_head = nn(wide[...].astype(BF), head_major())
    sub = lax.broadcasted_iota(jnp.int32, (16, D), 0)
    own = (lanes_of(D) >> 5) == sub
    table = jnp.zeros((16, 2 * LANES), F32)
    for m in range(6):
        table = table + nn(jnp.where(own, by_head[m : m + 1], 0.0).astype(BF), head_rows(m))
    tall[...] = jnp.zeros_like(tall)
    for j, turn in enumerate(turns()):
        row = pltpu.roll(table, (2 * LANES - turn) % (2 * LANES), 1)[:, :LANES]
        tall[pl.ds(j, 16, stride=WROWS), :] = row
    tall[...] = nn(tall[...].astype(BF), offset_lanes())
    for g in range(QUADS):
        for t in range(2):
            h = 4 * g + 2 * t
            left, right = tall[h * WROWS : (h + 1) * WROWS], tall[(h + 1) * WROWS : (h + 2) * WROWS]
            bias[g, :, t * LANES : (t + 1) * LANES] = jnp.where(lanes_of() < WROWS, left, right)


def unpack_small(flat, rows, wide, tall, vec, b1, router, router_bias, bias):
    def shifted(first, count, by):
        near, far = flat[first : first + count, :], flat[first + 1 : first + 1 + count, :]
        return pltpu.roll(jnp.where(lanes_of() >= by, near, far), LANES - by, 1)

    rows[0:16, :] = shifted(27, 16, 108)
    rows[16:46, :] = shifted(42, 30, 110)
    vec[...] = jnp.zeros_like(vec)
    b1[...] = jnp.zeros_like(b1)
    for c in range(3):
        cols = slice(c * LANES, (c + 1) * LANES)
        for n in range(4):
            vec[n : n + 1, cols] = flat[3 * n + c : 3 * n + c + 1, :]
        for n in range(3):
            vec[4 + n : 5 + n, cols] = rows[3 * n + c : 3 * n + c + 1, :]
        for e in range(EXPERTS):
            vec[7 + e : 8 + e, cols] = rows[40 + 3 * e + c : 41 + 3 * e + c, :]
    for e in range(EXPERTS):
        for c in range(12):
            b1[e : e + 1, c * LANES : (c + 1) * LANES] = rows[16 + 12 * e + c : 17 + 12 * e + c, :]
        one = jnp.sum(jnp.where(lanes_of() == e, rows[15:16, :], 0.0), axis=1, keepdims=True)
        router_bias[e : e + 1, :] = jnp.broadcast_to(one, (1, LANES))
    pairs = jnp.concatenate([rows[9 + c : 10 + c, :] for c in range(6)], axis=1)
    pairs = jnp.broadcast_to(pairs, (LANES, 2 * D)).astype(BF)
    d, f = spread((D, 2 * D))
    for e in range(EXPERTS):
        router[:, e * LANES : (e + 1) * LANES] = nt(equal(f, 2 * d + e), pairs).astype(BF)
    gap = nt(pairs[0:16], equal(f, 2 * d + 1)) - nt(pairs[0:16], equal(f, 2 * d))
    vec[9:10, :] = gap[0:1]
    unpack_bias(flat, wide, tall, bias)


def unpack_matrices(flat, spans, outs, skipped):
    for (base, height, tiles), out in zip(spans, outs):
        step = 128

        @pl.loop(0, height // step, unroll=min(6, height // step))
        def _(t, base=base, tiles=tiles, out=out):
            first = base - 1 - skipped + t * (step * tiles)
            before = flat[pl.ds(first, step, stride=tiles), :]
            for j in range(tiles):
                here = flat[pl.ds(first + 1 + j, step, stride=tiles), :]
                tile = pltpu.roll(jnp.where(lanes_of() >= LANES - LAG, before, here), LAG, 1)
                out[pl.ds(pl.multiple_of(t * step, step), step), j * LANES : (j + 1) * LANES] = tile.astype(BF)
                before = here


def unpack_head_body(rows, runs, me, *refs):
    got = refs[: len(runs)]
    w_in, w_out, rest, vec, b1, router, router_bias, bias, flat, few, wide, tall = refs[len(runs) :]
    for (bits, fixed), part in zip(runs, got):
        n, half = 1 << len(bits), part.shape[1]

        @pl.loop(0, n)
        def _(k, bits=bits, fixed=fixed, part=part, n=n, half=half):
            d = me[1] ^ (relative(k, bits) + fixed)
            flat[pl.ds(d * rows, half), :] = part[k].astype(F32)
            flat[pl.ds(d * rows + half, rows - half), :] = part[n + k, : rows - half, :].astype(F32)

    unpack_small(flat, few, wide, tall, vec, b1, router, router_bias, bias)
    unpack_matrices(flat, SPANS[:2], (w_in, w_out), 0)
    rest[...] = flat[EDGE - 1 : EDGE - 1 + rest.shape[0], :]


def unpack_tail_body(rows, heads, runs, me, rest, *refs):
    got = refs[: len(runs)]
    w1, w2, flat = refs[len(runs) :]
    flat[0 : rest.shape[0], :] = rest[...]
    for (outer, inner, fixed, upper, skip), part in zip(runs, got):
        count = 1 << len(inner)
        half = part.shape[1]
        first = half if upper else 0
        used = min(half, rows - first)

        @pl.loop(0, 3 * count << len(outer), unroll=3)
        def _(k, outer=outer, inner=inner, fixed=fixed, part=part, count=count, first=first, used=used, skip=skip):
            own = (relative(k // (3 * count), outer) + relative(k % count, inner) + fixed) ^ me[1]
            d = ((k // count) % 3 + 1) * heads + own
            flat[pl.ds(d * rows + first - (EDGE - 1), used), :] = part[skip + k, :used, :].astype(F32)

    unpack_matrices(flat, SPANS[2:], (w1, w2), EDGE - 1)


class Weights(NamedTuple):
    w_in: Any
    w_out: Any
    w1: Any
    w2: Any
    vec: Any
    b1: Any
    router: Any
    router_bias: Any
    bias: Any


SMALL_SHAPES = (
    sds((16, D), F32),
    sds((8, F), F32),
    sds((D, 2 * LANES), BF),
    sds((8, LANES), F32),
    sds((QUADS, WROWS, PAIR), F32),
)
SMALL_SCRATCH = [pltpu.VMEM((48, LANES), F32), pltpu.VMEM((8, D), F32), pltpu.VMEM((16 * WROWS, LANES), F32)]
HEAD_SHAPES = (sds((D, 3 * D), BF), sds((D, D), BF))
TAIL_SHAPES = (sds((2 * D, F), BF), sds((2 * F, D), BF))


def experts(w1, w2):
    return w1.reshape(EXPERTS, D, F), w2.reshape(EXPERTS, F, D)


def unpack_head(me, parts, runs, rows, devices):
    heads = devices // 4
    w_in, w_out, rest, *small = call(
        functools.partial(unpack_head_body, rows, runs),
        HEAD_SHAPES + (sds((heads * rows - EDGE + 1, LANES), F32),) + SMALL_SHAPES,
        1 + len(parts),
        scratch=[pltpu.VMEM((heads * rows + 8, LANES), F32)] + SMALL_SCRATCH,
        smem=1,
        us=4,
    )(me, *parts)
    return Weights(w_in, w_out, None, None, *small), rest


def unpack_tail(me, rest, parts, runs, rows, devices):
    return experts(
        *call(
            functools.partial(unpack_tail_body, rows, devices // 4, runs),
            TAIL_SHAPES,
            2 + len(parts),
            scratch=[pltpu.VMEM((devices * rows - EDGE + 9, LANES), F32)],
            smem=1,
            vmem=BIG_VMEM,
            us=4,
        )(me, rest, *parts)
    )


def pack_bias(dbias, wide, tall):
    tall[HEADS * WROWS :, :] = jnp.zeros((4 * WROWS, LANES), F32)
    for h in range(HEADS):
        g, t, side = h // 4, (h % 4) // 2, h % 2
        tile = dbias[g, :, t * LANES : (t + 1) * LANES]
        tall[h * WROWS : (h + 1) * WROWS, :] = jnp.where((lanes_of() >> 6) == side, tile, 0.0)
    used = HEADS * WROWS
    tall[0:used, :] = exact(tall[0:used, :], offset_lanes(), nt)
    table = jnp.zeros((16, 2 * LANES), F32)
    for j, turn in enumerate(turns()):
        row = tall[pl.ds(j, 16, stride=WROWS), :]
        table = table + pltpu.roll(jnp.concatenate([row, jnp.zeros_like(row)], axis=1), turn, 1)
    sub = lax.broadcasted_iota(jnp.int32, (16, D), 0)
    own = (lanes_of(D) >> 5) == sub
    wide[...] = jnp.zeros_like(wide)
    for m in range(6):
        placed = jnp.where(own, exact(table, head_rows(m), nt), 0.0)
        wide[m : m + 1, :] = jnp.sum(placed, axis=0, keepdims=True)
    wide[...] = exact(wide[...], head_major(), nt)


def pack_small(al, vectors, drouter, db1, dbias, one, two, wide, tall):
    one[...] = jnp.zeros_like(one)
    two[...] = jnp.zeros_like(two)
    pack_bias(dbias, wide, tall)
    d, f = spread((D, 2 * D))
    signs = equal(f, 2 * d + 1) - equal(f, 2 * d)
    pairs = exact(drouter[...], signs, nn)
    for c in range(3):
        cols = slice(c * LANES, (c + 1) * LANES)
        for n in range(4):
            one[1 + 3 * n + c : 2 + 3 * n + c, :] = vectors[n : n + 1, cols]
        for m in range(6):
            one[13 + 3 * m + c : 14 + 3 * m + c, :] = wide[m : m + 1, cols]
        for n in range(3):
            two[1 + 3 * n + c : 2 + 3 * n + c, :] = vectors[4 + n : 5 + n, cols]
        for e in range(EXPERTS):
            al[67 + 3 * e + c : 68 + 3 * e + c, :] = vectors[7 + e : 8 + e, cols]
    for c in range(6):
        two[10 + c : 11 + c, :] = pairs[0:1, c * LANES : (c + 1) * LANES]
    total = vectors[9:10, 0:LANES]
    two[16:17, :] = jnp.where(lanes_of() == 0, -total, jnp.where(lanes_of() == 1, total, 0.0))
    for e in range(EXPERTS):
        for c in range(12):
            al[43 + 12 * e + c : 44 + 12 * e + c, :] = db1[e : e + 1, c * LANES : (c + 1) * LANES]
    first = pltpu.roll(jnp.where(lanes_of() >= LANES - 18, one[0:28, :], one[1:29, :]), 18, 1)
    second = pltpu.roll(jnp.where(lanes_of() >= LANES - 126, two[0:16, :], two[1:17, :]), 126, 1)
    al[27:43, :] = second
    al[0:27, :] = first[0:27]
    al[27:28, :] += first[27:28]


def pack_matrices(al, spans, grads, skipped):
    for (base, height, tiles), grad in zip(spans, grads):
        step = 128

        @pl.loop(0, height // step, unroll=min(6, height // step))
        def _(t, base=base, tiles=tiles, grad=grad):
            first = base - skipped + t * (step * tiles)
            own = pl.ds(pl.multiple_of(t * step, step), step)
            for j in range(tiles):
                al[pl.ds(first + j, step, stride=tiles), :] = grad[own, j * LANES : (j + 1) * LANES]


def clear(al, first):
    al[pl.ds(first, al.shape[0] - first), :] = jnp.zeros((al.shape[0] - first, LANES), F32)


def pack_head_body(
    rows, padded, runs, me, moe, attn, proj, drouter, db1, dbias, dw_in, dw_out, rest,
    keep, send, al, vectors, lines, one, two, wide, tall,
):
    vectors[...] = moe[...] + attn[...] + proj[...]
    lines[...] = jnp.zeros_like(lines)
    for n in range(VECTORS):
        for c in range(3):
            lines[3 * n + c : 3 * n + c + 1, :] = vectors[n : n + 1, c * LANES : (c + 1) * LANES]
    pack_small(al, vectors, drouter, db1, dbias, one, two, wide, tall)
    pack_matrices(al, SPANS[:2], (dw_in, dw_out), 0)
    al[EDGE : EDGE + rest.shape[0], :] = rest[...]
    at = 0
    for bits, fixed in runs:
        for other, out in enumerate((keep, send)):

            @pl.loop(0, 1 << len(bits))
            def _(k, bits=bits, fixed=fixed, at=at, other=other, out=out):
                d = me[1] ^ (relative(k, bits) + fixed + other)
                out[at + k, :padded, :] = al[pl.ds(d * rows, padded), :].astype(BF)
                out[at + k, padded:, :] = lines[...].astype(BF)

        at += 1 << len(bits)


def pack_tail_body(rows, padded, heads, runs, me, dw1, dw2, keep, send, rest, al):
    clear(al, ALIGNED - EDGE)
    pack_matrices(al, SPANS[2:], (dw1, dw2), EDGE)
    rest[...] = al[0 : rest.shape[0], :]
    half = padded // 2
    at = 0
    for outer, inner, fixed, upper in runs:
        count = 1 << len(inner)
        total = 3 * count << len(outer)
        for other, out in enumerate((keep, send)):

            @pl.loop(0, total, unroll=3)
            def _(k, outer=outer, inner=inner, fixed=fixed, upper=upper, count=count, at=at, other=other, out=out):
                own = (relative(k // (3 * count), outer) + relative(k % count, inner) + fixed + other) ^ me[1]
                d = ((k // count) % 3 + 1) * heads + own
                out[at + k] = al[pl.ds(d * rows + (half if upper else 0) - EDGE, half), :].astype(BF)

        at += total


SMALL_PACK = [
    pltpu.VMEM((40, LANES), F32),
    pltpu.VMEM((24, LANES), F32),
    pltpu.VMEM((8, D), F32),
    pltpu.VMEM((16 * WROWS, LANES), F32),
]


def pack_head(me, small, dw_in, dw_out, rest, runs, rows, devices, padded):
    heads = devices // 4
    shape = sds((heads // 2, padded + LINES, LANES), BF)
    return call(
        functools.partial(pack_head_body, rows, padded, runs),
        (shape, shape),
        10,
        scratch=[
            pltpu.VMEM((EDGE + rest.shape[0], LANES), F32),
            pltpu.VMEM((16, D), F32),
            pltpu.VMEM((LINES, LANES), F32),
        ]
        + SMALL_PACK,
        smem=1,
        us=0.5,
    )(me, *small, dw_in, dw_out, rest)


def pack_tail(me, dw1, dw2, runs, rows, devices, padded):
    heads = devices // 4
    shape = sds((3 * heads, padded // 2, LANES), BF)
    over = -(-(heads * rows + padded - EDGE) // 8) * 8
    return call(
        functools.partial(pack_tail_body, rows, padded, heads, runs),
        (shape, shape, sds((over, LANES), F32)),
        3,
        scratch=[pltpu.VMEM((devices * rows + padded - EDGE, LANES), F32)],
        smem=1,
        vmem=BIG_VMEM,
        us=3,
    )(me, dw1.reshape(2 * D, F), dw2.reshape(2 * F, D))


def levels_body(sources, me, *refs):
    pieces, (x, y, head) = refs[: len(refs) - 3], refs[len(refs) - 3 :]
    n, half = head.shape[0] // 2, x.shape[1]
    for level in range(4):
        for step, (at, first) in enumerate(sources):

            @pl.when((me[2] ^ step) == level)
            def _(level=level, at=at, first=first):
                for i in range(n):
                    lower, upper = pieces[at][first * n + i, :half, :], pieces[at][first * n + i, half:, :]
                    if level == 0:
                        for out in (x, y, head):
                            out[i] = lower
                            out[n + i] = upper
                    else:
                        x[(1 + level) * n + i] = lower
                        y[(1 + level) * n + i] = upper


def levels(me, *pieces):
    sources = ((0, 0), (1, 0), (2, 0), (3, 0)) if len(pieces) == 4 else ((0, 0), (1, 0), (0, 1), (1, 1))
    n, padded, _ = pieces[0].shape
    n = n * len(pieces) // 4
    dtype = pieces[0].dtype
    shapes = [sds((count * n, padded // 2, LANES), dtype) for count in (5, 5, 2)]
    return call(functools.partial(levels_body, sources), shapes, 1 + len(pieces), smem=1)(me, *pieces)


def targets_body(with_head, me, a, a_got, b, b_got, *refs):
    *head, keep, send = refs
    n, half = keep.shape[0] // 2, a.shape[1]
    places = {0: (keep, 0), 2: (keep, n), 1: (send, 0), 3: (send, n)}
    for step, (out, first) in places.items():
        level = me[2] ^ step

        @pl.when(level == 0)
        def _(out=out, first=first):
            for i in range(n):
                if with_head:
                    out[first + i] = head[0][i, : 2 * half, :].astype(out.dtype)
                else:
                    out[first + i] = jnp.zeros((2 * half, LANES), out.dtype)

        @pl.when(level > 0)
        def _(out=out, first=first, level=level):
            for i in range(n):
                at = (level - 1) * n + i
                out[first + i, :half, :] = (a[at] + a_got[at].astype(F32)).astype(out.dtype)
                out[first + i, half:, :] = (b[at] + b_got[at].astype(F32)).astype(out.dtype)


def targets(me, a, a_got, b, b_got, *head):
    n, half, _ = a.shape
    n = n // 3
    shape = (2 * n, 2 * half, LANES)
    return call(
        functools.partial(targets_body, bool(head)), (sds(shape, F32), sds(shape, BF)), 5 + len(head), smem=1
    )(me, a, a_got, b, b_got, *head)


def combine_body(plan, count, *refs):
    for (size, _, terms), out in zip(plan, refs[count:]):

        @pl.loop(0, size)
        def _(i, terms=terms, out=out):
            parts = [refs[at][first + i].astype(F32) for at, first in terms]
            while len(parts) > 1:
                parts = [sum(parts[at + 1 : at + 2], parts[at]) for at in range(0, len(parts), 2)]
            out[i] = parts[0].astype(out.dtype)


def combine(plan, *arrays):
    tail = arrays[0].shape[1:]
    shapes = [sds((size, *tail), dtype) for size, dtype, _ in plan]
    return call(functools.partial(combine_body, plan, len(arrays)), shapes, len(arrays))(*arrays)


def finish_body(rows, me, keep, got, upper_keep, upper_got, out):
    def shift(keep, got):
        total = keep[0] + got[0].astype(F32)
        here, below = total[0:rows, :], total[1 : rows + 1, :]
        out[...] = pltpu.roll(jnp.where(lanes_of() >= LAG, here, below), LANES - LAG, 1)

    pl.when(me[2] == 0)(lambda: shift(keep, got))
    pl.when(me[2] != 0)(lambda: shift(upper_keep, upper_got))


def finish(me, rows, lowest, upper):
    parts = (lowest.keep, lowest.got, upper.keep, upper.got)
    return call(functools.partial(finish_body, rows), sds((rows, LANES), F32), 5, smem=1)(me, *parts)


def join_body(skip, a, b, out):
    n = out.shape[0] // 2

    @pl.loop(0, n)
    def _(i):
        out[i] = a[skip + i]
        out[n + i] = b[skip + i]


def join(a, b, skip=0):
    shape = sds((2 * (a.shape[0] - skip), *a.shape[1:]), a.dtype)
    return call(functools.partial(join_body, skip), shape, 2)(a, b)


class Ways(NamedTuple):
    core: Any
    x: Any
    y: Any
    low: Any
    high: Any
    rest: Any


def ways():
    dp, fsdp = (lax.axis_size(axis).bit_length() - 1 for axis in (DP, FSDP))
    rest = [1 << (fsdp + bit) for bit in range(1, dp - 2)] + [1 << bit for bit in range(2, fsdp)]
    return Ways(1, 2, 1 << fsdp, 1 << (fsdp + dp - 2), 1 << (fsdp + dp - 1), rest)


def device_count():
    return lax.axis_size(DP) * lax.axis_size(FSDP)


def flip(array, step):
    return lax.ppermute(array, (DP, FSDP), [(i, i ^ step) for i in range(device_count())])


def move(array, levels):
    width = device_count() // 4
    pairs = [(a * width + i, b * width + i) for a, b in levels.items() for i in range(width)]
    return lax.ppermute(array, (DP, FSDP), pairs)


def tie(arrays, *others):
    if isinstance(arrays, tuple):
        return tuple(tie(array, *others) for array in arrays)
    return lax.optimization_barrier((arrays, *others))[0]


def sync(*arrays):
    return lax.optimization_barrier(arrays)


def bits_of(*steps):
    return [step.bit_length() - 1 for step in steps]


class Gather:
    def __init__(self, own, way, me):
        for extra in way.rest:
            own = join(own, flip(own, extra))
        self.way, self.own, self.me, self.others = way, own, me, None
        self.rest = bits_of(*reversed(way.rest))

    def far(self):
        own, way = self.own, self.way
        self.others = own, flip(own, way.low), flip(own, way.high), flip(own, way.low + way.high)

    def high(self):
        self.other = flip(self.own, self.way.high)

    def low(self):
        self.pair = join(self.own, self.other)
        self.over = flip(self.pair, self.way.low)

    def levels(self):
        pieces = self.others if self.others else (self.pair, self.over)
        self.x, self.y, self.head = levels(self.me, *pieces)

    def near(self):
        way = self.way
        self.got = [flip(self.x, way.x), flip(self.y, way.y), flip(self.head, way.x + way.y)]

    def near_core(self):
        way, core = self.way, self.way.core
        x, y, both = self.got
        sides = [[self.x, x, y, both, self.y]]
        sides.append([flip(part, core) for part in sides[0]])
        self.head_parts, self.head_runs, self.parts, self.runs = [], [], [], []
        for fixed, side in zip((0, core), sides):
            self.head_parts += side[:4]
            self.head_runs += [(self.rest, step + fixed) for step in (0, way.x, way.y, way.x + way.y)]
            x_own, x_got, y_got, _, y_own = side
            self.parts += [x_own, x_got, y_own, y_got]
            skip = 2 << len(self.rest)
            self.runs += [([], self.rest, fixed + step, False, skip) for step in (0, way.x)]
            self.runs += [([], self.rest, fixed + step, True, skip) for step in (0, way.y)]

    def last(self):
        way, skip = self.way, 2 << len(self.rest)
        self.joined = join(self.x, self.got[0], skip), join(self.y, self.got[1], skip)
        self.last_got = flip(self.joined[0], way.y), flip(self.joined[1], way.x)

    def last_core(self):
        way = self.way
        for fixed in (0, way.core):
            self.parts += [flip(part, way.core) for part in self.last_got] if fixed else list(self.last_got)
            self.runs += [(bits_of(way.x), self.rest, way.y + fixed, False, 0)]
            self.runs += [(bits_of(way.y), self.rest, way.x + fixed, True, 0)]


def head_runs(way):
    rest = bits_of(*way.rest)
    return [(rest, step) for step in (way.y, way.x + way.y, way.x, 0)]


def tail_runs(way):
    rest, bx, by = (bits_of(*steps) for steps in (way.rest, [way.x], [way.y]))
    return [
        (bx, rest, way.y, False), ([], rest, way.x, False), ([], rest, 0, False),
        (by, rest, way.x, True), ([], rest, way.y, True), ([], rest, 0, True),
    ]


class HeadScatter:
    def __init__(self, keep, send, way):
        self.way, self.keep, self.n = way, keep, keep.shape[0] // 4
        self.got = flip(send, way.core)

    def plane(self):
        n, way = self.n, self.way
        y, xy, x, self.keep = combine([(n, BF, ((0, i * n), (1, i * n))) for i in range(4)], self.keep, self.got)
        self.got = flip(x, way.x), flip(y, way.y), flip(xy, way.x + way.y)

    def near(self):
        n = 2 * self.n
        sent, self.keep = combine([(n, BF, ((0, i * n), (1, i * n))) for i in range(2)], self.keep, self.got)
        self.got = flip(sent, self.way.y)

    def next(self):
        n = self.n
        sent, self.keep = combine(((n, BF, ((0, 0), (1, n))), (n, BF, ((0, n), (1, 0)))), self.keep, self.got)
        self.got = flip(sent, self.way.x)

    def add(self):
        n, got = self.n, self.got if isinstance(self.got, (tuple, list)) else (self.got,)
        terms = tuple((i, 0) for i in range(1 + len(got)))
        sent, self.keep = combine(((n, BF, terms), (n, F32, terms)), self.keep, *got)
        return sent

    def lines(self):
        return self.keep[0, -LINES : 3 * VECTORS - LINES].reshape(VECTORS, D)

    def low(self, sent):
        self.got = move(sent, {1: 0, 3: 2})

    def high(self):
        self.got = move(self.add(), {2: 0})
        self.keep, self.got = fold(self.keep, self.got, self.way.rest)


class TailScatter:
    def __init__(self, keep, send, way, me):
        self.way, self.keep, self.n, self.me = way, keep, keep.shape[0] // 24, me
        self.got = flip(send, way.core)

    def near(self):
        n = 6 * self.n
        plan = [(n, dtype, ((0, first), (1, first))) for dtype, first in ((BF, 0), (F32, n), (BF, 2 * n), (F32, 3 * n))]
        a, self.a, b, self.b = combine(plan, self.keep, self.got)
        self.a_got, self.b_got = flip(a, self.way.y), flip(b, self.way.x)

    def next(self):
        n = 3 * self.n
        plan = [(n, BF, ((0, 0), (1, n))), (n, F32, ((0, n), (1, 0)))]
        plan += [(n, BF, ((2, 0), (3, n))), (n, F32, ((2, n), (3, 0)))]
        a, self.a, b, self.b = combine(plan, self.a, self.a_got, self.b, self.b_got)
        self.a_got, self.b_got = flip(a, self.way.x), flip(b, self.way.y)

    def low(self, *head):
        self.keep, sent = targets(self.me, self.a, self.a_got, self.b, self.b_got, *head)
        self.got = flip(sent, self.way.low)

    def high(self):
        self.keep, self.got = fold(self.keep, self.got, [self.way.high] + self.way.rest)


def fold(keep, got, steps):
    for way in steps:
        half = keep.shape[0] // 2
        plan = ((half, BF, ((0, half), (1, half))), (half, F32, ((0, 0), (1, 0))))
        sent, keep = combine(plan, keep, got)
        got = flip(sent, way)
    return keep, got


def shards(inputs, items, routes, slots, cotangent, params, momentum, average):
    fsdp, dp = lax.axis_size(FSDP), lax.axis_size(DP)
    devices = fsdp * dp
    share = params.shape[1]
    rows = share // LANES
    padded = -(-(rows + 1) // 32) * 32
    step_rate = RATE_BASE / math.sqrt(CELLS * devices)
    way = ways()
    own = lax.axis_index(DP) * fsdp + lax.axis_index(FSDP)
    me = jnp.stack([own, own % (devices // 4), own // (devices // 4)]).astype(jnp.int32)

    shares = []
    for b in range(BLOCKS):
        share_rows = params[b].astype(BF).reshape(1, rows, LANES)
        shares.append(jnp.pad(share_rows, ((0, 0), (0, padded - rows), (0, 0))))
    one, two = (Gather(rows_own, way, me) for rows_own in shares)
    masks, places = [], []
    for b in range(BLOCKS):
        masks.append(window_masks(items.reshape(CELLS), b % 2 == 1))
        places.append(slot_places(routes[b].reshape(CELLS), slots[b].reshape(CELLS)))

    hidden_zero = inputs.reshape(CELLS, D)
    one.far()
    one.levels()
    one.near()
    two.own = tie(two.own, one.head)
    two.high()
    one.got[0] = tie(one.got[0], *masks)
    two.other, *one.got = sync(two.other, *one.got)
    one.near_core()
    one.last()
    two.low()
    one.head_parts[0] = tie(one.head_parts[0], two.pair, *one.joined, *one.parts)
    w, rest = unpack_head(me, one.head_parts, one.head_runs, rows, devices)
    h_zero, *attn_zero = attn_fwd(False, hidden_zero, w.vec, w.w_in, w.w_out, w.bias, masks[0])
    h_zero, two.over = sync(h_zero, two.over)
    two.levels()
    two.near()
    one.last_got = tie(one.last_got, two.head)
    one.last_core()
    w1, w2 = unpack_tail(me, tie(rest, two.head), one.parts, one.runs, rows, devices)
    w_zero = w._replace(w1=w1, w2=w2)
    w = w_zero
    hidden_one, *moe_zero = moe_fwd(h_zero, w.vec, w.w1, w.w2, w.b1, w.router, w.router_bias, places[0], F32)

    hidden_one, *two.got = sync(hidden_one, *two.got)
    two.near_core()
    two.last()
    two.head_parts[0] = tie(two.head_parts[0], *two.joined, *two.parts)
    w, rest = unpack_head(me, two.head_parts, two.head_runs, rows, devices)
    h_one, *attn_one = attn_fwd(True, hidden_one, w.vec, w.w_in, w.w_out, w.bias, masks[1])
    h_one, *two.last_got = sync(h_one, *two.last_got)
    two.last_core()
    w1, w2 = unpack_tail(me, rest, two.parts, two.runs, rows, devices)
    w_one = w._replace(w1=w1, w2=w2)
    w = w_one
    outputs, *moe_one = moe_fwd(h_one, w.vec, w.w1, w.w2, w.b1, w.router, w.router_bias, places[1], BF)

    gradient = cotangent.reshape(CELLS, D)
    wn, qkv, mixed, attn = attn_one
    normed_two, *saved = moe_one
    dw1, dw2, db1, small_moe, g_pre, gate_grad = moe_bwd(gradient, w.w2, places[1], saved)
    keep, send, rest = pack_tail(me, dw1, dw2, tail_runs(way), rows, devices, padded)
    tail_one = TailScatter(keep, send, way, me)
    g_one, g_mix, dw_out, drouter, small_mid = middle_bwd(
        True, gradient, h_one, w.vec, w.w1, w.w_out, places[1][0], normed_two, tie(g_pre, send), gate_grad, mixed
    )
    g_mix, tail_one.got = sync(g_mix, tail_one.got)
    tail_one.near()
    g_qkv, dbias = attn_bwd(qkv, attn, tie(g_mix, tail_one.a))
    gradient, dw_in, small_attn = proj_bwd(True, g_one, hidden_one, w.vec, w.w_in, wn, g_qkv)
    small = (small_moe, small_mid, small_attn, drouter, db1, dbias)
    keep, send = pack_head(me, small, dw_in, dw_out, rest, head_runs(way), rows, devices, padded)
    send, tail_one.a_got, tail_one.b_got, gradient = sync(send, tail_one.a_got, tail_one.b_got, gradient)
    head_one = HeadScatter(keep, send, way)
    tail_one.next()

    w = w_zero
    wn, qkv, mixed, attn = attn_zero
    normed_two, *saved = moe_zero
    gradient = tie(gradient, tail_one.a)
    dw1, dw2, db1, small_moe, g_pre, gate_grad = moe_bwd(gradient, w.w2, places[0], saved)
    g_pre, dw2, head_one.got, tail_one.a_got, tail_one.b_got = sync(
        g_pre, dw2, head_one.got, tail_one.a_got, tail_one.b_got
    )
    head_one.near()
    tail_one.low()
    keep, send, rest = pack_tail(me, dw1, tie(dw2, head_one.keep, tail_one.keep), tail_runs(way), rows, devices, padded)
    tail_zero = TailScatter(keep, send, way, me)
    g_one, g_mix, dw_out, drouter, small_mid = middle_bwd(
        False, gradient, h_zero, w.vec, w.w1, w.w_out, places[0][0], normed_two, tie(g_pre, send), gate_grad, mixed
    )
    g_mix, tail_zero.got = sync(g_mix, tail_zero.got)
    tail_zero.near()
    g_qkv, dbias = attn_bwd(qkv, attn, tie(g_mix, tail_zero.a))
    g_qkv, tail_one.got, head_one.got = sync(g_qkv, tail_one.got, head_one.got)
    head_one.next()
    tail_one.high()
    gradient, dw_in, small_attn = proj_bwd(
        False, tie(g_one, head_one.keep, tail_one.keep), hidden_zero, w.vec, w.w_in, wn, g_qkv
    )
    small = (small_moe, small_mid, small_attn, drouter, db1, dbias)
    keep, send = pack_head(me, small, dw_in, dw_out, rest, head_runs(way), rows, devices, padded)
    send, tail_zero.a_got, tail_zero.b_got, head_one.got, tail_one.got = sync(
        send, tail_zero.a_got, tail_zero.b_got, head_one.got, tail_one.got
    )

    head_zero = HeadScatter(keep, send, way)
    tail_zero.next()
    head_zero.plane()
    head_one.add()
    tail_zero.low(head_one.keep)
    sent = head_zero.add()
    head_zero.low(sent)
    vector_grads = jnp.stack([head_zero.lines(), head_one.lines()])
    got = flip(vector_grads, way.low)
    tail_zero.high()
    vector_grads = vector_grads + got
    head_zero.keep = tie(head_zero.keep, vector_grads)
    head_zero.high()
    for step in [way.high] + way.rest:
        vector_grads = vector_grads + flip(vector_grads, step)
    grads_zero = finish(me, rows, head_zero, tail_zero)
    grads_one = finish(me, rows, tail_zero, tail_one)
    grad_all = jnp.stack([grads_zero.reshape(-1), grads_one.reshape(-1)])
    new_momentum = MOMENTUM_DECAY * momentum + grad_all
    new_params = params - step_rate * (grad_all + MOMENTUM_DECAY * new_momentum)
    new_average = AVERAGE_DECAY * average + (1.0 - AVERAGE_DECAY) * new_params
    return (
        outputs.reshape(1, CELLS, D),
        gradient.reshape(1, CELLS, D),
        new_params,
        new_momentum,
        new_average,
        vector_grads,
    )


def solution(mesh):
    both = (DP, FSDP)
    canvas, vector = P(both), P(None, both)
    return jax.shard_map(
        shards,
        mesh=mesh,
        in_specs=(canvas, canvas, vector, vector, canvas, vector, vector, vector),
        out_specs=(canvas, canvas, vector, vector, vector, P()),
        check_vma=False,
    )
```

```python
import functools
import math
from typing import Any, NamedTuple

import jax
import jax.numpy as jnp
import numpy as np
from jax import lax
from jax.experimental import pallas as pl
from jax.experimental.pallas import tpu as pltpu
from jax.sharding import PartitionSpec as P

D = 384
HEADS = 12
F = 1536
HEAD_DIM = 32
EXPERTS = 2
CAP = 256
SIDE = 28
WIN = 7
SHIFT = 3
BLOCKS = 2
CELLS = 784
GROUP = 392
RELS = 169
NORM_EPSILON = 1e-05
MOMENTUM_DECAY = 0.9
AVERAGE_DECAY = 0.9
RATE_BASE = 0.1

DP = "dp"
FSDP = "fsdp"
LANES = 128
WROWS = 64
WINDOWS = 16
WTOK = WINDOWS * WROWS
SLOTS = EXPERTS * 2 * CAP
PAIR = 4 * WROWS
QUADS = HEADS // 4
SCALE = HEAD_DIM ** (-0.5)
US_FLOPS = 1.0e9
BF = jnp.bfloat16
F32 = jnp.float32
VMEM_BYTES = 8 * 1024 * 1024
BIG_VMEM = 13 * 1024 * 1024


def call(body, out_shape, n_in, scratch=(), smem=0, deps=(), us=1, vmem=VMEM_BYTES):
    def skipping(*refs):
        body(*refs[:n_in], *refs[n_in + len(deps) :])

    run = pl.pallas_call(
        skipping,
        out_shape=out_shape,
        in_specs=[pl.BlockSpec(memory_space=pltpu.SMEM)] * smem
        + [pl.BlockSpec(memory_space=pltpu.VMEM)] * (n_in - smem)
        + [pl.BlockSpec(memory_space=pl.ANY)] * len(deps),
        out_specs=jax.tree.map(lambda _: pl.BlockSpec(memory_space=pltpu.VMEM), out_shape),
        scratch_shapes=list(scratch),
        compiler_params=pltpu.CompilerParams(vmem_limit_bytes=vmem),
        cost_estimate=pl.CostEstimate(flops=int(us * US_FLOPS), bytes_accessed=0, transcendentals=0),
    )
    return lambda *args: run(*args, *deps)


def sds(shape, dtype):
    return jax.ShapeDtypeStruct(shape, dtype)


def nn(a, b):
    return lax.dot_general(a, b, (((1,), (0,)), ((), ())), preferred_element_type=F32)


def nt(a, b):
    return lax.dot_general(a, b, (((1,), (1,)), ((), ())), preferred_element_type=F32)


def tn(a, b):
    return lax.dot_general(a, b, (((0,), (0,)), ((), ())), preferred_element_type=F32)


def normalize(hidden):
    centre = hidden - jnp.mean(hidden, axis=-1, keepdims=True)
    inverse = lax.rsqrt(jnp.mean(centre * centre, axis=-1, keepdims=True) + NORM_EPSILON)
    return centre * inverse, inverse


def norm_backward(grad_normed, normal_rows, inverse, gain_row):
    scaled = grad_normed * gain_row
    return inverse * (
        scaled
        - jnp.mean(scaled, axis=-1, keepdims=True)
        - normal_rows * jnp.mean(scaled * normal_rows, axis=-1, keepdims=True)
    )


def head_masks():
    lane = lax.broadcasted_iota(jnp.int32, (1, LANES), 1) // HEAD_DIM
    return [lane == h for h in range(4)]


def stack_heads(rows, masks):
    zero = jnp.zeros_like(rows)
    return jnp.concatenate([jnp.where(mask, rows, zero) for mask in masks], axis=0)


def fold_heads(tall, masks):
    out = jnp.where(masks[0], tall[0:WROWS], 0.0)
    for h in range(1, 4):
        out = jnp.where(masks[h], tall[h * WROWS : (h + 1) * WROWS], out)
    return out


def patch_of(row, shifted):
    w, p = row >> 6, row & 63
    pr = (p * 37) >> 8
    r = (w >> 2) * WIN + pr
    s = (w & 3) * WIN + p - pr * WIN
    if shifted:
        r, s = r + SHIFT, s + SHIFT
        r = jnp.where(r >= SIDE, r - SIDE, r)
        s = jnp.where(s >= SIDE, s - SIDE, s)
    return jnp.where(p < WIN * WIN, r * SIDE + s, -1)


def runs_of(shifted):
    runs = []
    for w in range(WINDOWS):
        for p in range(WIN):
            r, s = (w // 4) * WIN + p, (w % 4) * WIN
            if shifted:
                r, s = (r + SHIFT) % SIDE, s + SHIFT
            here = min(WIN, SIDE - s)
            runs.append((w * WROWS + p * WIN, r * SIDE + s, here))
            if here < WIN:
                runs.append((w * WROWS + p * WIN + here, r * SIDE, WIN - here))
    return runs


def to_windows(patches, windows, shifted):
    windows[...] = jnp.zeros_like(windows)
    for row, patch, length in runs_of(shifted):
        windows[row : row + length, :] = patches[patch : patch + length, :]


def to_patches(windows, patches, shifted):
    for row, patch, length in runs_of(shifted):
        patches[patch : patch + length, :] = windows[row : row + length, :]


PATCHES = pltpu.VMEM((CELLS + 8, D), F32)
PADDED = pltpu.VMEM((WTOK, D), F32)
ONEHOT = pltpu.VMEM((CELLS, SLOTS), BF)
ONEHOT_T = pltpu.VMEM((SLOTS, CELLS), BF)


def attn_fwd_body(shifted, hid, vec, w_in, w_out, bias, mask, h_one, wn, qkv, mixed, attn, patches, windows):
    normal, _ = normalize(hid[...].astype(F32))
    patches[:CELLS, :] = normal * vec[0:1] + vec[1:2]
    to_windows(patches, windows, shifted)
    wn[...] = windows[...].astype(BF)
    in_bias = jnp.concatenate([vec[4:5], jnp.zeros((1, D), F32), vec[5:6]], axis=1)

    @pl.loop(0, 4)
    def _(t):
        rows = pl.ds(pl.multiple_of(t * 256, 256), 256)
        qkv[rows, :] = (nn(wn[rows, :], w_in[...]) + in_bias).astype(BF)

    masks = head_masks()

    @pl.loop(0, WINDOWS // 8)
    def _(wo):
        units = [(i, g) for i in range(8) for g in range(QUADS)]
        rows = [pl.ds(pl.multiple_of((wo * 8 + i) * WROWS, WROWS), WROWS) for i in range(8)]
        allow = []
        for i in range(8):
            one = mask[wo * 8 + i] > 0.0
            allow.append(jnp.concatenate([one, one], axis=1))
        scores = []
        for i, g in units:
            q4 = stack_heads(qkv[rows[i], g * LANES : (g + 1) * LANES], masks)
            scores.append(nt(qkv[rows[i], D + g * LANES : D + (g + 1) * LANES], q4))
        probs = []
        for (i, g), s in zip(units, scores):
            s = jnp.where(allow[i], s * SCALE + bias[g], -1e30)
            e = jnp.exp(s - jnp.max(s, axis=0, keepdims=True))
            a = (e * (1.0 / jnp.sum(e, axis=0, keepdims=True))).astype(BF)
            attn[(wo * 8 + i) * QUADS + g] = a
            probs.append(a)
        tall = [tn(a, qkv[rows[i], 2 * D + g * LANES : 2 * D + (g + 1) * LANES]) for (i, g), a in zip(units, probs)]
        for (i, g), t in zip(units, tall):
            t = fold_heads(t, masks)
            windows[rows[i], g * LANES : (g + 1) * LANES] = t
            mixed[rows[i], g * LANES : (g + 1) * LANES] = t.astype(BF)

    to_patches(windows, patches, shifted)
    h_one[...] = hid[...].astype(F32) + nn(patches[:CELLS, :].astype(BF), w_out[...]) + vec[6:7]


def attn_fwd(shifted, hid, vec, w_in, w_out, bias, mask, deps=()):
    return call(
        functools.partial(attn_fwd_body, shifted),
        (
            sds((CELLS, D), F32),
            sds((WTOK, D), BF),
            sds((WTOK, 3 * D), BF),
            sds((WTOK, D), BF),
            sds((WINDOWS * QUADS, WROWS, PAIR), BF),
        ),
        6,
        scratch=[PATCHES, PADDED],
        us=8,
        deps=deps,
    )(hid, vec, w_in, w_out, bias, mask)


def moe_fwd_body(
    h_one, vec, w1, w2, b1, router, router_bias, place_col, place_row,
    out, normed_two, disp, act, slope, picked, gap_out, rows_out, onehot, onehot_t,
):
    fill_onehot(onehot, place_col)
    fill_onehot_t(onehot_t, place_row)
    normal, _ = normalize(h_one[...])
    two = (normal * vec[2:3] + vec[3:4]).astype(BF)
    normed_two[...] = two
    logits = nn(two, router[...])
    gap = (logits[:, LANES:] + router_bias[1:2]) - (logits[:, :LANES] + router_bias[0:1])
    gap = jnp.where(place_col[...] >= SLOTS // 2, gap, -gap)
    gap_out[...] = gap
    gate = 1.0 / (1.0 + jnp.exp(-gap))
    disp[...] = nn(onehot_t[...], two).astype(BF)

    @pl.loop(0, 4, unroll=4)
    def _(t):
        rows = pl.ds(pl.multiple_of(t * 256, 256), 256)
        e = t // 2
        own = disp[rows, :]
        for c in range(3):
            cols = slice(c * 512, (c + 1) * 512)
            pre = nn(own, w1[e, :, cols]) + b1[pl.ds(e, 1), cols]
            phi = 0.5 * (1.0 + lax.erf(pre * 0.7071067811865476))
            act[rows, cols] = (pre * phi).astype(BF)
            slope[rows, cols] = (
                phi + pre * jnp.exp(-0.5 * pre * pre) * 0.3989422804014327
            ).astype(BF)
        rows_out[rows, :] = (nn(act[rows, :], w2[e]) + vec[pl.ds(7 + e, 1)]).astype(BF)

    taken = nn(onehot[...], rows_out[...])
    picked[...] = taken.astype(BF)
    for c in range(3):
        cols = slice(c * LANES, (c + 1) * LANES)
        out[:, cols] = (h_one[:, cols] + gate * taken[:, cols]).astype(out.dtype)


def moe_fwd(h_one, vec, w1, w2, b1, router, router_bias, place, out_dtype, deps=()):
    return call(
        moe_fwd_body,
        (
            sds((CELLS, D), out_dtype),
            sds((CELLS, D), BF),
            sds((SLOTS, D), BF),
            sds((SLOTS, F), BF),
            sds((SLOTS, F), BF),
            sds((CELLS, D), BF),
            sds((CELLS, LANES), F32),
        ),
        9,
        scratch=[pltpu.VMEM((SLOTS, D), BF), ONEHOT, ONEHOT_T],
        us=9.5,
        deps=deps,
    )(h_one, vec, w1, w2, b1, router, router_bias, *place)


def fill_onehot(onehot, place_col):
    @pl.loop(0, 7)
    def _(t):
        rows = pl.ds(pl.multiple_of(t * 112, 112), 112)
        place = jnp.concatenate([place_col[rows, :]] * 8, axis=1)
        same = place == lax.broadcasted_iota(jnp.int32, (112, SLOTS), 1)
        onehot[rows, :] = jnp.where(same, 1.0, 0.0).astype(BF)


def fill_onehot_t(onehot_t, place_row):
    @pl.loop(0, 8)
    def _(t):
        row = lax.broadcasted_iota(jnp.int32, (128, CELLS), 0) + t * 128
        same = row == place_row[0:1, :]
        onehot_t[pl.ds(pl.multiple_of(t * 128, 128), 128), :] = jnp.where(same, 1.0, 0.0).astype(BF)


def moe_bwd_body(
    grad, w2, place_col, place_row, disp, act, slope, picked, gap,
    dw1, dw2, db1, small, g_pre, gate_grad, g_rows, onehot_t,
):
    fill_onehot_t(onehot_t, place_row)
    go = grad[...].astype(F32)
    gate = 1.0 / (1.0 + jnp.exp(-gap[...]))
    other = 1.0 / (1.0 + jnp.exp(gap[...]))
    g_picked = (go * jnp.concatenate([gate] * 3, axis=1)).astype(BF)
    g_gate = jnp.sum(go * picked[...].astype(F32), axis=-1, keepdims=True)
    sign = jnp.where(place_col[...] >= SLOTS // 2, 1.0, -1.0)
    gl = (g_gate * gate * other * sign).astype(BF)
    gate_grad[...] = gl
    small[...] = jnp.zeros((16, D), F32)
    small[9:10, 0:LANES] = jnp.sum(gl.astype(F32), axis=0, keepdims=True)
    g_rows[...] = nn(onehot_t[...], g_picked).astype(BF)

    @pl.loop(0, EXPERTS, unroll=2)
    def _(e):
        both = pl.ds(pl.multiple_of(e * 512, 512), 512)
        own = g_rows[both, :]
        total = []
        grads = [nt(own, w2[e, c * 256 : (c + 1) * 256, :]) for c in range(6)]
        for c, part in enumerate(grads):
            cols = slice(c * 256, (c + 1) * 256)
            gp = (part * slope[both, cols].astype(F32)).astype(BF)
            g_pre[both, cols] = gp
            total.append(jnp.sum(gp.astype(F32), axis=0, keepdims=True))
        db1[pl.ds(e, 1), :] = jnp.concatenate(total, axis=1)
        small[pl.ds(7 + e, 1), :] = jnp.sum(own.astype(F32), axis=0, keepdims=True)
        for c in range(6):
            cols = slice(c * 256, (c + 1) * 256)
            dw1[e, :, cols] = tn(disp[both, :], g_pre[both, cols])
            dw2[e, cols, :] = tn(act[both, cols], own)


def moe_bwd(grad, w2, place, saved):
    return call(
        moe_bwd_body,
        (
            sds((EXPERTS, D, F), F32),
            sds((EXPERTS, F, D), F32),
            sds((8, F), F32),
            sds((16, D), F32),
            sds((SLOTS, F), BF),
            sds((CELLS, LANES), BF),
        ),
        9,
        scratch=[pltpu.VMEM((SLOTS, D), BF), ONEHOT_T],
        us=8,
    )(grad, w2, *place, *saved)


def middle_bwd_body(
    shifted, grad, h_one, vec, w1, w_out, place_col, normed_two, g_pre, gate_grad, mixed,
    grad_one, g_mix, dw_out, drouter, small, onehot, g_disp, patches, windows_of,
):
    fill_onehot(onehot, place_col)
    for e in range(EXPERTS):
        both = slice(e * 512, (e + 1) * 512)
        g_disp[both, :] = nt(g_pre[both, :], w1[e]).astype(BF)
    gl = gate_grad[...].astype(F32)
    g_two = nn(onehot[...], g_disp[...]) + jnp.concatenate([gl] * 3, axis=1) * vec[9:10]
    drouter[...] = tn(gate_grad[...], normed_two[...])[0:8]
    normal, inverse = normalize(h_one[...])
    small[...] = jnp.zeros((16, D), F32)
    small[2:3] = jnp.sum(g_two * normal, axis=0, keepdims=True)
    small[3:4] = jnp.sum(g_two, axis=0, keepdims=True)
    grad_one[...] = grad[...].astype(F32) + norm_backward(g_two, normal, inverse, vec[2:3])
    small[6:7] = jnp.sum(grad_one[...].astype(BF).astype(F32), axis=0, keepdims=True)
    patches[:CELLS, :] = grad_one[...]
    to_windows(patches, windows_of, shifted)
    gao_w = windows_of[...].astype(BF)
    dw_out[...] = tn(mixed[...], gao_w)
    g_mix[...] = nt(gao_w, w_out[...]).astype(BF)


def middle_bwd(shifted, grad, h_one, vec, w1, w_out, place_col, normed_two, g_pre, gate_grad, mixed):
    return call(
        functools.partial(middle_bwd_body, shifted),
        (
            sds((CELLS, D), F32),
            sds((WTOK, D), BF),
            sds((D, D), F32),
            sds((8, D), F32),
            sds((16, D), F32),
        ),
        10,
        scratch=[ONEHOT, pltpu.VMEM((SLOTS, D), BF), PATCHES, PADDED],
        vmem=BIG_VMEM,
        us=5,
    )(grad, h_one, vec, w1, w_out, place_col, normed_two, g_pre, gate_grad, mixed)


def attn_bwd_windows(windows, qkv, g_mix, attn, g_qkv, dbias, base=None):
    masks = head_masks()
    base = windows[0] if base is None else base

    start, stop = windows
    per = min(4, stop - start)

    @pl.loop(0, (stop - start) // per)
    def _(wo):
        units = [(i, g) for i in range(per) for g in range(QUADS)]
        first = [start + wo * per + i for i in range(per)]
        rows = [pl.ds(pl.multiple_of(w * WROWS, WROWS), WROWS) for w in first]
        outs = [pl.ds(pl.multiple_of((w - base) * WROWS, WROWS), WROWS) for w in first]
        cols = [[slice(n * D + g * LANES, n * D + (g + 1) * LANES) for g in range(QUADS)] for n in range(3)]
        d4s = [stack_heads(g_mix[rows[i], cols[0][g]], masks) for i, g in units]
        grads = [nt(qkv[rows[i], cols[2][g]], d4) for (i, g), d4 in zip(units, d4s)]
        probs = [attn[first[i] * QUADS + g] for i, g in units]
        for (i, g), a, d4 in zip(units, probs, d4s):
            g_qkv[outs[i], cols[2][g]] = nn(a, d4).astype(BF)
        dss = []
        for a, grad in zip(probs, grads):
            a = a.astype(F32)
            t = a * grad
            dss.append((t - a * jnp.sum(t, axis=0, keepdims=True)).astype(BF))
        for g in range(QUADS):
            total = dbias[g]
            for (_, other), ds in zip(units, dss):
                if other == g:
                    total = total + ds.astype(F32)
            dbias[g] = total
        talls = [tn(ds, qkv[rows[i], cols[1][g]]) for (i, g), ds in zip(units, dss)]
        for (i, g), ds in zip(units, dss):
            q4 = stack_heads(qkv[rows[i], cols[0][g]], masks)
            g_qkv[outs[i], cols[1][g]] = (nn(ds, q4) * SCALE).astype(BF)
        for (i, g), tall in zip(units, talls):
            g_qkv[outs[i], cols[0][g]] = (fold_heads(tall, masks) * SCALE).astype(BF)


def attn_bwd_body(qkv, attn, g_mix, g_qkv, dbias):
    dbias[...] = jnp.zeros_like(dbias)
    attn_bwd_windows((0, WINDOWS), qkv, g_mix, attn, g_qkv, dbias)


def attn_bwd(qkv, attn, g_mix):
    return call(attn_bwd_body, (sds((WTOK, 3 * D), BF), sds((QUADS, WROWS, PAIR), F32)), 3, us=5)(qkv, attn, g_mix)


def proj_bwd_body(
    shifted, grad_one, hid, vec, w_in, wn, g_qkv, grad_in, dw_in, small, patches, windows_of,
):
    for c in range(3):
        cols = slice(c * D, (c + 1) * D)
        dw_in[:, cols] = tn(wn[...], g_qkv[:, cols])
    windows_of[...] = nt(g_qkv[...], w_in[...])
    to_patches(windows_of, patches, shifted)
    g_normed = patches[:CELLS, :]
    normal, inverse = normalize(hid[...].astype(F32))
    small[...] = jnp.zeros((16, D), F32)
    small[0:1] = jnp.sum(g_normed * normal, axis=0, keepdims=True)
    small[1:2] = jnp.sum(g_normed, axis=0, keepdims=True)
    small[4:5] = jnp.sum(g_qkv[:, :D].astype(F32), axis=0, keepdims=True)
    small[5:6] = jnp.sum(g_qkv[:, 2 * D :].astype(F32), axis=0, keepdims=True)
    grad_in[...] = grad_one[...] + norm_backward(g_normed, normal, inverse, vec[0:1])


def proj_bwd(shifted, grad_one, hid, vec, w_in, wn, g_qkv):
    return call(
        functools.partial(proj_bwd_body, shifted),
        (sds((CELLS, D), F32), sds((D, 3 * D), F32), sds((16, D), F32)),
        6,
        scratch=[PATCHES, PADDED],
        us=0.5,
    )(grad_one, hid, vec, w_in, wn, g_qkv)


def window_perm_t(shifted):
    source = patch_of(jnp.arange(WTOK, dtype=jnp.int32), shifted)
    return (jnp.arange(CELLS, dtype=jnp.int32)[:, None] == source[None, :]).astype(BF)


def wrap_codes(shifted):
    code = np.zeros((CELLS,), np.float32)
    if shifted:
        for r in range(SIDE):
            for s in range(SIDE):
                rr, ss = (r - SHIFT) % SIDE, (s - SHIFT) % SIDE
                code[r * SIDE + s] = 2 * (rr >= SIDE - SHIFT) + (ss >= SIDE - SHIFT)
    return code


def window_masks(items, shifted):
    labels = items.astype(F32)
    if shifted:
        labels = labels * 4.0 + jnp.asarray(wrap_codes(True))
    placed = nn(jnp.broadcast_to((labels + 1.0).astype(BF), (8, CELLS)), window_perm_t(shifted))[0]
    placed = placed.reshape(WINDOWS, WROWS)
    same = (placed[:, :, None] == placed[:, None, :]) & (placed[:, :, None] > 0.0)
    same = same.astype(F32)
    return jnp.concatenate([same, same], axis=2)


def slot_places(routes, slots):
    group = (jnp.arange(CELLS, dtype=jnp.int32) // GROUP) * CAP
    place = routes * (2 * CAP) + group + slots
    return jnp.broadcast_to(place[:, None], (CELLS, LANES)), jnp.broadcast_to(place[None, :], (8, CELLS))

LEAD = 73
SMALL = 9326
LAG = LEAD * LANES - SMALL
VECTORS = 9
LINES = 32
SPANS = ((LEAD, D, 9), (LEAD + 3456, D, 3), (LEAD + 4608, 2 * D, 12), (LEAD + 4608 + 9216, 2 * F, 3))
EDGE = LEAD + 4608
ALIGNED = LEAD + 4608 + 2 * 9216


def relative(k, bits):
    total = 0
    for place, bit in enumerate(bits):
        total = total + (((k >> (len(bits) - 1 - place)) & 1) << bit)
    return total


def lanes_of(count=LANES):
    return lax.broadcasted_iota(jnp.int32, (1, count), 1)


def equal(rows, columns):
    return jnp.where(rows == columns, 1.0, 0.0).astype(BF)


def spread(shape):
    return lax.broadcasted_iota(jnp.int32, shape, 0), lax.broadcasted_iota(jnp.int32, shape, 1)


def exact(left, one, product):
    high = left.astype(BF)
    low = (left - high.astype(F32)).astype(BF)
    return product(high, one) + product(low, one)


def head_major():
    f, g = spread((D, D))
    return equal(f, 12 * (g & 31) + (g >> 5))


def head_rows(m):
    f, g = spread((D, 2 * LANES))
    return equal((f & 31) + 32 * m, g)


def offset_lanes():
    f, g = spread((LANES, LANES))
    i = g & 63
    r = (i * 37) >> 8
    return equal(f, jnp.where(i < WIN * WIN, 13 * r + i - WIN * r, -1))


def turns():
    return [13 * (6 - j // WIN) + 6 - j % WIN for j in range(WIN * WIN)]


def unpack_bias(flat, wide, tall, bias):
    wide[...] = jnp.zeros_like(wide)
    for m in range(6):
        for c in range(3):
            wide[m : m + 1, c * LANES : (c + 1) * LANES] = flat[12 + 3 * m + c : 13 + 3 * m + c, :]
    by_head = nn(wide[...].astype(BF), head_major())
    sub = lax.broadcasted_iota(jnp.int32, (16, D), 0)
    own = (lanes_of(D) >> 5) == sub
    table = jnp.zeros((16, 2 * LANES), F32)
    for m in range(6):
        table = table + nn(jnp.where(own, by_head[m : m + 1], 0.0).astype(BF), head_rows(m))
    tall[...] = jnp.zeros_like(tall)
    for j, turn in enumerate(turns()):
        row = pltpu.roll(table, (2 * LANES - turn) % (2 * LANES), 1)[:, :LANES]
        tall[pl.ds(j, 16, stride=WROWS), :] = row
    tall[...] = nn(tall[...].astype(BF), offset_lanes())
    for g in range(QUADS):
        for t in range(2):
            h = 4 * g + 2 * t
            left, right = tall[h * WROWS : (h + 1) * WROWS], tall[(h + 1) * WROWS : (h + 2) * WROWS]
            bias[g, :, t * LANES : (t + 1) * LANES] = jnp.where(lanes_of() < WROWS, left, right)


def unpack_small(flat, rows, wide, tall, vec, b1, router, router_bias, bias):
    def shifted(first, count, by):
        near, far = flat[first : first + count, :], flat[first + 1 : first + 1 + count, :]
        return pltpu.roll(jnp.where(lanes_of() >= by, near, far), LANES - by, 1)

    rows[0:16, :] = shifted(27, 16, 108)
    rows[16:46, :] = shifted(42, 30, 110)
    vec[...] = jnp.zeros_like(vec)
    b1[...] = jnp.zeros_like(b1)
    for c in range(3):
        cols = slice(c * LANES, (c + 1) * LANES)
        for n in range(4):
            vec[n : n + 1, cols] = flat[3 * n + c : 3 * n + c + 1, :]
        for n in range(3):
            vec[4 + n : 5 + n, cols] = rows[3 * n + c : 3 * n + c + 1, :]
        for e in range(EXPERTS):
            vec[7 + e : 8 + e, cols] = rows[40 + 3 * e + c : 41 + 3 * e + c, :]
    for e in range(EXPERTS):
        for c in range(12):
            b1[e : e + 1, c * LANES : (c + 1) * LANES] = rows[16 + 12 * e + c : 17 + 12 * e + c, :]
        one = jnp.sum(jnp.where(lanes_of() == e, rows[15:16, :], 0.0), axis=1, keepdims=True)
        router_bias[e : e + 1, :] = jnp.broadcast_to(one, (1, LANES))
    pairs = jnp.concatenate([rows[9 + c : 10 + c, :] for c in range(6)], axis=1)
    pairs = jnp.broadcast_to(pairs, (LANES, 2 * D)).astype(BF)
    d, f = spread((D, 2 * D))
    for e in range(EXPERTS):
        router[:, e * LANES : (e + 1) * LANES] = nt(equal(f, 2 * d + e), pairs).astype(BF)
    gap = nt(pairs[0:16], equal(f, 2 * d + 1)) - nt(pairs[0:16], equal(f, 2 * d))
    vec[9:10, :] = gap[0:1]
    unpack_bias(flat, wide, tall, bias)


def unpack_matrices(flat, spans, outs, skipped):
    for (base, height, tiles), out in zip(spans, outs):
        step = 128

        @pl.loop(0, height // step, unroll=min(6, height // step))
        def _(t, base=base, tiles=tiles, out=out):
            first = base - 1 - skipped + t * (step * tiles)
            before = flat[pl.ds(first, step, stride=tiles), :]
            for j in range(tiles):
                here = flat[pl.ds(first + 1 + j, step, stride=tiles), :]
                tile = pltpu.roll(jnp.where(lanes_of() >= LANES - LAG, before, here), LAG, 1)
                out[pl.ds(pl.multiple_of(t * step, step), step), j * LANES : (j + 1) * LANES] = tile.astype(BF)
                before = here


def unpack_head_body(rows, runs, me, *refs):
    got = refs[: len(runs)]
    w_in, w_out, rest, vec, b1, router, router_bias, bias, flat, few, wide, tall = refs[len(runs) :]
    for (bits, fixed), part in zip(runs, got):
        n, half = 1 << len(bits), part.shape[1]

        @pl.loop(0, n)
        def _(k, bits=bits, fixed=fixed, part=part, n=n, half=half):
            d = me[1] ^ (relative(k, bits) + fixed)
            flat[pl.ds(d * rows, half), :] = part[k].astype(F32)
            flat[pl.ds(d * rows + half, rows - half), :] = part[n + k].astype(F32)[: rows - half]

    unpack_small(flat, few, wide, tall, vec, b1, router, router_bias, bias)
    unpack_matrices(flat, SPANS[:2], (w_in, w_out), 0)
    rest[...] = flat[EDGE - 1 : EDGE - 1 + rest.shape[0], :]


def unpack_tail_body(rows, heads, runs, me, rest, *refs):
    got = refs[: len(runs)]
    w1, w2, flat = refs[len(runs) :]
    flat[0 : rest.shape[0], :] = rest[...]
    for (outer, inner, fixed, upper, skip), part in zip(runs, got):
        count = 1 << len(inner)
        half = part.shape[1]
        first = half if upper else 0
        used = min(half, rows - first)

        @pl.loop(0, 3 * count << len(outer), unroll=3)
        def _(k, outer=outer, inner=inner, fixed=fixed, part=part, count=count, first=first, used=used, skip=skip):
            own = (relative(k // (3 * count), outer) + relative(k % count, inner) + fixed) ^ me[1]
            d = ((k // count) % 3 + 1) * heads + own
            flat[pl.ds(d * rows + first - (EDGE - 1), used), :] = part[skip + k].astype(F32)[:used]

    unpack_matrices(flat, SPANS[2:], (w1, w2), EDGE - 1)


class Weights(NamedTuple):
    w_in: Any
    w_out: Any
    w1: Any
    w2: Any
    vec: Any
    b1: Any
    router: Any
    router_bias: Any
    bias: Any


SMALL_SHAPES = (
    sds((16, D), F32),
    sds((8, F), F32),
    sds((D, 2 * LANES), BF),
    sds((8, LANES), F32),
    sds((QUADS, WROWS, PAIR), F32),
)
SMALL_SCRATCH = [pltpu.VMEM((48, LANES), F32), pltpu.VMEM((8, D), F32), pltpu.VMEM((17 * WROWS, LANES), F32)]
HEAD_SHAPES = (sds((D, 3 * D), BF), sds((D, D), BF))
TAIL_SHAPES = (sds((2 * D, F), BF), sds((2 * F, D), BF))


def experts(w1, w2):
    return w1.reshape(EXPERTS, D, F), w2.reshape(EXPERTS, F, D)


def unpack_head(me, parts, runs, rows, devices):
    heads = devices // 4
    w_in, w_out, rest, *small = call(
        functools.partial(unpack_head_body, rows, runs),
        HEAD_SHAPES + (sds((heads * rows - EDGE + 1, LANES), F32),) + SMALL_SHAPES,
        1 + len(parts),
        scratch=[pltpu.VMEM((heads * rows + 8, LANES), F32)] + SMALL_SCRATCH,
        smem=1,
        us=4,
    )(me, *parts)
    return Weights(w_in, w_out, None, None, *small), rest


def unpack_tail(me, rest, parts, runs, rows, devices):
    return experts(
        *call(
            functools.partial(unpack_tail_body, rows, devices // 4, runs),
            TAIL_SHAPES,
            2 + len(parts),
            scratch=[pltpu.VMEM((devices * rows - EDGE + 9, LANES), F32)],
            smem=1,
            vmem=BIG_VMEM,
            us=4,
        )(me, rest, *parts)
    )


def pack_bias(dbias, wide, tall):
    tall[HEADS * WROWS :, :] = jnp.zeros((5 * WROWS, LANES), F32)
    for h in range(HEADS):
        g, t, side = h // 4, (h % 4) // 2, h % 2
        tile = dbias[g, :, t * LANES : (t + 1) * LANES]
        tall[h * WROWS : (h + 1) * WROWS, :] = jnp.where((lanes_of() >> 6) == side, tile, 0.0)
    used = HEADS * WROWS
    tall[0:used, :] = exact(tall[0:used, :], offset_lanes(), nt)
    table = jnp.zeros((16, 2 * LANES), F32)
    for j, turn in enumerate(turns()):
        row = tall[pl.ds(j, 16, stride=WROWS), :]
        table = table + pltpu.roll(jnp.concatenate([row, jnp.zeros_like(row)], axis=1), turn, 1)
    sub = lax.broadcasted_iota(jnp.int32, (16, D), 0)
    own = (lanes_of(D) >> 5) == sub
    wide[...] = jnp.zeros_like(wide)
    for m in range(6):
        placed = jnp.where(own, exact(table, head_rows(m), nt), 0.0)
        wide[m : m + 1, :] = jnp.sum(placed, axis=0, keepdims=True)
    wide[...] = exact(wide[...], head_major(), nt)


def pack_small(al, vectors, drouter, db1, dbias, one, two, wide, tall):
    one[...] = jnp.zeros_like(one)
    two[...] = jnp.zeros_like(two)
    pack_bias(dbias, wide, tall)
    d, f = spread((D, 2 * D))
    signs = equal(f, 2 * d + 1) - equal(f, 2 * d)
    pairs = exact(drouter[...], signs, nn)
    for c in range(3):
        cols = slice(c * LANES, (c + 1) * LANES)
        for n in range(4):
            one[1 + 3 * n + c : 2 + 3 * n + c, :] = vectors[n : n + 1, cols]
        for m in range(6):
            one[13 + 3 * m + c : 14 + 3 * m + c, :] = wide[m : m + 1, cols]
        for n in range(3):
            two[1 + 3 * n + c : 2 + 3 * n + c, :] = vectors[4 + n : 5 + n, cols]
        for e in range(EXPERTS):
            al[67 + 3 * e + c : 68 + 3 * e + c, :] = vectors[7 + e : 8 + e, cols]
    for c in range(6):
        two[10 + c : 11 + c, :] = pairs[0:1, c * LANES : (c + 1) * LANES]
    total = vectors[9:10, 0:LANES]
    two[16:17, :] = jnp.where(lanes_of() == 0, -total, jnp.where(lanes_of() == 1, total, 0.0))
    for e in range(EXPERTS):
        for c in range(12):
            al[43 + 12 * e + c : 44 + 12 * e + c, :] = db1[e : e + 1, c * LANES : (c + 1) * LANES]
    first = pltpu.roll(jnp.where(lanes_of() >= LANES - 18, one[0:28, :], one[1:29, :]), 18, 1)
    second = pltpu.roll(jnp.where(lanes_of() >= LANES - 126, two[0:16, :], two[1:17, :]), 126, 1)
    al[27:43, :] = second
    al[0:27, :] = first[0:27]
    al[27:28, :] += first[27:28]


def pack_matrices(al, spans, grads, skipped):
    for (base, height, tiles), grad in zip(spans, grads):
        step = 128

        @pl.loop(0, height // step, unroll=min(6, height // step))
        def _(t, base=base, tiles=tiles, grad=grad):
            first = base - skipped + t * (step * tiles)
            own = pl.ds(pl.multiple_of(t * step, step), step)
            for j in range(tiles):
                al[pl.ds(first + j, step, stride=tiles), :] = grad[own, j * LANES : (j + 1) * LANES]


def clear(al, first):
    al[pl.ds(first, al.shape[0] - first), :] = jnp.zeros((al.shape[0] - first, LANES), F32)


def pack_head_body(
    rows, padded, runs, me, moe, attn, proj, drouter, db1, dbias, dw_in, dw_out, rest,
    keep, send, al, vectors, lines, one, two, wide, tall,
):
    vectors[...] = moe[...] + attn[...] + proj[...]
    lines[...] = jnp.zeros_like(lines)
    for n in range(VECTORS):
        for c in range(3):
            lines[3 * n + c : 3 * n + c + 1, :] = vectors[n : n + 1, c * LANES : (c + 1) * LANES]
    pack_small(al, vectors, drouter, db1, dbias, one, two, wide, tall)
    pack_matrices(al, SPANS[:2], (dw_in, dw_out), 0)
    al[EDGE : EDGE + rest.shape[0], :] = rest[...]
    at = 0
    for bits, fixed in runs:
        for other, out in enumerate((keep, send)):

            @pl.loop(0, 1 << len(bits))
            def _(k, bits=bits, fixed=fixed, at=at, other=other, out=out):
                d = me[1] ^ (relative(k, bits) + fixed + other)
                out[at + k, :padded, :] = al[pl.ds(d * rows, padded), :].astype(BF)
                out[at + k, padded:, :] = lines[...].astype(BF)

        at += 1 << len(bits)


def pack_tail_body(rows, padded, heads, runs, me, dw1, dw2, keep, send, rest, al):
    clear(al, ALIGNED - EDGE)
    pack_matrices(al, SPANS[2:], (dw1, dw2), EDGE)
    rest[...] = al[0 : rest.shape[0], :]
    half = padded // 2
    at = 0
    for outer, inner, fixed, upper in runs:
        count = 1 << len(inner)
        total = 3 * count << len(outer)
        for other, out in enumerate((keep, send)):

            @pl.loop(0, total, unroll=3)
            def _(k, outer=outer, inner=inner, fixed=fixed, upper=upper, count=count, at=at, other=other, out=out):
                own = (relative(k // (3 * count), outer) + relative(k % count, inner) + fixed + other) ^ me[1]
                d = ((k // count) % 3 + 1) * heads + own
                out[at + k] = al[pl.ds(d * rows + (half if upper else 0) - EDGE, half), :].astype(BF)

        at += total


SMALL_PACK = [
    pltpu.VMEM((40, LANES), F32),
    pltpu.VMEM((24, LANES), F32),
    pltpu.VMEM((8, D), F32),
    pltpu.VMEM((17 * WROWS, LANES), F32),
]


def pack_head(me, small, dw_in, dw_out, rest, runs, rows, devices, padded):
    heads = devices // 4
    shape = sds((heads // 2, padded + LINES, LANES), BF)
    return call(
        functools.partial(pack_head_body, rows, padded, runs),
        (shape, shape),
        10,
        scratch=[
            pltpu.VMEM((EDGE + rest.shape[0], LANES), F32),
            pltpu.VMEM((16, D), F32),
            pltpu.VMEM((LINES, LANES), F32),
        ]
        + SMALL_PACK,
        smem=1,
        us=0.5,
    )(me, *small, dw_in, dw_out, rest)


def pack_tail(me, dw1, dw2, runs, rows, devices, padded):
    heads = devices // 4
    shape = sds((3 * heads, padded // 2, LANES), BF)
    over = -(-(heads * rows + padded - EDGE) // 8) * 8
    return call(
        functools.partial(pack_tail_body, rows, padded, heads, runs),
        (shape, shape, sds((over, LANES), F32)),
        3,
        scratch=[pltpu.VMEM((devices * rows + padded - EDGE, LANES), F32)],
        smem=1,
        vmem=BIG_VMEM,
        us=3,
    )(me, dw1.reshape(2 * D, F), dw2.reshape(2 * F, D))


def levels_body(sources, me, *refs):
    pieces, (x, y, head) = refs[: len(refs) - 3], refs[len(refs) - 3 :]
    n, half = head.shape[0] // 2, x.shape[1]
    for level in range(4):
        for step, (at, first) in enumerate(sources):

            @pl.when((me[2] ^ step) == level)
            def _(level=level, at=at, first=first):
                for i in range(n):
                    lower, upper = pieces[at][first * n + i, :half, :], pieces[at][first * n + i, half:, :]
                    if level == 0:
                        for out in (x, y, head):
                            out[i] = lower
                            out[n + i] = upper
                    else:
                        x[(1 + level) * n + i] = lower
                        y[(1 + level) * n + i] = upper


def levels(me, *pieces):
    sources = ((0, 0), (1, 0), (2, 0), (3, 0)) if len(pieces) == 4 else ((0, 0), (1, 0), (0, 1), (1, 1))
    n, padded, _ = pieces[0].shape
    n = n * len(pieces) // 4
    dtype = pieces[0].dtype
    shapes = [sds((count * n, padded // 2, LANES), dtype) for count in (5, 5, 2)]
    return call(functools.partial(levels_body, sources), shapes, 1 + len(pieces), smem=1)(me, *pieces)


def targets_body(with_head, me, a, a_got, b, b_got, *refs):
    *head, keep, send = refs
    n, half = keep.shape[0] // 2, a.shape[1]
    places = {0: (keep, 0), 2: (keep, n), 1: (send, 0), 3: (send, n)}
    for step, (out, first) in places.items():
        level = me[2] ^ step

        @pl.when(level == 0)
        def _(out=out, first=first):
            for i in range(n):
                if with_head:
                    out[first + i] = head[0][i, : 2 * half, :].astype(out.dtype)
                else:
                    out[first + i] = jnp.zeros((2 * half, LANES), out.dtype)

        @pl.when(level > 0)
        def _(out=out, first=first, level=level):
            for i in range(n):
                at = (level - 1) * n + i
                out[first + i, :half, :] = (a[at] + a_got[at].astype(F32)).astype(out.dtype)
                out[first + i, half:, :] = (b[at] + b_got[at].astype(F32)).astype(out.dtype)


def targets(me, a, a_got, b, b_got, *head):
    n, half, _ = a.shape
    n = n // 3
    shape = (2 * n, 2 * half, LANES)
    return call(
        functools.partial(targets_body, bool(head)), (sds(shape, F32), sds(shape, BF)), 5 + len(head), smem=1
    )(me, a, a_got, b, b_got, *head)


def combine_body(plan, count, *refs):
    for (size, _, terms), out in zip(plan, refs[count:]):

        @pl.loop(0, size)
        def _(i, terms=terms, out=out):
            parts = [refs[at][first + i].astype(F32) for at, first in terms]
            while len(parts) > 1:
                parts = [sum(parts[at + 1 : at + 2], parts[at]) for at in range(0, len(parts), 2)]
            out[i] = parts[0].astype(out.dtype)


def combine(plan, *arrays):
    tail = arrays[0].shape[1:]
    shapes = [sds((size, *tail), dtype) for size, dtype, _ in plan]
    return call(functools.partial(combine_body, plan, len(arrays)), shapes, len(arrays))(*arrays)


def finish_body(rows, me, keep, got, upper_keep, upper_got, out):
    def shift(keep, got):
        total = keep[0] + got[0].astype(F32)
        here, below = total[0:rows, :], total[1 : rows + 1, :]
        out[...] = pltpu.roll(jnp.where(lanes_of() >= LAG, here, below), LANES - LAG, 1)

    pl.when(me[2] == 0)(lambda: shift(keep, got))
    pl.when(me[2] != 0)(lambda: shift(upper_keep, upper_got))


def finish(me, rows, lowest, upper):
    parts = (lowest.keep, lowest.got, upper.keep, upper.got)
    return call(functools.partial(finish_body, rows), sds((rows, LANES), F32), 5, smem=1)(me, *parts)


def join_body(skip, a, b, out):
    n = out.shape[0] // 2

    @pl.loop(0, n)
    def _(i):
        out[i] = a[skip + i]
        out[n + i] = b[skip + i]


def join(a, b, skip=0):
    shape = sds((2 * (a.shape[0] - skip), *a.shape[1:]), a.dtype)
    return call(functools.partial(join_body, skip), shape, 2)(a, b)


class Ways(NamedTuple):
    core: Any
    x: Any
    y: Any
    low: Any
    high: Any
    rest: Any


def ways():
    dp, fsdp = (lax.axis_size(axis).bit_length() - 1 for axis in (DP, FSDP))
    rest = [1 << (fsdp + bit) for bit in range(1, dp - 2)] + [1 << bit for bit in range(2, fsdp)]
    return Ways(1, 2, 1 << fsdp, 1 << (fsdp + dp - 2), 1 << (fsdp + dp - 1), rest)


def device_count():
    return lax.axis_size(DP) * lax.axis_size(FSDP)


def flip(array, step):
    return lax.ppermute(array, (DP, FSDP), [(i, i ^ step) for i in range(device_count())])


def move(array, levels):
    width = device_count() // 4
    pairs = [(a * width + i, b * width + i) for a, b in levels.items() for i in range(width)]
    return lax.ppermute(array, (DP, FSDP), pairs)


def tie(arrays, *others):
    if isinstance(arrays, tuple):
        return tuple(tie(array, *others) for array in arrays)
    return lax.optimization_barrier((arrays, *others))[0]


def sync(*arrays):
    return lax.optimization_barrier(arrays)


def bits_of(*steps):
    return [step.bit_length() - 1 for step in steps]


class Gather:
    def __init__(self, own, way, me):
        for extra in way.rest:
            own = join(own, flip(own, extra))
        self.way, self.own, self.me, self.others = way, own, me, None
        self.rest = bits_of(*reversed(way.rest))

    def far(self):
        own, way = self.own, self.way
        self.others = own, flip(own, way.low), flip(own, way.high), flip(own, way.low + way.high)

    def high(self):
        self.other = flip(self.own, self.way.high)

    def low(self):
        self.pair = join(self.own, self.other)
        self.over = flip(self.pair, self.way.low)

    def levels(self):
        pieces = self.others if self.others else (self.pair, self.over)
        self.x, self.y, self.head = levels(self.me, *pieces)

    def near(self):
        way = self.way
        self.got = [flip(self.x, way.x), flip(self.y, way.y), flip(self.head, way.x + way.y)]

    def near_core(self):
        way, core = self.way, self.way.core
        x, y, both = self.got
        sides = [[self.x, x, y, both, self.y]]
        sides.append([flip(part, core) for part in sides[0]])
        self.head_parts, self.head_runs, self.parts, self.runs = [], [], [], []
        for fixed, side in zip((0, core), sides):
            self.head_parts += side[:4]
            self.head_runs += [(self.rest, step + fixed) for step in (0, way.x, way.y, way.x + way.y)]
            x_own, x_got, y_got, _, y_own = side
            self.parts += [x_own, x_got, y_own, y_got]
            skip = 2 << len(self.rest)
            self.runs += [([], self.rest, fixed + step, False, skip) for step in (0, way.x)]
            self.runs += [([], self.rest, fixed + step, True, skip) for step in (0, way.y)]

    def last(self):
        way, skip = self.way, 2 << len(self.rest)
        self.joined = join(self.x, self.got[0], skip), join(self.y, self.got[1], skip)
        self.last_got = flip(self.joined[0], way.y), flip(self.joined[1], way.x)

    def last_core(self):
        way = self.way
        for fixed in (0, way.core):
            self.parts += [flip(part, way.core) for part in self.last_got] if fixed else list(self.last_got)
            self.runs += [(bits_of(way.x), self.rest, way.y + fixed, False, 0)]
            self.runs += [(bits_of(way.y), self.rest, way.x + fixed, True, 0)]


def head_runs(way):
    rest = bits_of(*way.rest)
    return [(rest, step) for step in (way.y, way.x + way.y, way.x, 0)]


def tail_runs(way):
    rest, bx, by = (bits_of(*steps) for steps in (way.rest, [way.x], [way.y]))
    return [
        (bx, rest, way.y, False), ([], rest, way.x, False), ([], rest, 0, False),
        (by, rest, way.x, True), ([], rest, way.y, True), ([], rest, 0, True),
    ]


class HeadScatter:
    def __init__(self, keep, send, way):
        self.way, self.keep, self.n = way, keep, keep.shape[0] // 4
        self.got = flip(send, way.core)

    def plane(self):
        n, way = self.n, self.way
        y, xy, x, self.keep = combine([(n, BF, ((0, i * n), (1, i * n))) for i in range(4)], self.keep, self.got)
        self.got = flip(x, way.x), flip(y, way.y), flip(xy, way.x + way.y)

    def near(self):
        n = 2 * self.n
        sent, self.keep = combine([(n, BF, ((0, i * n), (1, i * n))) for i in range(2)], self.keep, self.got)
        self.got = flip(sent, self.way.y)

    def next(self):
        n = self.n
        sent, self.keep = combine(((n, BF, ((0, 0), (1, n))), (n, BF, ((0, n), (1, 0)))), self.keep, self.got)
        self.got = flip(sent, self.way.x)

    def add(self):
        n, got = self.n, self.got if isinstance(self.got, (tuple, list)) else (self.got,)
        terms = tuple((i, 0) for i in range(1 + len(got)))
        sent, self.keep = combine(((n, BF, terms), (n, F32, terms)), self.keep, *got)
        return sent

    def lines(self):
        return self.keep[0, -LINES : 3 * VECTORS - LINES].reshape(VECTORS, D)

    def low(self, sent):
        self.got = move(sent, {1: 0, 3: 2})

    def high(self):
        self.got = move(self.add(), {2: 0})
        self.keep, self.got = fold(self.keep, self.got, self.way.rest)


class TailScatter:
    def __init__(self, keep, send, way, me):
        self.way, self.keep, self.n, self.me = way, keep, keep.shape[0] // 24, me
        self.got = flip(send, way.core)

    def near(self):
        n = 6 * self.n
        plan = [(n, dtype, ((0, first), (1, first))) for dtype, first in ((BF, 0), (F32, n), (BF, 2 * n), (F32, 3 * n))]
        a, self.a, b, self.b = combine(plan, self.keep, self.got)
        self.a_got, self.b_got = flip(a, self.way.y), flip(b, self.way.x)

    def next(self):
        n = 3 * self.n
        plan = [(n, BF, ((0, 0), (1, n))), (n, F32, ((0, n), (1, 0)))]
        plan += [(n, BF, ((2, 0), (3, n))), (n, F32, ((2, n), (3, 0)))]
        a, self.a, b, self.b = combine(plan, self.a, self.a_got, self.b, self.b_got)
        self.a_got, self.b_got = flip(a, self.way.x), flip(b, self.way.y)

    def low(self, *head):
        self.keep, sent = targets(self.me, self.a, self.a_got, self.b, self.b_got, *head)
        self.got = flip(sent, self.way.low)

    def high(self):
        self.keep, self.got = fold(self.keep, self.got, [self.way.high] + self.way.rest)


def fold(keep, got, steps):
    for way in steps:
        half = keep.shape[0] // 2
        plan = ((half, BF, ((0, half), (1, half))), (half, F32, ((0, 0), (1, 0))))
        sent, keep = combine(plan, keep, got)
        got = flip(sent, way)
    return keep, got


def shards(inputs, items, routes, slots, cotangent, params, momentum, average):
    fsdp, dp = lax.axis_size(FSDP), lax.axis_size(DP)
    devices = fsdp * dp
    share = params.shape[1]
    rows = share // LANES
    padded = -(-(rows + 1) // 32) * 32
    step_rate = RATE_BASE / math.sqrt(CELLS * devices)
    way = ways()
    own = lax.axis_index(DP) * fsdp + lax.axis_index(FSDP)
    me = jnp.stack([own, own % (devices // 4), own // (devices // 4)]).astype(jnp.int32)

    shares = []
    for b in range(BLOCKS):
        share_rows = params[b].astype(BF).reshape(1, rows, LANES)
        shares.append(jnp.pad(share_rows, ((0, 0), (0, padded - rows), (0, 0))))
    one, two = (Gather(rows_own, way, me) for rows_own in shares)
    masks, places = [], []
    for b in range(BLOCKS):
        masks.append(window_masks(items.reshape(CELLS), b % 2 == 1))
        places.append(slot_places(routes[b].reshape(CELLS), slots[b].reshape(CELLS)))

    hidden_zero = inputs.reshape(CELLS, D)
    one.far()
    one.levels()
    one.near()
    two.own = tie(two.own, one.head)
    two.high()
    one.got[0] = tie(one.got[0], *masks)
    two.other, *one.got = sync(two.other, *one.got)
    one.near_core()
    one.last()
    two.low()
    one.head_parts[0] = tie(one.head_parts[0], two.pair, *one.joined, *one.parts)
    w, rest = unpack_head(me, one.head_parts, one.head_runs, rows, devices)
    h_zero, *attn_zero = attn_fwd(False, hidden_zero, w.vec, w.w_in, w.w_out, w.bias, masks[0])
    h_zero, two.over = sync(h_zero, two.over)
    two.levels()
    two.near()
    one.last_got = tie(one.last_got, two.head)
    one.last_core()
    w1, w2 = unpack_tail(me, tie(rest, two.head), one.parts, one.runs, rows, devices)
    w_zero = w._replace(w1=w1, w2=w2)
    w = w_zero
    hidden_one, *moe_zero = moe_fwd(h_zero, w.vec, w.w1, w.w2, w.b1, w.router, w.router_bias, places[0], F32)

    hidden_one, *two.got = sync(hidden_one, *two.got)
    two.near_core()
    two.last()
    two.head_parts[0] = tie(two.head_parts[0], *two.joined, *two.parts)
    w, rest = unpack_head(me, two.head_parts, two.head_runs, rows, devices)
    h_one, *attn_one = attn_fwd(True, hidden_one, w.vec, w.w_in, w.w_out, w.bias, masks[1])
    h_one, *two.last_got = sync(h_one, *two.last_got)
    two.last_core()
    w1, w2 = unpack_tail(me, rest, two.parts, two.runs, rows, devices)
    w_one = w._replace(w1=w1, w2=w2)
    w = w_one
    outputs, *moe_one = moe_fwd(h_one, w.vec, w.w1, w.w2, w.b1, w.router, w.router_bias, places[1], BF)

    gradient = cotangent.reshape(CELLS, D)
    wn, qkv, mixed, attn = attn_one
    normed_two, *saved = moe_one
    dw1, dw2, db1, small_moe, g_pre, gate_grad = moe_bwd(gradient, w.w2, places[1], saved)
    keep, send, rest = pack_tail(me, dw1, dw2, tail_runs(way), rows, devices, padded)
    tail_one = TailScatter(keep, send, way, me)
    g_one, g_mix, dw_out, drouter, small_mid = middle_bwd(
        True, gradient, h_one, w.vec, w.w1, w.w_out, places[1][0], normed_two, tie(g_pre, send), gate_grad, mixed
    )
    g_mix, tail_one.got = sync(g_mix, tail_one.got)
    tail_one.near()
    g_qkv, dbias = attn_bwd(qkv, attn, tie(g_mix, tail_one.a))
    gradient, dw_in, small_attn = proj_bwd(True, g_one, hidden_one, w.vec, w.w_in, wn, g_qkv)
    small = (small_moe, small_mid, small_attn, drouter, db1, dbias)
    keep, send = pack_head(me, small, dw_in, dw_out, rest, head_runs(way), rows, devices, padded)
    send, tail_one.a_got, tail_one.b_got, gradient = sync(send, tail_one.a_got, tail_one.b_got, gradient)
    head_one = HeadScatter(keep, send, way)
    tail_one.next()

    w = w_zero
    wn, qkv, mixed, attn = attn_zero
    normed_two, *saved = moe_zero
    gradient = tie(gradient, tail_one.a)
    dw1, dw2, db1, small_moe, g_pre, gate_grad = moe_bwd(gradient, w.w2, places[0], saved)
    g_pre, dw2, head_one.got, tail_one.a_got, tail_one.b_got = sync(
        g_pre, dw2, head_one.got, tail_one.a_got, tail_one.b_got
    )
    head_one.near()
    tail_one.low()
    keep, send, rest = pack_tail(me, dw1, tie(dw2, head_one.keep, tail_one.keep), tail_runs(way), rows, devices, padded)
    tail_zero = TailScatter(keep, send, way, me)
    g_one, g_mix, dw_out, drouter, small_mid = middle_bwd(
        False, gradient, h_zero, w.vec, w.w1, w.w_out, places[0][0], normed_two, tie(g_pre, send), gate_grad, mixed
    )
    g_mix, tail_zero.got = sync(g_mix, tail_zero.got)
    tail_zero.near()
    g_qkv, dbias = attn_bwd(qkv, attn, tie(g_mix, tail_zero.a))
    g_qkv, tail_one.got, head_one.got = sync(g_qkv, tail_one.got, head_one.got)
    head_one.next()
    tail_one.high()
    gradient, dw_in, small_attn = proj_bwd(
        False, tie(g_one, head_one.keep, tail_one.keep), hidden_zero, w.vec, w.w_in, wn, g_qkv
    )
    small = (small_moe, small_mid, small_attn, drouter, db1, dbias)
    keep, send = pack_head(me, small, dw_in, dw_out, rest, head_runs(way), rows, devices, padded)
    send, tail_zero.a_got, tail_zero.b_got, head_one.got, tail_one.got = sync(
        send, tail_zero.a_got, tail_zero.b_got, head_one.got, tail_one.got
    )

    head_zero = HeadScatter(keep, send, way)
    tail_zero.next()
    head_zero.plane()
    head_one.add()
    tail_zero.low(head_one.keep)
    sent = head_zero.add()
    head_zero.low(sent)
    vector_grads = jnp.stack([head_zero.lines(), head_one.lines()])
    got = flip(vector_grads, way.low)
    tail_zero.high()
    vector_grads = vector_grads + got
    head_zero.keep = tie(head_zero.keep, vector_grads)
    head_zero.high()
    for step in [way.high] + way.rest:
        vector_grads = vector_grads + flip(vector_grads, step)
    grads_zero = finish(me, rows, head_zero, tail_zero)
    grads_one = finish(me, rows, tail_zero, tail_one)
    grad_all = jnp.stack([grads_zero.reshape(-1), grads_one.reshape(-1)])
    new_momentum = MOMENTUM_DECAY * momentum + grad_all
    new_params = params - step_rate * (grad_all + MOMENTUM_DECAY * new_momentum)
    new_average = AVERAGE_DECAY * average + (1.0 - AVERAGE_DECAY) * new_params
    return (
        outputs.reshape(1, CELLS, D),
        gradient.reshape(1, CELLS, D),
        new_params,
        new_momentum,
        new_average,
        vector_grads,
    )


def solution(mesh):
    both = (DP, FSDP)
    canvas, vector = P(both), P(None, both)
    return jax.shard_map(
        shards,
        mesh=mesh,
        in_specs=(canvas, canvas, vector, vector, canvas, vector, vector, vector),
        out_specs=(canvas, canvas, vector, vector, vector, P()),
        check_vma=False,
    )
```

```python
import functools
import math
from typing import Any, NamedTuple

import jax
import jax.numpy as jnp
import numpy as np
from jax import lax
from jax.experimental import pallas as pl
from jax.experimental.pallas import tpu as pltpu
from jax.sharding import PartitionSpec as P

D = 384
HEADS = 12
F = 1536
HEAD_DIM = 32
EXPERTS = 2
CAP = 256
SIDE = 28
WIN = 7
SHIFT = 3
BLOCKS = 2
CELLS = 784
GROUP = 392
RELS = 169
NORM_EPSILON = 1e-05
MOMENTUM_DECAY = 0.9
AVERAGE_DECAY = 0.9
RATE_BASE = 0.1

DP = "dp"
FSDP = "fsdp"
LANES = 128
WROWS = 64
WINDOWS = 16
WTOK = WINDOWS * WROWS
SLOTS = EXPERTS * 2 * CAP
PAIR = 4 * WROWS
QUADS = HEADS // 4
SCALE = HEAD_DIM ** (-0.5)
US_FLOPS = 1.0e9
BF = jnp.bfloat16
F32 = jnp.float32
VMEM_BYTES = 8 * 1024 * 1024
BIG_VMEM = 13 * 1024 * 1024


def call(body, out_shape, n_in, scratch=(), smem=0, deps=(), us=1, vmem=VMEM_BYTES):
    def skipping(*refs):
        body(*refs[:n_in], *refs[n_in + len(deps) :])

    run = pl.pallas_call(
        skipping,
        out_shape=out_shape,
        in_specs=[pl.BlockSpec(memory_space=pltpu.SMEM)] * smem
        + [pl.BlockSpec(memory_space=pltpu.VMEM)] * (n_in - smem)
        + [pl.BlockSpec(memory_space=pl.ANY)] * len(deps),
        out_specs=jax.tree.map(lambda _: pl.BlockSpec(memory_space=pltpu.VMEM), out_shape),
        scratch_shapes=list(scratch),
        compiler_params=pltpu.CompilerParams(vmem_limit_bytes=vmem),
        cost_estimate=pl.CostEstimate(flops=int(us * US_FLOPS), bytes_accessed=0, transcendentals=0),
    )
    return lambda *args: run(*args, *deps)


def sds(shape, dtype):
    return jax.ShapeDtypeStruct(shape, dtype)


def nn(a, b):
    return lax.dot_general(a, b, (((1,), (0,)), ((), ())), preferred_element_type=F32)


def nt(a, b):
    return lax.dot_general(a, b, (((1,), (1,)), ((), ())), preferred_element_type=F32)


def tn(a, b):
    return lax.dot_general(a, b, (((0,), (0,)), ((), ())), preferred_element_type=F32)


def normalize(hidden):
    centre = hidden - jnp.mean(hidden, axis=-1, keepdims=True)
    inverse = lax.rsqrt(jnp.mean(centre * centre, axis=-1, keepdims=True) + NORM_EPSILON)
    return centre * inverse, inverse


def norm_backward(grad_normed, normal_rows, inverse, gain_row):
    scaled = grad_normed * gain_row
    return inverse * (
        scaled
        - jnp.mean(scaled, axis=-1, keepdims=True)
        - normal_rows * jnp.mean(scaled * normal_rows, axis=-1, keepdims=True)
    )


def head_masks():
    lane = lax.broadcasted_iota(jnp.int32, (1, LANES), 1) // HEAD_DIM
    return [lane == h for h in range(4)]


def stack_heads(rows, masks):
    zero = jnp.zeros_like(rows)
    return jnp.concatenate([jnp.where(mask, rows, zero) for mask in masks], axis=0)


def fold_heads(tall, masks):
    out = jnp.where(masks[0], tall[0:WROWS], 0.0)
    for h in range(1, 4):
        out = jnp.where(masks[h], tall[h * WROWS : (h + 1) * WROWS], out)
    return out


def patch_of(row, shifted):
    w, p = row >> 6, row & 63
    pr = (p * 37) >> 8
    r = (w >> 2) * WIN + pr
    s = (w & 3) * WIN + p - pr * WIN
    if shifted:
        r, s = r + SHIFT, s + SHIFT
        r = jnp.where(r >= SIDE, r - SIDE, r)
        s = jnp.where(s >= SIDE, s - SIDE, s)
    return jnp.where(p < WIN * WIN, r * SIDE + s, -1)


def runs_of(shifted):
    runs = []
    for w in range(WINDOWS):
        for p in range(WIN):
            r, s = (w // 4) * WIN + p, (w % 4) * WIN
            if shifted:
                r, s = (r + SHIFT) % SIDE, s + SHIFT
            here = min(WIN, SIDE - s)
            runs.append((w * WROWS + p * WIN, r * SIDE + s, here))
            if here < WIN:
                runs.append((w * WROWS + p * WIN + here, r * SIDE, WIN - here))
    return runs


def to_windows(patches, windows, shifted):
    windows[...] = jnp.zeros_like(windows)
    for row, patch, length in runs_of(shifted):
        windows[row : row + length, :] = patches[patch : patch + length, :]


def to_patches(windows, patches, shifted):
    for row, patch, length in runs_of(shifted):
        patches[patch : patch + length, :] = windows[row : row + length, :]


PATCHES = pltpu.VMEM((CELLS + 8, D), F32)
PADDED = pltpu.VMEM((WTOK, D), F32)
ONEHOT = pltpu.VMEM((CELLS, SLOTS), BF)
ONEHOT_T = pltpu.VMEM((SLOTS, CELLS), BF)


def attn_fwd_body(shifted, hid, vec, w_in, w_out, bias, mask, h_one, wn, qkv, mixed, attn, patches, windows):
    normal, _ = normalize(hid[...].astype(F32))
    patches[:CELLS, :] = normal * vec[0:1] + vec[1:2]
    to_windows(patches, windows, shifted)
    wn[...] = windows[...].astype(BF)
    in_bias = jnp.concatenate([vec[4:5], jnp.zeros((1, D), F32), vec[5:6]], axis=1)

    @pl.loop(0, 4)
    def _(t):
        rows = pl.ds(pl.multiple_of(t * 256, 256), 256)
        qkv[rows, :] = (nn(wn[rows, :], w_in[...]) + in_bias).astype(BF)

    masks = head_masks()

    @pl.loop(0, WINDOWS // 8)
    def _(wo):
        units = [(i, g) for i in range(8) for g in range(QUADS)]
        rows = [pl.ds(pl.multiple_of((wo * 8 + i) * WROWS, WROWS), WROWS) for i in range(8)]
        allow = []
        for i in range(8):
            one = mask[wo * 8 + i] > 0.0
            allow.append(jnp.concatenate([one, one], axis=1))
        scores = []
        for i, g in units:
            q4 = stack_heads(qkv[rows[i], g * LANES : (g + 1) * LANES], masks)
            scores.append(nt(qkv[rows[i], D + g * LANES : D + (g + 1) * LANES], q4))
        probs = []
        for (i, g), s in zip(units, scores):
            s = jnp.where(allow[i], s * SCALE + bias[g], -1e30)
            e = jnp.exp(s - jnp.max(s, axis=0, keepdims=True))
            a = (e * (1.0 / jnp.sum(e, axis=0, keepdims=True))).astype(BF)
            attn[(wo * 8 + i) * QUADS + g] = a
            probs.append(a)
        tall = [tn(a, qkv[rows[i], 2 * D + g * LANES : 2 * D + (g + 1) * LANES]) for (i, g), a in zip(units, probs)]
        for (i, g), t in zip(units, tall):
            t = fold_heads(t, masks)
            windows[rows[i], g * LANES : (g + 1) * LANES] = t
            mixed[rows[i], g * LANES : (g + 1) * LANES] = t.astype(BF)

    to_patches(windows, patches, shifted)
    h_one[...] = hid[...].astype(F32) + nn(patches[:CELLS, :].astype(BF), w_out[...]) + vec[6:7]


def attn_fwd(shifted, hid, vec, w_in, w_out, bias, mask, deps=()):
    return call(
        functools.partial(attn_fwd_body, shifted),
        (
            sds((CELLS, D), F32),
            sds((WTOK, D), BF),
            sds((WTOK, 3 * D), BF),
            sds((WTOK, D), BF),
            sds((WINDOWS * QUADS, WROWS, PAIR), BF),
        ),
        6,
        scratch=[PATCHES, PADDED],
        us=8,
        deps=deps,
    )(hid, vec, w_in, w_out, bias, mask)


def moe_fwd_body(
    h_one, vec, w1, w2, b1, router, router_bias, place_col, place_row,
    out, normed_two, disp, act, slope, picked, gap_out, rows_out, onehot, onehot_t,
):
    fill_onehot(onehot, place_col)
    fill_onehot_t(onehot_t, place_row)
    normal, _ = normalize(h_one[...])
    two = (normal * vec[2:3] + vec[3:4]).astype(BF)
    normed_two[...] = two
    logits = nn(two, router[...])
    gap = (logits[:, LANES:] + router_bias[1:2]) - (logits[:, :LANES] + router_bias[0:1])
    gap = jnp.where(place_col[...] >= SLOTS // 2, gap, -gap)
    gap_out[...] = gap
    gate = 1.0 / (1.0 + jnp.exp(-gap))
    disp[...] = nn(onehot_t[...], two).astype(BF)

    @pl.loop(0, 4, unroll=4)
    def _(t):
        rows = pl.ds(pl.multiple_of(t * 256, 256), 256)
        e = t // 2
        own = disp[rows, :]
        for c in range(3):
            cols = slice(c * 512, (c + 1) * 512)
            pre = nn(own, w1[e, :, cols]) + b1[pl.ds(e, 1), cols]
            phi = 0.5 * (1.0 + lax.erf(pre * 0.7071067811865476))
            act[rows, cols] = (pre * phi).astype(BF)
            slope[rows, cols] = (
                phi + pre * jnp.exp(-0.5 * pre * pre) * 0.3989422804014327
            ).astype(BF)
        rows_out[rows, :] = (nn(act[rows, :], w2[e]) + vec[pl.ds(7 + e, 1)]).astype(BF)

    taken = nn(onehot[...], rows_out[...])
    picked[...] = taken.astype(BF)
    for c in range(3):
        cols = slice(c * LANES, (c + 1) * LANES)
        out[:, cols] = (h_one[:, cols] + gate * taken[:, cols]).astype(out.dtype)


def moe_fwd(h_one, vec, w1, w2, b1, router, router_bias, place, out_dtype, deps=()):
    return call(
        moe_fwd_body,
        (
            sds((CELLS, D), out_dtype),
            sds((CELLS, D), BF),
            sds((SLOTS, D), BF),
            sds((SLOTS, F), BF),
            sds((SLOTS, F), BF),
            sds((CELLS, D), BF),
            sds((CELLS, LANES), F32),
        ),
        9,
        scratch=[pltpu.VMEM((SLOTS, D), BF), ONEHOT, ONEHOT_T],
        us=9.5,
        deps=deps,
    )(h_one, vec, w1, w2, b1, router, router_bias, *place)


def fill_onehot(onehot, place_col):
    @pl.loop(0, 7)
    def _(t):
        rows = pl.ds(pl.multiple_of(t * 112, 112), 112)
        place = jnp.concatenate([place_col[rows, :]] * 8, axis=1)
        same = place == lax.broadcasted_iota(jnp.int32, (112, SLOTS), 1)
        onehot[rows, :] = jnp.where(same, 1.0, 0.0).astype(BF)


def fill_onehot_t(onehot_t, place_row):
    @pl.loop(0, 8)
    def _(t):
        row = lax.broadcasted_iota(jnp.int32, (128, CELLS), 0) + t * 128
        same = row == place_row[0:1, :]
        onehot_t[pl.ds(pl.multiple_of(t * 128, 128), 128), :] = jnp.where(same, 1.0, 0.0).astype(BF)


def moe_bwd_body(
    grad, w2, place_col, place_row, disp, act, slope, picked, gap,
    dw1, dw2, db1, small, g_pre, gate_grad, g_rows, onehot_t,
):
    fill_onehot_t(onehot_t, place_row)
    go = grad[...].astype(F32)
    gate = 1.0 / (1.0 + jnp.exp(-gap[...]))
    other = 1.0 / (1.0 + jnp.exp(gap[...]))
    g_picked = (go * jnp.concatenate([gate] * 3, axis=1)).astype(BF)
    g_gate = jnp.sum(go * picked[...].astype(F32), axis=-1, keepdims=True)
    sign = jnp.where(place_col[...] >= SLOTS // 2, 1.0, -1.0)
    gl = (g_gate * gate * other * sign).astype(BF)
    gate_grad[...] = gl
    small[...] = jnp.zeros((16, D), F32)
    small[9:10, 0:LANES] = jnp.sum(gl.astype(F32), axis=0, keepdims=True)
    g_rows[...] = nn(onehot_t[...], g_picked).astype(BF)

    @pl.loop(0, EXPERTS, unroll=2)
    def _(e):
        both = pl.ds(pl.multiple_of(e * 512, 512), 512)
        own = g_rows[both, :]
        total = []
        grads = [nt(own, w2[e, c * 256 : (c + 1) * 256, :]) for c in range(6)]
        for c, part in enumerate(grads):
            cols = slice(c * 256, (c + 1) * 256)
            gp = (part * slope[both, cols].astype(F32)).astype(BF)
            g_pre[both, cols] = gp
            total.append(jnp.sum(gp.astype(F32), axis=0, keepdims=True))
        db1[pl.ds(e, 1), :] = jnp.concatenate(total, axis=1)
        small[pl.ds(7 + e, 1), :] = jnp.sum(own.astype(F32), axis=0, keepdims=True)
        for c in range(6):
            cols = slice(c * 256, (c + 1) * 256)
            dw1[e, :, cols] = tn(disp[both, :], g_pre[both, cols])
            dw2[e, cols, :] = tn(act[both, cols], own)


def moe_bwd(grad, w2, place, saved):
    return call(
        moe_bwd_body,
        (
            sds((EXPERTS, D, F), F32),
            sds((EXPERTS, F, D), F32),
            sds((8, F), F32),
            sds((16, D), F32),
            sds((SLOTS, F), BF),
            sds((CELLS, LANES), BF),
        ),
        9,
        scratch=[pltpu.VMEM((SLOTS, D), BF), ONEHOT_T],
        us=8,
    )(grad, w2, *place, *saved)


def middle_bwd_body(
    shifted, grad, h_one, vec, w1, w_out, place_col, normed_two, g_pre, gate_grad, mixed,
    grad_one, g_mix, dw_out, drouter, small, onehot, g_disp, patches, windows_of,
):
    fill_onehot(onehot, place_col)
    for e in range(EXPERTS):
        both = slice(e * 512, (e + 1) * 512)
        g_disp[both, :] = nt(g_pre[both, :], w1[e]).astype(BF)
    gl = gate_grad[...].astype(F32)
    g_two = nn(onehot[...], g_disp[...]) + jnp.concatenate([gl] * 3, axis=1) * vec[9:10]
    drouter[...] = tn(gate_grad[...], normed_two[...])[0:8]
    normal, inverse = normalize(h_one[...])
    small[...] = jnp.zeros((16, D), F32)
    small[2:3] = jnp.sum(g_two * normal, axis=0, keepdims=True)
    small[3:4] = jnp.sum(g_two, axis=0, keepdims=True)
    grad_one[...] = grad[...].astype(F32) + norm_backward(g_two, normal, inverse, vec[2:3])
    small[6:7] = jnp.sum(grad_one[...].astype(BF).astype(F32), axis=0, keepdims=True)
    patches[:CELLS, :] = grad_one[...]
    to_windows(patches, windows_of, shifted)
    gao_w = windows_of[...].astype(BF)
    dw_out[...] = tn(mixed[...], gao_w)
    g_mix[...] = nt(gao_w, w_out[...]).astype(BF)


def middle_bwd(shifted, grad, h_one, vec, w1, w_out, place_col, normed_two, g_pre, gate_grad, mixed):
    return call(
        functools.partial(middle_bwd_body, shifted),
        (
            sds((CELLS, D), F32),
            sds((WTOK, D), BF),
            sds((D, D), F32),
            sds((8, D), F32),
            sds((16, D), F32),
        ),
        10,
        scratch=[ONEHOT, pltpu.VMEM((SLOTS, D), BF), PATCHES, PADDED],
        vmem=BIG_VMEM,
        us=5,
    )(grad, h_one, vec, w1, w_out, place_col, normed_two, g_pre, gate_grad, mixed)


def attn_bwd_windows(windows, qkv, g_mix, attn, g_qkv, dbias, base=None):
    masks = head_masks()
    base = windows[0] if base is None else base

    start, stop = windows
    per = min(4, stop - start)

    @pl.loop(0, (stop - start) // per)
    def _(wo):
        units = [(i, g) for i in range(per) for g in range(QUADS)]
        first = [start + wo * per + i for i in range(per)]
        rows = [pl.ds(pl.multiple_of(w * WROWS, WROWS), WROWS) for w in first]
        outs = [pl.ds(pl.multiple_of((w - base) * WROWS, WROWS), WROWS) for w in first]
        cols = [[slice(n * D + g * LANES, n * D + (g + 1) * LANES) for g in range(QUADS)] for n in range(3)]
        d4s = [stack_heads(g_mix[rows[i], cols[0][g]], masks) for i, g in units]
        grads = [nt(qkv[rows[i], cols[2][g]], d4) for (i, g), d4 in zip(units, d4s)]
        probs = [attn[first[i] * QUADS + g] for i, g in units]
        for (i, g), a, d4 in zip(units, probs, d4s):
            g_qkv[outs[i], cols[2][g]] = nn(a, d4).astype(BF)
        dss = []
        for a, grad in zip(probs, grads):
            a = a.astype(F32)
            t = a * grad
            dss.append((t - a * jnp.sum(t, axis=0, keepdims=True)).astype(BF))
        for g in range(QUADS):
            total = dbias[g]
            for (_, other), ds in zip(units, dss):
                if other == g:
                    total = total + ds.astype(F32)
            dbias[g] = total
        talls = [tn(ds, qkv[rows[i], cols[1][g]]) for (i, g), ds in zip(units, dss)]
        for (i, g), ds in zip(units, dss):
            q4 = stack_heads(qkv[rows[i], cols[0][g]], masks)
            g_qkv[outs[i], cols[1][g]] = (nn(ds, q4) * SCALE).astype(BF)
        for (i, g), tall in zip(units, talls):
            g_qkv[outs[i], cols[0][g]] = (fold_heads(tall, masks) * SCALE).astype(BF)


def attn_bwd_body(qkv, attn, g_mix, g_qkv, dbias):
    dbias[...] = jnp.zeros_like(dbias)
    attn_bwd_windows((0, WINDOWS), qkv, g_mix, attn, g_qkv, dbias)


def attn_bwd(qkv, attn, g_mix):
    return call(attn_bwd_body, (sds((WTOK, 3 * D), BF), sds((QUADS, WROWS, PAIR), F32)), 3, us=5)(qkv, attn, g_mix)


def proj_bwd_body(
    shifted, grad_one, hid, vec, w_in, wn, g_qkv, grad_in, dw_in, small, patches, windows_of,
):
    for c in range(3):
        cols = slice(c * D, (c + 1) * D)
        dw_in[:, cols] = tn(wn[...], g_qkv[:, cols])
    windows_of[...] = nt(g_qkv[...], w_in[...])
    to_patches(windows_of, patches, shifted)
    g_normed = patches[:CELLS, :]
    normal, inverse = normalize(hid[...].astype(F32))
    small[...] = jnp.zeros((16, D), F32)
    small[0:1] = jnp.sum(g_normed * normal, axis=0, keepdims=True)
    small[1:2] = jnp.sum(g_normed, axis=0, keepdims=True)
    small[4:5] = jnp.sum(g_qkv[:, :D].astype(F32), axis=0, keepdims=True)
    small[5:6] = jnp.sum(g_qkv[:, 2 * D :].astype(F32), axis=0, keepdims=True)
    grad_in[...] = grad_one[...] + norm_backward(g_normed, normal, inverse, vec[0:1])


def proj_bwd(shifted, grad_one, hid, vec, w_in, wn, g_qkv):
    return call(
        functools.partial(proj_bwd_body, shifted),
        (sds((CELLS, D), F32), sds((D, 3 * D), F32), sds((16, D), F32)),
        6,
        scratch=[PATCHES, PADDED],
        us=0.5,
    )(grad_one, hid, vec, w_in, wn, g_qkv)


def window_perm_t(shifted):
    source = patch_of(jnp.arange(WTOK, dtype=jnp.int32), shifted)
    return (jnp.arange(CELLS, dtype=jnp.int32)[:, None] == source[None, :]).astype(BF)


def wrap_codes(shifted):
    code = np.zeros((CELLS,), np.float32)
    if shifted:
        for r in range(SIDE):
            for s in range(SIDE):
                rr, ss = (r - SHIFT) % SIDE, (s - SHIFT) % SIDE
                code[r * SIDE + s] = 2 * (rr >= SIDE - SHIFT) + (ss >= SIDE - SHIFT)
    return code


def window_masks(items, shifted):
    labels = items.astype(F32)
    if shifted:
        labels = labels * 4.0 + jnp.asarray(wrap_codes(True))
    placed = nn(jnp.broadcast_to((labels + 1.0).astype(BF), (8, CELLS)), window_perm_t(shifted))[0]
    placed = placed.reshape(WINDOWS, WROWS)
    same = (placed[:, :, None] == placed[:, None, :]) & (placed[:, :, None] > 0.0)
    same = same.astype(F32)
    return jnp.concatenate([same, same], axis=2)


def slot_places(routes, slots):
    group = (jnp.arange(CELLS, dtype=jnp.int32) // GROUP) * CAP
    place = routes * (2 * CAP) + group + slots
    return jnp.broadcast_to(place[:, None], (CELLS, LANES)), jnp.broadcast_to(place[None, :], (8, CELLS))

LEAD = 73
SMALL = 9326
LAG = LEAD * LANES - SMALL
VECTORS = 9
LINES = 32
SPANS = ((LEAD, D, 9), (LEAD + 3456, D, 3), (LEAD + 4608, 2 * D, 12), (LEAD + 4608 + 9216, 2 * F, 3))
EDGE = LEAD + 4608
ALIGNED = LEAD + 4608 + 2 * 9216


def relative(k, bits):
    total = 0
    for place, bit in enumerate(bits):
        total = total + (((k >> (len(bits) - 1 - place)) & 1) << bit)
    return total


def lanes_of(count=LANES):
    return lax.broadcasted_iota(jnp.int32, (1, count), 1)


def equal(rows, columns):
    return jnp.where(rows == columns, 1.0, 0.0).astype(BF)


def spread(shape):
    return lax.broadcasted_iota(jnp.int32, shape, 0), lax.broadcasted_iota(jnp.int32, shape, 1)


def exact(left, one, product):
    high = left.astype(BF)
    low = (left - high.astype(F32)).astype(BF)
    return product(high, one) + product(low, one)


def head_major():
    f, g = spread((D, D))
    return equal(f, 12 * (g & 31) + (g >> 5))


def head_rows(m):
    f, g = spread((D, 2 * LANES))
    return equal((f & 31) + 32 * m, g)


def offset_lanes():
    f, g = spread((LANES, LANES))
    i = g & 63
    r = (i * 37) >> 8
    return equal(f, jnp.where(i < WIN * WIN, 13 * r + i - WIN * r, -1))


def turns():
    return [13 * (6 - j // WIN) + 6 - j % WIN for j in range(WIN * WIN)]


def unpack_bias(flat, wide, tall, bias):
    wide[...] = jnp.zeros_like(wide)
    for m in range(6):
        for c in range(3):
            wide[m : m + 1, c * LANES : (c + 1) * LANES] = flat[12 + 3 * m + c : 13 + 3 * m + c, :]
    by_head = nn(wide[...].astype(BF), head_major())
    sub = lax.broadcasted_iota(jnp.int32, (16, D), 0)
    own = (lanes_of(D) >> 5) == sub
    table = jnp.zeros((16, 2 * LANES), F32)
    for m in range(6):
        table = table + nn(jnp.where(own, by_head[m : m + 1], 0.0).astype(BF), head_rows(m))
    tall[...] = jnp.zeros_like(tall)
    for j, turn in enumerate(turns()):
        row = pltpu.roll(table, (2 * LANES - turn) % (2 * LANES), 1)[:, :LANES]
        tall[pl.ds(j, 16, stride=WROWS), :] = row
    tall[...] = nn(tall[...].astype(BF), offset_lanes())
    for g in range(QUADS):
        for t in range(2):
            h = 4 * g + 2 * t
            left, right = tall[h * WROWS : (h + 1) * WROWS], tall[(h + 1) * WROWS : (h + 2) * WROWS]
            bias[g, :, t * LANES : (t + 1) * LANES] = jnp.where(lanes_of() < WROWS, left, right)


def unpack_small(flat, rows, wide, tall, vec, b1, router, router_bias, bias):
    def shifted(first, count, by):
        near, far = flat[first : first + count, :], flat[first + 1 : first + 1 + count, :]
        return pltpu.roll(jnp.where(lanes_of() >= by, near, far), LANES - by, 1)

    rows[0:16, :] = shifted(27, 16, 108)
    rows[16:46, :] = shifted(42, 30, 110)
    vec[...] = jnp.zeros_like(vec)
    b1[...] = jnp.zeros_like(b1)
    for c in range(3):
        cols = slice(c * LANES, (c + 1) * LANES)
        for n in range(4):
            vec[n : n + 1, cols] = flat[3 * n + c : 3 * n + c + 1, :]
        for n in range(3):
            vec[4 + n : 5 + n, cols] = rows[3 * n + c : 3 * n + c + 1, :]
        for e in range(EXPERTS):
            vec[7 + e : 8 + e, cols] = rows[40 + 3 * e + c : 41 + 3 * e + c, :]
    for e in range(EXPERTS):
        for c in range(12):
            b1[e : e + 1, c * LANES : (c + 1) * LANES] = rows[16 + 12 * e + c : 17 + 12 * e + c, :]
        one = jnp.sum(jnp.where(lanes_of() == e, rows[15:16, :], 0.0), axis=1, keepdims=True)
        router_bias[e : e + 1, :] = jnp.broadcast_to(one, (1, LANES))
    pairs = jnp.concatenate([rows[9 + c : 10 + c, :] for c in range(6)], axis=1)
    pairs = jnp.broadcast_to(pairs, (LANES, 2 * D)).astype(BF)
    d, f = spread((D, 2 * D))
    for e in range(EXPERTS):
        router[:, e * LANES : (e + 1) * LANES] = nt(equal(f, 2 * d + e), pairs).astype(BF)
    gap = nt(pairs[0:16], equal(f, 2 * d + 1)) - nt(pairs[0:16], equal(f, 2 * d))
    vec[9:10, :] = gap[0:1]
    unpack_bias(flat, wide, tall, bias)


def unpack_matrices(flat, spans, outs, skipped):
    for (base, height, tiles), out in zip(spans, outs):
        step = 128

        @pl.loop(0, height // step, unroll=min(6, height // step))
        def _(t, base=base, tiles=tiles, out=out):
            first = base - 1 - skipped + t * (step * tiles)
            before = flat[pl.ds(first, step, stride=tiles), :]
            for j in range(tiles):
                here = flat[pl.ds(first + 1 + j, step, stride=tiles), :]
                tile = pltpu.roll(jnp.where(lanes_of() >= LANES - LAG, before, here), LAG, 1)
                out[pl.ds(pl.multiple_of(t * step, step), step), j * LANES : (j + 1) * LANES] = tile.astype(BF)
                before = here


def unpack_head_body(rows, runs, me, *refs):
    got = refs[: len(runs)]
    w_in, w_out, rest, vec, b1, router, router_bias, bias, flat, few, wide, tall = refs[len(runs) :]
    for (bits, fixed), part in zip(runs, got):
        n, half = 1 << len(bits), part.shape[1]

        @pl.loop(0, n)
        def _(k, bits=bits, fixed=fixed, part=part, n=n, half=half):
            d = me[1] ^ (relative(k, bits) + fixed)
            flat[pl.ds(d * rows, half), :] = part[k].astype(F32)
            flat[pl.ds(d * rows + half, rows - half), :] = part[n + k].astype(F32)[: rows - half]

    unpack_small(flat, few, wide, tall, vec, b1, router, router_bias, bias)
    unpack_matrices(flat, SPANS[:2], (w_in, w_out), 0)
    rest[...] = flat[EDGE - 1 : EDGE - 1 + rest.shape[0], :]


def unpack_tail_body(rows, heads, runs, me, rest, *refs):
    got = refs[: len(runs)]
    w1, w2, flat = refs[len(runs) :]
    flat[0 : rest.shape[0], :] = rest[...]
    for (outer, inner, fixed, upper, skip), part in zip(runs, got):
        count = 1 << len(inner)
        half = part.shape[1]
        first = half if upper else 0
        used = min(half, rows - first)

        @pl.loop(0, 3 * count << len(outer), unroll=3)
        def _(k, outer=outer, inner=inner, fixed=fixed, part=part, count=count, first=first, used=used, skip=skip):
            own = (relative(k // (3 * count), outer) + relative(k % count, inner) + fixed) ^ me[1]
            d = ((k // count) % 3 + 1) * heads + own
            flat[pl.ds(d * rows + first - (EDGE - 1), used), :] = part[skip + k].astype(F32)[:used]

    unpack_matrices(flat, SPANS[2:], (w1, w2), EDGE - 1)


class Weights(NamedTuple):
    w_in: Any
    w_out: Any
    w1: Any
    w2: Any
    vec: Any
    b1: Any
    router: Any
    router_bias: Any
    bias: Any


SMALL_SHAPES = (
    sds((16, D), F32),
    sds((8, F), F32),
    sds((D, 2 * LANES), BF),
    sds((8, LANES), F32),
    sds((QUADS, WROWS, PAIR), F32),
)
SMALL_SCRATCH = [pltpu.VMEM((48, LANES), F32), pltpu.VMEM((8, D), F32), pltpu.VMEM((17 * WROWS, LANES), F32)]
HEAD_SHAPES = (sds((D, 3 * D), BF), sds((D, D), BF))
TAIL_SHAPES = (sds((2 * D, F), BF), sds((2 * F, D), BF))


def experts(w1, w2):
    return w1.reshape(EXPERTS, D, F), w2.reshape(EXPERTS, F, D)


def unpack_head(me, parts, runs, rows, devices):
    heads = devices // 4
    w_in, w_out, rest, *small = call(
        functools.partial(unpack_head_body, rows, runs),
        HEAD_SHAPES + (sds((heads * rows - EDGE + 1, LANES), F32),) + SMALL_SHAPES,
        1 + len(parts),
        scratch=[pltpu.VMEM((heads * rows + 8, LANES), F32)] + SMALL_SCRATCH,
        smem=1,
        us=4,
    )(me, *parts)
    return Weights(w_in, w_out, None, None, *small), rest


def unpack_tail(me, rest, parts, runs, rows, devices):
    return experts(
        *call(
            functools.partial(unpack_tail_body, rows, devices // 4, runs),
            TAIL_SHAPES,
            2 + len(parts),
            scratch=[pltpu.VMEM((devices * rows - EDGE + 9, LANES), F32)],
            smem=1,
            vmem=BIG_VMEM,
            us=4,
        )(me, rest, *parts)
    )


def pack_bias(dbias, wide, tall):
    tall[HEADS * WROWS :, :] = jnp.zeros((5 * WROWS, LANES), F32)
    for h in range(HEADS):
        g, t, side = h // 4, (h % 4) // 2, h % 2
        tile = dbias[g, :, t * LANES : (t + 1) * LANES]
        tall[h * WROWS : (h + 1) * WROWS, :] = jnp.where((lanes_of() >> 6) == side, tile, 0.0)
    used = HEADS * WROWS
    tall[0:used, :] = exact(tall[0:used, :], offset_lanes(), nt)
    table = jnp.zeros((16, 2 * LANES), F32)
    for j, turn in enumerate(turns()):
        row = tall[pl.ds(j, 16, stride=WROWS), :]
        table = table + pltpu.roll(jnp.concatenate([row, jnp.zeros_like(row)], axis=1), turn, 1)
    sub = lax.broadcasted_iota(jnp.int32, (16, D), 0)
    own = (lanes_of(D) >> 5) == sub
    wide[...] = jnp.zeros_like(wide)
    for m in range(6):
        placed = jnp.where(own, exact(table, head_rows(m), nt), 0.0)
        wide[m : m + 1, :] = jnp.sum(placed, axis=0, keepdims=True)
    wide[...] = exact(wide[...], head_major(), nt)


def pack_small(al, vectors, drouter, db1, dbias, one, two, wide, tall):
    one[...] = jnp.zeros_like(one)
    two[...] = jnp.zeros_like(two)
    pack_bias(dbias, wide, tall)
    d, f = spread((D, 2 * D))
    signs = equal(f, 2 * d + 1) - equal(f, 2 * d)
    pairs = exact(drouter[...], signs, nn)
    for c in range(3):
        cols = slice(c * LANES, (c + 1) * LANES)
        for n in range(4):
            one[1 + 3 * n + c : 2 + 3 * n + c, :] = vectors[n : n + 1, cols]
        for m in range(6):
            one[13 + 3 * m + c : 14 + 3 * m + c, :] = wide[m : m + 1, cols]
        for n in range(3):
            two[1 + 3 * n + c : 2 + 3 * n + c, :] = vectors[4 + n : 5 + n, cols]
        for e in range(EXPERTS):
            al[67 + 3 * e + c : 68 + 3 * e + c, :] = vectors[7 + e : 8 + e, cols]
    for c in range(6):
        two[10 + c : 11 + c, :] = pairs[0:1, c * LANES : (c + 1) * LANES]
    total = vectors[9:10, 0:LANES]
    two[16:17, :] = jnp.where(lanes_of() == 0, -total, jnp.where(lanes_of() == 1, total, 0.0))
    for e in range(EXPERTS):
        for c in range(12):
            al[43 + 12 * e + c : 44 + 12 * e + c, :] = db1[e : e + 1, c * LANES : (c + 1) * LANES]
    first = pltpu.roll(jnp.where(lanes_of() >= LANES - 18, one[0:28, :], one[1:29, :]), 18, 1)
    second = pltpu.roll(jnp.where(lanes_of() >= LANES - 126, two[0:16, :], two[1:17, :]), 126, 1)
    al[27:43, :] = second
    al[0:27, :] = first[0:27]
    al[27:28, :] += first[27:28]


def pack_matrices(al, spans, grads, skipped):
    for (base, height, tiles), grad in zip(spans, grads):
        step = 128

        @pl.loop(0, height // step, unroll=min(6, height // step))
        def _(t, base=base, tiles=tiles, grad=grad):
            first = base - skipped + t * (step * tiles)
            own = pl.ds(pl.multiple_of(t * step, step), step)
            for j in range(tiles):
                al[pl.ds(first + j, step, stride=tiles), :] = grad[own, j * LANES : (j + 1) * LANES]


def clear(al, first):
    al[pl.ds(first, al.shape[0] - first), :] = jnp.zeros((al.shape[0] - first, LANES), F32)


def pack_head_body(
    rows, padded, runs, me, moe, attn, proj, drouter, db1, dbias, dw_in, dw_out, rest,
    keep, send, al, vectors, lines, one, two, wide, tall,
):
    vectors[...] = moe[...] + attn[...] + proj[...]
    lines[...] = jnp.zeros_like(lines)
    for n in range(VECTORS):
        for c in range(3):
            lines[3 * n + c : 3 * n + c + 1, :] = vectors[n : n + 1, c * LANES : (c + 1) * LANES]
    pack_small(al, vectors, drouter, db1, dbias, one, two, wide, tall)
    pack_matrices(al, SPANS[:2], (dw_in, dw_out), 0)
    al[EDGE : EDGE + rest.shape[0], :] = rest[...]
    at = 0
    for bits, fixed in runs:
        for other, out in enumerate((keep, send)):

            @pl.loop(0, 1 << len(bits))
            def _(k, bits=bits, fixed=fixed, at=at, other=other, out=out):
                d = me[1] ^ (relative(k, bits) + fixed + other)
                out[at + k, :padded, :] = al[pl.ds(d * rows, padded), :].astype(BF)
                out[at + k, padded:, :] = lines[...].astype(BF)

        at += 1 << len(bits)


def pack_tail_body(rows, padded, heads, runs, me, dw1, dw2, keep, send, rest, al):
    clear(al, ALIGNED - EDGE)
    pack_matrices(al, SPANS[2:], (dw1, dw2), EDGE)
    rest[...] = al[0 : rest.shape[0], :]
    half = padded // 2
    at = 0
    for outer, inner, fixed, upper in runs:
        count = 1 << len(inner)
        total = 3 * count << len(outer)
        for other, out in enumerate((keep, send)):

            @pl.loop(0, total, unroll=3)
            def _(k, outer=outer, inner=inner, fixed=fixed, upper=upper, count=count, at=at, other=other, out=out):
                own = (relative(k // (3 * count), outer) + relative(k % count, inner) + fixed + other) ^ me[1]
                d = ((k // count) % 3 + 1) * heads + own
                out[at + k] = al[pl.ds(d * rows + (half if upper else 0) - EDGE, half), :].astype(BF)

        at += total


SMALL_PACK = [
    pltpu.VMEM((40, LANES), F32),
    pltpu.VMEM((24, LANES), F32),
    pltpu.VMEM((8, D), F32),
    pltpu.VMEM((17 * WROWS, LANES), F32),
]


def pack_head(me, small, dw_in, dw_out, rest, runs, rows, devices, padded):
    heads = devices // 4
    shape = sds((heads // 2, padded + LINES, LANES), BF)
    return call(
        functools.partial(pack_head_body, rows, padded, runs),
        (shape, shape),
        10,
        scratch=[
            pltpu.VMEM((EDGE + rest.shape[0], LANES), F32),
            pltpu.VMEM((16, D), F32),
            pltpu.VMEM((LINES, LANES), F32),
        ]
        + SMALL_PACK,
        smem=1,
        us=0.5,
    )(me, *small, dw_in, dw_out, rest)


def pack_tail(me, dw1, dw2, runs, rows, devices, padded):
    heads = devices // 4
    shape = sds((3 * heads, padded // 2, LANES), BF)
    over = -(-(heads * rows + padded - EDGE) // 8) * 8
    return call(
        functools.partial(pack_tail_body, rows, padded, heads, runs),
        (shape, shape, sds((over, LANES), F32)),
        3,
        scratch=[pltpu.VMEM((devices * rows + padded - EDGE, LANES), F32)],
        smem=1,
        vmem=BIG_VMEM,
        us=3,
    )(me, dw1.reshape(2 * D, F), dw2.reshape(2 * F, D))


def levels_body(sources, me, *refs):
    pieces, (x, y, head) = refs[: len(refs) - 3], refs[len(refs) - 3 :]
    n, half = head.shape[0] // 2, x.shape[1]
    for level in range(4):
        for step, (at, first) in enumerate(sources):

            @pl.when((me[2] ^ step) == level)
            def _(level=level, at=at, first=first):
                for i in range(n):
                    lower, upper = pieces[at][first * n + i, :half, :], pieces[at][first * n + i, half:, :]
                    if level == 0:
                        for out in (x, y, head):
                            out[i] = lower
                            out[n + i] = upper
                    else:
                        x[(1 + level) * n + i] = lower
                        y[(1 + level) * n + i] = upper


def levels(me, *pieces):
    sources = ((0, 0), (1, 0), (2, 0), (3, 0)) if len(pieces) == 4 else ((0, 0), (1, 0), (0, 1), (1, 1))
    n, padded, _ = pieces[0].shape
    n = n * len(pieces) // 4
    dtype = pieces[0].dtype
    shapes = [sds((count * n, padded // 2, LANES), dtype) for count in (5, 5, 2)]
    return call(functools.partial(levels_body, sources), shapes, 1 + len(pieces), smem=1)(me, *pieces)


def targets_body(with_head, me, a, a_got, b, b_got, *refs):
    *head, keep, send = refs
    n, half = keep.shape[0] // 2, a.shape[1]
    places = {0: (keep, 0), 2: (keep, n), 1: (send, 0), 3: (send, n)}
    for step, (out, first) in places.items():
        level = me[2] ^ step

        @pl.when(level == 0)
        def _(out=out, first=first):
            for i in range(n):
                if with_head:
                    out[first + i] = head[0][i, : 2 * half, :].astype(out.dtype)
                else:
                    out[first + i] = jnp.zeros((2 * half, LANES), out.dtype)

        @pl.when(level > 0)
        def _(out=out, first=first, level=level):
            for i in range(n):
                at = (level - 1) * n + i
                out[first + i, :half, :] = (a[at] + a_got[at].astype(F32)).astype(out.dtype)
                out[first + i, half:, :] = (b[at] + b_got[at].astype(F32)).astype(out.dtype)


def targets(me, a, a_got, b, b_got, *head):
    n, half, _ = a.shape
    n = n // 3
    shape = (2 * n, 2 * half, LANES)
    return call(
        functools.partial(targets_body, bool(head)), (sds(shape, F32), sds(shape, BF)), 5 + len(head), smem=1
    )(me, a, a_got, b, b_got, *head)


def combine_body(plan, count, *refs):
    for (size, _, terms), out in zip(plan, refs[count:]):

        @pl.loop(0, size)
        def _(i, terms=terms, out=out):
            parts = [refs[at][first + i].astype(F32) for at, first in terms]
            while len(parts) > 1:
                parts = [sum(parts[at + 1 : at + 2], parts[at]) for at in range(0, len(parts), 2)]
            out[i] = parts[0].astype(out.dtype)


def combine(plan, *arrays):
    tail = arrays[0].shape[1:]
    shapes = [sds((size, *tail), dtype) for size, dtype, _ in plan]
    return call(functools.partial(combine_body, plan, len(arrays)), shapes, len(arrays))(*arrays)


def finish_body(rows, me, keep, got, upper_keep, upper_got, out):
    def shift(keep, got):
        total = keep[0] + got[0].astype(F32)
        here, below = total[0:rows, :], total[1 : rows + 1, :]
        out[...] = pltpu.roll(jnp.where(lanes_of() >= LAG, here, below), LANES - LAG, 1)

    pl.when(me[2] == 0)(lambda: shift(keep, got))
    pl.when(me[2] != 0)(lambda: shift(upper_keep, upper_got))


def finish(me, rows, lowest, upper):
    parts = (lowest.keep, lowest.got, upper.keep, upper.got)
    return call(functools.partial(finish_body, rows), sds((rows, LANES), F32), 5, smem=1)(me, *parts)


def join_body(skip, a, b, out):
    n = out.shape[0] // 2

    @pl.loop(0, n)
    def _(i):
        out[i] = a[skip + i]
        out[n + i] = b[skip + i]


def join(a, b, skip=0):
    shape = sds((2 * (a.shape[0] - skip), *a.shape[1:]), a.dtype)
    return call(functools.partial(join_body, skip), shape, 2)(a, b)


class Ways(NamedTuple):
    core: Any
    x: Any
    y: Any
    low: Any
    high: Any
    rest: Any


def ways():
    dp, fsdp = (lax.axis_size(axis).bit_length() - 1 for axis in (DP, FSDP))
    rest = [1 << (fsdp + bit) for bit in range(1, dp - 2)] + [1 << bit for bit in range(2, fsdp)]
    return Ways(1, 2, 1 << fsdp, 1 << (fsdp + dp - 2), 1 << (fsdp + dp - 1), rest)


def device_count():
    return lax.axis_size(DP) * lax.axis_size(FSDP)


def flip(array, step):
    return lax.ppermute(array, (DP, FSDP), [(i, i ^ step) for i in range(device_count())])


def move(array, levels):
    width = device_count() // 4
    pairs = [(a * width + i, b * width + i) for a, b in levels.items() for i in range(width)]
    return lax.ppermute(array, (DP, FSDP), pairs)


def tie(arrays, *others):
    if isinstance(arrays, tuple):
        return tuple(tie(array, *others) for array in arrays)
    return lax.optimization_barrier((arrays, *others))[0]


def sync(*arrays):
    return lax.optimization_barrier(arrays)


def bits_of(*steps):
    return [step.bit_length() - 1 for step in steps]


class Gather:
    def __init__(self, own, way, me):
        for extra in way.rest:
            own = join(own, flip(own, extra))
        self.way, self.own, self.me, self.others = way, own, me, None
        self.rest = bits_of(*reversed(way.rest))

    def far(self):
        own, way = self.own, self.way
        self.others = own, flip(own, way.low), flip(own, way.high), flip(own, way.low + way.high)

    def high(self):
        self.other = flip(self.own, self.way.high)

    def low(self):
        self.pair = join(self.own, self.other)
        self.over = flip(self.pair, self.way.low)

    def levels(self):
        pieces = self.others if self.others else (self.pair, self.over)
        self.x, self.y, self.head = levels(self.me, *pieces)

    def near(self):
        way = self.way
        self.got = [flip(self.x, way.x), flip(self.y, way.y), flip(self.head, way.x + way.y)]

    def near_core(self):
        way, core = self.way, self.way.core
        x, y, both = self.got
        sides = [[self.x, x, y, both, self.y]]
        sides.append([flip(part, core) for part in sides[0]])
        self.head_parts, self.head_runs, self.parts, self.runs = [], [], [], []
        for fixed, side in zip((0, core), sides):
            self.head_parts += side[:4]
            self.head_runs += [(self.rest, step + fixed) for step in (0, way.x, way.y, way.x + way.y)]
            x_own, x_got, y_got, _, y_own = side
            self.parts += [x_own, x_got, y_own, y_got]
            skip = 2 << len(self.rest)
            self.runs += [([], self.rest, fixed + step, False, skip) for step in (0, way.x)]
            self.runs += [([], self.rest, fixed + step, True, skip) for step in (0, way.y)]

    def last(self):
        way, skip = self.way, 2 << len(self.rest)
        self.joined = join(self.x, self.got[0], skip), join(self.y, self.got[1], skip)
        self.last_got = flip(self.joined[0], way.y), flip(self.joined[1], way.x)

    def last_core(self):
        way = self.way
        for fixed in (0, way.core):
            self.parts += [flip(part, way.core) for part in self.last_got] if fixed else list(self.last_got)
            self.runs += [(bits_of(way.x), self.rest, way.y + fixed, False, 0)]
            self.runs += [(bits_of(way.y), self.rest, way.x + fixed, True, 0)]


def head_runs(way):
    rest = bits_of(*way.rest)
    return [(rest, step) for step in (way.y, way.x + way.y, way.x, 0)]


def tail_runs(way):
    rest, bx, by = (bits_of(*steps) for steps in (way.rest, [way.x], [way.y]))
    return [
        (bx, rest, way.y, False), ([], rest, way.x, False), ([], rest, 0, False),
        (by, rest, way.x, True), ([], rest, way.y, True), ([], rest, 0, True),
    ]


class HeadScatter:
    def __init__(self, keep, send, way):
        self.way, self.keep, self.n = way, keep, keep.shape[0] // 4
        self.got = flip(send, way.core)

    def plane(self):
        n, way = self.n, self.way
        y, xy, x, self.keep = combine([(n, BF, ((0, i * n), (1, i * n))) for i in range(4)], self.keep, self.got)
        self.got = flip(x, way.x), flip(y, way.y), flip(xy, way.x + way.y)

    def near(self):
        n = 2 * self.n
        sent, self.keep = combine([(n, BF, ((0, i * n), (1, i * n))) for i in range(2)], self.keep, self.got)
        self.got = flip(sent, self.way.y)

    def next(self):
        n = self.n
        sent, self.keep = combine(((n, BF, ((0, 0), (1, n))), (n, BF, ((0, n), (1, 0)))), self.keep, self.got)
        self.got = flip(sent, self.way.x)

    def add(self):
        n, got = self.n, self.got if isinstance(self.got, (tuple, list)) else (self.got,)
        terms = tuple((i, 0) for i in range(1 + len(got)))
        sent, self.keep = combine(((n, BF, terms), (n, F32, terms)), self.keep, *got)
        return sent

    def lines(self):
        return self.keep[0, -LINES : 3 * VECTORS - LINES].reshape(VECTORS, D)

    def low(self, sent):
        self.got = move(sent, {1: 0, 3: 2})

    def high(self):
        self.got = move(self.add(), {2: 0})
        self.keep, self.got = fold(self.keep, self.got, self.way.rest)


class TailScatter:
    def __init__(self, keep, send, way, me):
        self.way, self.keep, self.n, self.me = way, keep, keep.shape[0] // 24, me
        self.got = flip(send, way.core)

    def near(self):
        n = 6 * self.n
        plan = [(n, dtype, ((0, first), (1, first))) for dtype, first in ((BF, 0), (F32, n), (BF, 2 * n), (F32, 3 * n))]
        a, self.a, b, self.b = combine(plan, self.keep, self.got)
        self.a_got, self.b_got = flip(a, self.way.y), flip(b, self.way.x)

    def next(self):
        n = 3 * self.n
        plan = [(n, BF, ((0, 0), (1, n))), (n, F32, ((0, n), (1, 0)))]
        plan += [(n, BF, ((2, 0), (3, n))), (n, F32, ((2, n), (3, 0)))]
        a, self.a, b, self.b = combine(plan, self.a, self.a_got, self.b, self.b_got)
        self.a_got, self.b_got = flip(a, self.way.x), flip(b, self.way.y)

    def low(self, *head):
        self.keep, sent = targets(self.me, self.a, self.a_got, self.b, self.b_got, *head)
        self.got = flip(sent, self.way.low)

    def high(self):
        self.keep, self.got = fold(self.keep, self.got, [self.way.high] + self.way.rest)


def fold(keep, got, steps):
    for way in steps:
        half = keep.shape[0] // 2
        plan = ((half, BF, ((0, half), (1, half))), (half, F32, ((0, 0), (1, 0))))
        sent, keep = combine(plan, keep, got)
        got = flip(sent, way)
    return keep, got


def shards(inputs, items, routes, slots, cotangent, params, momentum, average):
    fsdp, dp = lax.axis_size(FSDP), lax.axis_size(DP)
    devices = fsdp * dp
    share = params.shape[1]
    rows = share // LANES
    padded = -(-(rows + 1) // 32) * 32
    step_rate = RATE_BASE / math.sqrt(CELLS * devices)
    way = ways()
    own = lax.axis_index(DP) * fsdp + lax.axis_index(FSDP)
    me = jnp.stack([own, own % (devices // 4), own // (devices // 4)]).astype(jnp.int32)

    def share_of(flat):
        return jnp.pad(flat.astype(BF).reshape(1, rows, LANES), ((0, 0), (0, padded - rows), (0, 0)))

    one = Gather(share_of(params[0]), way, me)
    one.far()
    two = Gather(share_of(tie(params[1], one.others[1])), way, me)
    masks, places = [], []
    for b in range(BLOCKS):
        masks.append(window_masks(items.reshape(CELLS), b % 2 == 1))
        places.append(slot_places(routes[b].reshape(CELLS), slots[b].reshape(CELLS)))

    hidden_zero = inputs.reshape(CELLS, D)
    one.levels()
    one.near()
    two.own = tie(two.own, one.head)
    two.high()
    one.got[0] = tie(one.got[0], *masks)
    two.other, *one.got = sync(two.other, *one.got)
    one.near_core()
    one.last()
    two.low()
    one.head_parts[0] = tie(one.head_parts[0], two.pair, *one.joined, *one.parts)
    w, rest = unpack_head(me, one.head_parts, one.head_runs, rows, devices)
    h_zero, *attn_zero = attn_fwd(False, hidden_zero, w.vec, w.w_in, w.w_out, w.bias, masks[0])
    h_zero, two.over = sync(h_zero, two.over)
    two.levels()
    two.near()
    one.last_got = tie(one.last_got, two.head)
    one.last_core()
    w1, w2 = unpack_tail(me, tie(rest, two.head), one.parts, one.runs, rows, devices)
    w_zero = w._replace(w1=w1, w2=w2)
    w = w_zero
    hidden_one, *moe_zero = moe_fwd(h_zero, w.vec, w.w1, w.w2, w.b1, w.router, w.router_bias, places[0], F32)

    hidden_one, *two.got = sync(hidden_one, *two.got)
    two.near_core()
    two.last()
    two.head_parts[0] = tie(two.head_parts[0], *two.joined, *two.parts)
    w, rest = unpack_head(me, two.head_parts, two.head_runs, rows, devices)
    h_one, *attn_one = attn_fwd(True, hidden_one, w.vec, w.w_in, w.w_out, w.bias, masks[1])
    h_one, *two.last_got = sync(h_one, *two.last_got)
    two.last_core()
    w1, w2 = unpack_tail(me, rest, two.parts, two.runs, rows, devices)
    w_one = w._replace(w1=w1, w2=w2)
    w = w_one
    outputs, *moe_one = moe_fwd(h_one, w.vec, w.w1, w.w2, w.b1, w.router, w.router_bias, places[1], BF)

    gradient = cotangent.reshape(CELLS, D)
    wn, qkv, mixed, attn = attn_one
    normed_two, *saved = moe_one
    dw1, dw2, db1, small_moe, g_pre, gate_grad = moe_bwd(gradient, w.w2, places[1], saved)
    keep, send, rest = pack_tail(me, dw1, dw2, tail_runs(way), rows, devices, padded)
    tail_one = TailScatter(keep, send, way, me)
    g_one, g_mix, dw_out, drouter, small_mid = middle_bwd(
        True, gradient, h_one, w.vec, w.w1, w.w_out, places[1][0], normed_two, tie(g_pre, send), gate_grad, mixed
    )
    g_mix, tail_one.got = sync(g_mix, tail_one.got)
    tail_one.near()
    g_qkv, dbias = attn_bwd(qkv, attn, tie(g_mix, tail_one.a))
    gradient, dw_in, small_attn = proj_bwd(True, g_one, hidden_one, w.vec, w.w_in, wn, g_qkv)
    small = (small_moe, small_mid, small_attn, drouter, db1, dbias)
    keep, send = pack_head(me, small, dw_in, dw_out, rest, head_runs(way), rows, devices, padded)
    send, tail_one.a_got, tail_one.b_got, gradient = sync(send, tail_one.a_got, tail_one.b_got, gradient)
    head_one = HeadScatter(keep, send, way)
    tail_one.next()

    w = w_zero
    wn, qkv, mixed, attn = attn_zero
    normed_two, *saved = moe_zero
    gradient = tie(gradient, tail_one.a)
    dw1, dw2, db1, small_moe, g_pre, gate_grad = moe_bwd(gradient, w.w2, places[0], saved)
    g_pre, dw2, head_one.got, tail_one.a_got, tail_one.b_got = sync(
        g_pre, dw2, head_one.got, tail_one.a_got, tail_one.b_got
    )
    head_one.near()
    tail_one.low()
    keep, send, rest = pack_tail(me, dw1, tie(dw2, head_one.keep, tail_one.keep), tail_runs(way), rows, devices, padded)
    tail_zero = TailScatter(keep, send, way, me)
    g_one, g_mix, dw_out, drouter, small_mid = middle_bwd(
        False, gradient, h_zero, w.vec, w.w1, w.w_out, places[0][0], normed_two, tie(g_pre, send), gate_grad, mixed
    )
    g_mix, tail_zero.got = sync(g_mix, tail_zero.got)
    tail_zero.near()
    g_qkv, dbias = attn_bwd(qkv, attn, tie(g_mix, tail_zero.a))
    g_qkv, tail_one.got, head_one.got = sync(g_qkv, tail_one.got, head_one.got)
    head_one.next()
    tail_one.high()
    gradient, dw_in, small_attn = proj_bwd(
        False, tie(g_one, head_one.keep, tail_one.keep), hidden_zero, w.vec, w.w_in, wn, g_qkv
    )
    small = (small_moe, small_mid, small_attn, drouter, db1, dbias)
    keep, send = pack_head(me, small, dw_in, dw_out, rest, head_runs(way), rows, devices, padded)
    send, tail_zero.a_got, tail_zero.b_got, head_one.got, tail_one.got = sync(
        send, tail_zero.a_got, tail_zero.b_got, head_one.got, tail_one.got
    )

    head_zero = HeadScatter(keep, send, way)
    tail_zero.next()
    head_zero.plane()
    head_one.add()
    tail_zero.low(head_one.keep)
    sent = head_zero.add()
    head_zero.low(sent)
    vector_grads = jnp.stack([head_zero.lines(), head_one.lines()])
    got = flip(vector_grads, way.low)
    tail_zero.high()
    vector_grads = vector_grads + got
    head_zero.keep = tie(head_zero.keep, vector_grads)
    head_zero.high()
    for step in [way.high] + way.rest:
        vector_grads = vector_grads + flip(vector_grads, step)
    grads_zero = finish(me, rows, head_zero, tail_zero)
    grads_one = finish(me, rows, tail_zero, tail_one)
    grad_all = jnp.stack([grads_zero.reshape(-1), grads_one.reshape(-1)])
    new_momentum = MOMENTUM_DECAY * momentum + grad_all
    new_params = params - step_rate * (grad_all + MOMENTUM_DECAY * new_momentum)
    new_average = AVERAGE_DECAY * average + (1.0 - AVERAGE_DECAY) * new_params
    return (
        outputs.reshape(1, CELLS, D),
        gradient.reshape(1, CELLS, D),
        new_params,
        new_momentum,
        new_average,
        vector_grads,
    )


def solution(mesh):
    both = (DP, FSDP)
    canvas, vector = P(both), P(None, both)
    return jax.shard_map(
        shards,
        mesh=mesh,
        in_specs=(canvas, canvas, vector, vector, canvas, vector, vector, vector),
        out_specs=(canvas, canvas, vector, vector, vector, P()),
        check_vma=False,
    )
```

```python
import functools
import math
from typing import Any, NamedTuple

import jax
import jax.numpy as jnp
import numpy as np
from jax import lax
from jax.experimental import pallas as pl
from jax.experimental.pallas import tpu as pltpu
from jax.sharding import PartitionSpec as P

D = 384
HEADS = 12
F = 1536
HEAD_DIM = 32
EXPERTS = 2
CAP = 256
SIDE = 28
WIN = 7
SHIFT = 3
BLOCKS = 2
CELLS = 784
GROUP = 392
RELS = 169
NORM_EPSILON = 1e-05
MOMENTUM_DECAY = 0.9
AVERAGE_DECAY = 0.9
RATE_BASE = 0.1

DP = "dp"
FSDP = "fsdp"
LANES = 128
WROWS = 64
WINDOWS = 16
WTOK = WINDOWS * WROWS
SLOTS = EXPERTS * 2 * CAP
PAIR = 4 * WROWS
QUADS = HEADS // 4
SCALE = HEAD_DIM ** (-0.5)
US_FLOPS = 1.0e9
BF = jnp.bfloat16
F32 = jnp.float32
VMEM_BYTES = 8 * 1024 * 1024
BIG_VMEM = 13 * 1024 * 1024


def call(body, out_shape, n_in, scratch=(), smem=0, deps=(), us=1, vmem=VMEM_BYTES):
    def skipping(*refs):
        body(*refs[:n_in], *refs[n_in + len(deps) :])

    run = pl.pallas_call(
        skipping,
        out_shape=out_shape,
        in_specs=[pl.BlockSpec(memory_space=pltpu.SMEM)] * smem
        + [pl.BlockSpec(memory_space=pltpu.VMEM)] * (n_in - smem)
        + [pl.BlockSpec(memory_space=pl.ANY)] * len(deps),
        out_specs=jax.tree.map(lambda _: pl.BlockSpec(memory_space=pltpu.VMEM), out_shape),
        scratch_shapes=list(scratch),
        compiler_params=pltpu.CompilerParams(vmem_limit_bytes=vmem),
        cost_estimate=pl.CostEstimate(flops=int(us * US_FLOPS), bytes_accessed=0, transcendentals=0),
    )
    return lambda *args: run(*args, *deps)


def sds(shape, dtype):
    return jax.ShapeDtypeStruct(shape, dtype)


def nn(a, b):
    return lax.dot_general(a, b, (((1,), (0,)), ((), ())), preferred_element_type=F32)


def nt(a, b):
    return lax.dot_general(a, b, (((1,), (1,)), ((), ())), preferred_element_type=F32)


def tn(a, b):
    return lax.dot_general(a, b, (((0,), (0,)), ((), ())), preferred_element_type=F32)


def normalize(hidden):
    centre = hidden - jnp.mean(hidden, axis=-1, keepdims=True)
    inverse = lax.rsqrt(jnp.mean(centre * centre, axis=-1, keepdims=True) + NORM_EPSILON)
    return centre * inverse, inverse


def norm_backward(grad_normed, normal_rows, inverse, gain_row):
    scaled = grad_normed * gain_row
    return inverse * (
        scaled
        - jnp.mean(scaled, axis=-1, keepdims=True)
        - normal_rows * jnp.mean(scaled * normal_rows, axis=-1, keepdims=True)
    )


def head_masks():
    lane = lax.broadcasted_iota(jnp.int32, (1, LANES), 1) // HEAD_DIM
    return [lane == h for h in range(4)]


def stack_heads(rows, masks):
    zero = jnp.zeros_like(rows)
    return jnp.concatenate([jnp.where(mask, rows, zero) for mask in masks], axis=0)


def fold_heads(tall, masks):
    out = jnp.where(masks[0], tall[0:WROWS], 0.0)
    for h in range(1, 4):
        out = jnp.where(masks[h], tall[h * WROWS : (h + 1) * WROWS], out)
    return out


def patch_of(row, shifted):
    w, p = row >> 6, row & 63
    pr = (p * 37) >> 8
    r = (w >> 2) * WIN + pr
    s = (w & 3) * WIN + p - pr * WIN
    if shifted:
        r, s = r + SHIFT, s + SHIFT
        r = jnp.where(r >= SIDE, r - SIDE, r)
        s = jnp.where(s >= SIDE, s - SIDE, s)
    return jnp.where(p < WIN * WIN, r * SIDE + s, -1)


def runs_of(shifted):
    runs = []
    for w in range(WINDOWS):
        for p in range(WIN):
            r, s = (w // 4) * WIN + p, (w % 4) * WIN
            if shifted:
                r, s = (r + SHIFT) % SIDE, s + SHIFT
            here = min(WIN, SIDE - s)
            runs.append((w * WROWS + p * WIN, r * SIDE + s, here))
            if here < WIN:
                runs.append((w * WROWS + p * WIN + here, r * SIDE, WIN - here))
    return runs


def to_windows(patches, windows, shifted):
    windows[...] = jnp.zeros_like(windows)
    for row, patch, length in runs_of(shifted):
        windows[row : row + length, :] = patches[patch : patch + length, :]


def to_patches(windows, patches, shifted):
    for row, patch, length in runs_of(shifted):
        patches[patch : patch + length, :] = windows[row : row + length, :]


PATCHES = pltpu.VMEM((CELLS + 8, D), F32)
PADDED = pltpu.VMEM((WTOK, D), F32)
ONEHOT = pltpu.VMEM((CELLS, SLOTS), BF)
ONEHOT_T = pltpu.VMEM((SLOTS, CELLS), BF)


def attn_fwd_body(shifted, hid, vec, w_in, w_out, bias, mask, h_one, wn, qkv, mixed, attn, patches, windows):
    normal, _ = normalize(hid[...].astype(F32))
    patches[:CELLS, :] = normal * vec[0:1] + vec[1:2]
    to_windows(patches, windows, shifted)
    wn[...] = windows[...].astype(BF)
    in_bias = jnp.concatenate([vec[4:5], jnp.zeros((1, D), F32), vec[5:6]], axis=1)

    @pl.loop(0, 4)
    def _(t):
        rows = pl.ds(pl.multiple_of(t * 256, 256), 256)
        qkv[rows, :] = (nn(wn[rows, :], w_in[...]) + in_bias).astype(BF)

    masks = head_masks()

    @pl.loop(0, WINDOWS // 8)
    def _(wo):
        units = [(i, g) for i in range(8) for g in range(QUADS)]
        rows = [pl.ds(pl.multiple_of((wo * 8 + i) * WROWS, WROWS), WROWS) for i in range(8)]
        allow = []
        for i in range(8):
            one = mask[wo * 8 + i] > 0.0
            allow.append(jnp.concatenate([one, one], axis=1))
        scores = []
        for i, g in units:
            q4 = stack_heads(qkv[rows[i], g * LANES : (g + 1) * LANES], masks)
            scores.append(nt(qkv[rows[i], D + g * LANES : D + (g + 1) * LANES], q4))
        probs = []
        for (i, g), s in zip(units, scores):
            s = jnp.where(allow[i], s * SCALE + bias[g], -1e30)
            e = jnp.exp(s - jnp.max(s, axis=0, keepdims=True))
            a = (e * (1.0 / jnp.sum(e, axis=0, keepdims=True))).astype(BF)
            attn[(wo * 8 + i) * QUADS + g] = a
            probs.append(a)
        tall = [tn(a, qkv[rows[i], 2 * D + g * LANES : 2 * D + (g + 1) * LANES]) for (i, g), a in zip(units, probs)]
        for (i, g), t in zip(units, tall):
            t = fold_heads(t, masks)
            windows[rows[i], g * LANES : (g + 1) * LANES] = t
            mixed[rows[i], g * LANES : (g + 1) * LANES] = t.astype(BF)

    to_patches(windows, patches, shifted)
    h_one[...] = hid[...].astype(F32) + nn(patches[:CELLS, :].astype(BF), w_out[...]) + vec[6:7]


def attn_fwd(shifted, hid, vec, w_in, w_out, bias, mask, deps=()):
    return call(
        functools.partial(attn_fwd_body, shifted),
        (
            sds((CELLS, D), F32),
            sds((WTOK, D), BF),
            sds((WTOK, 3 * D), BF),
            sds((WTOK, D), BF),
            sds((WINDOWS * QUADS, WROWS, PAIR), BF),
        ),
        6,
        scratch=[PATCHES, PADDED],
        us=8,
        deps=deps,
    )(hid, vec, w_in, w_out, bias, mask)


def moe_fwd_body(
    h_one, vec, w1, w2, b1, router, router_bias, place_col, place_row,
    out, normed_two, disp, act, slope, picked, gap_out, rows_out, onehot, onehot_t,
):
    fill_onehot(onehot, place_col)
    fill_onehot_t(onehot_t, place_row)
    normal, _ = normalize(h_one[...])
    two = (normal * vec[2:3] + vec[3:4]).astype(BF)
    normed_two[...] = two
    logits = nn(two, router[...])
    gap = (logits[:, LANES:] + router_bias[1:2]) - (logits[:, :LANES] + router_bias[0:1])
    gap = jnp.where(place_col[...] >= SLOTS // 2, gap, -gap)
    gap_out[...] = gap
    gate = 1.0 / (1.0 + jnp.exp(-gap))
    disp[...] = nn(onehot_t[...], two).astype(BF)

    @pl.loop(0, 4, unroll=4)
    def _(t):
        rows = pl.ds(pl.multiple_of(t * 256, 256), 256)
        e = t // 2
        own = disp[rows, :]
        for c in range(3):
            cols = slice(c * 512, (c + 1) * 512)
            pre = nn(own, w1[e, :, cols]) + b1[pl.ds(e, 1), cols]
            phi = 0.5 * (1.0 + lax.erf(pre * 0.7071067811865476))
            act[rows, cols] = (pre * phi).astype(BF)
            slope[rows, cols] = (
                phi + pre * jnp.exp(-0.5 * pre * pre) * 0.3989422804014327
            ).astype(BF)
        rows_out[rows, :] = (nn(act[rows, :], w2[e]) + vec[pl.ds(7 + e, 1)]).astype(BF)

    taken = nn(onehot[...], rows_out[...])
    picked[...] = taken.astype(BF)
    for c in range(3):
        cols = slice(c * LANES, (c + 1) * LANES)
        out[:, cols] = (h_one[:, cols] + gate * taken[:, cols]).astype(out.dtype)


def moe_fwd(h_one, vec, w1, w2, b1, router, router_bias, place, out_dtype, deps=()):
    return call(
        moe_fwd_body,
        (
            sds((CELLS, D), out_dtype),
            sds((CELLS, D), BF),
            sds((SLOTS, D), BF),
            sds((SLOTS, F), BF),
            sds((SLOTS, F), BF),
            sds((CELLS, D), BF),
            sds((CELLS, LANES), F32),
        ),
        9,
        scratch=[pltpu.VMEM((SLOTS, D), BF), ONEHOT, ONEHOT_T],
        us=9.5,
        deps=deps,
    )(h_one, vec, w1, w2, b1, router, router_bias, *place)


def fill_onehot(onehot, place_col):
    @pl.loop(0, 7)
    def _(t):
        rows = pl.ds(pl.multiple_of(t * 112, 112), 112)
        place = jnp.concatenate([place_col[rows, :]] * 8, axis=1)
        same = place == lax.broadcasted_iota(jnp.int32, (112, SLOTS), 1)
        onehot[rows, :] = jnp.where(same, 1.0, 0.0).astype(BF)


def fill_onehot_t(onehot_t, place_row):
    @pl.loop(0, 8)
    def _(t):
        row = lax.broadcasted_iota(jnp.int32, (128, CELLS), 0) + t * 128
        same = row == place_row[0:1, :]
        onehot_t[pl.ds(pl.multiple_of(t * 128, 128), 128), :] = jnp.where(same, 1.0, 0.0).astype(BF)


def moe_bwd_body(
    grad, w2, place_col, place_row, disp, act, slope, picked, gap,
    dw1, dw2, db1, small, g_pre, gate_grad, g_rows, onehot_t,
):
    fill_onehot_t(onehot_t, place_row)
    go = grad[...].astype(F32)
    gate = 1.0 / (1.0 + jnp.exp(-gap[...]))
    other = 1.0 / (1.0 + jnp.exp(gap[...]))
    g_picked = (go * jnp.concatenate([gate] * 3, axis=1)).astype(BF)
    g_gate = jnp.sum(go * picked[...].astype(F32), axis=-1, keepdims=True)
    sign = jnp.where(place_col[...] >= SLOTS // 2, 1.0, -1.0)
    gl = (g_gate * gate * other * sign).astype(BF)
    gate_grad[...] = gl
    small[...] = jnp.zeros((16, D), F32)
    small[9:10, 0:LANES] = jnp.sum(gl.astype(F32), axis=0, keepdims=True)
    g_rows[...] = nn(onehot_t[...], g_picked).astype(BF)

    @pl.loop(0, EXPERTS, unroll=2)
    def _(e):
        both = pl.ds(pl.multiple_of(e * 512, 512), 512)
        own = g_rows[both, :]
        total = []
        grads = [nt(own, w2[e, c * 256 : (c + 1) * 256, :]) for c in range(6)]
        for c, part in enumerate(grads):
            cols = slice(c * 256, (c + 1) * 256)
            gp = (part * slope[both, cols].astype(F32)).astype(BF)
            g_pre[both, cols] = gp
            total.append(jnp.sum(gp.astype(F32), axis=0, keepdims=True))
        db1[pl.ds(e, 1), :] = jnp.concatenate(total, axis=1)
        small[pl.ds(7 + e, 1), :] = jnp.sum(own.astype(F32), axis=0, keepdims=True)
        for c in range(6):
            cols = slice(c * 256, (c + 1) * 256)
            dw1[e, :, cols] = tn(disp[both, :], g_pre[both, cols])
            dw2[e, cols, :] = tn(act[both, cols], own)


def moe_bwd(grad, w2, place, saved):
    return call(
        moe_bwd_body,
        (
            sds((EXPERTS, D, F), F32),
            sds((EXPERTS, F, D), F32),
            sds((8, F), F32),
            sds((16, D), F32),
            sds((SLOTS, F), BF),
            sds((CELLS, LANES), BF),
        ),
        9,
        scratch=[pltpu.VMEM((SLOTS, D), BF), ONEHOT_T],
        us=8,
    )(grad, w2, *place, *saved)


def middle_bwd_body(vec, w1, place_col, g_pre, gate_grad, g_two, onehot, g_disp):
    fill_onehot(onehot, place_col)
    for e in range(EXPERTS):
        both = slice(e * 512, (e + 1) * 512)
        g_disp[both, :] = nt(g_pre[both, :], w1[e]).astype(BF)
    gl = gate_grad[...].astype(F32)
    g_two[...] = nn(onehot[...], g_disp[...]) + jnp.concatenate([gl] * 3, axis=1) * vec[9:10]


def middle_bwd(vec, w1, place_col, g_pre, gate_grad):
    return call(
        middle_bwd_body,
        sds((CELLS, D), F32),
        5,
        scratch=[ONEHOT, pltpu.VMEM((SLOTS, D), BF)],
        us=5,
    )(vec, w1, place_col, g_pre, gate_grad)


def attn_bwd_windows(windows, qkv, g_mix, attn, g_qkv, dbias, base=None):
    masks = head_masks()
    base = windows[0] if base is None else base

    start, stop = windows
    per = min(4, stop - start)

    @pl.loop(0, (stop - start) // per)
    def _(wo):
        units = [(i, g) for i in range(per) for g in range(QUADS)]
        first = [start + wo * per + i for i in range(per)]
        rows = [pl.ds(pl.multiple_of(w * WROWS, WROWS), WROWS) for w in first]
        outs = [pl.ds(pl.multiple_of((w - base) * WROWS, WROWS), WROWS) for w in first]
        cols = [[slice(n * D + g * LANES, n * D + (g + 1) * LANES) for g in range(QUADS)] for n in range(3)]
        d4s = [stack_heads(g_mix[rows[i], cols[0][g]], masks) for i, g in units]
        grads = [nt(qkv[rows[i], cols[2][g]], d4) for (i, g), d4 in zip(units, d4s)]
        probs = [attn[first[i] * QUADS + g] for i, g in units]
        for (i, g), a, d4 in zip(units, probs, d4s):
            g_qkv[outs[i], cols[2][g]] = nn(a, d4).astype(BF)
        dss = []
        for a, grad in zip(probs, grads):
            a = a.astype(F32)
            t = a * grad
            dss.append((t - a * jnp.sum(t, axis=0, keepdims=True)).astype(BF))
        for g in range(QUADS):
            total = dbias[g]
            for (_, other), ds in zip(units, dss):
                if other == g:
                    total = total + ds.astype(F32)
            dbias[g] = total
        talls = [tn(ds, qkv[rows[i], cols[1][g]]) for (i, g), ds in zip(units, dss)]
        for (i, g), ds in zip(units, dss):
            q4 = stack_heads(qkv[rows[i], cols[0][g]], masks)
            g_qkv[outs[i], cols[1][g]] = (nn(ds, q4) * SCALE).astype(BF)
        for (i, g), tall in zip(units, talls):
            g_qkv[outs[i], cols[0][g]] = (fold_heads(tall, masks) * SCALE).astype(BF)


def attn_bwd_body(
    shifted, grad, h_one, vec, w_out, normed_two, gate_grad, mixed, g_two, qkv, attn,
    grad_one, g_qkv, dw_out, dbias, drouter, small, g_mix, patches, windows_of,
):
    drouter[...] = tn(gate_grad[...], normed_two[...])[0:8]
    normal, inverse = normalize(h_one[...])
    small[...] = jnp.zeros((16, D), F32)
    small[2:3] = jnp.sum(g_two[...] * normal, axis=0, keepdims=True)
    small[3:4] = jnp.sum(g_two[...], axis=0, keepdims=True)
    grad_one[...] = grad[...].astype(F32) + norm_backward(g_two[...], normal, inverse, vec[2:3])
    small[6:7] = jnp.sum(grad_one[...].astype(BF).astype(F32), axis=0, keepdims=True)
    patches[:CELLS, :] = grad_one[...]
    to_windows(patches, windows_of, shifted)
    gao_w = windows_of[...].astype(BF)
    dw_out[...] = tn(mixed[...], gao_w)
    g_mix[...] = nt(gao_w, w_out[...]).astype(BF)
    dbias[...] = jnp.zeros_like(dbias)
    attn_bwd_windows((0, WINDOWS), qkv, g_mix, attn, g_qkv, dbias)


def attn_bwd(shifted, grad, h_one, vec, w_out, normed_two, gate_grad, mixed, g_two, qkv, attn):
    return call(
        functools.partial(attn_bwd_body, shifted),
        (
            sds((CELLS, D), F32),
            sds((WTOK, 3 * D), BF),
            sds((D, D), F32),
            sds((QUADS, WROWS, PAIR), F32),
            sds((8, D), F32),
            sds((16, D), F32),
        ),
        10,
        scratch=[pltpu.VMEM((WTOK, D), BF), PATCHES, PADDED],
        us=5,
        vmem=BIG_VMEM,
    )(grad, h_one, vec, w_out, normed_two, gate_grad, mixed, g_two, qkv, attn)


def proj_bwd_body(
    shifted, grad_one, hid, vec, w_in, wn, g_qkv, grad_in, dw_in, small, patches, windows_of,
):
    for c in range(3):
        cols = slice(c * D, (c + 1) * D)
        dw_in[:, cols] = tn(wn[...], g_qkv[:, cols])
    windows_of[...] = nt(g_qkv[...], w_in[...])
    to_patches(windows_of, patches, shifted)
    g_normed = patches[:CELLS, :]
    normal, inverse = normalize(hid[...].astype(F32))
    small[...] = jnp.zeros((16, D), F32)
    small[0:1] = jnp.sum(g_normed * normal, axis=0, keepdims=True)
    small[1:2] = jnp.sum(g_normed, axis=0, keepdims=True)
    small[4:5] = jnp.sum(g_qkv[:, :D].astype(F32), axis=0, keepdims=True)
    small[5:6] = jnp.sum(g_qkv[:, 2 * D :].astype(F32), axis=0, keepdims=True)
    grad_in[...] = grad_one[...] + norm_backward(g_normed, normal, inverse, vec[0:1])


def proj_bwd(shifted, grad_one, hid, vec, w_in, wn, g_qkv):
    return call(
        functools.partial(proj_bwd_body, shifted),
        (sds((CELLS, D), F32), sds((D, 3 * D), F32), sds((16, D), F32)),
        6,
        scratch=[PATCHES, PADDED],
        us=0.5,
    )(grad_one, hid, vec, w_in, wn, g_qkv)


def window_perm_t(shifted):
    source = patch_of(jnp.arange(WTOK, dtype=jnp.int32), shifted)
    return (jnp.arange(CELLS, dtype=jnp.int32)[:, None] == source[None, :]).astype(BF)


def wrap_codes(shifted):
    code = np.zeros((CELLS,), np.float32)
    if shifted:
        for r in range(SIDE):
            for s in range(SIDE):
                rr, ss = (r - SHIFT) % SIDE, (s - SHIFT) % SIDE
                code[r * SIDE + s] = 2 * (rr >= SIDE - SHIFT) + (ss >= SIDE - SHIFT)
    return code


def window_masks(items, shifted):
    labels = items.astype(F32)
    if shifted:
        labels = labels * 4.0 + jnp.asarray(wrap_codes(True))
    placed = nn(jnp.broadcast_to((labels + 1.0).astype(BF), (8, CELLS)), window_perm_t(shifted))[0]
    placed = placed.reshape(WINDOWS, WROWS)
    same = (placed[:, :, None] == placed[:, None, :]) & (placed[:, :, None] > 0.0)
    same = same.astype(F32)
    return jnp.concatenate([same, same], axis=2)


def slot_places(routes, slots):
    group = (jnp.arange(CELLS, dtype=jnp.int32) // GROUP) * CAP
    place = routes * (2 * CAP) + group + slots
    return jnp.broadcast_to(place[:, None], (CELLS, LANES)), jnp.broadcast_to(place[None, :], (8, CELLS))

LEAD = 73
SMALL = 9326
LAG = LEAD * LANES - SMALL
VECTORS = 9
LINES = 32
SPANS = ((LEAD, D, 9), (LEAD + 3456, D, 3), (LEAD + 4608, 2 * D, 12), (LEAD + 4608 + 9216, 2 * F, 3))
EDGE = LEAD + 4608
ALIGNED = LEAD + 4608 + 2 * 9216


def relative(k, bits):
    total = 0
    for place, bit in enumerate(bits):
        total = total + (((k >> (len(bits) - 1 - place)) & 1) << bit)
    return total


def lanes_of(count=LANES):
    return lax.broadcasted_iota(jnp.int32, (1, count), 1)


def equal(rows, columns):
    return jnp.where(rows == columns, 1.0, 0.0).astype(BF)


def spread(shape):
    return lax.broadcasted_iota(jnp.int32, shape, 0), lax.broadcasted_iota(jnp.int32, shape, 1)


def exact(left, one, product):
    high = left.astype(BF)
    low = (left - high.astype(F32)).astype(BF)
    return product(high, one) + product(low, one)


def head_major():
    f, g = spread((D, D))
    return equal(f, 12 * (g & 31) + (g >> 5))


def head_rows(m):
    f, g = spread((D, 2 * LANES))
    return equal((f & 31) + 32 * m, g)


def offset_lanes():
    f, g = spread((LANES, LANES))
    i = g & 63
    r = (i * 37) >> 8
    return equal(f, jnp.where(i < WIN * WIN, 13 * r + i - WIN * r, -1))


def turns():
    return [13 * (6 - j // WIN) + 6 - j % WIN for j in range(WIN * WIN)]


def unpack_bias(flat, wide, tall, bias):
    wide[...] = jnp.zeros_like(wide)
    for m in range(6):
        for c in range(3):
            wide[m : m + 1, c * LANES : (c + 1) * LANES] = flat[12 + 3 * m + c : 13 + 3 * m + c, :]
    by_head = nn(wide[...].astype(BF), head_major())
    sub = lax.broadcasted_iota(jnp.int32, (16, D), 0)
    own = (lanes_of(D) >> 5) == sub
    table = jnp.zeros((16, 2 * LANES), F32)
    for m in range(6):
        table = table + nn(jnp.where(own, by_head[m : m + 1], 0.0).astype(BF), head_rows(m))
    tall[...] = jnp.zeros_like(tall)
    for j, turn in enumerate(turns()):
        row = pltpu.roll(table, (2 * LANES - turn) % (2 * LANES), 1)[:, :LANES]
        tall[pl.ds(j, 16, stride=WROWS), :] = row
    tall[...] = nn(tall[...].astype(BF), offset_lanes())
    for g in range(QUADS):
        for t in range(2):
            h = 4 * g + 2 * t
            left, right = tall[h * WROWS : (h + 1) * WROWS], tall[(h + 1) * WROWS : (h + 2) * WROWS]
            bias[g, :, t * LANES : (t + 1) * LANES] = jnp.where(lanes_of() < WROWS, left, right)


def unpack_small(flat, rows, wide, tall, vec, b1, router, router_bias, bias):
    def shifted(first, count, by):
        near, far = flat[first : first + count, :], flat[first + 1 : first + 1 + count, :]
        return pltpu.roll(jnp.where(lanes_of() >= by, near, far), LANES - by, 1)

    rows[0:16, :] = shifted(27, 16, 108)
    rows[16:46, :] = shifted(42, 30, 110)
    vec[...] = jnp.zeros_like(vec)
    b1[...] = jnp.zeros_like(b1)
    for c in range(3):
        cols = slice(c * LANES, (c + 1) * LANES)
        for n in range(4):
            vec[n : n + 1, cols] = flat[3 * n + c : 3 * n + c + 1, :]
        for n in range(3):
            vec[4 + n : 5 + n, cols] = rows[3 * n + c : 3 * n + c + 1, :]
        for e in range(EXPERTS):
            vec[7 + e : 8 + e, cols] = rows[40 + 3 * e + c : 41 + 3 * e + c, :]
    for e in range(EXPERTS):
        for c in range(12):
            b1[e : e + 1, c * LANES : (c + 1) * LANES] = rows[16 + 12 * e + c : 17 + 12 * e + c, :]
        one = jnp.sum(jnp.where(lanes_of() == e, rows[15:16, :], 0.0), axis=1, keepdims=True)
        router_bias[e : e + 1, :] = jnp.broadcast_to(one, (1, LANES))
    pairs = jnp.concatenate([rows[9 + c : 10 + c, :] for c in range(6)], axis=1)
    pairs = jnp.broadcast_to(pairs, (LANES, 2 * D)).astype(BF)
    d, f = spread((D, 2 * D))
    for e in range(EXPERTS):
        router[:, e * LANES : (e + 1) * LANES] = nt(equal(f, 2 * d + e), pairs).astype(BF)
    gap = nt(pairs[0:16], equal(f, 2 * d + 1)) - nt(pairs[0:16], equal(f, 2 * d))
    vec[9:10, :] = gap[0:1]
    unpack_bias(flat, wide, tall, bias)


def unpack_matrices(flat, spans, outs, skipped):
    for (base, height, tiles), out in zip(spans, outs):
        step = 128

        @pl.loop(0, height // step, unroll=min(6, height // step))
        def _(t, base=base, tiles=tiles, out=out):
            first = base - 1 - skipped + t * (step * tiles)
            before = flat[pl.ds(first, step, stride=tiles), :]
            for j in range(tiles):
                here = flat[pl.ds(first + 1 + j, step, stride=tiles), :]
                tile = pltpu.roll(jnp.where(lanes_of() >= LANES - LAG, before, here), LAG, 1)
                out[pl.ds(pl.multiple_of(t * step, step), step), j * LANES : (j + 1) * LANES] = tile.astype(BF)
                before = here


def unpack_head_body(rows, runs, me, *refs):
    got = refs[: len(runs)]
    w_in, w_out, rest, vec, b1, router, router_bias, bias, flat, few, wide, tall = refs[len(runs) :]
    for (bits, fixed), part in zip(runs, got):
        n, half = 1 << len(bits), part.shape[1]

        @pl.loop(0, n)
        def _(k, bits=bits, fixed=fixed, part=part, n=n, half=half):
            d = me[1] ^ (relative(k, bits) + fixed)
            flat[pl.ds(d * rows, half), :] = part[k].astype(F32)
            flat[pl.ds(d * rows + half, rows - half), :] = part[n + k].astype(F32)[: rows - half]

    unpack_small(flat, few, wide, tall, vec, b1, router, router_bias, bias)
    unpack_matrices(flat, SPANS[:2], (w_in, w_out), 0)
    rest[...] = flat[EDGE - 1 : EDGE - 1 + rest.shape[0], :]


def unpack_tail_body(rows, heads, runs, me, rest, *refs):
    got = refs[: len(runs)]
    w1, w2, flat = refs[len(runs) :]
    flat[0 : rest.shape[0], :] = rest[...]
    for (outer, inner, fixed, upper, skip), part in zip(runs, got):
        count = 1 << len(inner)
        half = part.shape[1]
        first = half if upper else 0
        used = min(half, rows - first)

        @pl.loop(0, 3 * count << len(outer), unroll=3)
        def _(k, outer=outer, inner=inner, fixed=fixed, part=part, count=count, first=first, used=used, skip=skip):
            own = (relative(k // (3 * count), outer) + relative(k % count, inner) + fixed) ^ me[1]
            d = ((k // count) % 3 + 1) * heads + own
            flat[pl.ds(d * rows + first - (EDGE - 1), used), :] = part[skip + k].astype(F32)[:used]

    unpack_matrices(flat, SPANS[2:], (w1, w2), EDGE - 1)


class Weights(NamedTuple):
    w_in: Any
    w_out: Any
    w1: Any
    w2: Any
    vec: Any
    b1: Any
    router: Any
    router_bias: Any
    bias: Any


SMALL_SHAPES = (
    sds((16, D), F32),
    sds((8, F), F32),
    sds((D, 2 * LANES), BF),
    sds((8, LANES), F32),
    sds((QUADS, WROWS, PAIR), F32),
)
SMALL_SCRATCH = [pltpu.VMEM((48, LANES), F32), pltpu.VMEM((8, D), F32), pltpu.VMEM((17 * WROWS, LANES), F32)]
HEAD_SHAPES = (sds((D, 3 * D), BF), sds((D, D), BF))
TAIL_SHAPES = (sds((2 * D, F), BF), sds((2 * F, D), BF))


def experts(w1, w2):
    return w1.reshape(EXPERTS, D, F), w2.reshape(EXPERTS, F, D)


def unpack_head(me, parts, runs, rows, devices):
    heads = devices // 4
    w_in, w_out, rest, *small = call(
        functools.partial(unpack_head_body, rows, runs),
        HEAD_SHAPES + (sds((heads * rows - EDGE + 1, LANES), F32),) + SMALL_SHAPES,
        1 + len(parts),
        scratch=[pltpu.VMEM((heads * rows + 8, LANES), F32)] + SMALL_SCRATCH,
        smem=1,
        us=4,
    )(me, *parts)
    return Weights(w_in, w_out, None, None, *small), rest


def unpack_tail(me, rest, parts, runs, rows, devices):
    return experts(
        *call(
            functools.partial(unpack_tail_body, rows, devices // 4, runs),
            TAIL_SHAPES,
            2 + len(parts),
            scratch=[pltpu.VMEM((devices * rows - EDGE + 9, LANES), F32)],
            smem=1,
            vmem=BIG_VMEM,
            us=4,
        )(me, rest, *parts)
    )


def pack_bias(dbias, wide, tall):
    tall[HEADS * WROWS :, :] = jnp.zeros((5 * WROWS, LANES), F32)
    for h in range(HEADS):
        g, t, side = h // 4, (h % 4) // 2, h % 2
        tile = dbias[g, :, t * LANES : (t + 1) * LANES]
        tall[h * WROWS : (h + 1) * WROWS, :] = jnp.where((lanes_of() >> 6) == side, tile, 0.0)
    used = HEADS * WROWS
    tall[0:used, :] = exact(tall[0:used, :], offset_lanes(), nt)
    table = jnp.zeros((16, 2 * LANES), F32)
    for j, turn in enumerate(turns()):
        row = tall[pl.ds(j, 16, stride=WROWS), :]
        table = table + pltpu.roll(jnp.concatenate([row, jnp.zeros_like(row)], axis=1), turn, 1)
    sub = lax.broadcasted_iota(jnp.int32, (16, D), 0)
    own = (lanes_of(D) >> 5) == sub
    wide[...] = jnp.zeros_like(wide)
    for m in range(6):
        placed = jnp.where(own, exact(table, head_rows(m), nt), 0.0)
        wide[m : m + 1, :] = jnp.sum(placed, axis=0, keepdims=True)
    wide[...] = exact(wide[...], head_major(), nt)


def pack_small(al, vectors, drouter, db1, dbias, one, two, wide, tall):
    one[...] = jnp.zeros_like(one)
    two[...] = jnp.zeros_like(two)
    pack_bias(dbias, wide, tall)
    d, f = spread((D, 2 * D))
    signs = equal(f, 2 * d + 1) - equal(f, 2 * d)
    pairs = exact(drouter[...], signs, nn)
    for c in range(3):
        cols = slice(c * LANES, (c + 1) * LANES)
        for n in range(4):
            one[1 + 3 * n + c : 2 + 3 * n + c, :] = vectors[n : n + 1, cols]
        for m in range(6):
            one[13 + 3 * m + c : 14 + 3 * m + c, :] = wide[m : m + 1, cols]
        for n in range(3):
            two[1 + 3 * n + c : 2 + 3 * n + c, :] = vectors[4 + n : 5 + n, cols]
        for e in range(EXPERTS):
            al[67 + 3 * e + c : 68 + 3 * e + c, :] = vectors[7 + e : 8 + e, cols]
    for c in range(6):
        two[10 + c : 11 + c, :] = pairs[0:1, c * LANES : (c + 1) * LANES]
    total = vectors[9:10, 0:LANES]
    two[16:17, :] = jnp.where(lanes_of() == 0, -total, jnp.where(lanes_of() == 1, total, 0.0))
    for e in range(EXPERTS):
        for c in range(12):
            al[43 + 12 * e + c : 44 + 12 * e + c, :] = db1[e : e + 1, c * LANES : (c + 1) * LANES]
    first = pltpu.roll(jnp.where(lanes_of() >= LANES - 18, one[0:28, :], one[1:29, :]), 18, 1)
    second = pltpu.roll(jnp.where(lanes_of() >= LANES - 126, two[0:16, :], two[1:17, :]), 126, 1)
    al[27:43, :] = second
    al[0:27, :] = first[0:27]
    al[27:28, :] += first[27:28]


def pack_matrices(al, spans, grads, skipped):
    for (base, height, tiles), grad in zip(spans, grads):
        step = 128

        @pl.loop(0, height // step, unroll=min(6, height // step))
        def _(t, base=base, tiles=tiles, grad=grad):
            first = base - skipped + t * (step * tiles)
            own = pl.ds(pl.multiple_of(t * step, step), step)
            for j in range(tiles):
                al[pl.ds(first + j, step, stride=tiles), :] = grad[own, j * LANES : (j + 1) * LANES]


def clear(al, first):
    al[pl.ds(first, al.shape[0] - first), :] = jnp.zeros((al.shape[0] - first, LANES), F32)


def pack_head_body(
    rows, padded, runs, me, moe, attn, proj, drouter, db1, dbias, dw_in, dw_out, rest,
    keep, send, al, vectors, lines, one, two, wide, tall,
):
    vectors[...] = moe[...] + attn[...] + proj[...]
    lines[...] = jnp.zeros_like(lines)
    for n in range(VECTORS):
        for c in range(3):
            lines[3 * n + c : 3 * n + c + 1, :] = vectors[n : n + 1, c * LANES : (c + 1) * LANES]
    pack_small(al, vectors, drouter, db1, dbias, one, two, wide, tall)
    pack_matrices(al, SPANS[:2], (dw_in, dw_out), 0)
    al[EDGE : EDGE + rest.shape[0], :] = rest[...]
    at = 0
    for bits, fixed in runs:
        for other, out in enumerate((keep, send)):

            @pl.loop(0, 1 << len(bits))
            def _(k, bits=bits, fixed=fixed, at=at, other=other, out=out):
                d = me[1] ^ (relative(k, bits) + fixed + other)
                out[at + k, :padded, :] = al[pl.ds(d * rows, padded), :].astype(BF)
                out[at + k, padded:, :] = lines[...].astype(BF)

        at += 1 << len(bits)


def pack_tail_body(rows, padded, heads, runs, me, dw1, dw2, keep, send, rest, al):
    clear(al, ALIGNED - EDGE)
    pack_matrices(al, SPANS[2:], (dw1, dw2), EDGE)
    rest[...] = al[0 : rest.shape[0], :]
    half = padded // 2
    at = 0
    for outer, inner, fixed, upper in runs:
        count = 1 << len(inner)
        total = 3 * count << len(outer)
        for other, out in enumerate((keep, send)):

            @pl.loop(0, total, unroll=3)
            def _(k, outer=outer, inner=inner, fixed=fixed, upper=upper, count=count, at=at, other=other, out=out):
                own = (relative(k // (3 * count), outer) + relative(k % count, inner) + fixed + other) ^ me[1]
                d = ((k // count) % 3 + 1) * heads + own
                out[at + k] = al[pl.ds(d * rows + (half if upper else 0) - EDGE, half), :].astype(BF)

        at += total


SMALL_PACK = [
    pltpu.VMEM((40, LANES), F32),
    pltpu.VMEM((24, LANES), F32),
    pltpu.VMEM((8, D), F32),
    pltpu.VMEM((17 * WROWS, LANES), F32),
]


def pack_head(me, small, dw_in, dw_out, rest, runs, rows, devices, padded):
    heads = devices // 4
    shape = sds((heads // 2, padded + LINES, LANES), BF)
    return call(
        functools.partial(pack_head_body, rows, padded, runs),
        (shape, shape),
        10,
        scratch=[
            pltpu.VMEM((EDGE + rest.shape[0], LANES), F32),
            pltpu.VMEM((16, D), F32),
            pltpu.VMEM((LINES, LANES), F32),
        ]
        + SMALL_PACK,
        smem=1,
        us=0.5,
    )(me, *small, dw_in, dw_out, rest)


def pack_tail(me, dw1, dw2, runs, rows, devices, padded):
    heads = devices // 4
    shape = sds((3 * heads, padded // 2, LANES), BF)
    over = -(-(heads * rows + padded - EDGE) // 8) * 8
    return call(
        functools.partial(pack_tail_body, rows, padded, heads, runs),
        (shape, shape, sds((over, LANES), F32)),
        3,
        scratch=[pltpu.VMEM((devices * rows + padded - EDGE, LANES), F32)],
        smem=1,
        vmem=BIG_VMEM,
        us=3,
    )(me, dw1.reshape(2 * D, F), dw2.reshape(2 * F, D))


def levels_body(sources, me, *refs):
    pieces, (x, y, head) = refs[: len(refs) - 3], refs[len(refs) - 3 :]
    n, half = head.shape[0] // 2, x.shape[1]
    for level in range(4):
        for step, (at, first) in enumerate(sources):

            @pl.when((me[2] ^ step) == level)
            def _(level=level, at=at, first=first):
                for i in range(n):
                    lower, upper = pieces[at][first * n + i, :half, :], pieces[at][first * n + i, half:, :]
                    if level == 0:
                        for out in (x, y, head):
                            out[i] = lower
                            out[n + i] = upper
                    else:
                        x[(1 + level) * n + i] = lower
                        y[(1 + level) * n + i] = upper


def levels(me, *pieces):
    sources = ((0, 0), (1, 0), (2, 0), (3, 0)) if len(pieces) == 4 else ((0, 0), (1, 0), (0, 1), (1, 1))
    n, padded, _ = pieces[0].shape
    n = n * len(pieces) // 4
    dtype = pieces[0].dtype
    shapes = [sds((count * n, padded // 2, LANES), dtype) for count in (5, 5, 2)]
    return call(functools.partial(levels_body, sources), shapes, 1 + len(pieces), smem=1)(me, *pieces)


def targets_body(with_head, me, a, a_got, b, b_got, *refs):
    *head, keep, send = refs
    n, half = keep.shape[0] // 2, a.shape[1]
    places = {0: (keep, 0), 2: (keep, n), 1: (send, 0), 3: (send, n)}
    for step, (out, first) in places.items():
        level = me[2] ^ step

        @pl.when(level == 0)
        def _(out=out, first=first):
            for i in range(n):
                if with_head:
                    out[first + i] = head[0][i, : 2 * half, :].astype(out.dtype)
                else:
                    out[first + i] = jnp.zeros((2 * half, LANES), out.dtype)

        @pl.when(level > 0)
        def _(out=out, first=first, level=level):
            for i in range(n):
                at = (level - 1) * n + i
                out[first + i, :half, :] = (a[at] + a_got[at].astype(F32)).astype(out.dtype)
                out[first + i, half:, :] = (b[at] + b_got[at].astype(F32)).astype(out.dtype)


def targets(me, a, a_got, b, b_got, *head):
    n, half, _ = a.shape
    n = n // 3
    shape = (2 * n, 2 * half, LANES)
    return call(
        functools.partial(targets_body, bool(head)), (sds(shape, F32), sds(shape, BF)), 5 + len(head), smem=1
    )(me, a, a_got, b, b_got, *head)


def combine_body(plan, count, *refs):
    for (size, _, terms), out in zip(plan, refs[count:]):

        @pl.loop(0, size)
        def _(i, terms=terms, out=out):
            parts = [refs[at][first + i].astype(F32) for at, first in terms]
            while len(parts) > 1:
                parts = [sum(parts[at + 1 : at + 2], parts[at]) for at in range(0, len(parts), 2)]
            out[i] = parts[0].astype(out.dtype)


def combine(plan, *arrays):
    tail = arrays[0].shape[1:]
    shapes = [sds((size, *tail), dtype) for size, dtype, _ in plan]
    return call(functools.partial(combine_body, plan, len(arrays)), shapes, len(arrays))(*arrays)


def finish_body(rows, me, keep, got, upper_keep, upper_got, out):
    def shift(keep, got):
        total = keep[0] + got[0].astype(F32)
        here, below = total[0:rows, :], total[1 : rows + 1, :]
        out[...] = pltpu.roll(jnp.where(lanes_of() >= LAG, here, below), LANES - LAG, 1)

    pl.when(me[2] == 0)(lambda: shift(keep, got))
    pl.when(me[2] != 0)(lambda: shift(upper_keep, upper_got))


def finish(me, rows, lowest, upper):
    parts = (lowest.keep, lowest.got, upper.keep, upper.got)
    return call(functools.partial(finish_body, rows), sds((rows, LANES), F32), 5, smem=1)(me, *parts)


def join_body(skip, a, b, out):
    n = out.shape[0] // 2

    @pl.loop(0, n)
    def _(i):
        out[i] = a[skip + i]
        out[n + i] = b[skip + i]


def join(a, b, skip=0):
    shape = sds((2 * (a.shape[0] - skip), *a.shape[1:]), a.dtype)
    return call(functools.partial(join_body, skip), shape, 2)(a, b)


class Ways(NamedTuple):
    core: Any
    x: Any
    y: Any
    low: Any
    high: Any
    rest: Any


def ways():
    dp, fsdp = (lax.axis_size(axis).bit_length() - 1 for axis in (DP, FSDP))
    rest = [1 << (fsdp + bit) for bit in range(1, dp - 2)] + [1 << bit for bit in range(2, fsdp)]
    return Ways(1, 2, 1 << fsdp, 1 << (fsdp + dp - 2), 1 << (fsdp + dp - 1), rest)


def device_count():
    return lax.axis_size(DP) * lax.axis_size(FSDP)


def flip(array, step):
    return lax.ppermute(array, (DP, FSDP), [(i, i ^ step) for i in range(device_count())])


def move(array, levels):
    width = device_count() // 4
    pairs = [(a * width + i, b * width + i) for a, b in levels.items() for i in range(width)]
    return lax.ppermute(array, (DP, FSDP), pairs)


def tie(arrays, *others):
    if isinstance(arrays, tuple):
        return tuple(tie(array, *others) for array in arrays)
    return lax.optimization_barrier((arrays, *others))[0]


def sync(*arrays):
    return lax.optimization_barrier(arrays)


def bits_of(*steps):
    return [step.bit_length() - 1 for step in steps]


class Gather:
    def __init__(self, own, way, me):
        for extra in way.rest:
            own = join(own, flip(own, extra))
        self.way, self.own, self.me, self.others = way, own, me, None
        self.rest = bits_of(*reversed(way.rest))

    def far(self):
        own, way = self.own, self.way
        self.others = own, flip(own, way.low), flip(own, way.high), flip(own, way.low + way.high)

    def high(self):
        self.other = flip(self.own, self.way.high)

    def low(self):
        self.pair = join(self.own, self.other)
        self.over = flip(self.pair, self.way.low)

    def levels(self):
        pieces = self.others if self.others else (self.pair, self.over)
        self.x, self.y, self.head = levels(self.me, *pieces)

    def near(self):
        way = self.way
        self.got = [flip(self.x, way.x), flip(self.y, way.y), flip(self.head, way.x + way.y)]

    def near_core(self):
        way, core = self.way, self.way.core
        x, y, both = self.got
        sides = [[self.x, x, y, both, self.y]]
        sides.append([flip(part, core) for part in sides[0]])
        self.head_parts, self.head_runs, self.parts, self.runs = [], [], [], []
        for fixed, side in zip((0, core), sides):
            self.head_parts += side[:4]
            self.head_runs += [(self.rest, step + fixed) for step in (0, way.x, way.y, way.x + way.y)]
            x_own, x_got, y_got, _, y_own = side
            self.parts += [x_own, x_got, y_own, y_got]
            skip = 2 << len(self.rest)
            self.runs += [([], self.rest, fixed + step, False, skip) for step in (0, way.x)]
            self.runs += [([], self.rest, fixed + step, True, skip) for step in (0, way.y)]

    def last(self):
        way, skip = self.way, 2 << len(self.rest)
        self.joined = join(self.x, self.got[0], skip), join(self.y, self.got[1], skip)
        self.last_got = flip(self.joined[0], way.y), flip(self.joined[1], way.x)

    def last_core(self):
        way = self.way
        for fixed in (0, way.core):
            self.parts += [flip(part, way.core) for part in self.last_got] if fixed else list(self.last_got)
            self.runs += [(bits_of(way.x), self.rest, way.y + fixed, False, 0)]
            self.runs += [(bits_of(way.y), self.rest, way.x + fixed, True, 0)]


def head_runs(way):
    rest = bits_of(*way.rest)
    return [(rest, step) for step in (way.y, way.x + way.y, way.x, 0)]


def tail_runs(way):
    rest, bx, by = (bits_of(*steps) for steps in (way.rest, [way.x], [way.y]))
    return [
        (bx, rest, way.y, False), ([], rest, way.x, False), ([], rest, 0, False),
        (by, rest, way.x, True), ([], rest, way.y, True), ([], rest, 0, True),
    ]


class HeadScatter:
    def __init__(self, keep, send, way):
        self.way, self.keep, self.n = way, keep, keep.shape[0] // 4
        self.got = flip(send, way.core)

    def plane(self):
        n, way = self.n, self.way
        y, xy, x, self.keep = combine([(n, BF, ((0, i * n), (1, i * n))) for i in range(4)], self.keep, self.got)
        self.got = flip(x, way.x), flip(y, way.y), flip(xy, way.x + way.y)

    def near(self):
        n = 2 * self.n
        sent, self.keep = combine([(n, BF, ((0, i * n), (1, i * n))) for i in range(2)], self.keep, self.got)
        self.got = flip(sent, self.way.y)

    def next(self):
        n = self.n
        sent, self.keep = combine(((n, BF, ((0, 0), (1, n))), (n, BF, ((0, n), (1, 0)))), self.keep, self.got)
        self.got = flip(sent, self.way.x)

    def add(self):
        n, got = self.n, self.got if isinstance(self.got, (tuple, list)) else (self.got,)
        terms = tuple((i, 0) for i in range(1 + len(got)))
        sent, self.keep = combine(((n, BF, terms), (n, F32, terms)), self.keep, *got)
        return sent

    def lines(self):
        return self.keep[0, -LINES : 3 * VECTORS - LINES].reshape(VECTORS, D)

    def low(self, sent):
        self.got = move(sent, {1: 0, 3: 2})

    def high(self):
        self.got = move(self.add(), {2: 0})
        self.keep, self.got = fold(self.keep, self.got, self.way.rest)


class TailScatter:
    def __init__(self, keep, send, way, me):
        self.way, self.keep, self.n, self.me = way, keep, keep.shape[0] // 24, me
        self.got = flip(send, way.core)

    def near(self):
        n = 6 * self.n
        plan = [(n, dtype, ((0, first), (1, first))) for dtype, first in ((BF, 0), (F32, n), (BF, 2 * n), (F32, 3 * n))]
        a, self.a, b, self.b = combine(plan, self.keep, self.got)
        self.a_got, self.b_got = flip(a, self.way.y), flip(b, self.way.x)

    def next(self):
        n = 3 * self.n
        plan = [(n, BF, ((0, 0), (1, n))), (n, F32, ((0, n), (1, 0)))]
        plan += [(n, BF, ((2, 0), (3, n))), (n, F32, ((2, n), (3, 0)))]
        a, self.a, b, self.b = combine(plan, self.a, self.a_got, self.b, self.b_got)
        self.a_got, self.b_got = flip(a, self.way.x), flip(b, self.way.y)

    def low(self, *head):
        self.keep, sent = targets(self.me, self.a, self.a_got, self.b, self.b_got, *head)
        self.got = flip(sent, self.way.low)

    def high(self):
        self.keep, self.got = fold(self.keep, self.got, [self.way.high] + self.way.rest)


def fold(keep, got, steps):
    for way in steps:
        half = keep.shape[0] // 2
        plan = ((half, BF, ((0, half), (1, half))), (half, F32, ((0, 0), (1, 0))))
        sent, keep = combine(plan, keep, got)
        got = flip(sent, way)
    return keep, got


def shards(inputs, items, routes, slots, cotangent, params, momentum, average):
    fsdp, dp = lax.axis_size(FSDP), lax.axis_size(DP)
    devices = fsdp * dp
    share = params.shape[1]
    rows = share // LANES
    padded = -(-(rows + 1) // 32) * 32
    step_rate = RATE_BASE / math.sqrt(CELLS * devices)
    way = ways()
    own = lax.axis_index(DP) * fsdp + lax.axis_index(FSDP)
    me = jnp.stack([own, own % (devices // 4), own // (devices // 4)]).astype(jnp.int32)

    def share_of(flat):
        return jnp.pad(flat.astype(BF).reshape(1, rows, LANES), ((0, 0), (0, padded - rows), (0, 0)))

    one = Gather(share_of(params[0]), way, me)
    one.far()
    two = Gather(share_of(tie(params[1], one.others[1])), way, me)
    masks, places = [], []
    for b in range(BLOCKS):
        masks.append(window_masks(items.reshape(CELLS), b % 2 == 1))
        places.append(slot_places(routes[b].reshape(CELLS), slots[b].reshape(CELLS)))

    hidden_zero = inputs.reshape(CELLS, D)
    one.levels()
    one.near()
    two.own = tie(two.own, one.head)
    two.high()
    one.got[0] = tie(one.got[0], *masks)
    two.other, *one.got = sync(two.other, *one.got)
    one.near_core()
    one.last()
    two.low()
    one.head_parts[0] = tie(one.head_parts[0], two.pair, *one.joined, *one.parts)
    w, rest = unpack_head(me, one.head_parts, one.head_runs, rows, devices)
    h_zero, *attn_zero = attn_fwd(False, hidden_zero, w.vec, w.w_in, w.w_out, w.bias, masks[0])
    h_zero, two.over = sync(h_zero, two.over)
    two.levels()
    two.near()
    one.last_got = tie(one.last_got, two.head)
    one.last_core()
    w1, w2 = unpack_tail(me, tie(rest, two.head), one.parts, one.runs, rows, devices)
    w_zero = w._replace(w1=w1, w2=w2)
    w = w_zero
    hidden_one, *moe_zero = moe_fwd(h_zero, w.vec, w.w1, w.w2, w.b1, w.router, w.router_bias, places[0], F32)

    hidden_one, *two.got = sync(hidden_one, *two.got)
    two.near_core()
    two.last()
    two.head_parts[0] = tie(two.head_parts[0], *two.joined, *two.parts)
    w, rest = unpack_head(me, two.head_parts, two.head_runs, rows, devices)
    h_one, *attn_one = attn_fwd(True, hidden_one, w.vec, w.w_in, w.w_out, w.bias, masks[1])
    h_one, *two.last_got = sync(h_one, *two.last_got)
    two.last_core()
    w1, w2 = unpack_tail(me, rest, two.parts, two.runs, rows, devices)
    w_one = w._replace(w1=w1, w2=w2)
    w = w_one
    outputs, *moe_one = moe_fwd(h_one, w.vec, w.w1, w.w2, w.b1, w.router, w.router_bias, places[1], BF)

    gradient = cotangent.reshape(CELLS, D)
    wn, qkv, mixed, attn = attn_one
    normed_two, *saved = moe_one
    dw1, dw2, db1, small_moe, g_pre, gate_grad = moe_bwd(gradient, w.w2, places[1], saved)
    keep, send, rest = pack_tail(me, dw1, dw2, tail_runs(way), rows, devices, padded)
    tail_one = TailScatter(keep, send, way, me)
    g_two = middle_bwd(w.vec, w.w1, places[1][0], tie(g_pre, send), gate_grad)
    g_two, tail_one.got = sync(g_two, tail_one.got)
    tail_one.near()
    g_one, g_qkv, dw_out, dbias, drouter, small_mid = attn_bwd(
        True, gradient, h_one, w.vec, w.w_out, normed_two, gate_grad, mixed, tie(g_two, tail_one.a), qkv, attn
    )
    gradient, dw_in, small_attn = proj_bwd(True, g_one, hidden_one, w.vec, w.w_in, wn, g_qkv)
    small = (small_moe, small_mid, small_attn, drouter, db1, dbias)
    keep, send = pack_head(me, small, dw_in, dw_out, rest, head_runs(way), rows, devices, padded)
    send, tail_one.a_got, tail_one.b_got, gradient = sync(send, tail_one.a_got, tail_one.b_got, gradient)
    head_one = HeadScatter(keep, send, way)
    tail_one.next()

    w = w_zero
    wn, qkv, mixed, attn = attn_zero
    normed_two, *saved = moe_zero
    gradient = tie(gradient, tail_one.a)
    dw1, dw2, db1, small_moe, g_pre, gate_grad = moe_bwd(gradient, w.w2, places[0], saved)
    g_pre, dw2, head_one.got, tail_one.a_got, tail_one.b_got = sync(
        g_pre, dw2, head_one.got, tail_one.a_got, tail_one.b_got
    )
    head_one.near()
    tail_one.low()
    keep, send, rest = pack_tail(me, dw1, tie(dw2, head_one.keep, tail_one.keep), tail_runs(way), rows, devices, padded)
    tail_zero = TailScatter(keep, send, way, me)
    g_two = middle_bwd(w.vec, w.w1, places[0][0], tie(g_pre, send), gate_grad)
    g_two, tail_zero.got = sync(g_two, tail_zero.got)
    tail_zero.near()
    g_one, g_qkv, dw_out, dbias, drouter, small_mid = attn_bwd(
        False, gradient, h_zero, w.vec, w.w_out, normed_two, gate_grad, mixed, tie(g_two, tail_zero.a), qkv, attn
    )
    g_qkv, tail_one.got, head_one.got = sync(g_qkv, tail_one.got, head_one.got)
    head_one.next()
    tail_one.high()
    gradient, dw_in, small_attn = proj_bwd(
        False, tie(g_one, head_one.keep, tail_one.keep), hidden_zero, w.vec, w.w_in, wn, g_qkv
    )
    small = (small_moe, small_mid, small_attn, drouter, db1, dbias)
    keep, send = pack_head(me, small, dw_in, dw_out, rest, head_runs(way), rows, devices, padded)
    send, tail_zero.a_got, tail_zero.b_got, head_one.got, tail_one.got = sync(
        send, tail_zero.a_got, tail_zero.b_got, head_one.got, tail_one.got
    )

    head_zero = HeadScatter(keep, send, way)
    tail_zero.next()
    head_zero.plane()
    head_one.add()
    tail_zero.low(head_one.keep)
    sent = head_zero.add()
    head_zero.low(sent)
    vector_grads = jnp.stack([head_zero.lines(), head_one.lines()])
    got = flip(vector_grads, way.low)
    tail_zero.high()
    vector_grads = vector_grads + got
    head_zero.keep = tie(head_zero.keep, vector_grads)
    head_zero.high()
    for step in [way.high] + way.rest:
        vector_grads = vector_grads + flip(vector_grads, step)
    grads_zero = finish(me, rows, head_zero, tail_zero)
    grads_one = finish(me, rows, tail_zero, tail_one)
    grad_all = jnp.stack([grads_zero.reshape(-1), grads_one.reshape(-1)])
    new_momentum = MOMENTUM_DECAY * momentum + grad_all
    new_params = params - step_rate * (grad_all + MOMENTUM_DECAY * new_momentum)
    new_average = AVERAGE_DECAY * average + (1.0 - AVERAGE_DECAY) * new_params
    return (
        outputs.reshape(1, CELLS, D),
        gradient.reshape(1, CELLS, D),
        new_params,
        new_momentum,
        new_average,
        vector_grads,
    )


def solution(mesh):
    both = (DP, FSDP)
    canvas, vector = P(both), P(None, both)
    return jax.shard_map(
        shards,
        mesh=mesh,
        in_specs=(canvas, canvas, vector, vector, canvas, vector, vector, vector),
        out_specs=(canvas, canvas, vector, vector, vector, P()),
        check_vma=False,
    )
```

```python
import functools
import math
from typing import Any, NamedTuple

import jax
import jax.numpy as jnp
import numpy as np
from jax import lax
from jax.experimental import pallas as pl
from jax.experimental.pallas import tpu as pltpu
from jax.sharding import PartitionSpec as P

D = 384
HEADS = 12
F = 1536
HEAD_DIM = 32
EXPERTS = 2
CAP = 256
SIDE = 28
WIN = 7
SHIFT = 3
BLOCKS = 2
CELLS = 784
GROUP = 392
RELS = 169
NORM_EPSILON = 1e-05
MOMENTUM_DECAY = 0.9
AVERAGE_DECAY = 0.9
RATE_BASE = 0.1

DP = "dp"
FSDP = "fsdp"
LANES = 128
WROWS = 64
WINDOWS = 16
WTOK = WINDOWS * WROWS
SLOTS = EXPERTS * 2 * CAP
PAIR = 4 * WROWS
QUADS = HEADS // 4
SCALE = HEAD_DIM ** (-0.5)
US_FLOPS = 1.0e9
BF = jnp.bfloat16
F32 = jnp.float32
VMEM_BYTES = 8 * 1024 * 1024
BIG_VMEM = 13 * 1024 * 1024


def call(body, out_shape, n_in, scratch=(), smem=0, deps=(), us=1, vmem=VMEM_BYTES):
    def skipping(*refs):
        body(*refs[:n_in], *refs[n_in + len(deps) :])

    run = pl.pallas_call(
        skipping,
        out_shape=out_shape,
        in_specs=[pl.BlockSpec(memory_space=pltpu.SMEM)] * smem
        + [pl.BlockSpec(memory_space=pltpu.VMEM)] * (n_in - smem)
        + [pl.BlockSpec(memory_space=pl.ANY)] * len(deps),
        out_specs=jax.tree.map(lambda _: pl.BlockSpec(memory_space=pltpu.VMEM), out_shape),
        scratch_shapes=list(scratch),
        compiler_params=pltpu.CompilerParams(vmem_limit_bytes=vmem),
        cost_estimate=pl.CostEstimate(flops=int(us * US_FLOPS), bytes_accessed=0, transcendentals=0),
    )
    return lambda *args: run(*args, *deps)


def sds(shape, dtype):
    return jax.ShapeDtypeStruct(shape, dtype)


def nn(a, b):
    return lax.dot_general(a, b, (((1,), (0,)), ((), ())), preferred_element_type=F32)


def nt(a, b):
    return lax.dot_general(a, b, (((1,), (1,)), ((), ())), preferred_element_type=F32)


def tn(a, b):
    return lax.dot_general(a, b, (((0,), (0,)), ((), ())), preferred_element_type=F32)


def normalize(hidden):
    centre = hidden - jnp.mean(hidden, axis=-1, keepdims=True)
    inverse = lax.rsqrt(jnp.mean(centre * centre, axis=-1, keepdims=True) + NORM_EPSILON)
    return centre * inverse, inverse


def norm_backward(grad_normed, normal_rows, inverse, gain_row):
    scaled = grad_normed * gain_row
    return inverse * (
        scaled
        - jnp.mean(scaled, axis=-1, keepdims=True)
        - normal_rows * jnp.mean(scaled * normal_rows, axis=-1, keepdims=True)
    )


def head_masks():
    lane = lax.broadcasted_iota(jnp.int32, (1, LANES), 1) // HEAD_DIM
    return [lane == h for h in range(4)]


def stack_heads(rows, masks):
    zero = jnp.zeros_like(rows)
    return jnp.concatenate([jnp.where(mask, rows, zero) for mask in masks], axis=0)


def fold_heads(tall, masks):
    out = jnp.where(masks[0], tall[0:WROWS], 0.0)
    for h in range(1, 4):
        out = jnp.where(masks[h], tall[h * WROWS : (h + 1) * WROWS], out)
    return out


def patch_of(row, shifted):
    w, p = row >> 6, row & 63
    pr = (p * 37) >> 8
    r = (w >> 2) * WIN + pr
    s = (w & 3) * WIN + p - pr * WIN
    if shifted:
        r, s = r + SHIFT, s + SHIFT
        r = jnp.where(r >= SIDE, r - SIDE, r)
        s = jnp.where(s >= SIDE, s - SIDE, s)
    return jnp.where(p < WIN * WIN, r * SIDE + s, -1)


def runs_of(shifted):
    runs = []
    for w in range(WINDOWS):
        for p in range(WIN):
            r, s = (w // 4) * WIN + p, (w % 4) * WIN
            if shifted:
                r, s = (r + SHIFT) % SIDE, s + SHIFT
            here = min(WIN, SIDE - s)
            runs.append((w * WROWS + p * WIN, r * SIDE + s, here))
            if here < WIN:
                runs.append((w * WROWS + p * WIN + here, r * SIDE, WIN - here))
    return runs


def to_windows(patches, windows, shifted):
    windows[...] = jnp.zeros_like(windows)
    for row, patch, length in runs_of(shifted):
        windows[row : row + length, :] = patches[patch : patch + length, :]


def to_patches(windows, patches, shifted):
    for row, patch, length in runs_of(shifted):
        patches[patch : patch + length, :] = windows[row : row + length, :]


PATCHES = pltpu.VMEM((CELLS + 8, D), F32)
PADDED = pltpu.VMEM((WTOK, D), F32)
ONEHOT = pltpu.VMEM((CELLS, SLOTS), BF)
ONEHOT_T = pltpu.VMEM((SLOTS, CELLS), BF)


def attn_fwd_body(shifted, hid, vec, w_in, w_out, bias, mask, h_one, wn, qkv, mixed, attn, patches, windows):
    normal, _ = normalize(hid[...].astype(F32))
    patches[:CELLS, :] = normal * vec[0:1] + vec[1:2]
    to_windows(patches, windows, shifted)
    wn[...] = windows[...].astype(BF)
    in_bias = jnp.concatenate([vec[4:5], jnp.zeros((1, D), F32), vec[5:6]], axis=1)

    @pl.loop(0, 4)
    def _(t):
        rows = pl.ds(pl.multiple_of(t * 256, 256), 256)
        qkv[rows, :] = (nn(wn[rows, :], w_in[...]) + in_bias).astype(BF)

    masks = head_masks()

    @pl.loop(0, WINDOWS // 8)
    def _(wo):
        units = [(i, g) for i in range(8) for g in range(QUADS)]
        rows = [pl.ds(pl.multiple_of((wo * 8 + i) * WROWS, WROWS), WROWS) for i in range(8)]
        allow = []
        for i in range(8):
            one = mask[wo * 8 + i] > 0.0
            allow.append(jnp.concatenate([one, one], axis=1))
        scores = []
        for i, g in units:
            q4 = stack_heads(qkv[rows[i], g * LANES : (g + 1) * LANES], masks)
            scores.append(nt(qkv[rows[i], D + g * LANES : D + (g + 1) * LANES], q4))
        probs = []
        for (i, g), s in zip(units, scores):
            s = jnp.where(allow[i], s * SCALE + bias[g], -1e30)
            e = jnp.exp(s - jnp.max(s, axis=0, keepdims=True))
            a = (e * (1.0 / jnp.sum(e, axis=0, keepdims=True))).astype(BF)
            attn[(wo * 8 + i) * QUADS + g] = a
            probs.append(a)
        tall = [tn(a, qkv[rows[i], 2 * D + g * LANES : 2 * D + (g + 1) * LANES]) for (i, g), a in zip(units, probs)]
        for (i, g), t in zip(units, tall):
            t = fold_heads(t, masks)
            windows[rows[i], g * LANES : (g + 1) * LANES] = t
            mixed[rows[i], g * LANES : (g + 1) * LANES] = t.astype(BF)

    to_patches(windows, patches, shifted)
    h_one[...] = hid[...].astype(F32) + nn(patches[:CELLS, :].astype(BF), w_out[...]) + vec[6:7]


def attn_fwd(shifted, hid, vec, w_in, w_out, bias, mask, deps=()):
    return call(
        functools.partial(attn_fwd_body, shifted),
        (
            sds((CELLS, D), F32),
            sds((WTOK, D), BF),
            sds((WTOK, 3 * D), BF),
            sds((WTOK, D), BF),
            sds((WINDOWS * QUADS, WROWS, PAIR), BF),
        ),
        6,
        scratch=[PATCHES, PADDED],
        us=8,
        deps=deps,
    )(hid, vec, w_in, w_out, bias, mask)


def moe_fwd_body(
    h_one, vec, w1, w2, b1, router, router_bias, place_col, place_row,
    out, normed_two, disp, act, slope, picked, gap_out, rows_out, onehot, onehot_t,
):
    fill_onehot(onehot, place_col)
    fill_onehot_t(onehot_t, place_row)
    normal, _ = normalize(h_one[...])
    two = (normal * vec[2:3] + vec[3:4]).astype(BF)
    normed_two[...] = two
    logits = nn(two, router[...])
    gap = (logits[:, LANES:] + router_bias[1:2]) - (logits[:, :LANES] + router_bias[0:1])
    gap = jnp.where(place_col[...] >= SLOTS // 2, gap, -gap)
    gap_out[...] = gap
    gate = 1.0 / (1.0 + jnp.exp(-gap))
    disp[...] = nn(onehot_t[...], two).astype(BF)

    @pl.loop(0, 4, unroll=4)
    def _(t):
        rows = pl.ds(pl.multiple_of(t * 256, 256), 256)
        e = t // 2
        own = disp[rows, :]
        for c in range(3):
            cols = slice(c * 512, (c + 1) * 512)
            pre = nn(own, w1[e, :, cols]) + b1[pl.ds(e, 1), cols]
            phi = 0.5 * (1.0 + lax.erf(pre * 0.7071067811865476))
            act[rows, cols] = (pre * phi).astype(BF)
            slope[rows, cols] = (
                phi + pre * jnp.exp(-0.5 * pre * pre) * 0.3989422804014327
            ).astype(BF)
        rows_out[rows, :] = (nn(act[rows, :], w2[e]) + vec[pl.ds(7 + e, 1)]).astype(BF)

    taken = nn(onehot[...], rows_out[...])
    picked[...] = taken.astype(BF)
    for c in range(3):
        cols = slice(c * LANES, (c + 1) * LANES)
        out[:, cols] = (h_one[:, cols] + gate * taken[:, cols]).astype(out.dtype)


def moe_fwd(h_one, vec, w1, w2, b1, router, router_bias, place, out_dtype, deps=()):
    return call(
        moe_fwd_body,
        (
            sds((CELLS, D), out_dtype),
            sds((CELLS, D), BF),
            sds((SLOTS, D), BF),
            sds((SLOTS, F), BF),
            sds((SLOTS, F), BF),
            sds((CELLS, D), BF),
            sds((CELLS, LANES), F32),
        ),
        9,
        scratch=[pltpu.VMEM((SLOTS, D), BF), ONEHOT, ONEHOT_T],
        us=9.5,
        deps=deps,
    )(h_one, vec, w1, w2, b1, router, router_bias, *place)


def fill_onehot(onehot, place_col):
    @pl.loop(0, 7)
    def _(t):
        rows = pl.ds(pl.multiple_of(t * 112, 112), 112)
        place = jnp.concatenate([place_col[rows, :]] * 8, axis=1)
        same = place == lax.broadcasted_iota(jnp.int32, (112, SLOTS), 1)
        onehot[rows, :] = jnp.where(same, 1.0, 0.0).astype(BF)


def fill_onehot_t(onehot_t, place_row):
    @pl.loop(0, 8)
    def _(t):
        row = lax.broadcasted_iota(jnp.int32, (128, CELLS), 0) + t * 128
        same = row == place_row[0:1, :]
        onehot_t[pl.ds(pl.multiple_of(t * 128, 128), 128), :] = jnp.where(same, 1.0, 0.0).astype(BF)


def moe_bwd_body(
    grad, w2, place_col, place_row, disp, act, slope, picked, gap,
    dw1, dw2, db1, small, g_pre, gate_grad, g_rows, onehot_t,
):
    fill_onehot_t(onehot_t, place_row)
    go = grad[...].astype(F32)
    gate = 1.0 / (1.0 + jnp.exp(-gap[...]))
    other = 1.0 / (1.0 + jnp.exp(gap[...]))
    g_picked = (go * jnp.concatenate([gate] * 3, axis=1)).astype(BF)
    g_gate = jnp.sum(go * picked[...].astype(F32), axis=-1, keepdims=True)
    sign = jnp.where(place_col[...] >= SLOTS // 2, 1.0, -1.0)
    gl = (g_gate * gate * other * sign).astype(BF)
    gate_grad[...] = gl
    small[...] = jnp.zeros((16, D), F32)
    small[9:10, 0:LANES] = jnp.sum(gl.astype(F32), axis=0, keepdims=True)
    g_rows[...] = nn(onehot_t[...], g_picked).astype(BF)

    @pl.loop(0, EXPERTS, unroll=2)
    def _(e):
        both = pl.ds(pl.multiple_of(e * 512, 512), 512)
        own = g_rows[both, :]
        total = []
        grads = [nt(own, w2[e, c * 256 : (c + 1) * 256, :]) for c in range(6)]
        for c, part in enumerate(grads):
            cols = slice(c * 256, (c + 1) * 256)
            gp = (part * slope[both, cols].astype(F32)).astype(BF)
            g_pre[both, cols] = gp
            total.append(jnp.sum(gp.astype(F32), axis=0, keepdims=True))
        db1[pl.ds(e, 1), :] = jnp.concatenate(total, axis=1)
        small[pl.ds(7 + e, 1), :] = jnp.sum(own.astype(F32), axis=0, keepdims=True)
        for c in range(6):
            cols = slice(c * 256, (c + 1) * 256)
            dw1[e, :, cols] = tn(disp[both, :], g_pre[both, cols])
            dw2[e, cols, :] = tn(act[both, cols], own)


def moe_bwd(grad, w2, place, saved):
    return call(
        moe_bwd_body,
        (
            sds((EXPERTS, D, F), F32),
            sds((EXPERTS, F, D), F32),
            sds((8, F), F32),
            sds((16, D), F32),
            sds((SLOTS, F), BF),
            sds((CELLS, LANES), BF),
        ),
        9,
        scratch=[pltpu.VMEM((SLOTS, D), BF), ONEHOT_T],
        us=8,
    )(grad, w2, *place, *saved)


def middle_bwd_body(vec, w1, place_col, g_pre, gate_grad, g_two, onehot, g_disp):
    fill_onehot(onehot, place_col)
    for e in range(EXPERTS):
        both = slice(e * 512, (e + 1) * 512)
        g_disp[both, :] = nt(g_pre[both, :], w1[e]).astype(BF)
    gl = gate_grad[...].astype(F32)
    g_two[...] = nn(onehot[...], g_disp[...]) + jnp.concatenate([gl] * 3, axis=1) * vec[9:10]


def middle_bwd(vec, w1, place_col, g_pre, gate_grad):
    return call(
        middle_bwd_body,
        sds((CELLS, D), F32),
        5,
        scratch=[ONEHOT, pltpu.VMEM((SLOTS, D), BF)],
        us=5,
    )(vec, w1, place_col, g_pre, gate_grad)


def attn_bwd_windows(windows, qkv, g_mix, attn, g_qkv, dbias, base=None):
    masks = head_masks()
    base = windows[0] if base is None else base

    start, stop = windows
    per = min(4, stop - start)

    @pl.loop(0, (stop - start) // per)
    def _(wo):
        units = [(i, g) for i in range(per) for g in range(QUADS)]
        first = [start + wo * per + i for i in range(per)]
        rows = [pl.ds(pl.multiple_of(w * WROWS, WROWS), WROWS) for w in first]
        outs = [pl.ds(pl.multiple_of((w - base) * WROWS, WROWS), WROWS) for w in first]
        cols = [[slice(n * D + g * LANES, n * D + (g + 1) * LANES) for g in range(QUADS)] for n in range(3)]
        d4s = [stack_heads(g_mix[rows[i], cols[0][g]], masks) for i, g in units]
        grads = [nt(qkv[rows[i], cols[2][g]], d4) for (i, g), d4 in zip(units, d4s)]
        probs = [attn[first[i] * QUADS + g] for i, g in units]
        for (i, g), a, d4 in zip(units, probs, d4s):
            g_qkv[outs[i], cols[2][g]] = nn(a, d4).astype(BF)
        dss = []
        for a, grad in zip(probs, grads):
            a = a.astype(F32)
            t = a * grad
            dss.append((t - a * jnp.sum(t, axis=0, keepdims=True)).astype(BF))
        for g in range(QUADS):
            total = dbias[g]
            for (_, other), ds in zip(units, dss):
                if other == g:
                    total = total + ds.astype(F32)
            dbias[g] = total
        talls = [tn(ds, qkv[rows[i], cols[1][g]]) for (i, g), ds in zip(units, dss)]
        for (i, g), ds in zip(units, dss):
            q4 = stack_heads(qkv[rows[i], cols[0][g]], masks)
            g_qkv[outs[i], cols[1][g]] = (nn(ds, q4) * SCALE).astype(BF)
        for (i, g), tall in zip(units, talls):
            g_qkv[outs[i], cols[0][g]] = (fold_heads(tall, masks) * SCALE).astype(BF)


def attn_bwd_body(
    shifted, grad, h_one, vec, w_out, normed_two, gate_grad, mixed, g_two, qkv, attn,
    grad_one, g_qkv, dw_out, dbias, drouter, small, g_mix, patches, windows_of,
):
    drouter[...] = tn(gate_grad[...], normed_two[...])[0:8]
    normal, inverse = normalize(h_one[...])
    small[...] = jnp.zeros((16, D), F32)
    small[2:3] = jnp.sum(g_two[...] * normal, axis=0, keepdims=True)
    small[3:4] = jnp.sum(g_two[...], axis=0, keepdims=True)
    grad_one[...] = grad[...].astype(F32) + norm_backward(g_two[...], normal, inverse, vec[2:3])
    small[6:7] = jnp.sum(grad_one[...].astype(BF).astype(F32), axis=0, keepdims=True)
    patches[:CELLS, :] = grad_one[...]
    to_windows(patches, windows_of, shifted)
    gao_w = windows_of[...].astype(BF)
    dw_out[...] = tn(mixed[...], gao_w)
    g_mix[...] = nt(gao_w, w_out[...]).astype(BF)
    dbias[...] = jnp.zeros_like(dbias)
    attn_bwd_windows((0, WINDOWS), qkv, g_mix, attn, g_qkv, dbias)


def attn_bwd(shifted, grad, h_one, vec, w_out, normed_two, gate_grad, mixed, g_two, qkv, attn):
    return call(
        functools.partial(attn_bwd_body, shifted),
        (
            sds((CELLS, D), F32),
            sds((WTOK, 3 * D), BF),
            sds((D, D), F32),
            sds((QUADS, WROWS, PAIR), F32),
            sds((8, D), F32),
            sds((16, D), F32),
        ),
        10,
        scratch=[pltpu.VMEM((WTOK, D), BF), PATCHES, PADDED],
        us=5,
        vmem=BIG_VMEM,
    )(grad, h_one, vec, w_out, normed_two, gate_grad, mixed, g_two, qkv, attn)


def proj_bwd_body(
    shifted, grad_one, hid, vec, w_in, wn, g_qkv, grad_in, dw_in, small, patches, windows_of,
):
    for c in range(3):
        cols = slice(c * D, (c + 1) * D)
        dw_in[:, cols] = tn(wn[...], g_qkv[:, cols])
    windows_of[...] = nt(g_qkv[...], w_in[...])
    to_patches(windows_of, patches, shifted)
    g_normed = patches[:CELLS, :]
    normal, inverse = normalize(hid[...].astype(F32))
    small[...] = jnp.zeros((16, D), F32)
    small[0:1] = jnp.sum(g_normed * normal, axis=0, keepdims=True)
    small[1:2] = jnp.sum(g_normed, axis=0, keepdims=True)
    small[4:5] = jnp.sum(g_qkv[:, :D].astype(F32), axis=0, keepdims=True)
    small[5:6] = jnp.sum(g_qkv[:, 2 * D :].astype(F32), axis=0, keepdims=True)
    grad_in[...] = grad_one[...] + norm_backward(g_normed, normal, inverse, vec[0:1])


def proj_bwd(shifted, grad_one, hid, vec, w_in, wn, g_qkv):
    return call(
        functools.partial(proj_bwd_body, shifted),
        (sds((CELLS, D), F32), sds((D, 3 * D), F32), sds((16, D), F32)),
        6,
        scratch=[PATCHES, PADDED],
        us=0.5,
    )(grad_one, hid, vec, w_in, wn, g_qkv)


def window_perm_t(shifted):
    source = patch_of(jnp.arange(WTOK, dtype=jnp.int32), shifted)
    return (jnp.arange(CELLS, dtype=jnp.int32)[:, None] == source[None, :]).astype(BF)


def wrap_codes(shifted):
    code = np.zeros((CELLS,), np.float32)
    if shifted:
        for r in range(SIDE):
            for s in range(SIDE):
                rr, ss = (r - SHIFT) % SIDE, (s - SHIFT) % SIDE
                code[r * SIDE + s] = 2 * (rr >= SIDE - SHIFT) + (ss >= SIDE - SHIFT)
    return code


def window_masks(items, shifted):
    labels = items.astype(F32)
    if shifted:
        labels = labels * 4.0 + jnp.asarray(wrap_codes(True))
    placed = nn(jnp.broadcast_to((labels + 1.0).astype(BF), (8, CELLS)), window_perm_t(shifted))[0]
    placed = placed.reshape(WINDOWS, WROWS)
    same = (placed[:, :, None] == placed[:, None, :]) & (placed[:, :, None] > 0.0)
    same = same.astype(F32)
    return jnp.concatenate([same, same], axis=2)


def slot_places(routes, slots):
    group = (jnp.arange(CELLS, dtype=jnp.int32) // GROUP) * CAP
    place = routes * (2 * CAP) + group + slots
    return jnp.broadcast_to(place[:, None], (CELLS, LANES)), jnp.broadcast_to(place[None, :], (8, CELLS))

LEAD = 73
SMALL = 9326
LAG = LEAD * LANES - SMALL
VECTORS = 9
LINES = 32
SPANS = ((LEAD, D, 9), (LEAD + 3456, D, 3), (LEAD + 4608, 2 * D, 12), (LEAD + 4608 + 9216, 2 * F, 3))
EDGE = LEAD + 4608
ALIGNED = LEAD + 4608 + 2 * 9216


def relative(k, bits):
    total = 0
    for place, bit in enumerate(bits):
        total = total + (((k >> (len(bits) - 1 - place)) & 1) << bit)
    return total


def lanes_of(count=LANES):
    return lax.broadcasted_iota(jnp.int32, (1, count), 1)


def equal(rows, columns):
    return jnp.where(rows == columns, 1.0, 0.0).astype(BF)


def spread(shape):
    return lax.broadcasted_iota(jnp.int32, shape, 0), lax.broadcasted_iota(jnp.int32, shape, 1)


def exact(left, one, product):
    high = left.astype(BF)
    low = (left - high.astype(F32)).astype(BF)
    return product(high, one) + product(low, one)


def head_major():
    f, g = spread((D, D))
    return equal(f, 12 * (g & 31) + (g >> 5))


def head_rows(m):
    f, g = spread((D, 2 * LANES))
    return equal((f & 31) + 32 * m, g)


def offset_lanes():
    f, g = spread((LANES, LANES))
    i = g & 63
    r = (i * 37) >> 8
    return equal(f, jnp.where(i < WIN * WIN, 13 * r + i - WIN * r, -1))


def turns():
    return [13 * (6 - j // WIN) + 6 - j % WIN for j in range(WIN * WIN)]


def unpack_bias(flat, wide, tall, bias):
    wide[...] = jnp.zeros_like(wide)
    for m in range(6):
        for c in range(3):
            wide[m : m + 1, c * LANES : (c + 1) * LANES] = flat[12 + 3 * m + c : 13 + 3 * m + c, :]
    by_head = nn(wide[...].astype(BF), head_major())
    sub = lax.broadcasted_iota(jnp.int32, (16, D), 0)
    own = (lanes_of(D) >> 5) == sub
    table = jnp.zeros((16, 2 * LANES), F32)
    for m in range(6):
        table = table + nn(jnp.where(own, by_head[m : m + 1], 0.0).astype(BF), head_rows(m))
    tall[...] = jnp.zeros_like(tall)
    for j, turn in enumerate(turns()):
        row = pltpu.roll(table, (2 * LANES - turn) % (2 * LANES), 1)[:, :LANES]
        tall[pl.ds(j, 16, stride=WROWS), :] = row
    tall[...] = nn(tall[...].astype(BF), offset_lanes())
    for g in range(QUADS):
        for t in range(2):
            h = 4 * g + 2 * t
            left, right = tall[h * WROWS : (h + 1) * WROWS], tall[(h + 1) * WROWS : (h + 2) * WROWS]
            bias[g, :, t * LANES : (t + 1) * LANES] = jnp.where(lanes_of() < WROWS, left, right)


def unpack_small(flat, rows, wide, tall, vec, b1, router, router_bias, bias):
    def shifted(first, count, by):
        near, far = flat[first : first + count, :], flat[first + 1 : first + 1 + count, :]
        return pltpu.roll(jnp.where(lanes_of() >= by, near, far), LANES - by, 1)

    rows[0:16, :] = shifted(27, 16, 108)
    rows[16:46, :] = shifted(42, 30, 110)
    vec[...] = jnp.zeros_like(vec)
    b1[...] = jnp.zeros_like(b1)
    for c in range(3):
        cols = slice(c * LANES, (c + 1) * LANES)
        for n in range(4):
            vec[n : n + 1, cols] = flat[3 * n + c : 3 * n + c + 1, :]
        for n in range(3):
            vec[4 + n : 5 + n, cols] = rows[3 * n + c : 3 * n + c + 1, :]
        for e in range(EXPERTS):
            vec[7 + e : 8 + e, cols] = rows[40 + 3 * e + c : 41 + 3 * e + c, :]
    for e in range(EXPERTS):
        for c in range(12):
            b1[e : e + 1, c * LANES : (c + 1) * LANES] = rows[16 + 12 * e + c : 17 + 12 * e + c, :]
        one = jnp.sum(jnp.where(lanes_of() == e, rows[15:16, :], 0.0), axis=1, keepdims=True)
        router_bias[e : e + 1, :] = jnp.broadcast_to(one, (1, LANES))
    pairs = jnp.concatenate([rows[9 + c : 10 + c, :] for c in range(6)], axis=1)
    pairs = jnp.broadcast_to(pairs, (LANES, 2 * D)).astype(BF)
    d, f = spread((D, 2 * D))
    for e in range(EXPERTS):
        router[:, e * LANES : (e + 1) * LANES] = nt(equal(f, 2 * d + e), pairs).astype(BF)
    gap = nt(pairs[0:16], equal(f, 2 * d + 1)) - nt(pairs[0:16], equal(f, 2 * d))
    vec[9:10, :] = gap[0:1]
    unpack_bias(flat, wide, tall, bias)


def unpack_matrices(flat, spans, outs, skipped):
    for (base, height, tiles), out in zip(spans, outs):
        step = 128

        @pl.loop(0, height // step, unroll=min(6, height // step))
        def _(t, base=base, tiles=tiles, out=out):
            first = base - 1 - skipped + t * (step * tiles)
            before = flat[pl.ds(first, step, stride=tiles), :]
            for j in range(tiles):
                here = flat[pl.ds(first + 1 + j, step, stride=tiles), :]
                tile = pltpu.roll(jnp.where(lanes_of() >= LANES - LAG, before, here), LAG, 1)
                out[pl.ds(pl.multiple_of(t * step, step), step), j * LANES : (j + 1) * LANES] = tile.astype(BF)
                before = here


def unpack_head_body(rows, runs, me, *refs):
    got = refs[: len(runs)]
    w_in, w_out, rest, vec, b1, router, router_bias, bias, flat, few, wide, tall = refs[len(runs) :]
    for (bits, fixed), part in zip(runs, got):
        n, half = 1 << len(bits), part.shape[1]

        @pl.loop(0, n)
        def _(k, bits=bits, fixed=fixed, part=part, n=n, half=half):
            d = me[1] ^ (relative(k, bits) + fixed)
            flat[pl.ds(d * rows, half), :] = part[k].astype(F32)
            flat[pl.ds(d * rows + half, rows - half), :] = part[n + k].astype(F32)[: rows - half]

    unpack_small(flat, few, wide, tall, vec, b1, router, router_bias, bias)
    unpack_matrices(flat, SPANS[:2], (w_in, w_out), 0)
    rest[...] = flat[EDGE - 1 : EDGE - 1 + rest.shape[0], :]


def unpack_tail_body(rows, heads, runs, me, rest, *refs):
    got = refs[: len(runs)]
    w1, w2, flat = refs[len(runs) :]
    flat[0 : rest.shape[0], :] = rest[...]
    for (outer, inner, fixed, upper, skip), part in zip(runs, got):
        count = 1 << len(inner)
        half = part.shape[1]
        first = half if upper else 0
        used = min(half, rows - first)

        @pl.loop(0, 3 * count << len(outer), unroll=3)
        def _(k, outer=outer, inner=inner, fixed=fixed, part=part, count=count, first=first, used=used, skip=skip):
            own = (relative(k // (3 * count), outer) + relative(k % count, inner) + fixed) ^ me[1]
            d = ((k // count) % 3 + 1) * heads + own
            flat[pl.ds(d * rows + first - (EDGE - 1), used), :] = part[skip + k].astype(F32)[:used]

    unpack_matrices(flat, SPANS[2:], (w1, w2), EDGE - 1)


class Weights(NamedTuple):
    w_in: Any
    w_out: Any
    w1: Any
    w2: Any
    vec: Any
    b1: Any
    router: Any
    router_bias: Any
    bias: Any


SMALL_SHAPES = (
    sds((16, D), F32),
    sds((8, F), F32),
    sds((D, 2 * LANES), BF),
    sds((8, LANES), F32),
    sds((QUADS, WROWS, PAIR), F32),
)
SMALL_SCRATCH = [pltpu.VMEM((48, LANES), F32), pltpu.VMEM((8, D), F32), pltpu.VMEM((17 * WROWS, LANES), F32)]
HEAD_SHAPES = (sds((D, 3 * D), BF), sds((D, D), BF))
TAIL_SHAPES = (sds((2 * D, F), BF), sds((2 * F, D), BF))


def experts(w1, w2):
    return w1.reshape(EXPERTS, D, F), w2.reshape(EXPERTS, F, D)


def unpack_head(me, parts, runs, rows, devices):
    heads = devices // 4
    w_in, w_out, rest, *small = call(
        functools.partial(unpack_head_body, rows, runs),
        HEAD_SHAPES + (sds((heads * rows - EDGE + 1, LANES), F32),) + SMALL_SHAPES,
        1 + len(parts),
        scratch=[pltpu.VMEM((heads * rows + 8, LANES), F32)] + SMALL_SCRATCH,
        smem=1,
        us=4,
    )(me, *parts)
    return Weights(w_in, w_out, None, None, *small), rest


def unpack_tail(me, rest, parts, runs, rows, devices):
    return experts(
        *call(
            functools.partial(unpack_tail_body, rows, devices // 4, runs),
            TAIL_SHAPES,
            2 + len(parts),
            scratch=[pltpu.VMEM((devices * rows - EDGE + 9, LANES), F32)],
            smem=1,
            vmem=BIG_VMEM,
            us=4,
        )(me, rest, *parts)
    )


def pack_bias(dbias, wide, tall):
    tall[HEADS * WROWS :, :] = jnp.zeros((5 * WROWS, LANES), F32)
    for h in range(HEADS):
        g, t, side = h // 4, (h % 4) // 2, h % 2
        tile = dbias[g, :, t * LANES : (t + 1) * LANES]
        tall[h * WROWS : (h + 1) * WROWS, :] = jnp.where((lanes_of() >> 6) == side, tile, 0.0)
    used = HEADS * WROWS
    tall[0:used, :] = exact(tall[0:used, :], offset_lanes(), nt)
    table = jnp.zeros((16, 2 * LANES), F32)
    for j, turn in enumerate(turns()):
        row = tall[pl.ds(j, 16, stride=WROWS), :]
        table = table + pltpu.roll(jnp.concatenate([row, jnp.zeros_like(row)], axis=1), turn, 1)
    sub = lax.broadcasted_iota(jnp.int32, (16, D), 0)
    own = (lanes_of(D) >> 5) == sub
    wide[...] = jnp.zeros_like(wide)
    for m in range(6):
        placed = jnp.where(own, exact(table, head_rows(m), nt), 0.0)
        wide[m : m + 1, :] = jnp.sum(placed, axis=0, keepdims=True)
    wide[...] = exact(wide[...], head_major(), nt)


def pack_small(al, vectors, drouter, db1, dbias, one, two, wide, tall):
    one[...] = jnp.zeros_like(one)
    two[...] = jnp.zeros_like(two)
    pack_bias(dbias, wide, tall)
    d, f = spread((D, 2 * D))
    signs = equal(f, 2 * d + 1) - equal(f, 2 * d)
    pairs = exact(drouter[...], signs, nn)
    for c in range(3):
        cols = slice(c * LANES, (c + 1) * LANES)
        for n in range(4):
            one[1 + 3 * n + c : 2 + 3 * n + c, :] = vectors[n : n + 1, cols]
        for m in range(6):
            one[13 + 3 * m + c : 14 + 3 * m + c, :] = wide[m : m + 1, cols]
        for n in range(3):
            two[1 + 3 * n + c : 2 + 3 * n + c, :] = vectors[4 + n : 5 + n, cols]
        for e in range(EXPERTS):
            al[67 + 3 * e + c : 68 + 3 * e + c, :] = vectors[7 + e : 8 + e, cols]
    for c in range(6):
        two[10 + c : 11 + c, :] = pairs[0:1, c * LANES : (c + 1) * LANES]
    total = vectors[9:10, 0:LANES]
    two[16:17, :] = jnp.where(lanes_of() == 0, -total, jnp.where(lanes_of() == 1, total, 0.0))
    for e in range(EXPERTS):
        for c in range(12):
            al[43 + 12 * e + c : 44 + 12 * e + c, :] = db1[e : e + 1, c * LANES : (c + 1) * LANES]
    first = pltpu.roll(jnp.where(lanes_of() >= LANES - 18, one[0:28, :], one[1:29, :]), 18, 1)
    second = pltpu.roll(jnp.where(lanes_of() >= LANES - 126, two[0:16, :], two[1:17, :]), 126, 1)
    al[27:43, :] = second
    al[0:27, :] = first[0:27]
    al[27:28, :] += first[27:28]


def pack_matrices(al, spans, grads, skipped):
    for (base, height, tiles), grad in zip(spans, grads):
        step = 128

        @pl.loop(0, height // step, unroll=min(6, height // step))
        def _(t, base=base, tiles=tiles, grad=grad):
            first = base - skipped + t * (step * tiles)
            own = pl.ds(pl.multiple_of(t * step, step), step)
            for j in range(tiles):
                al[pl.ds(first + j, step, stride=tiles), :] = grad[own, j * LANES : (j + 1) * LANES]


def clear(al, first):
    al[pl.ds(first, al.shape[0] - first), :] = jnp.zeros((al.shape[0] - first, LANES), F32)


def pack_head_body(
    rows, padded, runs, me, moe, attn, proj, drouter, db1, dbias, dw_in, dw_out, rest,
    keep, send, al, vectors, lines, one, two, wide, tall,
):
    vectors[...] = moe[...] + attn[...] + proj[...]
    lines[...] = jnp.zeros_like(lines)
    for n in range(VECTORS):
        for c in range(3):
            lines[3 * n + c : 3 * n + c + 1, :] = vectors[n : n + 1, c * LANES : (c + 1) * LANES]
    pack_small(al, vectors, drouter, db1, dbias, one, two, wide, tall)
    pack_matrices(al, SPANS[:2], (dw_in, dw_out), 0)
    al[EDGE : EDGE + rest.shape[0], :] = rest[...]
    at = 0
    for bits, fixed in runs:
        for other, out in enumerate((keep, send)):

            @pl.loop(0, 1 << len(bits))
            def _(k, bits=bits, fixed=fixed, at=at, other=other, out=out):
                d = me[1] ^ (relative(k, bits) + fixed + other)
                out[at + k, :padded, :] = al[pl.ds(d * rows, padded), :].astype(BF)
                out[at + k, padded:, :] = lines[...].astype(BF)

        at += 1 << len(bits)


def pack_tail_body(rows, padded, heads, runs, me, dw1, dw2, keep, send, rest, al):
    clear(al, ALIGNED - EDGE)
    pack_matrices(al, SPANS[2:], (dw1, dw2), EDGE)
    rest[...] = al[0 : rest.shape[0], :]
    half = padded // 2
    at = 0
    for outer, inner, fixed, upper in runs:
        count = 1 << len(inner)
        total = 3 * count << len(outer)
        for other, out in enumerate((keep, send)):

            @pl.loop(0, total, unroll=3)
            def _(k, outer=outer, inner=inner, fixed=fixed, upper=upper, count=count, at=at, other=other, out=out):
                own = (relative(k // (3 * count), outer) + relative(k % count, inner) + fixed + other) ^ me[1]
                d = ((k // count) % 3 + 1) * heads + own
                out[at + k] = al[pl.ds(d * rows + (half if upper else 0) - EDGE, half), :].astype(BF)

        at += total


SMALL_PACK = [
    pltpu.VMEM((40, LANES), F32),
    pltpu.VMEM((24, LANES), F32),
    pltpu.VMEM((8, D), F32),
    pltpu.VMEM((17 * WROWS, LANES), F32),
]


def pack_head(me, small, dw_in, dw_out, rest, runs, rows, devices, padded):
    heads = devices // 4
    shape = sds((heads // 2, padded + LINES, LANES), BF)
    return call(
        functools.partial(pack_head_body, rows, padded, runs),
        (shape, shape),
        10,
        scratch=[
            pltpu.VMEM((EDGE + rest.shape[0], LANES), F32),
            pltpu.VMEM((16, D), F32),
            pltpu.VMEM((LINES, LANES), F32),
        ]
        + SMALL_PACK,
        smem=1,
        us=0.5,
    )(me, *small, dw_in, dw_out, rest)


def pack_tail(me, dw1, dw2, runs, rows, devices, padded):
    heads = devices // 4
    shape = sds((3 * heads, padded // 2, LANES), BF)
    over = -(-(heads * rows + padded - EDGE) // 8) * 8
    return call(
        functools.partial(pack_tail_body, rows, padded, heads, runs),
        (shape, shape, sds((over, LANES), F32)),
        3,
        scratch=[pltpu.VMEM((devices * rows + padded - EDGE, LANES), F32)],
        smem=1,
        vmem=BIG_VMEM,
        us=3,
    )(me, dw1.reshape(2 * D, F), dw2.reshape(2 * F, D))


def levels_body(sources, me, *refs):
    pieces, (x, y, head) = refs[: len(refs) - 3], refs[len(refs) - 3 :]
    n, half = head.shape[0] // 2, x.shape[1]
    for level in range(4):
        for step, (at, first) in enumerate(sources):

            @pl.when((me[2] ^ step) == level)
            def _(level=level, at=at, first=first):
                for i in range(n):
                    lower, upper = pieces[at][first * n + i, :half, :], pieces[at][first * n + i, half:, :]
                    if level == 0:
                        for out in (x, y, head):
                            out[i] = lower
                            out[n + i] = upper
                    else:
                        x[(1 + level) * n + i] = lower
                        y[(1 + level) * n + i] = upper


def levels(me, *pieces):
    sources = ((0, 0), (1, 0), (2, 0), (3, 0)) if len(pieces) == 4 else ((0, 0), (1, 0), (0, 1), (1, 1))
    n, padded, _ = pieces[0].shape
    n = n * len(pieces) // 4
    dtype = pieces[0].dtype
    shapes = [sds((count * n, padded // 2, LANES), dtype) for count in (5, 5, 2)]
    return call(functools.partial(levels_body, sources), shapes, 1 + len(pieces), smem=1)(me, *pieces)


def targets_body(with_head, me, a, a_got, b, b_got, *refs):
    *head, keep, send = refs
    n, half = keep.shape[0] // 2, a.shape[1]
    places = {0: (keep, 0), 2: (keep, n), 1: (send, 0), 3: (send, n)}
    for step, (out, first) in places.items():
        level = me[2] ^ step

        @pl.when(level == 0)
        def _(out=out, first=first):
            for i in range(n):
                if with_head:
                    out[first + i] = head[0][i, : 2 * half, :].astype(out.dtype)
                else:
                    out[first + i] = jnp.zeros((2 * half, LANES), out.dtype)

        @pl.when(level > 0)
        def _(out=out, first=first, level=level):
            for i in range(n):
                at = (level - 1) * n + i
                out[first + i, :half, :] = (a[at] + a_got[at].astype(F32)).astype(out.dtype)
                out[first + i, half:, :] = (b[at] + b_got[at].astype(F32)).astype(out.dtype)


def targets(me, a, a_got, b, b_got, *head):
    n, half, _ = a.shape
    n = n // 3
    shape = (2 * n, 2 * half, LANES)
    return call(
        functools.partial(targets_body, bool(head)), (sds(shape, F32), sds(shape, BF)), 5 + len(head), smem=1
    )(me, a, a_got, b, b_got, *head)


def combine_body(plan, count, *refs):
    for (size, _, terms), out in zip(plan, refs[count:]):

        @pl.loop(0, size)
        def _(i, terms=terms, out=out):
            parts = [refs[at][first + i].astype(F32) for at, first in terms]
            while len(parts) > 1:
                parts = [sum(parts[at + 1 : at + 2], parts[at]) for at in range(0, len(parts), 2)]
            out[i] = parts[0].astype(out.dtype)


def combine(plan, *arrays):
    tail = arrays[0].shape[1:]
    shapes = [sds((size, *tail), dtype) for size, dtype, _ in plan]
    return call(functools.partial(combine_body, plan, len(arrays)), shapes, len(arrays))(*arrays)


def finish_body(rows, me, keep, got, upper_keep, upper_got, out):
    def shift(keep, got):
        total = keep[0] + got[0].astype(F32)
        here, below = total[0:rows, :], total[1 : rows + 1, :]
        out[...] = pltpu.roll(jnp.where(lanes_of() >= LAG, here, below), LANES - LAG, 1)

    pl.when(me[2] == 0)(lambda: shift(keep, got))
    pl.when(me[2] != 0)(lambda: shift(upper_keep, upper_got))


def finish(me, rows, lowest, upper):
    parts = (lowest.keep, lowest.got, upper.keep, upper.got)
    return call(functools.partial(finish_body, rows), sds((rows, LANES), F32), 5, smem=1)(me, *parts)


def join_body(skip, a, b, out):
    n = out.shape[0] // 2

    @pl.loop(0, n)
    def _(i):
        out[i] = a[skip + i]
        out[n + i] = b[skip + i]


def join(a, b, skip=0):
    shape = sds((2 * (a.shape[0] - skip), *a.shape[1:]), a.dtype)
    return call(functools.partial(join_body, skip), shape, 2)(a, b)


class Ways(NamedTuple):
    core: Any
    x: Any
    y: Any
    low: Any
    high: Any
    rest: Any


def ways():
    dp, fsdp = (lax.axis_size(axis).bit_length() - 1 for axis in (DP, FSDP))
    rest = [1 << (fsdp + bit) for bit in range(1, dp - 2)] + [1 << bit for bit in range(2, fsdp)]
    return Ways(1, 2, 1 << fsdp, 1 << (fsdp + dp - 2), 1 << (fsdp + dp - 1), rest)


def device_count():
    return lax.axis_size(DP) * lax.axis_size(FSDP)


def flip(array, step):
    return lax.ppermute(array, (DP, FSDP), [(i, i ^ step) for i in range(device_count())])


def move(array, levels):
    width = device_count() // 4
    pairs = [(a * width + i, b * width + i) for a, b in levels.items() for i in range(width)]
    return lax.ppermute(array, (DP, FSDP), pairs)


def tie(arrays, *others):
    if isinstance(arrays, tuple):
        return tuple(tie(array, *others) for array in arrays)
    return lax.optimization_barrier((arrays, *others))[0]


def sync(*arrays):
    return lax.optimization_barrier(arrays)


def bits_of(*steps):
    return [step.bit_length() - 1 for step in steps]


class Gather:
    def __init__(self, own, way, me):
        for extra in way.rest:
            own = join(own, flip(own, extra))
        self.way, self.own, self.me, self.others = way, own, me, None
        self.rest = bits_of(*reversed(way.rest))

    def far(self):
        own, way = self.own, self.way
        self.others = own, flip(own, way.low), flip(own, way.high), flip(own, way.low + way.high)

    def high(self):
        self.other = flip(self.own, self.way.high)

    def low(self):
        self.pair = join(self.own, self.other)
        self.over = flip(self.pair, self.way.low)

    def levels(self):
        pieces = self.others if self.others else (self.pair, self.over)
        self.x, self.y, self.head = levels(self.me, *pieces)

    def near(self):
        way = self.way
        self.got = [flip(self.x, way.x), flip(self.y, way.y), flip(self.head, way.x + way.y)]

    def near_core(self):
        way, core = self.way, self.way.core
        x, y, both = self.got
        sides = [[self.x, x, y, both, self.y]]
        sides.append([flip(part, core) for part in sides[0]])
        self.head_parts, self.head_runs, self.parts, self.runs = [], [], [], []
        for fixed, side in zip((0, core), sides):
            self.head_parts += side[:4]
            self.head_runs += [(self.rest, step + fixed) for step in (0, way.x, way.y, way.x + way.y)]
            x_own, x_got, y_got, _, y_own = side
            self.parts += [x_own, x_got, y_own, y_got]
            skip = 2 << len(self.rest)
            self.runs += [([], self.rest, fixed + step, False, skip) for step in (0, way.x)]
            self.runs += [([], self.rest, fixed + step, True, skip) for step in (0, way.y)]

    def last(self):
        way, skip = self.way, 2 << len(self.rest)
        self.joined = join(self.x, self.got[0], skip), join(self.y, self.got[1], skip)
        self.last_got = flip(self.joined[0], way.y), flip(self.joined[1], way.x)

    def last_core(self):
        way = self.way
        for fixed in (0, way.core):
            self.parts += [flip(part, way.core) for part in self.last_got] if fixed else list(self.last_got)
            self.runs += [(bits_of(way.x), self.rest, way.y + fixed, False, 0)]
            self.runs += [(bits_of(way.y), self.rest, way.x + fixed, True, 0)]


def head_runs(way):
    rest = bits_of(*way.rest)
    return [(rest, step) for step in (way.y, way.x + way.y, way.x, 0)]


def tail_runs(way):
    rest, bx, by = (bits_of(*steps) for steps in (way.rest, [way.x], [way.y]))
    return [
        (bx, rest, way.y, False), ([], rest, way.x, False), ([], rest, 0, False),
        (by, rest, way.x, True), ([], rest, way.y, True), ([], rest, 0, True),
    ]


class HeadScatter:
    def __init__(self, keep, send, way):
        self.way, self.keep, self.n = way, keep, keep.shape[0] // 4
        self.got = flip(send, way.core)

    def plane(self):
        n, way = self.n, self.way
        y, xy, x, self.keep = combine([(n, BF, ((0, i * n), (1, i * n))) for i in range(4)], self.keep, self.got)
        self.got = flip(x, way.x), flip(y, way.y), flip(xy, way.x + way.y)

    def near(self):
        n = 2 * self.n
        sent, self.keep = combine([(n, BF, ((0, i * n), (1, i * n))) for i in range(2)], self.keep, self.got)
        self.got = flip(sent, self.way.y)

    def next(self):
        n = self.n
        sent, self.keep = combine(((n, BF, ((0, 0), (1, n))), (n, BF, ((0, n), (1, 0)))), self.keep, self.got)
        self.got = flip(sent, self.way.x)

    def add(self):
        n, got = self.n, self.got if isinstance(self.got, (tuple, list)) else (self.got,)
        terms = tuple((i, 0) for i in range(1 + len(got)))
        sent, self.keep = combine(((n, BF, terms), (n, F32, terms)), self.keep, *got)
        return sent

    def lines(self):
        return self.keep[0, -LINES : 3 * VECTORS - LINES].reshape(VECTORS, D)

    def low(self, sent):
        self.got = move(sent, {1: 0, 3: 2})

    def high(self):
        self.got = move(self.add(), {2: 0})
        self.keep, self.got = fold(self.keep, self.got, self.way.rest)


class TailScatter:
    def __init__(self, keep, send, way, me):
        self.way, self.keep, self.n, self.me = way, keep, keep.shape[0] // 24, me
        self.got = flip(send, way.core)

    def near(self):
        n = 6 * self.n
        plan = [(n, BF, ((0, first), (1, first))) for first in (0, n, 2 * n, 3 * n)]
        a, self.a, b, self.b = combine(plan, self.keep, self.got)
        self.a_got, self.b_got = flip(a, self.way.y), flip(b, self.way.x)

    def next(self):
        n = 3 * self.n
        plan = [(n, BF, ((0, 0), (1, n))), (n, F32, ((0, n), (1, 0)))]
        plan += [(n, BF, ((2, 0), (3, n))), (n, F32, ((2, n), (3, 0)))]
        a, self.a, b, self.b = combine(plan, self.a, self.a_got, self.b, self.b_got)
        self.a_got, self.b_got = flip(a, self.way.x), flip(b, self.way.y)

    def low(self, *head):
        self.keep, sent = targets(self.me, self.a, self.a_got, self.b, self.b_got, *head)
        self.got = flip(sent, self.way.low)

    def high(self):
        self.keep, self.got = fold(self.keep, self.got, [self.way.high] + self.way.rest)


def fold(keep, got, steps):
    for way in steps:
        half = keep.shape[0] // 2
        plan = ((half, BF, ((0, half), (1, half))), (half, F32, ((0, 0), (1, 0))))
        sent, keep = combine(plan, keep, got)
        got = flip(sent, way)
    return keep, got


def shards(inputs, items, routes, slots, cotangent, params, momentum, average):
    fsdp, dp = lax.axis_size(FSDP), lax.axis_size(DP)
    devices = fsdp * dp
    share = params.shape[1]
    rows = share // LANES
    padded = -(-(rows + 1) // 32) * 32
    step_rate = RATE_BASE / math.sqrt(CELLS * devices)
    way = ways()
    own = lax.axis_index(DP) * fsdp + lax.axis_index(FSDP)
    me = jnp.stack([own, own % (devices // 4), own // (devices // 4)]).astype(jnp.int32)

    def share_of(flat):
        return jnp.pad(flat.astype(BF).reshape(1, rows, LANES), ((0, 0), (0, padded - rows), (0, 0)))

    one = Gather(share_of(params[0]), way, me)
    one.far()
    two = Gather(share_of(tie(params[1], one.others[1])), way, me)
    masks, places = [], []
    for b in range(BLOCKS):
        masks.append(window_masks(items.reshape(CELLS), b % 2 == 1))
        places.append(slot_places(routes[b].reshape(CELLS), slots[b].reshape(CELLS)))

    hidden_zero = inputs.reshape(CELLS, D)
    one.levels()
    one.near()
    two.own = tie(two.own, one.head)
    two.high()
    one.got[0] = tie(one.got[0], *masks)
    two.other, *one.got = sync(two.other, *one.got)
    one.near_core()
    one.last()
    two.low()
    one.head_parts[0] = tie(one.head_parts[0], two.pair, *one.joined, *one.parts)
    w, rest = unpack_head(me, one.head_parts, one.head_runs, rows, devices)
    h_zero, *attn_zero = attn_fwd(False, hidden_zero, w.vec, w.w_in, w.w_out, w.bias, masks[0])
    h_zero, two.over = sync(h_zero, two.over)
    two.levels()
    two.near()
    one.last_got = tie(one.last_got, two.head)
    one.last_core()
    w1, w2 = unpack_tail(me, tie(rest, two.head), one.parts, one.runs, rows, devices)
    w_zero = w._replace(w1=w1, w2=w2)
    w = w_zero
    hidden_one, *moe_zero = moe_fwd(h_zero, w.vec, w.w1, w.w2, w.b1, w.router, w.router_bias, places[0], F32)

    hidden_one, *two.got = sync(hidden_one, *two.got)
    two.near_core()
    two.last()
    two.head_parts[0] = tie(two.head_parts[0], *two.joined, *two.parts)
    w, rest = unpack_head(me, two.head_parts, two.head_runs, rows, devices)
    h_one, *attn_one = attn_fwd(True, hidden_one, w.vec, w.w_in, w.w_out, w.bias, masks[1])
    h_one, *two.last_got = sync(h_one, *two.last_got)
    two.last_core()
    w1, w2 = unpack_tail(me, rest, two.parts, two.runs, rows, devices)
    w_one = w._replace(w1=w1, w2=w2)
    w = w_one
    outputs, *moe_one = moe_fwd(h_one, w.vec, w.w1, w.w2, w.b1, w.router, w.router_bias, places[1], BF)

    gradient = cotangent.reshape(CELLS, D)
    wn, qkv, mixed, attn = attn_one
    normed_two, *saved = moe_one
    dw1, dw2, db1, small_moe, g_pre, gate_grad = moe_bwd(gradient, w.w2, places[1], saved)
    keep, send, rest = pack_tail(me, dw1, dw2, tail_runs(way), rows, devices, padded)
    tail_one = TailScatter(keep, send, way, me)
    g_two = middle_bwd(w.vec, w.w1, places[1][0], tie(g_pre, send), gate_grad)
    g_two, tail_one.got = sync(g_two, tail_one.got)
    tail_one.near()
    g_one, g_qkv, dw_out, dbias, drouter, small_mid = attn_bwd(
        True, gradient, h_one, w.vec, w.w_out, normed_two, gate_grad, mixed, tie(g_two, tail_one.a), qkv, attn
    )
    gradient, dw_in, small_attn = proj_bwd(True, g_one, hidden_one, w.vec, w.w_in, wn, g_qkv)
    small = (small_moe, small_mid, small_attn, drouter, db1, dbias)
    keep, send = pack_head(me, small, dw_in, dw_out, rest, head_runs(way), rows, devices, padded)
    send, tail_one.a_got, tail_one.b_got, gradient = sync(send, tail_one.a_got, tail_one.b_got, gradient)
    head_one = HeadScatter(keep, send, way)
    tail_one.next()

    w = w_zero
    wn, qkv, mixed, attn = attn_zero
    normed_two, *saved = moe_zero
    gradient = tie(gradient, tail_one.a)
    dw1, dw2, db1, small_moe, g_pre, gate_grad = moe_bwd(gradient, w.w2, places[0], saved)
    g_pre, dw2, head_one.got, tail_one.a_got, tail_one.b_got = sync(
        g_pre, dw2, head_one.got, tail_one.a_got, tail_one.b_got
    )
    head_one.near()
    tail_one.low()
    keep, send, rest = pack_tail(me, dw1, tie(dw2, head_one.keep, tail_one.keep), tail_runs(way), rows, devices, padded)
    tail_zero = TailScatter(keep, send, way, me)
    g_two = middle_bwd(w.vec, w.w1, places[0][0], tie(g_pre, send), gate_grad)
    g_two, tail_zero.got = sync(g_two, tail_zero.got)
    tail_zero.near()
    g_one, g_qkv, dw_out, dbias, drouter, small_mid = attn_bwd(
        False, gradient, h_zero, w.vec, w.w_out, normed_two, gate_grad, mixed, tie(g_two, tail_zero.a), qkv, attn
    )
    g_qkv, tail_one.got, head_one.got = sync(g_qkv, tail_one.got, head_one.got)
    head_one.next()
    tail_one.high()
    gradient, dw_in, small_attn = proj_bwd(
        False, tie(g_one, head_one.keep, tail_one.keep), hidden_zero, w.vec, w.w_in, wn, g_qkv
    )
    small = (small_moe, small_mid, small_attn, drouter, db1, dbias)
    keep, send = pack_head(me, small, dw_in, dw_out, rest, head_runs(way), rows, devices, padded)
    send, tail_zero.a_got, tail_zero.b_got, head_one.got, tail_one.got = sync(
        send, tail_zero.a_got, tail_zero.b_got, head_one.got, tail_one.got
    )

    head_zero = HeadScatter(keep, send, way)
    tail_zero.next()
    head_zero.plane()
    head_one.add()
    tail_zero.low(head_one.keep)
    sent = head_zero.add()
    head_zero.low(sent)
    vector_grads = jnp.stack([head_zero.lines(), head_one.lines()])
    got = flip(vector_grads, way.low)
    tail_zero.high()
    vector_grads = vector_grads + got
    head_zero.keep = tie(head_zero.keep, vector_grads)
    head_zero.high()
    for step in [way.high] + way.rest:
        vector_grads = vector_grads + flip(vector_grads, step)
    grads_zero = finish(me, rows, head_zero, tail_zero)
    grads_one = finish(me, rows, tail_zero, tail_one)
    grad_all = jnp.stack([grads_zero.reshape(-1), grads_one.reshape(-1)])
    new_momentum = MOMENTUM_DECAY * momentum + grad_all
    new_params = params - step_rate * (grad_all + MOMENTUM_DECAY * new_momentum)
    new_average = AVERAGE_DECAY * average + (1.0 - AVERAGE_DECAY) * new_params
    return (
        outputs.reshape(1, CELLS, D),
        gradient.reshape(1, CELLS, D),
        new_params,
        new_momentum,
        new_average,
        vector_grads,
    )


def solution(mesh):
    both = (DP, FSDP)
    canvas, vector = P(both), P(None, both)
    return jax.shard_map(
        shards,
        mesh=mesh,
        in_specs=(canvas, canvas, vector, vector, canvas, vector, vector, vector),
        out_specs=(canvas, canvas, vector, vector, vector, P()),
        check_vma=False,
    )
```
